32 devices in a mesh: dp: 16 (over z, y, x), tensor: 2 (over core).
Axes of the slice: x: 2, y: 2, z: 4, core: 2. Of those that a mesh axis runs over, the one named last changes fastest.
Arguments:
- tokens: bfloat16 [4096, 2048], P(('dp', 'tensor')), may hold values from -6 to 6
- w_query: bfloat16 [2048, 2048], P('dp', 'tensor'), may hold values from -0.125 to 0.125
- key_weight: bfloat16 [2048, 1024], P('dp', 'tensor'), may hold values from -0.125 to 0.125
- value_weight: bfloat16 [2048, 1024], P('dp', 'tensor'), may hold values from -0.125 to 0.125
- w_out: bfloat16 [2048, 2048], P('tensor', 'dp'), may hold values from -0.375 to 0.375
- gain_attn: bfloat16 [2048], P('dp'), may hold values from 0.25 to 1.75
- w_gate: bfloat16 [2048, 8192], P('dp', 'tensor'), may hold values from -0.125 to 0.125
- w_up: bfloat16 [2048, 8192], P('dp', 'tensor'), may hold values from -0.125 to 0.125
- w_down: bfloat16 [8192, 2048], P('tensor', 'dp'), may hold values from -0.09375 to 0.09375
- gain_mlp: bfloat16 [2048], P('dp'), may hold values from 0.25 to 1.75
- cotangent: bfloat16 [4096, 2048], P(('dp', 'tensor')), may hold values from -6 to 6
- lengths: int32 [16], replicated, may hold values from 160 to 256, as said below
- seq_of_group: int32 [16], P('dp'), may hold values from 0 to 15, each once
Outputs:
- output: bfloat16 [4096, 2048], P(('dp', 'tensor'))
- grad_tokens: float32 [4096, 2048], P(('dp', 'tensor'))
- grad_w_query: float32 [2048, 2048], P('dp', 'tensor')
- grad_w_key: float32 [2048, 1024], P('dp', 'tensor')
- grad_w_value: float32 [2048, 1024], P('dp', 'tensor')
- grad_w_out: float32 [2048, 2048], P('tensor', 'dp')
- grad_gain_attn: float32 [2048], P('dp')
- grad_w_gate: float32 [2048, 8192], P('dp', 'tensor')
- grad_w_up: float32 [2048, 8192], P('dp', 'tensor')
- grad_w_down: float32 [8192, 2048], P('tensor', 'dp')
- grad_gain_mlp: float32 [2048], P('dp')
The draws below stay inside these ranges and needn't reach their ends.
Inputs may be any that keep to these rules, and one draw needn't show every extreme that they name: `lengths`: every length lies in 160 to 256; both ends are reached in every draw. `seq_of_group`: A permutation of 0 to 15.
All inputs are finite; a program needn't handle non-finite values.
Results may differ from the reference program's by a relative error of at most 0.015.
Values may be sent and summed in bfloat16 or wider, within the bound.
A program may use at most 320 MiB of HBM per device.

```python
import math
import jax
import jax.numpy as jnp
from jax import lax

MODEL_WIDTH = 2048
QUERY_HEADS = 8
KEY_VALUE_HEADS = 4
HEAD_SIZE = 256
FF = 8192
SEQUENCE_SLOTS = 256
SEQS = 16
TOKENS = 4096
MIN_LEN = 160


def draw_lengths(key, part):
    key = jax.random.fold_in(key, 11)
    first_key, second_key = jax.random.split(key)
    values = jax.random.randint(first_key, (SEQS,), MIN_LEN, SEQUENCE_SLOTS + 1)
    order = jax.random.permutation(second_key, SEQS)
    values = values.at[order[0]].set(SEQUENCE_SLOTS).at[order[1]].set(MIN_LEN)
    return values.astype(jnp.int32)


def block_scale(key, shape, shards, low, high):
    factor_of = 1.0
    for position, blocks in shards:
        draws = jax.random.uniform(jax.random.fold_in(jax.random.fold_in(key, 6), position), (blocks,), jnp.float32, low / len(shards), high / len(shards))
        factor_of = factor_of * jnp.repeat(jnp.exp(draws), shape[position] // blocks).reshape((-1,) + (1,) * (len(shape) - 1 - position))
    return factor_of


def scatter_about(key, dims, spread, bound, cuts=(), held_as=jnp.bfloat16):
    drawn = spread * jax.random.normal(key, dims, jnp.float32)
    if cuts:
        drawn = drawn * block_scale(key, dims, cuts, -0.22, 0.18)
    return jnp.clip(drawn, -bound, bound).astype(held_as)


def setup_inputs(seed: int = 0) -> dict:
    streams_of = jax.random.split(jax.random.key(seed), 14)
    return {
        "tokens": scatter_about(streams_of[0], (TOKENS, MODEL_WIDTH), 1.0, 6.0, ((0, 32),)),
        "w_query": scatter_about(streams_of[1], (MODEL_WIDTH, QUERY_HEADS * HEAD_SIZE), MODEL_WIDTH ** -0.5, 0.125, ((0, 16), (1, 2))),
        "key_weight": scatter_about(streams_of[2], (MODEL_WIDTH, KEY_VALUE_HEADS * HEAD_SIZE), MODEL_WIDTH ** -0.5, 0.125, ((0, 16), (1, 2))),
        "value_weight": scatter_about(streams_of[3], (MODEL_WIDTH, KEY_VALUE_HEADS * HEAD_SIZE), MODEL_WIDTH ** -0.5, 0.125, ((0, 16), (1, 2))),
        "w_out": scatter_about(streams_of[4], (QUERY_HEADS * HEAD_SIZE, MODEL_WIDTH), (QUERY_HEADS * HEAD_SIZE // 8) ** -0.5, 0.375, ((0, 2), (1, 16))),
        "gain_attn": jnp.clip(1.0 + 0.15 * jax.random.normal(streams_of[5], (MODEL_WIDTH,), jnp.float32), 0.25, 1.75).astype(jnp.bfloat16),
        "w_gate": scatter_about(streams_of[6], (MODEL_WIDTH, FF), MODEL_WIDTH ** -0.5, 0.125, ((0, 16), (1, 2))),
        "w_up": scatter_about(streams_of[7], (MODEL_WIDTH, FF), MODEL_WIDTH ** -0.5, 0.125, ((0, 16), (1, 2))),
        "w_down": scatter_about(streams_of[8], (FF, MODEL_WIDTH), (FF // 2) ** -0.5, 0.09375, ((0, 2), (1, 16))),
        "gain_mlp": jnp.clip(1.0 + 0.15 * jax.random.normal(streams_of[9], (MODEL_WIDTH,), jnp.float32), 0.25, 1.75).astype(jnp.bfloat16),
        "cotangent": scatter_about(streams_of[10], (TOKENS, MODEL_WIDTH), 1.0, 6.0, ((0, 32),)),
        "lengths": draw_lengths(jax.random.fold_in(streams_of[13], 71), 0),
        "seq_of_group": jax.random.permutation(streams_of[12], SEQS).astype(jnp.int32),
    }


EPS = 1e-06
THETA = 1000042.0

@jax.custom_vjp
def lower_precision(v):
    return lax.optimization_barrier(v.astype(jnp.bfloat16)).astype(jnp.float32)

@jax.custom_vjp
def lower_precision_backward(v):
    return v

def low_keep(v):
    return (lower_precision(v), None)

def low_pass(kept, grad):
    return (grad,)

def back_keep(v):
    return (v, None)

def back_low(kept, grad):
    return (lower_precision(grad),)
lower_precision.defvjp(low_keep, low_pass)
lower_precision_backward.defvjp(back_keep, back_low)

def rope_tables(count, head_dim):
    half = head_dim // 2
    index = jnp.arange(half, dtype=jnp.float32)
    freqs = jnp.exp(index * (-2.0 * math.log(THETA) / head_dim))
    angles = jnp.arange(count, dtype=jnp.float32)[:, None] * freqs[None, :]
    return (jnp.cos(angles)[:, None, :], jnp.sin(angles)[:, None, :])

def apply_rotary(values, cosine_table, rotary_sine_table):
    half = values.shape[-1] // 2
    first = values[..., :half]
    second = values[..., half:]
    return jnp.concatenate([first * cosine_table - second * rotary_sine_table, second * cosine_table + first * rotary_sine_table], -1)

def rms_scale(values, gain):
    factor = lax.rsqrt(lax.optimization_barrier(jnp.mean(values * values, -1, keepdims=True)) + EPS)
    return values * factor * gain

def layer(inputs, w_query, key_weight, value_weight, w_out, gain_attn, w_gate, w_up, w_down, gain_mlp, seq_length):
    highest_precision = lax.Precision.HIGHEST
    row_ids = jnp.arange(SEQUENCE_SLOTS, dtype=jnp.int32)
    key_allowed = (row_ids[None, :] <= row_ids[:, None]) & (row_ids[None, :] < seq_length)
    cosine_table, rotary_sine_table = rope_tables(SEQUENCE_SLOTS, HEAD_SIZE)
    attention_normed_input = lower_precision(rms_scale(inputs, gain_attn))
    query_rows = lower_precision(apply_rotary(lower_precision_backward(jnp.dot(attention_normed_input, w_query, precision=highest_precision)).reshape(SEQUENCE_SLOTS, QUERY_HEADS, HEAD_SIZE), cosine_table, rotary_sine_table))
    key_row_block = lower_precision(apply_rotary(lower_precision_backward(jnp.dot(attention_normed_input, key_weight, precision=highest_precision)).reshape(SEQUENCE_SLOTS, KEY_VALUE_HEADS, HEAD_SIZE), cosine_table, rotary_sine_table))
    value_row_block = lower_precision(lower_precision_backward(jnp.dot(attention_normed_input, value_weight, precision=highest_precision))).reshape(SEQUENCE_SLOTS, KEY_VALUE_HEADS, HEAD_SIZE)
    grouped_query_rows = query_rows.reshape(SEQUENCE_SLOTS, KEY_VALUE_HEADS, QUERY_HEADS // KEY_VALUE_HEADS, HEAD_SIZE)
    scores = lower_precision_backward(jnp.einsum('skgd,tkd->kgst', grouped_query_rows, key_row_block, precision=highest_precision) * HEAD_SIZE ** (-0.5))
    scores = jnp.where(key_allowed, scores, -1e+30)
    row_max = lax.optimization_barrier(jnp.max(scores, -1, keepdims=True))
    row_exp = jnp.exp(scores - row_max)
    softmax_probs = row_exp / lax.optimization_barrier(jnp.sum(row_exp, -1, keepdims=True))
    attended = jnp.einsum('kgst,tkd->skgd', lower_precision(softmax_probs), value_row_block, precision=highest_precision).reshape(SEQUENCE_SLOTS, QUERY_HEADS * HEAD_SIZE)
    attn_out = lower_precision_backward(jnp.dot(lower_precision(lower_precision_backward(attended)), w_out, precision=highest_precision))
    middle = inputs + attn_out
    normed_mlp = lower_precision(rms_scale(middle, gain_mlp))
    gate_lin = lower_precision_backward(jnp.dot(normed_mlp, w_gate, precision=highest_precision))
    up_lin = lower_precision_backward(jnp.dot(normed_mlp, w_up, precision=highest_precision))
    hidden = lower_precision(gate_lin * jax.nn.sigmoid(gate_lin) * up_lin)
    mlp_out = lower_precision_backward(jnp.dot(hidden, w_down, precision=highest_precision))
    return middle + mlp_out

def reference(tokens, w_query, key_weight, value_weight, w_out, gain_attn, w_gate, w_up, w_down, gain_mlp, cotangent, lengths, seq_of_group):
    params = tuple((weight.astype(jnp.float32) for weight in (w_query, key_weight, value_weight, w_out, gain_attn, w_gate, w_up, w_down, gain_mlp)))
    seq_lengths = jnp.take(lengths, seq_of_group).astype(jnp.int32)
    blocks = tokens.astype(jnp.float32).reshape(SEQS, SEQUENCE_SLOTS, MODEL_WIDTH)
    cot_blocks = cotangent.astype(jnp.float32).reshape(SEQS, SEQUENCE_SLOTS, MODEL_WIDTH)

    def visit(totals, element):
        block, cot_block, seq_length = element
        rows_valid = (jnp.arange(SEQUENCE_SLOTS, dtype=jnp.int32) < seq_length).astype(jnp.float32)[:, None]
        result, pull = jax.vjp(lambda inputs, *weights: layer(inputs, *weights, seq_length), block, *params)
        grads = pull(cot_block * rows_valid)
        totals = tuple((total + grad for total, grad in zip(totals, grads[1:])))
        return (totals, (result, grads[0]))
    zeros = tuple((jnp.zeros_like(param) for param in params))
    totals, (results, grad_in) = lax.scan(visit, zeros, (blocks, cot_blocks, seq_lengths))
    return (results.reshape(TOKENS, MODEL_WIDTH).astype(jnp.bfloat16), grad_in.reshape(TOKENS, MODEL_WIDTH), totals[0], totals[1], totals[2], totals[3], totals[4], totals[5], totals[6], totals[7], totals[8])
```

```python
import functools
import math

import jax
import jax.numpy as jnp
from jax import lax
from jax.experimental import pallas as pl
from jax.experimental.pallas import tpu as pltpu
from jax.sharding import PartitionSpec as P

HEAD_SIZE = 256
EPS = 1e-06
THETA = 1000042.0
LINE = 4
MESH = pl.DeviceIdType.MESH
BF16 = jnp.bfloat16
F32 = jnp.float32
MB = 1024 * 1024


def rope_tables(count, head_dim):
    half = head_dim // 2
    index = jnp.arange(half, dtype=jnp.float32)
    freqs = jnp.exp(index * (-2.0 * math.log(THETA) / head_dim))
    angles = jnp.arange(count, dtype=jnp.float32)[:, None] * freqs[None, :]
    return (jnp.cos(angles)[:, None, :], jnp.sin(angles)[:, None, :])


def apply_rotary(values, cosine_table, rotary_sine_table):
    half = values.shape[-1] // 2
    first = values[..., :half]
    second = values[..., half:]
    return jnp.concatenate(
        [
            first * cosine_table - second * rotary_sine_table,
            second * cosine_table + first * rotary_sine_table,
        ],
        -1,
    )


def rotate_back(grads, cosine_table, rotary_sine_table):
    return apply_rotary(grads, cosine_table, -rotary_sine_table)


def dot_nn(left, right):
    return jnp.dot(left, right, preferred_element_type=F32)


def dot_nt(left, right):
    return lax.dot_general(left, right, (((1,), (1,)), ((), ())), preferred_element_type=F32)


def dot_tn(left, right):
    return lax.dot_general(left, right, (((0,), (0,)), ((), ())), preferred_element_type=F32)


def gather_rows(values):
    return lax.all_gather(values, "tensor", axis=0, tiled=True)


def sum_rows(values):
    return lax.psum_scatter(values, "tensor", scatter_dimension=0, tiled=True)


def norm_back(inputs, factor, gain, upstream):
    scaled = upstream * gain
    grad_in = factor * scaled - inputs * factor**3 * jnp.mean(scaled * inputs, -1, keepdims=True)
    return (grad_in, jnp.sum(upstream * inputs * factor, 0))


class Place:
    def __init__(self, plane):
        self.d = lax.axis_index("dp")
        self.t = lax.axis_index("tensor")
        self.plane = plane
        self.z = lax.div(self.d, plane)
        self.p = lax.rem(self.d, plane)
        if plane == 4:
            x = lax.rem(self.p, 2)
            y = lax.div(self.p, 2)
            self.px = 2 * y + 1 - x
            self.py = 2 * (1 - y) + x
            self.pd = 2 * (1 - y) + 1 - x

    def at(self, z, p):
        return (z * self.plane + p, self.t)

    def sibling(self):
        return (self.d, 1 - self.t)


def remote(src, dst, send, recv, device):
    return pltpu.make_async_remote_copy(
        src_ref=src, dst_ref=dst, send_sem=send, recv_sem=recv, device_id=device, device_id_type=MESH
    )


def arrival(ref, sem):
    pltpu.make_async_copy(ref, ref, sem).wait()


def greet_all(me, count):
    barrier = pltpu.get_barrier_semaphore()
    for step in range(1, count):
        pl.semaphore_signal(
            barrier, inc=1, device_id=(lax.rem(me.d + step, count), me.t), device_id_type=MESH
        )
    pl.semaphore_signal(barrier, inc=1, device_id=me.sibling(), device_id_type=MESH)
    pl.semaphore_wait(barrier, count)


def greet_line(me):
    barrier = pltpu.get_barrier_semaphore()
    for step in range(1, LINE):
        pl.semaphore_signal(
            barrier, inc=1, device_id=me.at(lax.rem(me.z + step, LINE), me.p), device_id_type=MESH
        )
    pl.semaphore_signal(barrier, inc=1, device_id=me.sibling(), device_id_type=MESH)
    pl.semaphore_wait(barrier, LINE)


def reach(me, way, k):
    return (me.z >= k, me.z - k) if way == 0 else (me.z + k < LINE, me.z + k)


class Chain:
    def __init__(self, me, first, held, send, recv):
        self.me, self.first, self.held, self.send, self.recv = me, first, held, send, recv

    def copy(self, way, k):
        me = self.me
        _, origin = reach(me, way, k)
        target = me.z + 1 if way == 0 else me.z - 1
        src = self.first if k == 0 else self.held(origin)
        return remote(
            src, self.held(origin), self.send.at[way, k], self.recv.at[way, k + 1], me.at(target, me.p)
        )

    def goes(self, way, k):
        have, _ = reach(self.me, way, k)
        ahead, _ = reach(self.me, 1 - way, 1)
        return jnp.logical_and(have, ahead)

    def start(self, way, k):
        if k < LINE - 1:

            @pl.when(self.goes(way, k))
            def _():
                self.copy(way, k).start()

    def wait_block(self, way, k):
        _, origin = reach(self.me, way, k)
        arrival(self.held(origin), self.recv.at[way, k])

    def finish(self):
        for way in range(2):
            for k in range(LINE - 1):

                @pl.when(self.goes(way, k))
                def _():
                    self.copy(way, k).wait_send()


class PlaneGather:
    def __init__(self, me, job, held, rows, send, recv):
        self.me, self.job, self.held, self.send, self.recv = me, job, held, send, recv
        self.half = rows // 2

    def piece(self, z, p, half):
        return self.held.at[z * self.me.plane + p, pl.ds(half * self.half, self.half)]

    def copy(self, z, kind, first=None):
        me = self.me
        if me.plane != 4:
            ref = first if first is not None else self.held.at[z * me.plane + me.p]
            target = lax.rem(me.p + kind + 1, me.plane)
            dst = self.held.at[z * me.plane + me.p]
        else:
            owner = (me.p, me.p, me.p, me.p, me.px, me.py)[kind]
            half = (0, 1, 1, 0, 0, 1)[kind]
            target = (me.px, me.px, me.py, me.py, me.py, me.px)[kind]
            dst = self.piece(z, owner, half)
            ref = dst if first is None else first.at[pl.ds(half * self.half, self.half)]
        return remote(
            ref, dst, self.send.at[self.job, z, kind], self.recv.at[self.job, z, kind], me.at(me.z, target)
        )

    def start(self, z, first=None):
        kinds = (0, 2, 1, 3) if self.me.plane == 4 else range(self.me.plane - 1)
        for kind in kinds:
            self.copy(z, kind, first).start()

    def forward(self, z):
        if self.me.plane == 4:
            self.copy(z, 0).wait_recv()
            self.copy(z, 4).start()
            self.copy(z, 2).wait_recv()
            self.copy(z, 5).start()

    def finish(self):
        kinds = 6 if self.me.plane == 4 else self.me.plane - 1
        for z in range(LINE):
            for kind in range(kinds):
                copy = self.copy(z, kind)
                if self.me.plane != 4 or kind not in (0, 2):
                    copy.wait_recv()
                copy.wait_send()


def gather_kernel(
    count, a_ref, w_ref, gain_ref, tok_ref, dm_ref, a_all, w_all, gain_all, tok_all, dm_all,
    chain_send, chain_recv, part_send, part_recv, plane_send, plane_recv, gain_send, gain_recv,
    pair_send, pair_recv, local_sem,
):
    plane = count // LINE
    me = Place(plane)
    rows = a_ref.shape[0]
    local = [
        pltpu.make_async_copy(a_ref, a_all.at[me.d], local_sem.at[0]),
        pltpu.make_async_copy(w_ref.at[me.z], w_all.at[me.d], local_sem.at[1]),
        pltpu.make_async_copy(gain_ref, gain_all.at[me.d], local_sem.at[2]),
        pltpu.make_async_copy(tok_ref, tok_all.at[me.t], local_sem.at[3]),
        pltpu.make_async_copy(dm_ref, dm_all.at[me.z, me.t], local_sem.at[4]),
    ]
    for copy in local:
        copy.start()
    greet_all(me, count)

    attn = Chain(me, a_ref, lambda z: a_all.at[z * plane + me.p], chain_send.at[0], chain_recv.at[0])
    dms = Chain(me, dm_ref, lambda z: dm_all.at[z, me.t], chain_send.at[1], chain_recv.at[1])
    planes = (
        PlaneGather(me, 0, a_all, rows, plane_send, plane_recv),
        PlaneGather(me, 1, w_all, rows, plane_send, plane_recv),
    )

    def part(way, k):
        _, target = reach(me, 1 - way, k)
        return remote(
            w_ref.at[target], w_all.at[me.d], part_send.at[way, k], part_recv.at[way, k],
            me.at(target, me.p),
        )

    def pair(z, first=None):
        src = dm_all.at[z, me.t] if first is None else first
        return remote(src, dm_all.at[z, me.t], pair_send.at[z], pair_recv.at[z], me.sibling())

    for way in range(2):
        attn.start(way, 0)
    planes[0].start(me.z, a_ref)
    for k in range(1, LINE):
        for way in range(2):

            @pl.when(reach(me, 1 - way, k)[0])
            def _():
                part(way, k).start()

    def give_gain(step):
        target = lax.rem(me.d + step, count)
        return remote(
            gain_ref, gain_all.at[me.d], gain_send.at[step], gain_recv.at[step], (target, me.t)
        )

    for step in range(1, count):
        give_gain(step).start()
    tokens = remote(tok_ref, tok_all.at[me.t], pair_send.at[LINE], pair_recv.at[LINE], me.sibling())
    tokens.start()
    planes[1].start(me.z, w_ref.at[me.z])
    for way in range(2):
        dms.start(way, 0)
    pair(me.z, dm_ref).start()

    for k in range(1, LINE + 1):
        if k < LINE:
            for way in range(2):
                have, z = reach(me, way, k)

                @pl.when(have)
                def _():
                    attn.wait_block(way, k)
                    attn.start(way, k)
                    planes[0].start(z)
                    arrival(w_all.at[z * plane + me.p], part_recv.at[way, k])
                    planes[1].start(z)
                    dms.wait_block(way, k)
                    dms.start(way, k)
                    pair(z).start()

        if k == 1:
            planes[0].forward(me.z)
            planes[1].forward(me.z)
        else:
            for way in range(2):
                have, z = reach(me, way, k - 1)

                @pl.when(have)
                def _():
                    planes[0].forward(z)
                    planes[1].forward(z)

    attn.finish()
    dms.finish()
    for k in range(1, LINE):
        for way in range(2):

            @pl.when(reach(me, 1 - way, k)[0])
            def _():
                part(way, k).wait_send()

    for step in range(1, count):
        give_gain(step).wait()
    tokens.wait()
    for z in range(LINE):
        pair(z).wait()
    for job in planes:
        job.finish()
    for copy in local:
        copy.wait()


ANY = pl.BlockSpec(memory_space=pl.ANY)
DMA = pltpu.SemaphoreType.DMA


def gather_all(count, attn, mlp, gains, tokens, dm):
    rows, width = attn.shape
    kinds = max(6, count // LINE - 1)
    return pl.pallas_call(
        functools.partial(gather_kernel, count),
        name="gather_all",
        out_shape=(
            jax.ShapeDtypeStruct((count, rows, width), BF16),
            jax.ShapeDtypeStruct((count, rows, width), BF16),
            jax.ShapeDtypeStruct((count,) + gains.shape, gains.dtype),
            jax.ShapeDtypeStruct((2,) + tokens.shape, BF16),
            jax.ShapeDtypeStruct((LINE, 2) + dm.shape, BF16),
        ),
        in_specs=[ANY] * 5,
        out_specs=(ANY,) * 5,
        scratch_shapes=[
            DMA((2, 2, LINE)), DMA((2, 2, LINE)), DMA((2, LINE)), DMA((2, LINE)),
            DMA((2, LINE, kinds)), DMA((2, LINE, kinds)), DMA((count,)), DMA((count,)),
            DMA((LINE + 1,)), DMA((LINE + 1,)), DMA((5,)),
        ],
        compiler_params=pltpu.CompilerParams(collective_id=0, has_side_effects=True),
    )(attn, mlp, gains, tokens, dm)


def line_gather_kernel(plane, h_ref, h_all, chain_send, chain_recv, pair_send, pair_recv, local_sem):
    me = Place(plane)
    local = pltpu.make_async_copy(h_ref, h_all.at[me.z, me.t], local_sem)
    local.start()
    greet_line(me)
    chain = Chain(me, h_ref, lambda z: h_all.at[z, me.t], chain_send, chain_recv)

    def pair(z, first=None):
        src = h_all.at[z, me.t] if first is None else first
        return remote(src, h_all.at[z, me.t], pair_send.at[z], pair_recv.at[z], me.sibling())

    for way in range(2):
        chain.start(way, 0)
    pair(me.z, h_ref).start()
    for k in range(1, LINE):
        for way in range(2):
            have, z = reach(me, way, k)

            @pl.when(have)
            def _():
                chain.wait_block(way, k)
                chain.start(way, k)
                pair(z).start()

    chain.finish()
    for z in range(LINE):
        pair(z).wait()
    local.wait()


def line_gather(count, values):
    return pl.pallas_call(
        functools.partial(line_gather_kernel, count // LINE),
        name="line_gather",
        out_shape=jax.ShapeDtypeStruct((LINE, 2) + values.shape, values.dtype),
        in_specs=[ANY],
        out_specs=ANY,
        scratch_shapes=[DMA((2, LINE)), DMA((2, LINE)), DMA((LINE,)), DMA((LINE,)), DMA],
        compiler_params=pltpu.CompilerParams(collective_id=1, has_side_effects=True),
    )(values)


def line_sum_kernel(
    plane, part_ref, total_ref, own, from_pair, from_line, pair_send, pair_recv, line_send, line_recv, local_sem
):
    me = Place(plane)
    jobs = part_ref.shape[0]

    def load(job, z):
        return pltpu.make_async_copy(part_ref.at[job, z, me.t], own.at[job, z], local_sem.at[job, z])

    def pair(job, z):
        return remote(
            part_ref.at[job, z, 1 - me.t], from_pair.at[job, z], pair_send.at[job, z],
            pair_recv.at[job, z], me.sibling(),
        )

    def pass_on(job, way, k):
        _, target = reach(me, 1 - way, k)
        ahead = me.z + 1 if way == 0 else me.z - 1
        return remote(
            own.at[job, target], from_line.at[job, way, k - 1], line_send.at[job, way, k],
            line_recv.at[job, way, k - 1], me.at(ahead, me.p),
        )

    for job in range(jobs):
        for z in range(LINE):
            load(job, z).start()
    greet_line(me)
    order = [(way, k) for k in range(LINE - 1, 0, -1) for way in range(2)]
    for job in range(jobs):
        for way, k in order:
            have, z = reach(me, 1 - way, k)

            @pl.when(have)
            def _():
                pair(job, z).start()

        pair(job, me.z).start()
    for job in range(jobs):
        for way, k in order:
            have, z = reach(me, 1 - way, k)

            @pl.when(have)
            def _():
                load(job, z).wait()
                pair(job, z).wait_recv()
                both = own[job, z].astype(F32) + from_pair[job, z].astype(F32)
                own[job, z] = both.astype(BF16)
                behind, _ = reach(me, way, 1)

                @pl.when(behind)
                def _():
                    arrival(from_line.at[job, way, k], line_recv.at[job, way, k])
                    own[job, z] = (both + from_line[job, way, k].astype(F32)).astype(BF16)

                pass_on(job, way, k).start()

        load(job, me.z).wait()
        pair(job, me.z).wait_recv()
        total_ref[job] = own[job, me.z].astype(F32) + from_pair[job, me.z].astype(F32)
        for way in range(2):
            behind, _ = reach(me, way, 1)

            @pl.when(behind)
            def _():
                arrival(from_line.at[job, way, 0], line_recv.at[job, way, 0])
                total_ref[job] += from_line[job, way, 0].astype(F32)

    for job in range(jobs):
        for way, k in order:
            have, z = reach(me, 1 - way, k)

            @pl.when(have)
            def _():
                pass_on(job, way, k).wait_send()

        for z in range(LINE):
            pair(job, z).wait_send()


def line_sum(count, parts):
    jobs, _, _, rows, width = parts.shape
    return pl.pallas_call(
        functools.partial(line_sum_kernel, count // LINE),
        name="line_sum",
        out_shape=jax.ShapeDtypeStruct((jobs, rows, width), F32),
        in_specs=[ANY],
        out_specs=pl.BlockSpec(memory_space=pltpu.VMEM),
        scratch_shapes=[
            pltpu.VMEM((jobs, LINE, rows, width), BF16),
            pltpu.VMEM((jobs, LINE, rows, width), BF16),
            pltpu.VMEM((jobs, 2, LINE, rows, width), BF16),
            DMA((jobs, LINE)), DMA((jobs, LINE)),
            DMA((jobs, 2, LINE + 1)), DMA((jobs, 2, LINE + 1)),
            DMA((jobs, LINE)),
        ],
        compiler_params=pltpu.CompilerParams(
            collective_id=2, has_side_effects=True, vmem_limit_bytes=40 * MB
        ),
    )(parts)


def add_rows(target, terms, rows, start=0):
    step = 16

    @pl.loop(0, rows // step)
    def _(i):
        at = pl.ds(pl.multiple_of(start + i * step, step), step)
        total = terms[0][at].astype(F32)
        for term in terms[1:]:
            total += term[at].astype(F32)
        target[at] = total.astype(target.dtype)


def grad_sum_kernel(
    count, ga_ref, gw_ref, gain_ref, a_out, w_out, gain_out, own, other, first, second, from_line,
    gain_in, gain_pair, first_send, first_recv, second_send, second_recv, line_send, line_recv,
    part_send, part_recv, gain_send, gain_recv, load_sem, other_sem, local_sem,
):
    plane = count // LINE
    me = Place(plane)
    rows = a_out.shape[0]
    half = rows // 2
    grads = (ga_ref, gw_ref)
    halves = (pl.ds(0, half), pl.ds(half, half))
    square = plane == 4
    if square:
        near = (me.px, me.py)
        far = (me.py, me.px)

    def load(job, z):
        return pltpu.make_async_copy(grads[job].at[z * plane + me.p], own.at[job, z], load_sem.at[job, z])

    def load_other(job, z, i):
        return pltpu.make_async_copy(
            grads[job].at[z * plane + far[i], halves[i]], other.at[job, z, halves[i]],
            other_sem.at[job, z, i],
        )

    def give(job, z, i, which):
        if not square:
            return remote(
                grads[job].at[z * plane + lax.rem(me.p + which + 1, plane)], first.at[job, z, which],
                first_send.at[job, z, which], first_recv.at[job, z, which],
                me.at(me.z, lax.rem(me.p + which + 1, plane)),
            )
        block = (near[i], me.pd)[which]
        return remote(
            grads[job].at[z * plane + block, halves[i]], first.at[job, z, which, halves[i]],
            first_send.at[job, z, 2 * i + which], first_recv.at[job, z, 2 * i + which],
            me.at(me.z, near[i]),
        )

    def give_both(job, z, i):
        return remote(
            other.at[job, z, halves[i]], second.at[job, z, halves[i]], second_send.at[job, z, i],
            second_recv.at[job, z, i], me.at(me.z, far[i]),
        )

    def gives(job, z):
        if square:
            return [give(job, z, i, which) for which in (1, 0) for i in range(2)]
        return [give(job, z, 0, which) for which in range(plane - 1)]

    def begin(job, z):
        for copy in gives(job, z):
            copy.start()

    def middle(job, z):
        if not square:
            return
        for i in range(2):
            arrival(first.at[job, z, 1, halves[i]], first_recv.at[job, z, 2 * i + 1])
            load_other(job, z, i).wait()
            add_rows(other.at[job, z], (other.at[job, z], first.at[job, z, 1]), half, i * half)
            give_both(job, z, i).start()

    def end(job, z):
        load(job, z).wait()
        if square:
            for i in range(2):
                arrival(first.at[job, z, 0, halves[i]], first_recv.at[job, z, 2 * i])
                arrival(second.at[job, z, halves[i]], second_recv.at[job, z, i])
            terms = (first.at[job, z, 0], second.at[job, z])
        else:
            for which in range(plane - 1):
                arrival(first.at[job, z, which], first_recv.at[job, z, which])
            terms = tuple(first.at[job, z, which] for which in range(plane - 1))
        add_rows(own.at[job, z], (own.at[job, z],) + terms, rows)

    def pass_on(way, k):
        _, target = reach(me, 1 - way, k)
        ahead = me.z + 1 if way == 0 else me.z - 1
        return remote(
            own.at[0, target], from_line.at[way, k - 1], line_send.at[way, k], line_recv.at[way, k - 1],
            me.at(ahead, me.p),
        )

    def part(way, k):
        _, target = reach(me, 1 - way, k)
        return remote(
            own.at[1, target], w_out.at[me.z], part_send.at[way, k], part_recv.at[way, k],
            me.at(target, me.p),
        )

    def line(way, k, z):
        behind, _ = reach(me, way, 1)

        @pl.when(behind)
        def _():
            arrival(from_line.at[way, k], line_recv.at[way, k])
            add_rows(own.at[0, z], (own.at[0, z], from_line.at[way, k]), rows)

        pass_on(way, k).start()

    for job in range(2):
        for z in range(LINE):
            load(job, z).start()
            if square:
                for i in range(2):
                    load_other(job, z, i).start()
    greet_all(me, count)

    def give_gain(step):
        target = lax.rem(me.d + step, count)
        return remote(
            gain_ref.at[target], gain_in.at[step], gain_send.at[step], gain_recv.at[step], (target, me.t)
        )

    order = [(way, k) for k in range(LINE - 1, 0, -1) for way in range(2)] + [(0, 0)]
    events = [(job, way, k) for job in range(2) for way, k in order]

    def on(event, act):
        job, way, k = event
        have, z = reach(me, 1 - way, k)
        if k == 0:
            act(job, me.z)
        else:

            @pl.when(have)
            def _():
                act(job, z)

    lead, lag, line_lag = 4, 2, 6
    last = len(events)
    for i in range(-lead, last + line_lag):
        if 0 <= i + lead < last:
            on(events[i + lead], begin)
        if i + lead == last:
            for step in range(1, count):
                give_gain(step).start()
        if 0 <= i < last:
            on(events[i], middle)
        if 0 <= i - lag < last:
            job, way, k = events[i - lag]
            on(events[i - lag], end)
            if job == 1 and k > 0:
                on(events[i - lag], lambda job, z: part(way, k).start())
        if 0 <= i - line_lag < last:
            job, way, k = events[i - line_lag]
            if job == 0 and k > 0:
                on(events[i - line_lag], lambda job, z: line(way, k, z))

    keep = pltpu.make_async_copy(own.at[1, me.z], w_out.at[me.z], local_sem)
    keep.start()
    add_rows(a_out, (own.at[0, me.z],), rows)
    for way in range(2):

        @pl.when(reach(me, way, 1)[0])
        def _():
            arrival(from_line.at[way, 0], line_recv.at[way, 0])
            add_rows(a_out, (a_out, from_line.at[way, 0]), rows)

    total = gain_ref[me.d]
    for step in range(1, count):
        give_gain(step).wait()
        total += gain_in[step]
    gain_pair[0] = total
    swap = remote(gain_pair.at[0], gain_pair.at[1], gain_send.at[0], gain_recv.at[0], me.sibling())
    swap.start()
    swap.wait()
    gain_out[...] = gain_pair[0] + gain_pair[1]

    for way, k in order[:-1]:

        @pl.when(reach(me, 1 - way, k)[0])
        def _():
            pass_on(way, k).wait_send()
            part(way, k).wait_send()

        @pl.when(reach(me, way, k)[0])
        def _():
            arrival(w_out.at[me.z], part_recv.at[way, k])

    for job in range(2):
        for z in range(LINE):
            for copy in gives(job, z):
                copy.wait_send()
            if square:
                for i in range(2):
                    give_both(job, z, i).wait_send()
    keep.wait()


def grad_sum(count, ga, gw, gains):
    _, rows, width = ga.shape
    plane = count // LINE
    square = plane == 4
    slots = 2 if square else plane - 1
    block = (2, LINE, rows, width)
    small = (2, LINE, rows, width) if square else (1, 1, 16, 128)
    vmem = pl.BlockSpec(memory_space=pltpu.VMEM)
    return pl.pallas_call(
        functools.partial(grad_sum_kernel, count),
        name="grad_sum",
        out_shape=(
            jax.ShapeDtypeStruct((rows, width), F32),
            jax.ShapeDtypeStruct((LINE, rows, width), BF16),
            jax.ShapeDtypeStruct(gains.shape[1:], F32),
        ),
        in_specs=[ANY, ANY, vmem],
        out_specs=(vmem, ANY, vmem),
        scratch_shapes=[
            pltpu.VMEM(block, BF16),
            pltpu.VMEM(small, BF16),
            pltpu.VMEM((2, LINE, slots, rows, width), BF16),
            pltpu.VMEM(small, BF16),
            pltpu.VMEM((2, LINE, rows, width), BF16),
            pltpu.VMEM(gains.shape, F32),
            pltpu.VMEM((2,) + gains.shape[1:], F32),
            DMA((2, LINE, max(4, slots))), DMA((2, LINE, max(4, slots))),
            DMA((2, LINE, 2)), DMA((2, LINE, 2)),
            DMA((2, LINE)), DMA((2, LINE)), DMA((2, LINE)), DMA((2, LINE)),
            DMA((count,)), DMA((count,)),
            DMA((2, LINE)), DMA((2, LINE, 2)), DMA,
        ],
        compiler_params=pltpu.CompilerParams(
            collective_id=3, has_side_effects=True, vmem_limit_bytes=56 * MB
        ),
    )(ga, gw, gains)


def shards(
    tokens, w_query, key_weight, value_weight, w_out, gain_attn, w_gate, w_up, w_down, gain_mlp,
    cotangent, lengths, seq_of_group,
):
    count = lax.axis_size("dp")
    local_rows = tokens.shape[0]
    full_rows = local_rows * lax.axis_size("tensor")
    rows = w_query.shape[0]
    model = rows * count
    q_width = w_query.shape[1]
    kv_width = key_weight.shape[1]
    q_heads = q_width // HEAD_SIZE
    kv_heads = kv_width // HEAD_SIZE
    group_size = q_heads // kv_heads
    units = w_gate.shape[1] // LINE
    score_scale = HEAD_SIZE ** (-0.5)
    chosen = jnp.sum(
        jnp.where(jnp.arange(lengths.shape[0], dtype=jnp.int32) == seq_of_group[0], lengths, 0)
    )
    positions = lax.axis_index("tensor") * local_rows + jnp.arange(local_rows, dtype=jnp.int32)
    valid_rows = (positions < chosen).astype(F32)[:, None]
    row_ids = jnp.arange(full_rows, dtype=jnp.int32)
    key_allowed = (row_ids[None, :] <= row_ids[:, None]) & (row_ids[None, :] < chosen)
    cosine_table, rotary_sine_table = rope_tables(full_rows, HEAD_SIZE)
    inputs = tokens.astype(F32)
    grad_out = cotangent.astype(F32) * valid_rows

    attn_pack = jnp.concatenate([w_query, key_weight, value_weight, w_out.T], axis=1)
    down_t = w_down.T
    mlp_pack = jnp.stack(
        [
            jnp.concatenate([m[:, z * units : (z + 1) * units] for m in (w_gate, w_up, down_t)], axis=1)
            for z in range(LINE)
        ]
    )
    lanes = -rows % 128
    gains = jnp.pad(jnp.stack([gain_attn, gain_mlp]), ((0, 14), (0, lanes)))
    attn_all, mlp_all, gains_all, tokens_all, dm_all = gather_all(
        count, attn_pack, mlp_pack, gains, tokens, grad_out.astype(BF16)
    )
    attn_gain, mlp_gain = (gains_all[:, i, :rows].reshape(model).astype(F32) for i in range(2))
    attn_all = attn_all.reshape(model, -1)
    mlp_all = mlp_all.reshape(model, -1)
    qkv_full = attn_all[:, : q_width + 2 * kv_width]
    out_t = attn_all[:, q_width + 2 * kv_width :]
    gate_up, down_full = mlp_all[:, : 2 * units], mlp_all[:, 2 * units :]
    dm_all = dm_all.reshape(-1, model)

    both = tokens_all.reshape(full_rows, model).astype(F32)
    both_factor = lax.rsqrt(jnp.mean(both * both, -1, keepdims=True) + EPS)
    normed_attn = (both * both_factor * attn_gain).astype(BF16)
    attn_factor = lax.rsqrt(jnp.mean(inputs * inputs, -1, keepdims=True) + EPS)
    qkv = dot_nn(normed_attn, qkv_full)
    query_rows = apply_rotary(
        qkv[:, :q_width].reshape(full_rows, q_heads, HEAD_SIZE), cosine_table, rotary_sine_table
    ).astype(BF16)
    key_rows = apply_rotary(
        qkv[:, q_width : q_width + kv_width].reshape(full_rows, kv_heads, HEAD_SIZE),
        cosine_table,
        rotary_sine_table,
    ).astype(BF16)
    value_rows = qkv[:, q_width + kv_width :].astype(BF16).reshape(full_rows, kv_heads, HEAD_SIZE)
    grouped = query_rows.reshape(full_rows, kv_heads, group_size, HEAD_SIZE)
    scores = (
        jnp.einsum("skgd,tkd->kgst", grouped, key_rows, preferred_element_type=F32) * score_scale
    )
    scores = jnp.where(key_allowed, scores, -1e30)
    row_exp = jnp.exp(scores - jnp.max(scores, -1, keepdims=True))
    probs = row_exp / jnp.sum(row_exp, -1, keepdims=True)
    probs_low = probs.astype(BF16)
    attended = (
        jnp.einsum("kgst,tkd->skgd", probs_low, value_rows, preferred_element_type=F32)
        .reshape(full_rows, q_width)
        .astype(BF16)
    )
    middle = inputs + sum_rows(dot_nt(attended, out_t))
    mlp_factor = lax.rsqrt(jnp.mean(middle * middle, -1, keepdims=True) + EPS)
    normed_mlp = (middle * mlp_factor * mlp_gain).astype(BF16)

    normed_all = line_gather(count, normed_mlp).reshape(-1, model)
    gate_up_lin = dot_nn(normed_all, gate_up)
    gate_lin, up_lin = gate_up_lin[:, :units], gate_up_lin[:, units:]
    sigmoid_gate = jax.nn.sigmoid(gate_lin)
    silu_gate = gate_lin * sigmoid_gate
    hidden = (silu_gate * up_lin).astype(BF16)
    grad_hidden = dot_nn(dm_all, down_full)
    grad_gate = (
        grad_hidden * up_lin * sigmoid_gate * (1.0 + gate_lin * (1.0 - sigmoid_gate))
    ).astype(BF16)
    grad_up = (grad_hidden * silu_gate).astype(BF16)
    grad_gate_up = jnp.concatenate([grad_gate, grad_up], axis=1)
    parts = jnp.stack([dot_nt(grad_gate_up, gate_up), dot_nt(hidden, down_full)]).astype(BF16)
    grad_norm_mlp, mlp_out = line_sum(
        count, parts.reshape(2, LINE, 2, local_rows, model)
    )
    outputs = middle + mlp_out
    grad_mlp_w = jnp.concatenate(
        [dot_tn(normed_all, grad_gate_up), dot_tn(dm_all, hidden)], axis=1
    ).astype(BF16)

    grad_mid_norm, gain_mlp_part = norm_back(middle, mlp_factor, mlp_gain, grad_norm_mlp)
    grad_middle = grad_out + grad_mid_norm
    grad_attn = gather_rows(grad_middle.astype(BF16))
    grad_out_t = dot_tn(grad_attn, attended)
    grad_groups = (
        dot_nn(grad_attn, out_t).astype(BF16).reshape(full_rows, kv_heads, group_size, HEAD_SIZE)
    )
    grad_probs = jnp.einsum("skgd,tkd->kgst", grad_groups, value_rows, preferred_element_type=F32)
    grad_scores = (probs * (grad_probs - jnp.sum(probs * grad_probs, -1, keepdims=True))).astype(BF16)
    grad_queries = (
        jnp.einsum("kgst,tkd->skgd", grad_scores, key_rows, preferred_element_type=F32) * score_scale
    )
    grad_keys = (
        jnp.einsum("kgst,skgd->tkd", grad_scores, grouped, preferred_element_type=F32) * score_scale
    )
    grad_values = jnp.einsum("kgst,skgd->tkd", probs_low, grad_groups, preferred_element_type=F32)
    grad_qkv = jnp.concatenate(
        [
            rotate_back(
                grad_queries.reshape(full_rows, q_heads, HEAD_SIZE), cosine_table, rotary_sine_table
            ).reshape(full_rows, q_width),
            rotate_back(grad_keys, cosine_table, rotary_sine_table).reshape(full_rows, kv_width),
            grad_values.reshape(full_rows, kv_width),
        ],
        axis=1,
    ).astype(BF16)
    grad_norm_attn = sum_rows(dot_nt(grad_qkv, qkv_full))
    grad_attn_w = jnp.concatenate([dot_tn(normed_attn, grad_qkv), grad_out_t], axis=1).astype(BF16)
    grad_in_norm, gain_attn_part = norm_back(inputs, attn_factor, attn_gain, grad_norm_attn)
    grad_inputs = grad_middle + grad_in_norm

    gain_parts = jnp.stack([gain_attn_part, gain_mlp_part]).reshape(2, count, rows)
    gain_parts = jnp.pad(gain_parts.transpose(1, 0, 2), ((0, 0), (0, 6), (0, lanes)))
    attn_sum, mlp_sum, gain_sum = grad_sum(
        count,
        grad_attn_w.reshape(count, rows, -1),
        grad_mlp_w.reshape(count, rows, -1),
        gain_parts,
    )
    mlp_sum = mlp_sum.astype(F32)
    grad_gate_w, grad_up_w, grad_down_t = (
        jnp.concatenate([mlp_sum[z, :, i * units : (i + 1) * units] for z in range(LINE)], axis=1)
        for i in range(3)
    )
    return (
        outputs.astype(BF16),
        grad_inputs,
        attn_sum[:, :q_width],
        attn_sum[:, q_width : q_width + kv_width],
        attn_sum[:, q_width + kv_width : q_width + 2 * kv_width],
        attn_sum[:, q_width + 2 * kv_width :].T,
        gain_sum[0, :rows],
        grad_gate_w,
        grad_up_w,
        grad_down_t.T,
        gain_sum[1, :rows],
    )


def solution(mesh):
    both = P(("dp", "tensor"), None)
    row = P("dp", "tensor")
    column = P("tensor", "dp")
    in_specs = (
        both, row, row, row, column, P("dp"), row, row, column, P("dp"), both, P(), P("dp"),
    )
    out_specs = (both, both, row, row, row, column, P("dp"), row, row, column, P("dp"))
    return jax.shard_map(shards, mesh=mesh, in_specs=in_specs, out_specs=out_specs, check_vma=False)
```

```python
import functools
import math

import jax
import jax.numpy as jnp
from jax import lax
from jax.experimental import pallas as pl
from jax.experimental.pallas import tpu as pltpu
from jax.sharding import PartitionSpec as P

HEAD_SIZE = 256
EPS = 1e-06
THETA = 1000042.0
LINE = 4
MESH = pl.DeviceIdType.MESH
BF16 = jnp.bfloat16
F32 = jnp.float32
MB = 1024 * 1024


def rope_tables(count, head_dim):
    half = head_dim // 2
    index = jnp.arange(half, dtype=jnp.float32)
    freqs = jnp.exp(index * (-2.0 * math.log(THETA) / head_dim))
    angles = jnp.arange(count, dtype=jnp.float32)[:, None] * freqs[None, :]
    return (jnp.cos(angles)[:, None, :], jnp.sin(angles)[:, None, :])


def dot_tn(left, right):
    return lax.dot_general(left, right, (((0,), (0,)), ((), ())), preferred_element_type=F32)


class Place:
    def __init__(self, plane):
        self.d = lax.axis_index("dp")
        self.t = lax.axis_index("tensor")
        self.plane = plane
        self.z = lax.div(self.d, plane)
        self.p = lax.rem(self.d, plane)
        if plane == 4:
            x = lax.rem(self.p, 2)
            y = lax.div(self.p, 2)
            self.px = 2 * y + 1 - x
            self.py = 2 * (1 - y) + x
            self.pd = 2 * (1 - y) + 1 - x

    def at(self, z, p):
        return (z * self.plane + p, self.t)

    def sibling(self):
        return (self.d, 1 - self.t)


def remote(src, dst, send, recv, device):
    return pltpu.make_async_remote_copy(
        src_ref=src, dst_ref=dst, send_sem=send, recv_sem=recv, device_id=device, device_id_type=MESH
    )


def arrival(ref, sem):
    pltpu.make_async_copy(ref, ref, sem).wait()


def greet_all(me, count):
    barrier = pltpu.get_barrier_semaphore()
    for step in range(1, count):
        pl.semaphore_signal(
            barrier, inc=1, device_id=(lax.rem(me.d + step, count), me.t), device_id_type=MESH
        )
    pl.semaphore_signal(barrier, inc=1, device_id=me.sibling(), device_id_type=MESH)
    pl.semaphore_wait(barrier, count)


def greet_line(me):
    barrier = pltpu.get_barrier_semaphore()
    for step in range(1, LINE):
        pl.semaphore_signal(
            barrier, inc=1, device_id=me.at(lax.rem(me.z + step, LINE), me.p), device_id_type=MESH
        )
    pl.semaphore_signal(barrier, inc=1, device_id=me.sibling(), device_id_type=MESH)
    pl.semaphore_wait(barrier, LINE)


def reach(me, way, k):
    return (me.z >= k, me.z - k) if way == 0 else (me.z + k < LINE, me.z + k)


class Chain:
    def __init__(self, me, first, held, send, recv):
        self.me, self.first, self.held, self.send, self.recv = me, first, held, send, recv

    def copy(self, way, k):
        me = self.me
        _, origin = reach(me, way, k)
        target = me.z + 1 if way == 0 else me.z - 1
        src = self.first if k == 0 else self.held(origin)
        return remote(
            src, self.held(origin), self.send.at[way, k], self.recv.at[way, k + 1], me.at(target, me.p)
        )

    def goes(self, way, k):
        have, _ = reach(self.me, way, k)
        ahead, _ = reach(self.me, 1 - way, 1)
        return jnp.logical_and(have, ahead)

    def start(self, way, k):
        if k < LINE - 1:

            @pl.when(self.goes(way, k))
            def _():
                self.copy(way, k).start()

    def wait_block(self, way, k):
        _, origin = reach(self.me, way, k)
        arrival(self.held(origin), self.recv.at[way, k])

    def finish(self):
        for way in range(2):
            for k in range(LINE - 1):

                @pl.when(self.goes(way, k))
                def _():
                    self.copy(way, k).wait_send()


class PlaneGather:
    def __init__(self, me, job, held, rows, send, recv, late=None):
        self.me, self.job, self.held, self.send, self.recv = me, job, held, send, recv
        self.late = late
        self.half = rows // 2

    def piece(self, z, p, half):
        return self.held.at[z * self.me.plane + p, pl.ds(half * self.half, self.half)]

    def copy(self, z, kind, first=None):
        me = self.me
        if me.plane != 4:
            ref = first if first is not None else self.held.at[z * me.plane + me.p]
            target = lax.rem(me.p + kind + 1, me.plane)
            dst = self.held.at[z * me.plane + me.p]
        else:
            owner = (me.p, me.p, me.p, me.p, me.px, me.py)[kind]
            half = (0, 1, 1, 0, 0, 1)[kind]
            target = (me.px, me.px, me.py, me.py, me.py, me.px)[kind]
            dst = self.piece(z, owner, half)
            ref = dst if first is None else first.at[pl.ds(half * self.half, self.half)]
        return remote(
            ref, dst, self.send.at[self.job, z, kind], self.recv.at[self.job, z, kind], me.at(me.z, target)
        )

    def unless_late(self, z, act):
        if self.late is None:
            act()
        else:
            pl.when(z != self.late)(act)

    def start(self, z, first=None):
        kinds = (0, 2, 1, 3) if self.me.plane == 4 else range(self.me.plane - 1)

        def act():
            for kind in kinds:
                self.copy(z, kind, first).start()

        self.unless_late(z, act)

    def forward(self, z):
        def act():
            self.copy(z, 0).wait_recv()
            self.copy(z, 4).start()
            self.copy(z, 2).wait_recv()
            self.copy(z, 5).start()

        if self.me.plane == 4:
            self.unless_late(z, act)

    def finish(self, zs=range(LINE)):
        kinds = 6 if self.me.plane == 4 else self.me.plane - 1
        for z in zs:
            if z == self.late:
                continue
            for kind in range(kinds):
                copy = self.copy(z, kind)
                if self.me.plane != 4 or kind not in (0, 2):
                    copy.wait_recv()
                copy.wait_send()


def gather_kernel(
    count, a_ref, w_ref, gain_ref, tok_ref, dm_ref, a_all, w_all, w_last, gain_all, tok_all, dm_all,
    chain_send, chain_recv, part_send, part_recv, plane_send, plane_recv, gain_send, gain_recv,
    pair_send, pair_recv, local_sem,
):
    plane = count // LINE
    me = Place(plane)
    rows = a_ref.shape[0]
    late = LINE - 1
    own_w = [
        pltpu.make_async_copy(w_ref.at[me.z], w_all.at[me.d], local_sem.at[1]),
        pltpu.make_async_copy(w_ref.at[me.z], w_last, local_sem.at[1]),
    ]
    for ref, here in zip(own_w, (me.z != late, me.z == late)):

        @pl.when(here)
        def _():
            ref.start()

    local = [
        pltpu.make_async_copy(a_ref, a_all.at[me.d], local_sem.at[0]),
        pltpu.make_async_copy(gain_ref, gain_all.at[me.d], local_sem.at[2]),
        pltpu.make_async_copy(tok_ref, tok_all.at[me.t], local_sem.at[3]),
        pltpu.make_async_copy(dm_ref, dm_all.at[me.z, me.t], local_sem.at[4]),
    ]
    for copy in local:
        copy.start()
    greet_all(me, count)

    attn = Chain(me, a_ref, lambda z: a_all.at[z * plane + me.p], chain_send.at[0], chain_recv.at[0])
    dms = Chain(me, dm_ref, lambda z: dm_all.at[z, me.t], chain_send.at[1], chain_recv.at[1])
    planes = (
        PlaneGather(me, 0, a_all, rows, plane_send, plane_recv),
        PlaneGather(me, 1, w_all, rows, plane_send, plane_recv, late),
    )

    def part(way, k, last):
        _, target = reach(me, 1 - way, k)
        dst = w_last if last else w_all.at[me.d]
        return remote(
            w_ref.at[target], dst, part_send.at[way, k], part_recv.at[way, k], me.at(target, me.p)
        )

    def pair(z, first=None):
        src = dm_all.at[z, me.t] if first is None else first
        return remote(src, dm_all.at[z, me.t], pair_send.at[z], pair_recv.at[z], me.sibling())

    for way in range(2):
        attn.start(way, 0)
    planes[0].start(me.z, a_ref)
    for k in range(1, LINE):
        for way in range(2):

            for last in range(2):

                @pl.when(jnp.logical_and(reach(me, 1 - way, k)[0], (me.z == late) == bool(last)))
                def _():
                    part(way, k, last).start()

    def give_gain(step):
        target = lax.rem(me.d + step, count)
        return remote(
            gain_ref, gain_all.at[me.d], gain_send.at[step], gain_recv.at[step], (target, me.t)
        )

    for step in range(1, count):
        give_gain(step).start()
    tokens = remote(tok_ref, tok_all.at[me.t], pair_send.at[LINE], pair_recv.at[LINE], me.sibling())
    tokens.start()
    planes[1].start(me.z, w_ref.at[me.z])
    for way in range(2):
        dms.start(way, 0)
    pair(me.z, dm_ref).start()

    for k in range(1, LINE + 1):
        if k < LINE:
            for way in range(2):
                have, z = reach(me, way, k)

                @pl.when(have)
                def _():
                    attn.wait_block(way, k)
                    attn.start(way, k)
                    planes[0].start(z)
                    arrival(w_last, part_recv.at[way, k])
                    planes[1].start(z)
                    dms.wait_block(way, k)
                    dms.start(way, k)
                    pair(z).start()

        if k == 1:
            planes[0].forward(me.z)
            planes[1].forward(me.z)
        else:
            for way in range(2):
                have, z = reach(me, way, k - 1)

                @pl.when(have)
                def _():
                    planes[0].forward(z)
                    planes[1].forward(z)

    attn.finish()
    dms.finish()
    for k in range(1, LINE):
        for way in range(2):

            @pl.when(reach(me, 1 - way, k)[0])
            def _():
                part(way, k, 1).wait_send()

    for step in range(1, count):
        give_gain(step).wait()
    tokens.wait()
    for z in range(LINE):
        pair(z).wait()
    for job in planes:
        job.finish()
    for copy in local:
        copy.wait()
    own_w[1].wait()


ANY = pl.BlockSpec(memory_space=pl.ANY)
DMA = pltpu.SemaphoreType.DMA


def gather_all(count, attn, mlp, gains, tokens, dm):
    rows, width = attn.shape
    kinds = max(6, count // LINE - 1)
    return pl.pallas_call(
        functools.partial(gather_kernel, count),
        name="gather_all",
        out_shape=(
            jax.ShapeDtypeStruct((count, rows, width), BF16),
            jax.ShapeDtypeStruct((count - count // LINE, rows, width), BF16),
            jax.ShapeDtypeStruct((rows, width), BF16),
            jax.ShapeDtypeStruct((count,) + gains.shape, gains.dtype),
            jax.ShapeDtypeStruct((2,) + tokens.shape, BF16),
            jax.ShapeDtypeStruct((LINE, 2) + dm.shape, BF16),
        ),
        in_specs=[ANY] * 5,
        out_specs=(ANY,) * 6,
        scratch_shapes=[
            DMA((2, 2, LINE)), DMA((2, 2, LINE)), DMA((2, LINE)), DMA((2, LINE)),
            DMA((2, LINE, kinds)), DMA((2, LINE, kinds)), DMA((count,)), DMA((count,)),
            DMA((LINE + 1,)), DMA((LINE + 1,)), DMA((5,)),
        ],
        compiler_params=pltpu.CompilerParams(collective_id=0, has_side_effects=True),
    )(attn, mlp, gains, tokens, dm)


def dot_cols(left, right):
    return lax.dot_general(left, right, (((1,), (1,)), ((), ())), preferred_element_type=F32)


def feed_forward_kernel(
    plane, h_ref, dm_ref, w_ref, w_late, total_ref, out_ref, grad_ref, rows_in, weights, inner, part,
    from_pair, from_line, chain_send, chain_recv, pass_send, pass_recv, pair_send, pair_recv,
    line_send, line_recv, load_sem, dm_sem, grad_sem, out_sem,
):
    me = Place(plane)
    rows, model = h_ref.shape
    units = inner.shape[1]
    wide = 2 * rows
    tokens = LINE * wide
    most, block, _ = w_ref.shape
    tile = 512

    def slot(z, t):
        return rows_in.at[pl.ds(pl.multiple_of((z * 2 + t) * rows, rows), rows)]

    loads = [
        pltpu.make_async_copy(w_ref, weights.at[pl.ds(0, most)], load_sem.at[0]),
        pltpu.make_async_copy(w_late, weights.at[pl.ds(most, plane)], load_sem.at[2]),
    ]
    for load in loads:
        load.start()
    load_dm = pltpu.make_async_copy(dm_ref, rows_in.at[pl.ds(tokens, tokens)], dm_sem)
    load_dm.start()
    keep = pltpu.make_async_copy(h_ref, slot(me.z, me.t), load_sem.at[1])
    keep.start()
    greet_line(me)
    chain = Chain(me, h_ref, lambda z: slot(z, me.t), chain_send, chain_recv)

    def share(z, first=None):
        src = slot(z, me.t) if first is None else first
        return remote(src, slot(z, me.t), pass_send.at[z], pass_recv.at[z], me.sibling())

    for way in range(2):
        chain.start(way, 0)
    share(me.z, h_ref).start()

    def w_rows(n, width, column):
        return weights[pl.ds(n * (width // block), width // block), :, pl.ds(column, units)].reshape(
            width, units
        )

    def compute(z):
        at = pl.ds(pl.multiple_of(z * wide, wide), wide)
        dm_at = pl.ds(pl.multiple_of(tokens + z * wide, wide), wide)

        @pl.loop(0, units // tile)
        def _(c):
            def column(job):
                return weights[:, :, pl.ds(pl.multiple_of(job * units + c * tile, tile), tile)].reshape(
                    model, tile
                )

            h = rows_in[at, :]
            gate = jnp.dot(h, column(0), preferred_element_type=F32)
            up = jnp.dot(h, column(1), preferred_element_type=F32)
            grad_hidden = jnp.dot(rows_in[dm_at, :], column(2), preferred_element_type=F32)
            sigmoid = jax.nn.sigmoid(gate)
            silu = gate * sigmoid
            here = pl.ds(pl.multiple_of(c * tile, tile), tile)
            inner[at, here] = (silu * up).astype(BF16)
            inner[pl.ds(pl.multiple_of(tokens + z * wide, wide), wide), here] = (
                grad_hidden * up * sigmoid * (1.0 + gate * (1.0 - sigmoid))
            ).astype(BF16)
            inner[pl.ds(pl.multiple_of(2 * tokens + z * wide, wide), wide), here] = (
                grad_hidden * silu
            ).astype(BF16)

        @pl.loop(0, model // tile)
        def _(n):
            here = pl.ds(pl.multiple_of(n * tile, tile), tile)
            grad = dot_cols(inner[pl.ds(pl.multiple_of(tokens + z * wide, wide), wide)], w_rows(n, tile, 0))
            grad += dot_cols(
                inner[pl.ds(pl.multiple_of(2 * tokens + z * wide, wide), wide)], w_rows(n, tile, units)
            )
            part[0, z, :, :, here] = grad.astype(BF16).reshape(2, rows, tile)
            out = dot_cols(inner[at, :], w_rows(n, tile, 2 * units))
            part[1, z, :, :, here] = out.astype(BF16).reshape(2, rows, tile)

    def pair(job, z):
        return remote(
            part.at[job, z, 1 - me.t], from_pair.at[job, z], pair_send.at[job, z],
            pair_recv.at[job, z], me.sibling(),
        )

    def pass_on(job, way, k):
        _, target = reach(me, 1 - way, k)
        ahead = me.z + 1 if way == 0 else me.z - 1
        return remote(
            part.at[job, target, me.t], from_line.at[way, k - 1], line_send.at[way, k],
            line_recv.at[way, k - 1], me.at(ahead, me.p),
        )

    def line(job, way, k, behind):
        have, z = reach(me, 1 - way, k)
        before = me.z if way == 0 else LINE - 1 - me.z

        @pl.when(jnp.logical_and(have, before == behind))
        def _():
            pair(job, z).wait_recv()
            terms = (part.at[job, z, me.t], from_pair.at[job, z])
            if behind:
                arrival(from_line.at[way, k], line_recv.at[way, k])
                terms += (from_line.at[way, k],)
            add_rows(part.at[job, z, me.t], terms, rows)
            pass_on(job, way, k).start()

    def total(job):
        pair(job, me.z).wait_recv()
        add_rows(total_ref, (part.at[job, me.z, me.t], from_pair.at[job, me.z]), rows)
        for way in range(2):

            @pl.when(reach(me, way, 1)[0])
            def _():
                arrival(from_line.at[way, 0], line_recv.at[way, 0])
                add_rows(total_ref, (total_ref, from_line.at[way, 0]), rows)

    def grads(z):
        per = plane * block

        @pl.loop(0, per // tile)
        def _(n):
            column = pl.ds(pl.multiple_of(z * per + n * tile, tile), tile)
            h = rows_in[pl.ds(0, tokens), column].T
            dm = rows_in[pl.ds(tokens, tokens), column].T
            there = pl.ds((z * per + n * tile) // block, tile // block)
            for job in range(3):
                left = (h, h, dm)[job]
                start = (tokens, 2 * tokens, 0)[job]
                for c in range(units // 512):
                    grad = jnp.dot(
                        left, inner[pl.ds(start, tokens), c * 512 : (c + 1) * 512],
                        preferred_element_type=F32,
                    )
                    weights[there, :, job * units + c * 512 : job * units + (c + 1) * 512] = (
                        grad.astype(BF16).reshape(tile // block, block, 512)
                    )

        keep_grads(z).start()

    def keep_grads(z):
        return pltpu.make_async_copy(
            weights.at[pl.ds(z * plane, plane)], grad_ref.at[pl.ds(z * plane, plane)], grad_sem.at[z]
        )

    keep.wait()
    for load in loads:
        load.wait()
    load_dm.wait()
    for k in range(LINE):
        for way in range(2 if k else 1):
            have, z = reach(me, way, k)

            @pl.when(have)
            def _():
                if k:
                    chain.wait_block(way, k)
                    chain.start(way, k)
                    share(z).start()
                arrival(slot(z, 1 - me.t), pass_recv.at[z])
                compute(z)
                for job in range(2):
                    pair(job, z).start()

        if k:
            for way in range(2):
                line(0, 1 - way, k, 0)
    order = [(behind, k) for behind in range(1, LINE) for k in range(1, LINE - behind)]
    order.sort(key=lambda e: (2 * e[0] + e[1], e[0]))
    for i in range(max(LINE, len(order))):
        if i < LINE:
            grads(i)
        if i < len(order):
            for way in range(2):
                line(0, way, order[i][1], order[i][0])

    def keep_out(z):
        return pltpu.make_async_copy(part.at[1, z, me.t], out_ref.at[z], out_sem.at[z])

    for z in range(LINE):
        pair(1, z).wait_recv()
        add_rows(part.at[1, z, me.t], (part.at[1, z, me.t], from_pair.at[1, z]), rows)
        keep_out(z).start()
    total(0)

    chain.finish()
    for z in range(LINE):
        share(z).wait_send()
        keep_grads(z).wait()
        keep_out(z).wait()
        for job in range(2):
            pair(job, z).wait_send()
    for k in range(1, LINE):
        for way in range(2):

            @pl.when(reach(me, 1 - way, k)[0])
            def _():
                pass_on(0, way, k).wait_send()


def feed_forward(count, h, dm_all, w_all, w_late):
    rows, model = h.shape
    units = w_all.shape[2] // 3
    grads = (count,) + w_all.shape[1:]
    tokens = LINE * 2 * rows
    vmem = pl.BlockSpec(memory_space=pltpu.VMEM)
    return pl.pallas_call(
        functools.partial(feed_forward_kernel, count // LINE),
        name="feed_forward",
        out_shape=(
            jax.ShapeDtypeStruct((rows, model), F32),
            jax.ShapeDtypeStruct((LINE, rows, model), BF16),
            jax.ShapeDtypeStruct(grads, BF16),
        ),
        in_specs=[vmem, ANY, ANY, ANY],
        out_specs=(vmem, ANY, ANY),
        scratch_shapes=[
            pltpu.VMEM((2 * tokens, model), BF16),
            pltpu.VMEM(grads, BF16),
            pltpu.VMEM((3 * tokens, units), BF16),
            pltpu.VMEM((2, LINE, 2, rows, model), BF16),
            pltpu.VMEM((2, LINE, rows, model), BF16),
            pltpu.VMEM((2, LINE - 1, rows, model), BF16),
            DMA((2, LINE)), DMA((2, LINE)), DMA((LINE,)), DMA((LINE,)), DMA((2, LINE)), DMA((2, LINE)),
            DMA((2, LINE)), DMA((2, LINE)), DMA((3,)), DMA, DMA((LINE,)), DMA((LINE,)),
        ],
        compiler_params=pltpu.CompilerParams(
            collective_id=1, has_side_effects=True, vmem_limit_bytes=60 * MB
        ),
    )(h, dm_all, w_all, w_late)


def add_rows(target, terms, rows, start=0):
    step = 16

    @pl.loop(0, rows // step)
    def _(i):
        at = pl.ds(pl.multiple_of(start + i * step, step), step)
        total = terms[0][at].astype(F32)
        for term in terms[1:]:
            total += term[at].astype(F32)
        target[at] = total.astype(target.dtype)


class PlaneSum:
    def __init__(self, me, grad, own, other, first, second, sems):
        self.me, self.grad, self.own, self.other, self.first, self.second = me, grad, own, other, first, second
        (
            self.first_send, self.first_recv, self.second_send, self.second_recv, self.load_sem, self.other_sem,
        ) = sems
        self.rows = own.shape[1]
        half = self.rows // 2
        self.half = half
        self.halves = (pl.ds(0, half), pl.ds(half, half))
        self.square = me.plane == 4
        if self.square:
            self.near = (me.px, me.py)
            self.far = (me.py, me.px)

    def load(self, z):
        return pltpu.make_async_copy(
            self.grad.at[z * self.me.plane + self.me.p], self.own.at[z], self.load_sem.at[z]
        )

    def load_other(self, z, i):
        return pltpu.make_async_copy(
            self.grad.at[z * self.me.plane + self.far[i], self.halves[i]],
            self.other.at[z, self.halves[i]], self.other_sem.at[z, i],
        )

    def load_all(self):
        for z in range(LINE):
            self.load(z).start()
            if self.square:
                for i in range(2):
                    self.load_other(z, i).start()

    def give(self, z, i, which):
        me = self.me
        if not self.square:
            target = lax.rem(me.p + which + 1, me.plane)
            return remote(
                self.grad.at[z * me.plane + target], self.first.at[z, which],
                self.first_send.at[z, which], self.first_recv.at[z, which], me.at(me.z, target),
            )
        block = (self.near[i], me.pd)[which]
        return remote(
            self.grad.at[z * me.plane + block, self.halves[i]], self.first.at[z, which, self.halves[i]],
            self.first_send.at[z, 2 * i + which], self.first_recv.at[z, 2 * i + which],
            me.at(me.z, self.near[i]),
        )

    def give_both(self, z, i):
        return remote(
            self.other.at[z, self.halves[i]], self.second.at[z, self.halves[i]],
            self.second_send.at[z, i], self.second_recv.at[z, i], self.me.at(self.me.z, self.far[i]),
        )

    def gives(self, z):
        if self.square:
            return [self.give(z, i, which) for which in (1, 0) for i in range(2)]
        return [self.give(z, 0, which) for which in range(self.me.plane - 1)]

    def begin(self, z):
        for copy in self.gives(z):
            copy.start()

    def middle(self, z):
        if not self.square:
            return
        for i in range(2):
            arrival(self.first.at[z, 1, self.halves[i]], self.first_recv.at[z, 2 * i + 1])
            self.load_other(z, i).wait()
            add_rows(
                self.other.at[z], (self.other.at[z], self.first.at[z, 1]), self.half, i * self.half
            )
            self.give_both(z, i).start()

    def end(self, z):
        self.load(z).wait()
        if self.square:
            for i in range(2):
                arrival(self.first.at[z, 0, self.halves[i]], self.first_recv.at[z, 2 * i])
                arrival(self.second.at[z, self.halves[i]], self.second_recv.at[z, i])
            terms = (self.first.at[z, 0], self.second.at[z])
        else:
            for which in range(self.me.plane - 1):
                arrival(self.first.at[z, which], self.first_recv.at[z, which])
            terms = tuple(self.first.at[z, which] for which in range(self.me.plane - 1))
        add_rows(self.own.at[z], (self.own.at[z],) + terms, self.rows)

    def finish(self):
        for z in range(LINE):
            for copy in self.gives(z):
                copy.wait_send()
            if self.square:
                for i in range(2):
                    self.give_both(z, i).wait_send()

    @staticmethod
    def scratch(count, rows, width):
        plane = count // LINE
        square = plane == 4
        slots = 2 if square else plane - 1
        small = (LINE, rows, width) if square else (1, 16, 128)
        return [
            pltpu.VMEM((LINE, rows, width), BF16),
            pltpu.VMEM(small, BF16),
            pltpu.VMEM((LINE, slots, rows, width), BF16),
            pltpu.VMEM(small, BF16),
        ], [
            DMA((LINE, max(4, slots))), DMA((LINE, max(4, slots))), DMA((LINE, 2)), DMA((LINE, 2)),
            DMA((LINE,)), DMA((LINE, 2)),
        ]


FAR_FIRST = [(way, k) for k in range(LINE - 1, 0, -1) for way in range(2)] + [(0, 0)]


def on(me, event, act):
    way, k = event
    have, z = reach(me, 1 - way, k)
    if k == 0:
        act(me.z)
    else:

        @pl.when(have)
        def _():
            act(z)


def greet_plane(me):
    barrier = pltpu.get_barrier_semaphore()
    for step in range(1, me.plane):
        target = lax.rem(me.p + step, me.plane)
        pl.semaphore_signal(barrier, inc=1, device_id=me.at(me.z, target), device_id_type=MESH)
    pl.semaphore_signal(barrier, inc=1, device_id=me.sibling(), device_id_type=MESH)
    pl.semaphore_wait(barrier, me.plane)


def row_loop(rows, step, act):
    @pl.loop(0, rows // step)
    def _(i):
        act(pl.ds(pl.multiple_of(i * step, step), step))


def columns_of(weights, start, width):
    count, rows, _ = weights.shape
    return weights[:, :, pl.ds(start, width)].reshape(count * rows, width)


def rows_of(weights, n, height, start, width):
    _, rows, _ = weights.shape
    per = height // rows
    return weights[pl.ds(n * per, per), :, pl.ds(start, width)].reshape(height, width)


def attention_forward_kernel(
    plane, tok_ref, gain_ref, cos_ref, sin_ref, mask_ref, a_ref, w_last, x1_ref, h2_ref, h1_ref,
    qkv_ref, probs_ref, o_ref, w_late, weights, part, from_pair, plane_send, plane_recv, pair_send,
    pair_recv, load_sem,
):
    me = Place(plane)
    _, rows, model = tok_ref.shape
    wide = 2 * rows
    heads, _, _ = probs_ref.shape
    q_width = heads * HEAD_SIZE
    kv_width = (qkv_ref.shape[1] - q_width) // 2
    kv_heads = kv_width // HEAD_SIZE
    half = HEAD_SIZE // 2
    load = pltpu.make_async_copy(a_ref, weights, load_sem.at[0])
    load.start()
    keep = pltpu.make_async_copy(w_last, w_late.at[me.p], load_sem.at[1])
    keep.start()
    greet_plane(me)
    gather = PlaneGather(me, 0, w_late, w_last.shape[0], plane_send, plane_recv)
    gather.start(0, w_last)

    for t in range(2):

        def norm(at, t=t):
            x = tok_ref[t, at, :].astype(F32)
            factor = lax.rsqrt(jnp.mean(x * x, -1, keepdims=True) + EPS)
            h1_ref[pl.ds(t * rows + at.start, at.size), :] = (x * factor * gain_ref[0:1, :]).astype(BF16)

        row_loop(rows, 32, norm)
    load.wait()

    def project(i):
        start = pl.multiple_of(i * HEAD_SIZE, HEAD_SIZE)
        return start, jnp.dot(
            h1_ref[...], columns_of(weights, start, HEAD_SIZE), preferred_element_type=F32
        )

    @pl.loop(0, heads + kv_heads)
    def _(i):
        start, values = project(i)
        first, second = values[:, :half], values[:, half:]
        cos, sin = cos_ref[...], sin_ref[...]
        qkv_ref[:, pl.ds(start, half)] = (first * cos - second * sin).astype(BF16)
        qkv_ref[:, pl.ds(start + half, half)] = (second * cos + first * sin).astype(BF16)

    @pl.loop(heads + kv_heads, heads + 2 * kv_heads)
    def _(i):
        start, values = project(i)
        qkv_ref[:, pl.ds(start, HEAD_SIZE)] = values.astype(BF16)

    gather.forward(0)
    for i in range(heads):
        m = i * kv_heads // heads
        q = qkv_ref[:, i * HEAD_SIZE : (i + 1) * HEAD_SIZE]
        k = qkv_ref[:, q_width + m * HEAD_SIZE : q_width + (m + 1) * HEAD_SIZE]
        v = qkv_ref[:, q_width + kv_width + m * HEAD_SIZE : q_width + kv_width + (m + 1) * HEAD_SIZE]
        scores = dot_cols(q, k) * HEAD_SIZE ** (-0.5)
        scores = jnp.where(mask_ref[...] > 0, scores, -1e30)
        grown = jnp.exp(scores - jnp.max(scores, -1, keepdims=True))
        probs = grown / jnp.sum(grown, -1, keepdims=True)
        probs_ref[i] = probs
        o_ref[:, i * HEAD_SIZE : (i + 1) * HEAD_SIZE] = jnp.dot(
            probs.astype(BF16), v, preferred_element_type=F32
        ).astype(BF16)

    tile = 512

    @pl.loop(0, model // tile)
    def _(n):
        here = pl.ds(pl.multiple_of(n * tile, tile), tile)
        value = dot_cols(o_ref[...], rows_of(weights, n, tile, q_width + 2 * kv_width, q_width))
        part[:, :, here] = value.reshape(2, rows, tile)

    swap = remote(part.at[1 - me.t], from_pair, pair_send, pair_recv, me.sibling())
    swap.start()
    swap.wait_recv()

    def add(at):
        x1 = tok_ref[me.t, at, :].astype(F32) + (part[me.t, at, :] + from_pair[at, :])
        x1_ref[at, :] = x1
        factor = lax.rsqrt(jnp.mean(x1 * x1, -1, keepdims=True) + EPS)
        h2_ref[at, :] = (x1 * factor * gain_ref[1:2, :]).astype(BF16)

    row_loop(rows, 32, add)
    swap.wait_send()
    gather.finish(range(1))
    keep.wait()


VMEM = pl.BlockSpec(memory_space=pltpu.VMEM)


def attention_forward(count, heads, tokens_all, gains, cos, sin, mask, attn_all, w_last):
    _, rows, model = tokens_all.shape
    wide = 2 * rows
    q_width = heads * HEAD_SIZE
    qkv_width = attn_all.shape[2] - q_width
    plane = count // LINE
    kinds = max(6, plane - 1)
    return pl.pallas_call(
        functools.partial(attention_forward_kernel, plane),
        name="attention_forward",
        out_shape=(
            jax.ShapeDtypeStruct((rows, model), F32),
            jax.ShapeDtypeStruct((rows, model), BF16),
            jax.ShapeDtypeStruct((wide, model), BF16),
            jax.ShapeDtypeStruct((wide, qkv_width), BF16),
            jax.ShapeDtypeStruct((heads, wide, wide), F32),
            jax.ShapeDtypeStruct((wide, q_width), BF16),
            jax.ShapeDtypeStruct((plane,) + w_last.shape, BF16),
        ),
        in_specs=[VMEM] * 5 + [ANY] * 2,
        out_specs=(VMEM,) * 6 + (ANY,),
        scratch_shapes=[
            pltpu.VMEM(attn_all.shape, BF16),
            pltpu.VMEM((2, rows, model), F32),
            pltpu.VMEM((rows, model), F32),
            DMA((1, 1, kinds)), DMA((1, 1, kinds)), DMA, DMA, DMA((2,)),
        ],
        compiler_params=pltpu.CompilerParams(
            collective_id=2, has_side_effects=True, vmem_limit_bytes=48 * MB
        ),
    )(tokens_all, gains, cos, sin, mask, attn_all, w_last)


def attention_backward_kernel(
    plane, total_ref, x1_ref, dm_ref, tok_ref, gain_ref, cos_ref, sin_ref, h1_ref, qkv_ref, probs_ref,
    o_ref, a_ref, gw_ref, ga_ref, w_out, grad_tokens, gain_parts, weights, own, other, first, second,
    dx, da, do, dqkv, dh1, from_pair, first_send, first_recv, second_send, second_recv, load_sem,
    other_sem, part_send, part_recv, pair_send, pair_recv, a_sem, keep_sem, grad_sem,
):
    me = Place(plane)
    _, rows, model = tok_ref.shape
    block = weights.shape[1]
    heads, _, _ = probs_ref.shape
    q_width = heads * HEAD_SIZE
    qkv_width = qkv_ref.shape[1]
    kv_width = (qkv_width - q_width) // 2
    kv_heads = kv_width // HEAD_SIZE
    half = HEAD_SIZE // 2
    scale = HEAD_SIZE ** (-0.5)
    summed = PlaneSum(
        me, gw_ref, own, other, first, second,
        (first_send, first_recv, second_send, second_recv, load_sem, other_sem),
    )
    load = pltpu.make_async_copy(a_ref, weights, a_sem)
    load.start()
    summed.load_all()
    greet_all(me, plane * LINE)

    def part(way, k):
        _, target = reach(me, 1 - way, k)
        return remote(
            own.at[target], w_out.at[me.z], part_send.at[way, k], part_recv.at[way, k],
            me.at(target, me.p),
        )

    give_da = remote(da.at[me.t], da.at[me.t], pair_send.at[0], pair_recv.at[0], me.sibling())
    give_dh1 = remote(dh1.at[1 - me.t], from_pair, pair_send.at[1], pair_recv.at[1], me.sibling())

    def mid_norm():
        gain_parts[...] = jnp.zeros_like(gain_parts)

        def act(at):
            x, up = x1_ref[at, :], total_ref[at, :]
            factor = lax.rsqrt(jnp.mean(x * x, -1, keepdims=True) + EPS)
            scaled = up * gain_ref[1:2, :]
            grad = dm_ref[at, :].astype(F32) + (
                factor * scaled - x * factor**3 * jnp.mean(scaled * x, -1, keepdims=True)
            )
            dx[at, :] = grad
            da[me.t, at, :] = grad.astype(BF16)
            gain_parts[1:2, :] += jnp.sum(up * x * factor, 0, keepdims=True)

        row_loop(rows, 32, act)
        give_da.start()

    def grad_o():
        load.wait()
        give_da.wait_recv()

        @pl.loop(0, q_width // HEAD_SIZE)
        def _(c):
            here = pl.multiple_of(c * HEAD_SIZE, HEAD_SIZE)
            value = jnp.dot(
                da[...].reshape(2 * rows, model),
                columns_of(weights, qkv_width + here, HEAD_SIZE),
                preferred_element_type=F32,
            )
            do[:, pl.ds(here, HEAD_SIZE)] = value.astype(BF16)

    def rotate(values, start):
        first, second = values[:, :half], values[:, half:]
        cos, sin = cos_ref[...], sin_ref[...]
        dqkv[:, start : start + half] = (first * cos + second * sin).astype(BF16)
        dqkv[:, start + half : start + 2 * half] = (second * cos - first * sin).astype(BF16)

    def grad_heads():
        group = heads // kv_heads
        for m in range(kv_heads):
            at_k = q_width + m * HEAD_SIZE
            at_v = at_k + kv_width
            k = qkv_ref[:, at_k : at_k + HEAD_SIZE]
            v = qkv_ref[:, at_v : at_v + HEAD_SIZE]
            grad_k = grad_v = None
            for i in range(m * group, (m + 1) * group):
                at = slice(i * HEAD_SIZE, (i + 1) * HEAD_SIZE)
                probs = probs_ref[i]
                grad_probs = dot_cols(do[:, at], v)
                grad_scores = probs * (
                    grad_probs - jnp.sum(probs * grad_probs, -1, keepdims=True)
                )
                low = grad_scores.astype(BF16)
                rotate(jnp.dot(low, k, preferred_element_type=F32) * scale, i * HEAD_SIZE)
                more_k = dot_tn(low, qkv_ref[:, at])
                more_v = dot_tn(probs.astype(BF16), do[:, at])
                grad_k = more_k if grad_k is None else grad_k + more_k
                grad_v = more_v if grad_v is None else grad_v + more_v
            rotate(grad_k * scale, at_k)
            dqkv[:, at_v : at_v + HEAD_SIZE] = grad_v.astype(BF16)

    tile = 512

    def grad_h1():
        @pl.loop(0, model // tile)
        def _(n):
            here = pl.ds(pl.multiple_of(n * tile, tile), tile)
            value = dot_cols(dqkv[...], rows_of(weights, n, tile, 0, qkv_width))
            dh1[:, :, here] = value.reshape(2, rows, tile)

        give_dh1.start()

    def keep_grads(n):
        per = tile // block
        return pltpu.make_async_copy(
            weights.at[pl.ds(n * per, per)], ga_ref.at[pl.ds(n * per, per)], grad_sem.at[n]
        )

    def grads():
        @pl.loop(0, model // tile)
        def _(n):
            here = pl.ds(pl.multiple_of(n * tile, tile), tile)
            there = pl.ds(n * (tile // block), tile // block)
            left = h1_ref[:, here].T
            for c in range(qkv_width // tile):
                at = slice(c * tile, (c + 1) * tile)
                value = jnp.dot(left, dqkv[:, at], preferred_element_type=F32)
                weights[there, :, at] = value.astype(BF16).reshape(tile // block, block, tile)
            left = da[:, :, here].reshape(2 * rows, tile).T
            for c in range(q_width // tile):
                at = slice(c * tile, (c + 1) * tile)
                value = jnp.dot(left, o_ref[:, at], preferred_element_type=F32)
                at = slice(qkv_width + c * tile, qkv_width + (c + 1) * tile)
                weights[there, :, at] = value.astype(BF16).reshape(tile // block, block, tile)

        for n in range(model // tile):
            keep_grads(n).start()

    def in_norm():
        give_dh1.wait_recv()

        def act(at):
            x = tok_ref[me.t, at, :].astype(F32)
            up = dh1[me.t, at, :] + from_pair[at, :]
            factor = lax.rsqrt(jnp.mean(x * x, -1, keepdims=True) + EPS)
            scaled = up * gain_ref[0:1, :]
            grad_tokens[at, :] = dx[at, :] + (
                factor * scaled - x * factor**3 * jnp.mean(scaled * x, -1, keepdims=True)
            )
            gain_parts[0:1, :] += jnp.sum(up * x * factor, 0, keepdims=True)

        row_loop(rows, 32, act)

    lead, lag = 4, 2
    last = len(FAR_FIRST)
    for i in range(lead):
        on(me, FAR_FIRST[i], summed.begin)
    mid_norm()
    grad_o()
    stages = [grad_heads, grad_h1, grads, in_norm]
    for i in range(last + lag):
        if i + lead < last:
            on(me, FAR_FIRST[i + lead], summed.begin)
        if i < len(stages):
            stages[i]()
        if i < last:
            on(me, FAR_FIRST[i], summed.middle)
        if i >= lag:
            event = FAR_FIRST[i - lag]
            on(me, event, summed.end)
            if event[1]:
                on(me, event, lambda z: part(*event).start())

    keep = pltpu.make_async_copy(own.at[me.z], w_out.at[me.z], keep_sem)
    keep.start()
    for way, k in FAR_FIRST[:-1]:

        @pl.when(reach(me, 1 - way, k)[0])
        def _():
            part(way, k).wait_send()

        @pl.when(reach(me, way, k)[0])
        def _():
            arrival(w_out.at[me.z], part_recv.at[way, k])

    summed.finish()
    give_da.wait_send()
    give_dh1.wait_send()
    for n in range(model // tile):
        keep_grads(n).wait()
    keep.wait()


def attention_backward(
    count, total, x1, dm, tokens_all, gains, cos, sin, h1, qkv, probs, o, attn_all, grad_mlp
):
    _, rows, model = tokens_all.shape
    _, block, width = attn_all.shape
    wide = 2 * rows
    heads = probs.shape[0]
    q_width = heads * HEAD_SIZE
    buffers, sems = PlaneSum.scratch(count, block, width)
    return pl.pallas_call(
        functools.partial(attention_backward_kernel, count // LINE),
        name="attention_backward",
        out_shape=(
            jax.ShapeDtypeStruct(attn_all.shape, BF16),
            jax.ShapeDtypeStruct((LINE, block, width), BF16),
            jax.ShapeDtypeStruct((rows, model), F32),
            jax.ShapeDtypeStruct((2, model), F32),
        ),
        in_specs=[VMEM] * 11 + [ANY] * 2,
        out_specs=(ANY, ANY, VMEM, VMEM),
        scratch_shapes=[
            pltpu.VMEM(attn_all.shape, BF16),
            *buffers,
            pltpu.VMEM((rows, model), F32),
            pltpu.VMEM((2, rows, model), BF16),
            pltpu.VMEM((wide, q_width), BF16),
            pltpu.VMEM(qkv.shape, BF16),
            pltpu.VMEM((2, rows, model), F32),
            pltpu.VMEM((rows, model), F32),
            *sems,
            DMA((2, LINE)), DMA((2, LINE)), DMA((2,)), DMA((2,)), DMA, DMA, DMA((model // 512,)),
        ],
        compiler_params=pltpu.CompilerParams(
            collective_id=3, has_side_effects=True, vmem_limit_bytes=60 * MB
        ),
    )(total, x1, dm, tokens_all, gains, cos, sin, h1, qkv, probs, o, attn_all, grad_mlp)


def grad_sum_kernel(
    count, x1_ref, ga_ref, out_ref, gain_ref, a_out, output, gain_out, own, other, first, second,
    from_line, out_own, out_line, gain_in, gain_pair, first_send, first_recv, second_send, second_recv,
    load_sem, other_sem, line_send, line_recv, out_send, out_recv, out_sem, gain_send, gain_recv,
):
    plane = count // LINE
    me = Place(plane)
    rows = a_out.shape[0]
    summed = PlaneSum(
        me, ga_ref, own, other, first, second,
        (first_send, first_recv, second_send, second_recv, load_sem, other_sem),
    )

    class Line:
        def __init__(self, held, landing, send, recv):
            self.held, self.landing, self.send, self.recv = held, landing, send, recv

        def pass_on(self, way, k):
            _, target = reach(me, 1 - way, k)
            ahead = me.z + 1 if way == 0 else me.z - 1
            return remote(
                self.held.at[target], self.landing.at[way, k - 1], self.send.at[way, k],
                self.recv.at[way, k - 1], me.at(ahead, me.p),
            )

        def step(self, way, k, behind=None):
            have, z = reach(me, 1 - way, k)
            before = me.z if way == 0 else LINE - 1 - me.z

            @pl.when(have if behind is None else jnp.logical_and(have, before == behind))
            def _():
                @pl.when(before > 0)
                def _():
                    arrival(self.landing.at[way, k], self.recv.at[way, k])
                    add_rows(
                        self.held.at[z], (self.held.at[z], self.landing.at[way, k]), self.held.shape[1]
                    )

                self.pass_on(way, k).start()

        def total(self, act):
            for way in range(2):

                @pl.when(reach(me, way, 1)[0])
                def _():
                    arrival(self.landing.at[way, 0], self.recv.at[way, 0])
                    act(self.landing.at[way, 0])

        def finish(self):
            for way, k in FAR_FIRST[:-1]:

                @pl.when(reach(me, 1 - way, k)[0])
                def _():
                    self.pass_on(way, k).wait_send()

    grads = Line(own, from_line, line_send, line_recv)
    outs = Line(out_own, out_line, out_send, out_recv)
    summed.load_all()
    load_out = pltpu.make_async_copy(out_ref, out_own, out_sem)
    load_out.start()
    greet_all(me, count)

    def give_gain(step):
        target = lax.rem(me.d + step, count)
        return remote(
            gain_ref.at[target], gain_in.at[step], gain_send.at[step], gain_recv.at[step], (target, me.t)
        )

    lead, lag, line_lag = 4, 2, 5
    last = len(FAR_FIRST)
    for i in range(lead):
        on(me, FAR_FIRST[i], summed.begin)
    for step in range(1, count):
        give_gain(step).start()
    load_out.wait()
    for k in range(LINE - 1, 0, -1):
        for way in range(2):
            outs.step(way, k, 0)
    order = [(behind, k) for behind in range(1, LINE) for k in range(LINE - 1 - behind, 0, -1)]
    for i in range(last + line_lag):
        if i + lead < last:
            on(me, FAR_FIRST[i + lead], summed.begin)
        if i < last:
            on(me, FAR_FIRST[i], summed.middle)
        if i < len(order):
            for way in range(2):
                outs.step(way, order[i][1], order[i][0])
        if 0 <= i - lag < last:
            on(me, FAR_FIRST[i - lag], summed.end)
        if 0 <= i - line_lag < last - 1:
            grads.step(*FAR_FIRST[i - line_lag])

    def add_out(landed):
        def act(at):
            output[at, :] = output[at, :] + landed[at, :].astype(F32)

        row_loop(output.shape[0], 16, act)

    def out_start(at):
        output[at, :] = x1_ref[at, :] + out_own[me.z, at, :].astype(F32)

    row_loop(output.shape[0], 16, out_start)
    outs.total(add_out)
    add_rows(a_out, (own.at[me.z],), rows)
    grads.total(lambda landed: add_rows(a_out, (a_out, landed), rows))

    total = gain_ref[me.d]
    for step in range(1, count):
        give_gain(step).wait()
        total += gain_in[step]
    gain_pair[0] = total
    swap = remote(gain_pair.at[0], gain_pair.at[1], gain_send.at[0], gain_recv.at[0], me.sibling())
    swap.start()
    swap.wait()
    gain_out[...] = gain_pair[0] + gain_pair[1]
    outs.finish()
    grads.finish()
    summed.finish()


def grad_sum(count, x1, ga, out_parts, gains):
    _, block, width = ga.shape
    _, rows, model = out_parts.shape
    buffers, sems = PlaneSum.scratch(count, block, width)
    return pl.pallas_call(
        functools.partial(grad_sum_kernel, count),
        name="grad_sum",
        out_shape=(
            jax.ShapeDtypeStruct((block, width), F32),
            jax.ShapeDtypeStruct((rows, model), F32),
            jax.ShapeDtypeStruct(gains.shape[1:], F32),
        ),
        in_specs=[VMEM, ANY, ANY, VMEM],
        out_specs=(VMEM,) * 3,
        scratch_shapes=[
            *buffers,
            pltpu.VMEM((2, LINE - 1, block, width), BF16),
            pltpu.VMEM(out_parts.shape, BF16),
            pltpu.VMEM((2, LINE - 1, rows, model), BF16),
            pltpu.VMEM(gains.shape, F32),
            pltpu.VMEM((2,) + gains.shape[1:], F32),
            *sems,
            DMA((2, LINE)), DMA((2, LINE)), DMA((2, LINE)), DMA((2, LINE)), DMA,
            DMA((count,)), DMA((count,)),
        ],
        compiler_params=pltpu.CompilerParams(
            collective_id=4, has_side_effects=True, vmem_limit_bytes=48 * MB
        ),
    )(x1, ga, out_parts, gains)


def shards(
    tokens, w_query, key_weight, value_weight, w_out, gain_attn, w_gate, w_up, w_down, gain_mlp,
    cotangent, lengths, seq_of_group,
):
    count = lax.axis_size("dp")
    local_rows = tokens.shape[0]
    full_rows = local_rows * lax.axis_size("tensor")
    rows = w_query.shape[0]
    model = rows * count
    q_width = w_query.shape[1]
    kv_width = key_weight.shape[1]
    units = w_gate.shape[1] // LINE
    chosen = jnp.sum(
        jnp.where(jnp.arange(lengths.shape[0], dtype=jnp.int32) == seq_of_group[0], lengths, 0)
    )
    positions = lax.axis_index("tensor") * local_rows + jnp.arange(local_rows, dtype=jnp.int32)
    row_ids = jnp.arange(full_rows, dtype=jnp.int32)
    key_allowed = (row_ids[None, :] <= row_ids[:, None]) & (row_ids[None, :] < chosen)
    cos, sin = (table[:, 0, :] for table in rope_tables(full_rows, HEAD_SIZE))
    dm = jnp.where((positions < chosen)[:, None], cotangent, jnp.zeros_like(cotangent))

    attn_pack = jnp.concatenate([w_query, key_weight, value_weight, w_out.T], axis=1)
    down_t = w_down.T
    mlp_pack = jnp.stack(
        [
            jnp.concatenate([m[:, z * units : (z + 1) * units] for m in (w_gate, w_up, down_t)], axis=1)
            for z in range(LINE)
        ]
    )
    lanes = -rows % 128
    gains = jnp.pad(jnp.stack([gain_attn, gain_mlp]), ((0, 14), (0, lanes)))
    attn_all, mlp_all, mlp_last, gains_all, tokens_all, dm_all = gather_all(
        count, attn_pack, mlp_pack, gains, tokens, dm
    )
    gains_full = gains_all[:, :2, :rows].transpose(1, 0, 2).reshape(2, model).astype(F32)
    x1, h2, h1, qkv, probs, attended, mlp_late = attention_forward(
        count, q_width // HEAD_SIZE, tokens_all, gains_full, cos, sin, key_allowed.astype(F32),
        attn_all, mlp_last,
    )
    grad_h2, out_parts, grad_mlp_w = feed_forward(
        count, h2, dm_all.reshape(-1, model), mlp_all, mlp_late
    )
    grad_attn_w, mlp_sum, grad_tokens, gain_parts = attention_backward(
        count, grad_h2, x1, dm, tokens_all, gains_full, cos, sin, h1, qkv, probs, attended, attn_all,
        grad_mlp_w,
    )
    gain_parts = gain_parts.reshape(2, count, rows).transpose(1, 0, 2)
    gain_parts = jnp.pad(gain_parts, ((0, 0), (0, 6), (0, lanes)))
    attn_sum, output, gain_sum = grad_sum(count, x1, grad_attn_w, out_parts, gain_parts)
    mlp_sum = mlp_sum.astype(F32)
    grad_gate_w, grad_up_w, grad_down_t = (
        jnp.concatenate([mlp_sum[z, :, i * units : (i + 1) * units] for z in range(LINE)], axis=1)
        for i in range(3)
    )
    return (
        output.astype(BF16),
        grad_tokens,
        attn_sum[:, :q_width],
        attn_sum[:, q_width : q_width + kv_width],
        attn_sum[:, q_width + kv_width : q_width + 2 * kv_width],
        attn_sum[:, q_width + 2 * kv_width :].T,
        gain_sum[0, :rows],
        grad_gate_w,
        grad_up_w,
        grad_down_t.T,
        gain_sum[1, :rows],
    )


def solution(mesh):
    both = P(("dp", "tensor"), None)
    row = P("dp", "tensor")
    column = P("tensor", "dp")
    in_specs = (
        both, row, row, row, column, P("dp"), row, row, column, P("dp"), both, P(), P("dp"),
    )
    out_specs = (both, both, row, row, row, column, P("dp"), row, row, column, P("dp"))
    return jax.shard_map(shards, mesh=mesh, in_specs=in_specs, out_specs=out_specs, check_vma=False)
```

```python
import functools
import math

import jax
import jax.numpy as jnp
from jax import lax
from jax.experimental import pallas as pl
from jax.experimental.pallas import tpu as pltpu
from jax.sharding import PartitionSpec as P

HEAD_SIZE = 256
EPS = 1e-06
THETA = 1000042.0
LINE = 4
MESH = pl.DeviceIdType.MESH
BF16 = jnp.bfloat16
F32 = jnp.float32
MB = 1024 * 1024


def rope_tables(count, head_dim):
    half = head_dim // 2
    index = jnp.arange(half, dtype=jnp.float32)
    freqs = jnp.exp(index * (-2.0 * math.log(THETA) / head_dim))
    angles = jnp.arange(count, dtype=jnp.float32)[:, None] * freqs[None, :]
    return (jnp.cos(angles)[:, None, :], jnp.sin(angles)[:, None, :])


def dot_tn(left, right):
    return lax.dot_general(left, right, (((0,), (0,)), ((), ())), preferred_element_type=F32)


class Place:
    def __init__(self, plane):
        self.d = lax.axis_index("dp")
        self.t = lax.axis_index("tensor")
        self.plane = plane
        self.z = lax.div(self.d, plane)
        self.p = lax.rem(self.d, plane)
        if plane == 4:
            x = lax.rem(self.p, 2)
            y = lax.div(self.p, 2)
            self.px = 2 * y + 1 - x
            self.py = 2 * (1 - y) + x
            self.pd = 2 * (1 - y) + 1 - x

    def at(self, z, p):
        return (z * self.plane + p, self.t)

    def sibling(self):
        return (self.d, 1 - self.t)


def remote(src, dst, send, recv, device):
    return pltpu.make_async_remote_copy(
        src_ref=src, dst_ref=dst, send_sem=send, recv_sem=recv, device_id=device, device_id_type=MESH
    )


def arrival(ref, sem):
    pltpu.make_async_copy(ref, ref, sem).wait()


def greet_all(me, count):
    barrier = pltpu.get_barrier_semaphore()
    for step in range(1, count):
        pl.semaphore_signal(
            barrier, inc=1, device_id=(lax.rem(me.d + step, count), me.t), device_id_type=MESH
        )
    pl.semaphore_signal(barrier, inc=1, device_id=me.sibling(), device_id_type=MESH)
    pl.semaphore_wait(barrier, count)


def greet_line(me):
    barrier = pltpu.get_barrier_semaphore()
    for step in range(1, LINE):
        pl.semaphore_signal(
            barrier, inc=1, device_id=me.at(lax.rem(me.z + step, LINE), me.p), device_id_type=MESH
        )
    pl.semaphore_signal(barrier, inc=1, device_id=me.sibling(), device_id_type=MESH)
    pl.semaphore_wait(barrier, LINE)


def reach(me, way, k):
    return (me.z >= k, me.z - k) if way == 0 else (me.z + k < LINE, me.z + k)


class Chain:
    def __init__(self, me, first, held, send, recv):
        self.me, self.first, self.held, self.send, self.recv = me, first, held, send, recv

    def copy(self, way, k):
        me = self.me
        _, origin = reach(me, way, k)
        target = me.z + 1 if way == 0 else me.z - 1
        src = self.first if k == 0 else self.held(origin)
        return remote(
            src, self.held(origin), self.send.at[way, k], self.recv.at[way, k + 1], me.at(target, me.p)
        )

    def goes(self, way, k):
        have, _ = reach(self.me, way, k)
        ahead, _ = reach(self.me, 1 - way, 1)
        return jnp.logical_and(have, ahead)

    def start(self, way, k):
        if k < LINE - 1:

            @pl.when(self.goes(way, k))
            def _():
                self.copy(way, k).start()

    def wait_block(self, way, k):
        _, origin = reach(self.me, way, k)
        arrival(self.held(origin), self.recv.at[way, k])

    def finish(self):
        for way in range(2):
            for k in range(LINE - 1):

                @pl.when(self.goes(way, k))
                def _():
                    self.copy(way, k).wait_send()


class PlaneGather:
    def __init__(self, me, job, held, rows, send, recv, late=None):
        self.me, self.job, self.held, self.send, self.recv = me, job, held, send, recv
        self.late = late
        self.half = rows // 2

    def piece(self, z, p, half):
        return self.held.at[z * self.me.plane + p, pl.ds(half * self.half, self.half)]

    def copy(self, z, kind, first=None):
        me = self.me
        if me.plane != 4:
            ref = first if first is not None else self.held.at[z * me.plane + me.p]
            target = lax.rem(me.p + kind + 1, me.plane)
            dst = self.held.at[z * me.plane + me.p]
        else:
            owner = (me.p, me.p, me.p, me.p, me.px, me.py)[kind]
            half = (0, 1, 1, 0, 0, 1)[kind]
            target = (me.px, me.px, me.py, me.py, me.py, me.px)[kind]
            dst = self.piece(z, owner, half)
            ref = dst if first is None else first.at[pl.ds(half * self.half, self.half)]
        return remote(
            ref, dst, self.send.at[self.job, z, kind], self.recv.at[self.job, z, kind], me.at(me.z, target)
        )

    def unless_late(self, z, act):
        if self.late is None:
            act()
        else:
            pl.when(z != self.late)(act)

    def start(self, z, first=None):
        kinds = (0, 2, 1, 3) if self.me.plane == 4 else range(self.me.plane - 1)

        def act():
            for kind in kinds:
                self.copy(z, kind, first).start()

        self.unless_late(z, act)

    def forward(self, z):
        def act():
            self.copy(z, 0).wait_recv()
            self.copy(z, 4).start()
            self.copy(z, 2).wait_recv()
            self.copy(z, 5).start()

        if self.me.plane == 4:
            self.unless_late(z, act)

    def finish(self, zs=range(LINE)):
        kinds = 6 if self.me.plane == 4 else self.me.plane - 1
        for z in zs:
            if z == self.late:
                continue
            for kind in range(kinds):
                copy = self.copy(z, kind)
                if self.me.plane != 4 or kind not in (0, 2):
                    copy.wait_recv()
                copy.wait_send()


def gather_kernel(
    count, a_ref, w_ref, gain_ref, tok_ref, dm_ref, a_all, w_all, w_last, gain_all, tok_all, dm_all,
    chain_send, chain_recv, part_send, part_recv, plane_send, plane_recv, gain_send, gain_recv,
    pair_send, pair_recv, local_sem,
):
    plane = count // LINE
    me = Place(plane)
    rows = a_ref.shape[0]
    late = LINE - 1
    own_w = [
        pltpu.make_async_copy(w_ref.at[me.z], w_all.at[me.d], local_sem.at[1]),
        pltpu.make_async_copy(w_ref.at[me.z], w_last, local_sem.at[1]),
    ]
    for ref, here in zip(own_w, (me.z != late, me.z == late)):

        @pl.when(here)
        def _():
            ref.start()

    local = [
        pltpu.make_async_copy(a_ref, a_all.at[me.d], local_sem.at[0]),
        pltpu.make_async_copy(gain_ref, gain_all.at[me.d], local_sem.at[2]),
        pltpu.make_async_copy(tok_ref, tok_all.at[me.t], local_sem.at[3]),
        pltpu.make_async_copy(dm_ref, dm_all.at[me.z, me.t], local_sem.at[4]),
    ]
    for copy in local:
        copy.start()
    greet_all(me, count)

    attn = Chain(me, a_ref, lambda z: a_all.at[z * plane + me.p], chain_send.at[0], chain_recv.at[0])
    dms = Chain(me, dm_ref, lambda z: dm_all.at[z, me.t], chain_send.at[1], chain_recv.at[1])
    planes = (
        PlaneGather(me, 0, a_all, rows, plane_send, plane_recv),
        PlaneGather(me, 1, w_all, rows, plane_send, plane_recv, late),
    )

    def part(way, k, last):
        _, target = reach(me, 1 - way, k)
        dst = w_last if last else w_all.at[me.d]
        return remote(
            w_ref.at[target], dst, part_send.at[way, k], part_recv.at[way, k], me.at(target, me.p)
        )

    def pair(z, first=None):
        src = dm_all.at[z, me.t] if first is None else first
        return remote(src, dm_all.at[z, me.t], pair_send.at[z], pair_recv.at[z], me.sibling())

    def start_parts(k):
        for way in range(2):
            for last in range(2):

                @pl.when(jnp.logical_and(reach(me, 1 - way, k)[0], (me.z == late) == bool(last)))
                def _():
                    part(way, k, last).start()

    def each(k, act):
        for way in range(2):
            have, z = reach(me, way, k)

            @pl.when(have)
            def _():
                act(way, k, z)

    def attn_step(way, k, z):
        attn.wait_block(way, k)
        attn.start(way, k)
        planes[0].start(z)

    def part_step(way, k, z):
        arrival(w_last, part_recv.at[way, k])
        planes[1].start(z)

    def dm_step(way, k, z):
        dms.wait_block(way, k)
        dms.start(way, k)
        pair(z).start()

    def give_gain(step):
        target = lax.rem(me.d + step, count)
        return remote(
            gain_ref, gain_all.at[me.d], gain_send.at[step], gain_recv.at[step], (target, me.t)
        )

    for way in range(2):
        attn.start(way, 0)
    planes[0].start(me.z, a_ref)
    tokens = remote(tok_ref, tok_all.at[me.t], pair_send.at[LINE], pair_recv.at[LINE], me.sibling())
    tokens.start()
    for step in range(1, count):
        give_gain(step).start()
    for k in range(1, LINE):
        each(k, attn_step)
        start_parts(k)
        if k == 1:
            planes[0].forward(me.z)
            planes[1].start(me.z, w_ref.at[me.z])
        else:
            each(k - 1, lambda way, k, z: planes[0].forward(z))
    for way in range(2):
        dms.start(way, 0)
    pair(me.z, dm_ref).start()
    for k in range(1, LINE):
        each(k, part_step)
        if k == 1:
            each(LINE - 1, lambda way, k, z: planes[0].forward(z))
            planes[1].forward(me.z)
        else:
            each(k - 1, lambda way, k, z: planes[1].forward(z))
            each(k - 1, dm_step)
    each(LINE - 1, lambda way, k, z: planes[1].forward(z))
    each(LINE - 1, dm_step)

    attn.finish()
    dms.finish()
    for k in range(1, LINE):
        for way in range(2):

            @pl.when(reach(me, 1 - way, k)[0])
            def _():
                part(way, k, 1).wait_send()

    for step in range(1, count):
        give_gain(step).wait()
    tokens.wait()
    for z in range(LINE):
        pair(z).wait()
    for job in planes:
        job.finish()
    for copy in local:
        copy.wait()
    own_w[1].wait()


ANY = pl.BlockSpec(memory_space=pl.ANY)
DMA = pltpu.SemaphoreType.DMA


def gather_all(count, attn, mlp, gains, tokens, dm):
    rows, width = attn.shape
    kinds = max(6, count // LINE - 1)
    return pl.pallas_call(
        functools.partial(gather_kernel, count),
        name="gather_all",
        out_shape=(
            jax.ShapeDtypeStruct((count, rows, width), BF16),
            jax.ShapeDtypeStruct((count - count // LINE, rows, width), BF16),
            jax.ShapeDtypeStruct((rows, width), BF16),
            jax.ShapeDtypeStruct((count,) + gains.shape, gains.dtype),
            jax.ShapeDtypeStruct((2,) + tokens.shape, BF16),
            jax.ShapeDtypeStruct((LINE, 2) + dm.shape, BF16),
        ),
        in_specs=[ANY] * 5,
        out_specs=(ANY,) * 6,
        scratch_shapes=[
            DMA((2, 2, LINE)), DMA((2, 2, LINE)), DMA((2, LINE)), DMA((2, LINE)),
            DMA((2, LINE, kinds)), DMA((2, LINE, kinds)), DMA((count,)), DMA((count,)),
            DMA((LINE + 1,)), DMA((LINE + 1,)), DMA((5,)),
        ],
        compiler_params=pltpu.CompilerParams(collective_id=0, has_side_effects=True),
    )(attn, mlp, gains, tokens, dm)


RANKS = ((3, 2, 1, 0), (3, 0, 2, 1), (0, 3, 1, 2), (0, 1, 2, 3))
FAR_FIRST = [(way, k) for k in range(LINE - 1, 0, -1) for way in range(2)]


def ranked(me, rank):
    z = jnp.int32(RANKS[0][rank])
    for at in range(1, LINE):
        z = jnp.where(me.z == at, RANKS[at][rank], z)
    return z


def way_to(me, z):
    down = (z < me.z).astype(jnp.int32)
    return down, jnp.where(z < me.z, me.z - z, z - me.z)


def add_rows(target, terms, rows, start=0):
    step = 16

    @pl.loop(0, rows // step)
    def _(i):
        at = pl.ds(pl.multiple_of(start + i * step, step), step)
        total = terms[0][at].astype(F32)
        for term in terms[1:]:
            total += term[at].astype(F32)
        target[at] = total.astype(target.dtype)


class PlaneSum:
    def __init__(self, me, grad, own, other, first, second, sems, ranks=range(LINE)):
        self.me, self.grad, self.own, self.other, self.first, self.second = me, grad, own, other, first, second
        (
            self.first_send, self.first_recv, self.second_send, self.second_recv, self.load_sem, self.other_sem,
        ) = sems
        self.ranks = ranks
        self.rows = own.shape[1]
        half = self.rows // 2
        self.half = half
        self.halves = (pl.ds(0, half), pl.ds(half, half))
        self.square = me.plane == 4
        if self.square:
            self.near = (me.px, me.py)
            self.far = (me.py, me.px)

    def slot(self, rank):
        return rank - self.ranks[0]

    def block(self, rank, p):
        return self.grad.at[ranked(self.me, rank) * self.me.plane + p]

    def load(self, rank):
        s = self.slot(rank)
        return pltpu.make_async_copy(self.block(rank, self.me.p), self.own.at[s], self.load_sem.at[s])

    def load_other(self, rank, i):
        s = self.slot(rank)
        return pltpu.make_async_copy(
            self.block(rank, self.far[i]).at[self.halves[i]], self.other.at[s, self.halves[i]],
            self.other_sem.at[s, i],
        )

    def load_all(self):
        for rank in self.ranks:
            self.load(rank).start()
            if self.square:
                for i in range(2):
                    self.load_other(rank, i).start()

    def give(self, rank, i, which):
        me, s = self.me, self.slot(rank)
        if not self.square:
            target = lax.rem(me.p + which + 1, me.plane)
            return remote(
                self.block(rank, target), self.first.at[s, which], self.first_send.at[s, which],
                self.first_recv.at[s, which], me.at(me.z, target),
            )
        owner = (self.near[i], me.pd)[which]
        return remote(
            self.block(rank, owner).at[self.halves[i]], self.first.at[s, which, self.halves[i]],
            self.first_send.at[s, 2 * i + which], self.first_recv.at[s, 2 * i + which],
            me.at(me.z, self.near[i]),
        )

    def give_both(self, rank, i):
        s = self.slot(rank)
        return remote(
            self.other.at[s, self.halves[i]], self.second.at[s, self.halves[i]],
            self.second_send.at[s, i], self.second_recv.at[s, i], self.me.at(self.me.z, self.far[i]),
        )

    def gives(self, rank):
        if self.square:
            return [self.give(rank, i, which) for which in (1, 0) for i in range(2)]
        return [self.give(rank, 0, which) for which in range(self.me.plane - 1)]

    def begin(self, rank):
        for copy in self.gives(rank):
            copy.start()

    def middle(self, rank):
        if not self.square:
            return
        s = self.slot(rank)
        for i in range(2):
            arrival(self.first.at[s, 1, self.halves[i]], self.first_recv.at[s, 2 * i + 1])
            self.load_other(rank, i).wait()
            add_rows(
                self.other.at[s], (self.other.at[s], self.first.at[s, 1]), self.half, i * self.half
            )
            self.give_both(rank, i).start()

    def end(self, rank):
        s = self.slot(rank)
        self.load(rank).wait()
        if self.square:
            for i in range(2):
                arrival(self.first.at[s, 0, self.halves[i]], self.first_recv.at[s, 2 * i])
                arrival(self.second.at[s, self.halves[i]], self.second_recv.at[s, i])
            terms = (self.first.at[s, 0], self.second.at[s])
        else:
            for which in range(self.me.plane - 1):
                arrival(self.first.at[s, which], self.first_recv.at[s, which])
            terms = tuple(self.first.at[s, which] for which in range(self.me.plane - 1))
        add_rows(self.own.at[s], (self.own.at[s],) + terms, self.rows)

    def finish(self):
        for rank in self.ranks:
            for copy in self.gives(rank):
                copy.wait_send()
            if self.square:
                for i in range(2):
                    self.give_both(rank, i).wait_send()

    @staticmethod
    def scratch(count, rows, width, ranks=LINE):
        plane = count // LINE
        square = plane == 4
        slots = 2 if square else plane - 1
        small = (ranks, rows, width) if square else (1, 16, 128)
        return [
            pltpu.VMEM((ranks, rows, width), BF16),
            pltpu.VMEM(small, BF16),
            pltpu.VMEM((ranks, slots, rows, width), BF16),
            pltpu.VMEM(small, BF16),
        ], [
            DMA((ranks, max(4, slots))), DMA((ranks, max(4, slots))), DMA((ranks, 2)), DMA((ranks, 2)),
            DMA((ranks,)), DMA((ranks, 2)),
        ]


def dot_cols(left, right):
    return lax.dot_general(left, right, (((1,), (1,)), ((), ())), preferred_element_type=F32)


def feed_forward_kernel(
    plane, h_ref, dm_ref, w_ref, w_late, total_ref, out_ref, grad_ref, sum_ref, rows_in, weights, inner, part,
    from_pair, from_line, own, other, first, second, first_send, first_recv, second_send, second_recv,
    own_sem, other_sem, chain_send, chain_recv, pass_send, pass_recv, pair_send, pair_recv,
    line_send, line_recv, load_sem, dm_sem, grad_sem, out_sem,
):
    me = Place(plane)
    rows, model = h_ref.shape
    units = inner.shape[1]
    wide = 2 * rows
    tokens = LINE * wide
    most, block, _ = w_ref.shape
    tile = 512

    def slot(z, t):
        return rows_in.at[pl.ds(pl.multiple_of((z * 2 + t) * rows, rows), rows)]

    loads = [
        pltpu.make_async_copy(w_ref, weights.at[pl.ds(0, most)], load_sem.at[0]),
        pltpu.make_async_copy(w_late, weights.at[pl.ds(most, plane)], load_sem.at[2]),
    ]
    for load in loads:
        load.start()
    load_dm = pltpu.make_async_copy(dm_ref, rows_in.at[pl.ds(tokens, tokens)], dm_sem)
    load_dm.start()
    keep = pltpu.make_async_copy(h_ref, slot(me.z, me.t), load_sem.at[1])
    keep.start()
    greet_all(me, plane * LINE)
    summed = PlaneSum(
        me, weights, own, other, first, second,
        (first_send, first_recv, second_send, second_recv, own_sem, other_sem), range(1),
    )
    chain = Chain(me, h_ref, lambda z: slot(z, me.t), chain_send, chain_recv)

    def share(z, first=None):
        src = slot(z, me.t) if first is None else first
        return remote(src, slot(z, me.t), pass_send.at[z], pass_recv.at[z], me.sibling())

    for way in range(2):
        chain.start(way, 0)
    share(me.z, h_ref).start()

    def w_rows(n, width, column):
        return weights[pl.ds(n * (width // block), width // block), :, pl.ds(column, units)].reshape(
            width, units
        )

    def compute(z):
        at = pl.ds(pl.multiple_of(z * wide, wide), wide)
        dm_at = pl.ds(pl.multiple_of(tokens + z * wide, wide), wide)

        @pl.loop(0, units // tile)
        def _(c):
            def column(job):
                return weights[:, :, pl.ds(pl.multiple_of(job * units + c * tile, tile), tile)].reshape(
                    model, tile
                )

            h = rows_in[at, :]
            gate = jnp.dot(h, column(0), preferred_element_type=F32)
            up = jnp.dot(h, column(1), preferred_element_type=F32)
            grad_hidden = jnp.dot(rows_in[dm_at, :], column(2), preferred_element_type=F32)
            sigmoid = jax.nn.sigmoid(gate)
            silu = gate * sigmoid
            here = pl.ds(pl.multiple_of(c * tile, tile), tile)
            inner[at, here] = (silu * up).astype(BF16)
            inner[pl.ds(pl.multiple_of(tokens + z * wide, wide), wide), here] = (
                grad_hidden * up * sigmoid * (1.0 + gate * (1.0 - sigmoid))
            ).astype(BF16)
            inner[pl.ds(pl.multiple_of(2 * tokens + z * wide, wide), wide), here] = (
                grad_hidden * silu
            ).astype(BF16)

        @pl.loop(0, model // tile)
        def _(n):
            here = pl.ds(pl.multiple_of(n * tile, tile), tile)
            grad = dot_cols(inner[pl.ds(pl.multiple_of(tokens + z * wide, wide), wide)], w_rows(n, tile, 0))
            grad += dot_cols(
                inner[pl.ds(pl.multiple_of(2 * tokens + z * wide, wide), wide)], w_rows(n, tile, units)
            )
            part[0, z, :, :, here] = grad.astype(BF16).reshape(2, rows, tile)

        pair(0, z).start()

        @pl.loop(0, model // tile)
        def _(n):
            here = pl.ds(pl.multiple_of(n * tile, tile), tile)
            out = dot_cols(inner[at, :], w_rows(n, tile, 2 * units))
            part[1, z, :, :, here] = out.astype(BF16).reshape(2, rows, tile)

        pair(1, z).start()

    def pair(job, z):
        return remote(
            part.at[job, z, 1 - me.t], from_pair.at[job, z], pair_send.at[job, z],
            pair_recv.at[job, z], me.sibling(),
        )

    half = rows // 2
    halves = (pl.ds(0, half), pl.ds(half, half))

    def pass_on(way, k, i):
        _, target = reach(me, 1 - way, k)
        ahead = me.z + 1 if way == 0 else me.z - 1
        return remote(
            part.at[0, target, me.t, halves[i]], from_line.at[way, k - 1, halves[i]],
            line_send.at[way, k, i], line_recv.at[way, k - 1, i], me.at(ahead, me.p),
        )

    def line(way, k, behind):
        have, z = reach(me, 1 - way, k)
        before = me.z if way == 0 else LINE - 1 - me.z

        @pl.when(jnp.logical_and(have, before == behind))
        def _():
            pair(0, z).wait_recv()
            terms = (part.at[0, z, me.t], from_pair.at[0, z])
            if behind:
                terms += (from_line.at[way, k],)
            for i in range(2):
                if behind:
                    arrival(from_line.at[way, k, halves[i]], line_recv.at[way, k, i])
                add_rows(part.at[0, z, me.t], terms, half, i * half)
                pass_on(way, k, i).start()

    def total():
        pair(0, me.z).wait_recv()
        add_rows(total_ref, (part.at[0, me.z, me.t], from_pair.at[0, me.z]), rows)
        for way in range(2):

            @pl.when(reach(me, way, 1)[0])
            def _():
                for i in range(2):
                    arrival(from_line.at[way, 0, halves[i]], line_recv.at[way, 0, i])
                    add_rows(total_ref, (total_ref, from_line.at[way, 0]), half, i * half)

    def grads(z):
        per = plane * block

        @pl.loop(0, per // tile)
        def _(n):
            column = pl.ds(pl.multiple_of(z * per + n * tile, tile), tile)
            h = rows_in[pl.ds(0, tokens), column].T
            dm = rows_in[pl.ds(tokens, tokens), column].T
            there = pl.ds((z * per + n * tile) // block, tile // block)
            for job in range(3):
                left = (h, h, dm)[job]
                start = (tokens, 2 * tokens, 0)[job]
                for c in range(units // 512):
                    grad = jnp.dot(
                        left, inner[pl.ds(start, tokens), c * 512 : (c + 1) * 512],
                        preferred_element_type=F32,
                    )
                    weights[there, :, job * units + c * 512 : job * units + (c + 1) * 512] = (
                        grad.astype(BF16).reshape(tile // block, block, 512)
                    )

        keep_grads(z).start()

    def keep_grads(z):
        return pltpu.make_async_copy(
            weights.at[pl.ds(z * plane, plane)], grad_ref.at[pl.ds(z * plane, plane)], grad_sem.at[z]
        )

    keep.wait()
    for load in loads:
        load.wait()
    load_dm.wait()
    for k in range(LINE):
        for way in range(2 if k else 1):
            have, z = reach(me, way, k)

            @pl.when(have)
            def _():
                if k:
                    chain.wait_block(way, k)
                    chain.start(way, k)
                    share(z).start()
                arrival(slot(z, 1 - me.t), pass_recv.at[z])
                compute(z)

        if k:
            for way in range(2):
                line(1 - way, k, 0)
    order = [(behind, k) for behind in range(1, LINE) for k in range(1, LINE - behind)]
    order.sort(key=lambda e: (2 * e[0] + e[1], e[0]))

    def keep_out(z):
        return pltpu.make_async_copy(part.at[1, z, me.t], out_ref.at[z], out_sem.at[z])

    for i in range(LINE):
        grads(ranked(me, i))
        if i == 0:
            summed.load_all()
            summed.begin(0)
        if i == 1:
            summed.middle(0)
        if i < len(order):
            for way in range(2):
                line(way, order[i][1], order[i][0])
    for z in range(LINE):
        pair(1, z).wait_recv()
        add_rows(part.at[1, z, me.t], (part.at[1, z, me.t], from_pair.at[1, z]), rows)
        keep_out(z).start()
    summed.end(0)
    keep_sum = pltpu.make_async_copy(own.at[0], sum_ref, load_sem.at[0])
    keep_sum.start()
    total()

    summed.finish()
    keep_sum.wait()
    chain.finish()
    for z in range(LINE):
        share(z).wait_send()
        keep_grads(z).wait()
        keep_out(z).wait()
        for job in range(2):
            pair(job, z).wait_send()
    for k in range(1, LINE):
        for way in range(2):

            @pl.when(reach(me, 1 - way, k)[0])
            def _():
                for i in range(2):
                    pass_on(way, k, i).wait_send()


def feed_forward(count, h, dm_all, w_all, w_late):
    rows, model = h.shape
    units = w_all.shape[2] // 3
    grads = (count,) + w_all.shape[1:]
    buffers, sems = PlaneSum.scratch(count, *w_late.shape[1:], 1)
    tokens = LINE * 2 * rows
    vmem = pl.BlockSpec(memory_space=pltpu.VMEM)
    return pl.pallas_call(
        functools.partial(feed_forward_kernel, count // LINE),
        name="feed_forward",
        out_shape=(
            jax.ShapeDtypeStruct((rows, model), F32),
            jax.ShapeDtypeStruct((LINE, rows, model), BF16),
            jax.ShapeDtypeStruct(grads, BF16),
            jax.ShapeDtypeStruct(w_late.shape[1:], BF16),
        ),
        in_specs=[vmem, ANY, ANY, ANY],
        out_specs=(vmem, ANY, ANY, ANY),
        scratch_shapes=[
            pltpu.VMEM((2 * tokens, model), BF16),
            pltpu.VMEM(grads, BF16),
            pltpu.VMEM((3 * tokens, units), BF16),
            pltpu.VMEM((2, LINE, 2, rows, model), BF16),
            pltpu.VMEM((2, LINE, rows, model), BF16),
            pltpu.VMEM((2, LINE - 1, rows, model), BF16),
            *buffers,
            *sems,
            DMA((2, LINE)), DMA((2, LINE)), DMA((LINE,)), DMA((LINE,)), DMA((2, LINE)), DMA((2, LINE)),
            DMA((2, LINE, 2)), DMA((2, LINE, 2)), DMA((3,)), DMA, DMA((LINE,)), DMA((LINE,)),
        ],
        compiler_params=pltpu.CompilerParams(
            collective_id=1, has_side_effects=True, vmem_limit_bytes=60 * MB
        ),
    )(h, dm_all, w_all, w_late)


def greet_plane(me):
    barrier = pltpu.get_barrier_semaphore()
    for step in range(1, me.plane):
        target = lax.rem(me.p + step, me.plane)
        pl.semaphore_signal(barrier, inc=1, device_id=me.at(me.z, target), device_id_type=MESH)
    pl.semaphore_signal(barrier, inc=1, device_id=me.sibling(), device_id_type=MESH)
    pl.semaphore_wait(barrier, me.plane)


def row_loop(rows, step, act):
    @pl.loop(0, rows // step)
    def _(i):
        act(pl.ds(pl.multiple_of(i * step, step), step))


def columns_of(weights, start, width):
    count, rows, _ = weights.shape
    return weights[:, :, pl.ds(start, width)].reshape(count * rows, width)


def rows_of(weights, n, height, start, width):
    _, rows, _ = weights.shape
    per = height // rows
    return weights[pl.ds(n * per, per), :, pl.ds(start, width)].reshape(height, width)


def attention_forward_kernel(
    plane, tok_ref, gain_ref, cos_ref, sin_ref, mask_ref, a_ref, w_last, x1_ref, h2_ref, h1_ref,
    qkv_ref, probs_ref, o_ref, w_late, weights, part, from_pair, plane_send, plane_recv, pair_send,
    pair_recv, load_sem,
):
    me = Place(plane)
    _, rows, model = tok_ref.shape
    wide = 2 * rows
    heads, _, _ = probs_ref.shape
    q_width = heads * HEAD_SIZE
    kv_width = (qkv_ref.shape[1] - q_width) // 2
    kv_heads = kv_width // HEAD_SIZE
    half = HEAD_SIZE // 2
    load = pltpu.make_async_copy(a_ref, weights, load_sem.at[0])
    load.start()
    keep = pltpu.make_async_copy(w_last, w_late.at[me.p], load_sem.at[1])
    keep.start()
    greet_plane(me)
    gather = PlaneGather(me, 0, w_late, w_last.shape[0], plane_send, plane_recv)
    gather.start(0, w_last)

    for t in range(2):

        def norm(at, t=t):
            x = tok_ref[t, at, :].astype(F32)
            factor = lax.rsqrt(jnp.mean(x * x, -1, keepdims=True) + EPS)
            h1_ref[pl.ds(t * rows + at.start, at.size), :] = (x * factor * gain_ref[0:1, :]).astype(BF16)

        row_loop(rows, 32, norm)
    load.wait()

    def project(i):
        start = pl.multiple_of(i * HEAD_SIZE, HEAD_SIZE)
        return start, jnp.dot(
            h1_ref[...], columns_of(weights, start, HEAD_SIZE), preferred_element_type=F32
        )

    @pl.loop(0, heads + kv_heads)
    def _(i):
        start, values = project(i)
        first, second = values[:, :half], values[:, half:]
        cos, sin = cos_ref[...], sin_ref[...]
        qkv_ref[:, pl.ds(start, half)] = (first * cos - second * sin).astype(BF16)
        qkv_ref[:, pl.ds(start + half, half)] = (second * cos + first * sin).astype(BF16)

    @pl.loop(heads + kv_heads, heads + 2 * kv_heads)
    def _(i):
        start, values = project(i)
        qkv_ref[:, pl.ds(start, HEAD_SIZE)] = values.astype(BF16)

    gather.forward(0)
    for i in range(heads):
        m = i * kv_heads // heads
        q = qkv_ref[:, i * HEAD_SIZE : (i + 1) * HEAD_SIZE]
        k = qkv_ref[:, q_width + m * HEAD_SIZE : q_width + (m + 1) * HEAD_SIZE]
        v = qkv_ref[:, q_width + kv_width + m * HEAD_SIZE : q_width + kv_width + (m + 1) * HEAD_SIZE]
        scores = dot_cols(q, k) * HEAD_SIZE ** (-0.5)
        scores = jnp.where(mask_ref[...] > 0, scores, -1e30)
        grown = jnp.exp(scores - jnp.max(scores, -1, keepdims=True))
        probs = grown / jnp.sum(grown, -1, keepdims=True)
        probs_ref[i] = probs
        o_ref[:, i * HEAD_SIZE : (i + 1) * HEAD_SIZE] = jnp.dot(
            probs.astype(BF16), v, preferred_element_type=F32
        ).astype(BF16)

    tile = 512

    @pl.loop(0, model // tile)
    def _(n):
        here = pl.ds(pl.multiple_of(n * tile, tile), tile)
        value = dot_cols(o_ref[...], rows_of(weights, n, tile, q_width + 2 * kv_width, q_width))
        part[:, :, here] = value.reshape(2, rows, tile)

    swap = remote(part.at[1 - me.t], from_pair, pair_send, pair_recv, me.sibling())
    swap.start()
    swap.wait_recv()

    def add(at):
        x1 = tok_ref[me.t, at, :].astype(F32) + (part[me.t, at, :] + from_pair[at, :])
        x1_ref[at, :] = x1
        factor = lax.rsqrt(jnp.mean(x1 * x1, -1, keepdims=True) + EPS)
        h2_ref[at, :] = (x1 * factor * gain_ref[1:2, :]).astype(BF16)

    row_loop(rows, 32, add)
    swap.wait_send()
    gather.finish(range(1))
    keep.wait()


VMEM = pl.BlockSpec(memory_space=pltpu.VMEM)


def attention_forward(count, heads, tokens_all, gains, cos, sin, mask, attn_all, w_last):
    _, rows, model = tokens_all.shape
    wide = 2 * rows
    q_width = heads * HEAD_SIZE
    qkv_width = attn_all.shape[2] - q_width
    plane = count // LINE
    kinds = max(6, plane - 1)
    return pl.pallas_call(
        functools.partial(attention_forward_kernel, plane),
        name="attention_forward",
        out_shape=(
            jax.ShapeDtypeStruct((rows, model), F32),
            jax.ShapeDtypeStruct((rows, model), BF16),
            jax.ShapeDtypeStruct((wide, model), BF16),
            jax.ShapeDtypeStruct((wide, qkv_width), BF16),
            jax.ShapeDtypeStruct((heads, wide, wide), F32),
            jax.ShapeDtypeStruct((wide, q_width), BF16),
            jax.ShapeDtypeStruct((plane,) + w_last.shape, BF16),
        ),
        in_specs=[VMEM] * 5 + [ANY] * 2,
        out_specs=(VMEM,) * 6 + (ANY,),
        scratch_shapes=[
            pltpu.VMEM(attn_all.shape, BF16),
            pltpu.VMEM((2, rows, model), F32),
            pltpu.VMEM((rows, model), F32),
            DMA((1, 1, kinds)), DMA((1, 1, kinds)), DMA, DMA, DMA((2,)),
        ],
        compiler_params=pltpu.CompilerParams(
            collective_id=2, has_side_effects=True, vmem_limit_bytes=48 * MB
        ),
    )(tokens_all, gains, cos, sin, mask, attn_all, w_last)


def attention_backward_kernel(
    plane, total_ref, x1_ref, dm_ref, tok_ref, gain_ref, cos_ref, sin_ref, h1_ref, qkv_ref, probs_ref,
    o_ref, a_ref, gw_ref, sum_ref, ga_ref, w_out, grad_tokens, gain_parts, weights, own, other, first, second,
    dx, da, do, dqkv, dh1, from_pair, first_send, first_recv, second_send, second_recv, load_sem,
    other_sem, part_send, part_recv, pair_send, pair_recv, a_sem, keep_sem, grad_sem,
):
    me = Place(plane)
    _, rows, model = tok_ref.shape
    block = weights.shape[1]
    heads, _, _ = probs_ref.shape
    q_width = heads * HEAD_SIZE
    qkv_width = qkv_ref.shape[1]
    kv_width = (qkv_width - q_width) // 2
    kv_heads = kv_width // HEAD_SIZE
    half = HEAD_SIZE // 2
    scale = HEAD_SIZE ** (-0.5)
    summed = PlaneSum(
        me, gw_ref, own, other, first, second,
        (first_send, first_recv, second_send, second_recv, load_sem, other_sem), range(1, LINE),
    )
    load = pltpu.make_async_copy(a_ref, weights, a_sem)
    load.start()
    summed.load_all()
    greet_all(me, plane * LINE)

    def part(rank):
        target = ranked(me, rank)
        way, k = way_to(me, target)
        src = own.at[summed.slot(rank)] if rank else sum_ref
        return remote(
            src, w_out.at[me.z], part_send.at[way, k], part_recv.at[way, k], me.at(target, me.p)
        )

    give_da = remote(da.at[me.t], da.at[me.t], pair_send.at[0], pair_recv.at[0], me.sibling())
    give_dh1 = remote(dh1.at[1 - me.t], from_pair, pair_send.at[1], pair_recv.at[1], me.sibling())

    def mid_norm():
        gain_parts[...] = jnp.zeros_like(gain_parts)

        def act(at):
            x, up = x1_ref[at, :], total_ref[at, :]
            factor = lax.rsqrt(jnp.mean(x * x, -1, keepdims=True) + EPS)
            scaled = up * gain_ref[1:2, :]
            grad = dm_ref[at, :].astype(F32) + (
                factor * scaled - x * factor**3 * jnp.mean(scaled * x, -1, keepdims=True)
            )
            dx[at, :] = grad
            da[me.t, at, :] = grad.astype(BF16)
            gain_parts[1:2, :] += jnp.sum(up * x * factor, 0, keepdims=True)

        row_loop(rows, 32, act)
        give_da.start()

    def grad_o():
        load.wait()
        give_da.wait_recv()

        @pl.loop(0, q_width // HEAD_SIZE)
        def _(c):
            here = pl.multiple_of(c * HEAD_SIZE, HEAD_SIZE)
            value = jnp.dot(
                da[...].reshape(2 * rows, model),
                columns_of(weights, qkv_width + here, HEAD_SIZE),
                preferred_element_type=F32,
            )
            do[:, pl.ds(here, HEAD_SIZE)] = value.astype(BF16)

    def rotate(values, start):
        first, second = values[:, :half], values[:, half:]
        cos, sin = cos_ref[...], sin_ref[...]
        dqkv[:, start : start + half] = (first * cos + second * sin).astype(BF16)
        dqkv[:, start + half : start + 2 * half] = (second * cos - first * sin).astype(BF16)

    def grad_heads():
        group = heads // kv_heads
        for m in range(kv_heads):
            at_k = q_width + m * HEAD_SIZE
            at_v = at_k + kv_width
            k = qkv_ref[:, at_k : at_k + HEAD_SIZE]
            v = qkv_ref[:, at_v : at_v + HEAD_SIZE]
            grad_k = grad_v = None
            for i in range(m * group, (m + 1) * group):
                at = slice(i * HEAD_SIZE, (i + 1) * HEAD_SIZE)
                probs = probs_ref[i]
                grad_probs = dot_cols(do[:, at], v)
                grad_scores = probs * (
                    grad_probs - jnp.sum(probs * grad_probs, -1, keepdims=True)
                )
                low = grad_scores.astype(BF16)
                rotate(jnp.dot(low, k, preferred_element_type=F32) * scale, i * HEAD_SIZE)
                more_k = dot_tn(low, qkv_ref[:, at])
                more_v = dot_tn(probs.astype(BF16), do[:, at])
                grad_k = more_k if grad_k is None else grad_k + more_k
                grad_v = more_v if grad_v is None else grad_v + more_v
            rotate(grad_k * scale, at_k)
            dqkv[:, at_v : at_v + HEAD_SIZE] = grad_v.astype(BF16)

    tile = 512

    def grad_h1():
        @pl.loop(0, model // tile)
        def _(n):
            here = pl.ds(pl.multiple_of(n * tile, tile), tile)
            value = dot_cols(dqkv[...], rows_of(weights, n, tile, 0, qkv_width))
            dh1[:, :, here] = value.reshape(2, rows, tile)

        give_dh1.start()

    def keep_grads(n):
        per = tile // block
        return pltpu.make_async_copy(
            weights.at[pl.ds(n * per, per)], ga_ref.at[pl.ds(n * per, per)], grad_sem.at[n]
        )

    def grads():
        @pl.loop(0, model // tile)
        def _(n):
            here = pl.ds(pl.multiple_of(n * tile, tile), tile)
            there = pl.ds(n * (tile // block), tile // block)
            left = h1_ref[:, here].T
            for c in range(qkv_width // tile):
                at = slice(c * tile, (c + 1) * tile)
                value = jnp.dot(left, dqkv[:, at], preferred_element_type=F32)
                weights[there, :, at] = value.astype(BF16).reshape(tile // block, block, tile)
            left = da[:, :, here].reshape(2 * rows, tile).T
            for c in range(q_width // tile):
                at = slice(c * tile, (c + 1) * tile)
                value = jnp.dot(left, o_ref[:, at], preferred_element_type=F32)
                at = slice(qkv_width + c * tile, qkv_width + (c + 1) * tile)
                weights[there, :, at] = value.astype(BF16).reshape(tile // block, block, tile)

        for n in range(model // tile):
            keep_grads(n).start()

    def in_norm():
        give_dh1.wait_recv()

        def act(at):
            x = tok_ref[me.t, at, :].astype(F32)
            up = dh1[me.t, at, :] + from_pair[at, :]
            factor = lax.rsqrt(jnp.mean(x * x, -1, keepdims=True) + EPS)
            scaled = up * gain_ref[0:1, :]
            grad_tokens[at, :] = dx[at, :] + (
                factor * scaled - x * factor**3 * jnp.mean(scaled * x, -1, keepdims=True)
            )
            gain_parts[0:1, :] += jnp.sum(up * x * factor, 0, keepdims=True)

        row_loop(rows, 32, act)

    summed.begin(1)
    part(0).start()
    mid_norm()
    grad_o()
    stages = [[], [grad_heads, grad_h1], [grads], [in_norm]]
    for rank in range(1, LINE):
        summed.middle(rank)
        if rank + 1 < LINE:
            summed.begin(rank + 1)
        for stage in stages[rank]:
            stage()
        summed.end(rank)
        if rank < LINE - 1:
            part(rank).start()

    keep = pltpu.make_async_copy(own.at[LINE - 2], w_out.at[me.z], keep_sem)
    keep.start()
    for rank in range(LINE - 1):
        part(rank).wait_send()
    for way, k in FAR_FIRST:

        @pl.when(reach(me, way, k)[0])
        def _():
            arrival(w_out.at[me.z], part_recv.at[way, k])

    summed.finish()
    give_da.wait_send()
    give_dh1.wait_send()
    for n in range(model // tile):
        keep_grads(n).wait()
    keep.wait()


def attention_backward(
    count, total, x1, dm, tokens_all, gains, cos, sin, h1, qkv, probs, o, attn_all, grad_mlp, first_sum
):
    _, rows, model = tokens_all.shape
    _, block, width = attn_all.shape
    wide = 2 * rows
    heads = probs.shape[0]
    q_width = heads * HEAD_SIZE
    buffers, sems = PlaneSum.scratch(count, block, width, LINE - 1)
    return pl.pallas_call(
        functools.partial(attention_backward_kernel, count // LINE),
        name="attention_backward",
        out_shape=(
            jax.ShapeDtypeStruct(attn_all.shape, BF16),
            jax.ShapeDtypeStruct((LINE, block, width), BF16),
            jax.ShapeDtypeStruct((rows, model), F32),
            jax.ShapeDtypeStruct((2, model), F32),
        ),
        in_specs=[VMEM] * 11 + [ANY] * 3,
        out_specs=(ANY, ANY, VMEM, VMEM),
        scratch_shapes=[
            pltpu.VMEM(attn_all.shape, BF16),
            *buffers,
            pltpu.VMEM((rows, model), F32),
            pltpu.VMEM((2, rows, model), BF16),
            pltpu.VMEM((wide, q_width), BF16),
            pltpu.VMEM(qkv.shape, BF16),
            pltpu.VMEM((2, rows, model), F32),
            pltpu.VMEM((rows, model), F32),
            *sems,
            DMA((2, LINE)), DMA((2, LINE)), DMA((2,)), DMA((2,)), DMA, DMA, DMA((model // 512,)),
        ],
        compiler_params=pltpu.CompilerParams(
            collective_id=3, has_side_effects=True, vmem_limit_bytes=60 * MB
        ),
    )(total, x1, dm, tokens_all, gains, cos, sin, h1, qkv, probs, o, attn_all, grad_mlp, first_sum)


def grad_sum_kernel(
    count, x1_ref, ga_ref, out_ref, gain_ref, a_out, output, gain_out, own, other, first, second,
    from_line, out_own, out_line, gain_in, gain_pair, first_send, first_recv, second_send, second_recv,
    load_sem, other_sem, line_send, line_recv, out_send, out_recv, out_sem, gain_send, gain_recv,
):
    plane = count // LINE
    me = Place(plane)
    rows = a_out.shape[0]
    summed = PlaneSum(
        me, ga_ref, own, other, first, second,
        (first_send, first_recv, second_send, second_recv, load_sem, other_sem),
    )

    class Line:
        def __init__(self, held, landing, send, recv):
            self.held, self.landing, self.send, self.recv = held, landing, send, recv

        def pass_on(self, rank):
            way, k = way_to(me, ranked(me, rank))
            ahead = jnp.where(way == 0, me.z + 1, me.z - 1)
            return remote(
                self.held(rank), self.landing.at[way, k - 1], self.send.at[way, k],
                self.recv.at[way, k - 1], me.at(ahead, me.p),
            )

        def step(self, rank):
            way, k = way_to(me, ranked(me, rank))
            before = jnp.where(way == 0, me.z, LINE - 1 - me.z)
            held = self.held(rank)

            @pl.when(before > 0)
            def _():
                arrival(self.landing.at[way, k], self.recv.at[way, k])
                add_rows(held, (held, self.landing.at[way, k]), held.shape[0])

            self.pass_on(rank).start()

        def total(self, act):
            for way in range(2):

                @pl.when(reach(me, way, 1)[0])
                def _():
                    arrival(self.landing.at[way, 0], self.recv.at[way, 0])
                    act(self.landing.at[way, 0])

        def finish(self):
            for rank in range(LINE - 1):
                self.pass_on(rank).wait_send()

    grads = Line(lambda rank: own.at[rank], from_line, line_send, line_recv)
    outs = Line(lambda rank: out_own.at[ranked(me, rank)], out_line, out_send, out_recv)
    summed.load_all()
    load_out = pltpu.make_async_copy(out_ref, out_own, out_sem)
    load_out.start()
    greet_all(me, count)

    def give_gain(step):
        target = lax.rem(me.d + step, count)
        return remote(
            gain_ref.at[target], gain_in.at[step], gain_send.at[step], gain_recv.at[step], (target, me.t)
        )

    summed.begin(0)
    for step in range(1, count):
        give_gain(step).start()
    load_out.wait()
    for rank in range(LINE - 1):

        @pl.when(jnp.logical_or(me.z == 0, me.z == LINE - 1))
        def _():
            outs.step(rank)

    for rank in range(LINE):
        summed.middle(rank)
        if rank + 1 < LINE:
            summed.begin(rank + 1)
        if rank < LINE - 1:

            @pl.when(jnp.logical_and(me.z > 0, me.z < LINE - 1))
            def _():
                outs.step(rank)

        summed.end(rank)
        if rank:
            grads.step(rank - 1)

    def add_out(landed):
        def act(at):
            output[at, :] = output[at, :] + landed[at, :].astype(F32)

        row_loop(output.shape[0], 16, act)

    def out_start(at):
        output[at, :] = x1_ref[at, :] + out_own[me.z, at, :].astype(F32)

    row_loop(output.shape[0], 16, out_start)
    outs.total(add_out)
    add_rows(a_out, (own.at[LINE - 1],), rows)
    grads.total(lambda landed: add_rows(a_out, (a_out, landed), rows))

    total = gain_ref[me.d]
    for step in range(1, count):
        give_gain(step).wait()
        total += gain_in[step]
    gain_pair[0] = total
    swap = remote(gain_pair.at[0], gain_pair.at[1], gain_send.at[0], gain_recv.at[0], me.sibling())
    swap.start()
    swap.wait()
    gain_out[...] = gain_pair[0] + gain_pair[1]
    outs.finish()
    grads.finish()
    summed.finish()


def grad_sum(count, x1, ga, out_parts, gains):
    _, block, width = ga.shape
    _, rows, model = out_parts.shape
    buffers, sems = PlaneSum.scratch(count, block, width)
    return pl.pallas_call(
        functools.partial(grad_sum_kernel, count),
        name="grad_sum",
        out_shape=(
            jax.ShapeDtypeStruct((block, width), F32),
            jax.ShapeDtypeStruct((rows, model), F32),
            jax.ShapeDtypeStruct(gains.shape[1:], F32),
        ),
        in_specs=[VMEM, ANY, ANY, VMEM],
        out_specs=(VMEM,) * 3,
        scratch_shapes=[
            *buffers,
            pltpu.VMEM((2, LINE - 1, block, width), BF16),
            pltpu.VMEM(out_parts.shape, BF16),
            pltpu.VMEM((2, LINE - 1, rows, model), BF16),
            pltpu.VMEM(gains.shape, F32),
            pltpu.VMEM((2,) + gains.shape[1:], F32),
            *sems,
            DMA((2, LINE)), DMA((2, LINE)), DMA((2, LINE)), DMA((2, LINE)), DMA,
            DMA((count,)), DMA((count,)),
        ],
        compiler_params=pltpu.CompilerParams(
            collective_id=4, has_side_effects=True, vmem_limit_bytes=48 * MB
        ),
    )(x1, ga, out_parts, gains)


def shards(
    tokens, w_query, key_weight, value_weight, w_out, gain_attn, w_gate, w_up, w_down, gain_mlp,
    cotangent, lengths, seq_of_group,
):
    count = lax.axis_size("dp")
    local_rows = tokens.shape[0]
    full_rows = local_rows * lax.axis_size("tensor")
    rows = w_query.shape[0]
    model = rows * count
    q_width = w_query.shape[1]
    kv_width = key_weight.shape[1]
    units = w_gate.shape[1] // LINE
    chosen = jnp.sum(
        jnp.where(jnp.arange(lengths.shape[0], dtype=jnp.int32) == seq_of_group[0], lengths, 0)
    )
    positions = lax.axis_index("tensor") * local_rows + jnp.arange(local_rows, dtype=jnp.int32)
    row_ids = jnp.arange(full_rows, dtype=jnp.int32)
    key_allowed = (row_ids[None, :] <= row_ids[:, None]) & (row_ids[None, :] < chosen)
    cos, sin = (table[:, 0, :] for table in rope_tables(full_rows, HEAD_SIZE))
    dm = jnp.where((positions < chosen)[:, None], cotangent, jnp.zeros_like(cotangent))

    attn_pack = jnp.concatenate([w_query, key_weight, value_weight, w_out.T], axis=1)
    down_t = w_down.T
    mlp_pack = jnp.stack(
        [
            jnp.concatenate([m[:, z * units : (z + 1) * units] for m in (w_gate, w_up, down_t)], axis=1)
            for z in range(LINE)
        ]
    )
    lanes = -rows % 128
    gains = jnp.pad(jnp.stack([gain_attn, gain_mlp]), ((0, 14), (0, lanes)))
    attn_all, mlp_all, mlp_last, gains_all, tokens_all, dm_all = gather_all(
        count, attn_pack, mlp_pack, gains, tokens, dm
    )
    gains_full = gains_all[:, :2, :rows].transpose(1, 0, 2).reshape(2, model).astype(F32)
    x1, h2, h1, qkv, probs, attended, mlp_late = attention_forward(
        count, q_width // HEAD_SIZE, tokens_all, gains_full, cos, sin, key_allowed.astype(F32),
        attn_all, mlp_last,
    )
    grad_h2, out_parts, grad_mlp_w, first_sum = feed_forward(
        count, h2, dm_all.reshape(-1, model), mlp_all, mlp_late
    )
    grad_attn_w, mlp_sum, grad_tokens, gain_parts = attention_backward(
        count, grad_h2, x1, dm, tokens_all, gains_full, cos, sin, h1, qkv, probs, attended, attn_all,
        grad_mlp_w, first_sum,
    )
    gain_parts = gain_parts.reshape(2, count, rows).transpose(1, 0, 2)
    gain_parts = jnp.pad(gain_parts, ((0, 0), (0, 6), (0, lanes)))
    attn_sum, output, gain_sum = grad_sum(count, x1, grad_attn_w, out_parts, gain_parts)
    mlp_sum = mlp_sum.astype(F32)
    grad_gate_w, grad_up_w, grad_down_t = (
        jnp.concatenate([mlp_sum[z, :, i * units : (i + 1) * units] for z in range(LINE)], axis=1)
        for i in range(3)
    )
    return (
        output.astype(BF16),
        grad_tokens,
        attn_sum[:, :q_width],
        attn_sum[:, q_width : q_width + kv_width],
        attn_sum[:, q_width + kv_width : q_width + 2 * kv_width],
        attn_sum[:, q_width + 2 * kv_width :].T,
        gain_sum[0, :rows],
        grad_gate_w,
        grad_up_w,
        grad_down_t.T,
        gain_sum[1, :rows],
    )


def solution(mesh):
    both = P(("dp", "tensor"), None)
    row = P("dp", "tensor")
    column = P("tensor", "dp")
    in_specs = (
        both, row, row, row, column, P("dp"), row, row, column, P("dp"), both, P(), P("dp"),
    )
    out_specs = (both, both, row, row, row, column, P("dp"), row, row, column, P("dp"))
    return jax.shard_map(shards, mesh=mesh, in_specs=in_specs, out_specs=out_specs, check_vma=False)
```

```python
import functools
import math

import jax
import jax.numpy as jnp
from jax import lax
from jax.experimental import pallas as pl
from jax.experimental.pallas import tpu as pltpu
from jax.sharding import PartitionSpec as P

HEAD_SIZE = 256
EPS = 1e-06
THETA = 1000042.0
LINE = 4
MESH = pl.DeviceIdType.MESH
BF16 = jnp.bfloat16
F32 = jnp.float32
MB = 1024 * 1024
LATE = 1
EARLY = 1


def rope_tables(count, head_dim):
    half = head_dim // 2
    index = jnp.arange(half, dtype=jnp.float32)
    freqs = jnp.exp(index * (-2.0 * math.log(THETA) / head_dim))
    angles = jnp.arange(count, dtype=jnp.float32)[:, None] * freqs[None, :]
    return jnp.cos(angles), jnp.sin(angles)


def dot_tn(left, right):
    return lax.dot_general(left, right, (((0,), (0,)), ((), ())), preferred_element_type=F32)


class Place:
    def __init__(self, plane):
        self.d = lax.axis_index("dp")
        self.t = lax.axis_index("tensor")
        self.plane = plane
        self.z = lax.div(self.d, plane)
        self.p = lax.rem(self.d, plane)
        if plane == 4:
            x = lax.rem(self.p, 2)
            y = lax.div(self.p, 2)
            self.px = 2 * y + 1 - x
            self.py = 2 * (1 - y) + x
            self.pd = 2 * (1 - y) + 1 - x

    def at(self, z, p):
        return (z * self.plane + p, self.t)

    def sibling(self):
        return (self.d, 1 - self.t)


def remote(src, dst, send, recv, device):
    return pltpu.make_async_remote_copy(
        src_ref=src, dst_ref=dst, send_sem=send, recv_sem=recv, device_id=device, device_id_type=MESH
    )


def arrival(ref, sem):
    pltpu.make_async_copy(ref, ref, sem).wait()


def greet_all(me, count):
    barrier = pltpu.get_barrier_semaphore()
    for step in range(1, count):
        pl.semaphore_signal(
            barrier, inc=1, device_id=(lax.rem(me.d + step, count), me.t), device_id_type=MESH
        )
    pl.semaphore_signal(barrier, inc=1, device_id=me.sibling(), device_id_type=MESH)
    pl.semaphore_wait(barrier, count)


def greet_line(me):
    barrier = pltpu.get_barrier_semaphore()
    for step in range(1, LINE):
        pl.semaphore_signal(
            barrier, inc=1, device_id=me.at(lax.rem(me.z + step, LINE), me.p), device_id_type=MESH
        )
    pl.semaphore_signal(barrier, inc=1, device_id=me.sibling(), device_id_type=MESH)
    pl.semaphore_wait(barrier, LINE)


def reach(me, way, k):
    return (me.z >= k, me.z - k) if way == 0 else (me.z + k < LINE, me.z + k)


class Chain:
    def __init__(self, me, first, held, send, recv):
        self.me, self.first, self.held, self.send, self.recv = me, first, held, send, recv

    def copy(self, way, k):
        me = self.me
        _, origin = reach(me, way, k)
        target = me.z + 1 if way == 0 else me.z - 1
        src = self.first if k == 0 else self.held(origin)
        return remote(
            src, self.held(origin), self.send.at[way, k], self.recv.at[way, k + 1], me.at(target, me.p)
        )

    def goes(self, way, k):
        have, _ = reach(self.me, way, k)
        ahead, _ = reach(self.me, 1 - way, 1)
        return jnp.logical_and(have, ahead)

    def start(self, way, k):
        if k < LINE - 1:

            @pl.when(self.goes(way, k))
            def _():
                self.copy(way, k).start()

    def wait_block(self, way, k):
        _, origin = reach(self.me, way, k)
        arrival(self.held(origin), self.recv.at[way, k])

    def finish(self):
        for way in range(2):
            for k in range(LINE - 1):

                @pl.when(self.goes(way, k))
                def _():
                    self.copy(way, k).wait_send()


class PlaneGather:
    def __init__(self, me, job, held, rows, send, recv):
        self.me, self.job, self.held, self.send, self.recv = me, job, held, send, recv
        self.half = rows // 2

    def piece(self, z, p, half):
        return self.held.at[z * self.me.plane + p, pl.ds(half * self.half, self.half)]

    def copy(self, z, kind, first=None):
        me = self.me
        if me.plane != 4:
            ref = first if first is not None else self.held.at[z * me.plane + me.p]
            target = lax.rem(me.p + kind + 1, me.plane)
            dst = self.held.at[z * me.plane + me.p]
        else:
            owner = (me.p, me.p, me.p, me.p, me.px, me.py)[kind]
            half = (0, 1, 1, 0, 0, 1)[kind]
            target = (me.px, me.px, me.py, me.py, me.py, me.px)[kind]
            dst = self.piece(z, owner, half)
            ref = dst if first is None else first.at[pl.ds(half * self.half, self.half)]
        return remote(
            ref, dst, self.send.at[self.job, z, kind], self.recv.at[self.job, z, kind], me.at(me.z, target)
        )

    def start(self, z, first=None):
        kinds = (0, 2, 1, 3) if self.me.plane == 4 else range(self.me.plane - 1)
        for kind in kinds:
            self.copy(z, kind, first).start()

    def forward(self, z):
        if self.me.plane == 4:
            self.copy(z, 0).wait_recv()
            self.copy(z, 4).start()
            self.copy(z, 2).wait_recv()
            self.copy(z, 5).start()

    def finish(self, zs=range(LINE)):
        kinds = 6 if self.me.plane == 4 else self.me.plane - 1
        for z in zs:
            for kind in range(kinds):
                copy = self.copy(z, kind)
                if self.me.plane != 4 or kind not in (0, 2):
                    copy.wait_recv()
                copy.wait_send()


def copy_in(src, dst, sem):
    return pltpu.make_async_copy(src, dst, sem)


def row_loop(rows, step, act):
    @pl.loop(0, rows // step)
    def _(i):
        act(pl.ds(pl.multiple_of(i * step, step), step))


def gather_kernel(
    count, len_ref, seq_ref, q_ref, k_ref, v_ref, o_ref, g_ref, u_ref, d_ref, gain_ref, tok_ref, cot_ref,
    a_all, gu_all, down, gain_all, tok_all, dm_all, o_v, a_v, gu_v, d_v, d_t, dm, chain_send, chain_recv,
    part_send, part_recv, plane_send, plane_recv, gain_send, gain_recv, pair_send, pair_recv, local_sem,
):
    plane = count // LINE
    me = Place(plane)
    rows, q_width = q_ref.shape
    kv_width = k_ref.shape[1]
    units = g_ref.shape[1] // LINE
    qkv_width = q_width + 2 * kv_width

    def columns(ref, z):
        return ref.at[:, pl.ds(pl.multiple_of(z * units, units), units)]

    local = [
        copy_in(o_ref, o_v, local_sem.at[0]),
        copy_in(q_ref, a_v.at[:, pl.ds(0, q_width)], local_sem.at[1]),
        copy_in(k_ref, a_v.at[:, pl.ds(q_width, kv_width)], local_sem.at[2]),
        copy_in(v_ref, a_v.at[:, pl.ds(q_width + kv_width, kv_width)], local_sem.at[3]),
        copy_in(d_ref, d_v, local_sem.at[4]),
        copy_in(cot_ref, dm, local_sem.at[5]),
        copy_in(columns(g_ref, me.z), gu_v.at[:, pl.ds(0, units)], local_sem.at[6]),
        copy_in(columns(u_ref, me.z), gu_v.at[:, pl.ds(units, units)], local_sem.at[7]),
        copy_in(gain_ref, gain_all.at[me.d], local_sem.at[8]),
        copy_in(tok_ref, tok_all.at[me.t], local_sem.at[9]),
    ]
    for copy in local[:4]:
        copy.start()
    keep_a = copy_in(a_v, a_all.at[me.d], local_sem.at[10])
    keep_down = copy_in(d_t.at[me.z], down.at[me.z], local_sem.at[11])
    keep_dm = copy_in(dm, dm_all.at[me.z, me.t], local_sem.at[12])
    keep_gu = copy_in(gu_v, gu_all.at[me.d], local_sem.at[13])

    attn = Chain(me, a_v, lambda z: a_all.at[z * plane + me.p], chain_send.at[0], chain_recv.at[0])
    dms = Chain(me, dm, lambda z: dm_all.at[z, me.t], chain_send.at[1], chain_recv.at[1])
    planes = (
        PlaneGather(me, 0, a_all, rows, plane_send, plane_recv),
        PlaneGather(me, 1, gu_all, rows, plane_send, plane_recv),
    )

    def part(way, k, kind):
        _, target = reach(me, 1 - way, k)
        src = d_t.at[target] if kind == 2 else columns((g_ref, u_ref)[kind], target)
        dst = down.at[me.z] if kind == 2 else gu_all.at[me.d, :, pl.ds(kind * units, units)]
        return remote(
            src, dst, part_send.at[way, k, kind], part_recv.at[way, k, kind], me.at(target, me.p)
        )

    def pair(z, first=None):
        src = dm_all.at[z, me.t] if first is None else first
        return remote(src, dm_all.at[z, me.t], pair_send.at[z], pair_recv.at[z], me.sibling())

    def start_parts(k, kinds):
        for way in range(2):

            @pl.when(reach(me, 1 - way, k)[0])
            def _():
                for kind in kinds:
                    part(way, k, kind).start()

    def each(k, act):
        for way in range(2):
            have, z = reach(me, way, k)

            @pl.when(have)
            def _():
                act(way, k, z)

    def attn_step(way, k, z):
        attn.wait_block(way, k)
        attn.start(way, k)
        planes[0].start(z)

    def part_step(way, k, z):
        for kind in range(2):
            arrival(gu_all.at[z * plane + me.p, :, pl.ds(kind * units, units)], part_recv.at[way, k, kind])
        planes[1].start(z)

    def dm_step(way, k, z):
        dms.wait_block(way, k)
        dms.start(way, k)
        pair(z).start()

    def give_gain(step):
        target = lax.rem(me.d + step, count)
        return remote(
            gain_ref, gain_all.at[me.d], gain_send.at[step], gain_recv.at[step], (target, me.t)
        )

    local[0].wait()
    a_v[:, qkv_width:] = o_v[...].T
    greet_all(me, count)
    for copy in local[1:4]:
        copy.wait()
    for way in range(2):
        attn.start(way, 0)
    planes[0].start(me.z, a_v)
    for copy in local[4:]:
        copy.start()
    keep_a.start()
    tokens = remote(tok_ref, tok_all.at[me.t], pair_send.at[LINE], pair_recv.at[LINE], me.sibling())
    tokens.start()
    for step in range(1, count):
        give_gain(step).start()

    local[4].wait()
    for z in range(LINE):
        d_t[z] = d_v[z * units : (z + 1) * units, :].T
    keep_down.start()
    local[5].wait()
    chosen = len_ref[seq_ref[0]]

    def mask(at):
        value = dm[at, :].astype(F32)
        row = lax.broadcasted_iota(jnp.int32, value.shape, 0) + (me.t * dm.shape[0] + at.start)
        dm[at, :] = jnp.where(row < chosen, value, 0.0).astype(BF16)

    row_loop(dm.shape[0], 32, mask)
    keep_dm.start()

    for k in range(1, LINE):
        each(k, attn_step)
        start_parts(k, (0, 1))
        if k == 1:
            planes[0].forward(me.z)
            for copy in local[6:8]:
                copy.wait()
            keep_gu.start()
            planes[1].start(me.z, gu_v)
        else:
            each(k - 1, lambda way, k, z: planes[0].forward(z))
    for k in range(1, LINE):
        start_parts(k, (2,))
    for way in range(2):
        dms.start(way, 0)
    pair(me.z, dm).start()
    for k in range(1, LINE):
        each(k, part_step)
        if k == 1:
            each(LINE - 1, lambda way, k, z: planes[0].forward(z))
            planes[1].forward(me.z)
        else:
            each(k - 1, lambda way, k, z: planes[1].forward(z))
            each(k - 1, dm_step)
    each(LINE - 1, lambda way, k, z: planes[1].forward(z))
    each(LINE - 1, dm_step)

    attn.finish()
    dms.finish()
    for k in range(1, LINE):
        for way in range(2):

            @pl.when(reach(me, 1 - way, k)[0])
            def _():
                for kind in range(3):
                    part(way, k, kind).wait_send()

        each(k, lambda way, k, z: arrival(down.at[z], part_recv.at[way, k, 2]))
    for step in range(1, count):
        give_gain(step).wait()
    tokens.wait()
    for z in range(LINE):
        pair(z).wait()
    for job in planes:
        job.finish()
    for copy in local[8:] + [keep_a, keep_down, keep_dm, keep_gu]:
        copy.wait()


ANY = pl.BlockSpec(memory_space=pl.ANY)
VMEM = pl.BlockSpec(memory_space=pltpu.VMEM)
SMEM = pl.BlockSpec(memory_space=pltpu.SMEM)
DMA = pltpu.SemaphoreType.DMA


def gather_all(count, lengths, seq, weights, gains, tokens, cotangent):
    w_query, key_weight, _, w_out, w_gate, _, w_down = weights
    rows, q_width = w_query.shape
    width = 2 * (q_width + key_weight.shape[1])
    units = w_gate.shape[1] // LINE
    kinds = max(6, count // LINE - 1)
    return pl.pallas_call(
        functools.partial(gather_kernel, count),
        name="gather_all",
        out_shape=(
            jax.ShapeDtypeStruct((count, rows, width), BF16),
            jax.ShapeDtypeStruct((count, rows, 2 * units), BF16),
            jax.ShapeDtypeStruct((LINE, rows, units), BF16),
            jax.ShapeDtypeStruct((count,) + gains.shape, gains.dtype),
            jax.ShapeDtypeStruct((2,) + tokens.shape, BF16),
            jax.ShapeDtypeStruct((LINE, 2) + cotangent.shape, BF16),
        ),
        in_specs=[SMEM] * 2 + [ANY] * 10,
        out_specs=(ANY,) * 6,
        scratch_shapes=[
            pltpu.VMEM(w_out.shape, BF16),
            pltpu.VMEM((rows, width), BF16),
            pltpu.VMEM((rows, 2 * units), BF16),
            pltpu.VMEM(w_down.shape, BF16),
            pltpu.VMEM((LINE, rows, units), BF16),
            pltpu.VMEM(cotangent.shape, BF16),
            DMA((2, 2, LINE)), DMA((2, 2, LINE)), DMA((2, LINE, 3)), DMA((2, LINE, 3)),
            DMA((2, LINE, kinds)), DMA((2, LINE, kinds)), DMA((count,)), DMA((count,)),
            DMA((LINE + 1,)), DMA((LINE + 1,)), DMA((14,)),
        ],
        compiler_params=pltpu.CompilerParams(
            collective_id=0, has_side_effects=True, vmem_limit_bytes=60 * MB
        ),
    )(lengths, seq, *weights, gains, tokens, cotangent)


RANKS = ((3, 2, 1, 0), (3, 0, 2, 1), (0, 3, 1, 2), (0, 1, 2, 3))
FAR_FIRST = [(way, k) for k in range(LINE - 1, 0, -1) for way in range(2)]


def ranked(me, rank):
    z = jnp.int32(RANKS[0][rank])
    for at in range(1, LINE):
        z = jnp.where(me.z == at, RANKS[at][rank], z)
    return z


def way_to(me, z):
    down = (z < me.z).astype(jnp.int32)
    return down, jnp.where(z < me.z, me.z - z, z - me.z)


def add_rows(target, terms, rows, start=0):
    step = 16

    @pl.loop(0, rows // step)
    def _(i):
        at = pl.ds(pl.multiple_of(start + i * step, step), step)
        total = terms[0][at].astype(F32)
        for term in terms[1:]:
            total += term[at].astype(F32)
        target[at] = total.astype(target.dtype)


class PlaneSum:
    def __init__(self, me, grad, own, other, first, second, sems, ranks=range(LINE)):
        self.me, self.grad, self.own, self.other, self.first, self.second = me, grad, own, other, first, second
        (
            self.first_send, self.first_recv, self.second_send, self.second_recv, self.load_sem, self.other_sem,
        ) = sems
        self.ranks = ranks
        self.rows = own.shape[1]
        half = self.rows // 2
        self.half = half
        self.halves = (pl.ds(0, half), pl.ds(half, half))
        self.square = me.plane == 4
        if self.square:
            self.near = (me.px, me.py)
            self.far = (me.py, me.px)

    def slot(self, rank):
        return rank - self.ranks[0]

    def block(self, rank, p):
        return self.grad.at[ranked(self.me, rank) * self.me.plane + p]

    def load(self, rank):
        s = self.slot(rank)
        return pltpu.make_async_copy(self.block(rank, self.me.p), self.own.at[s], self.load_sem.at[s])

    def load_other(self, rank, i):
        s = self.slot(rank)
        return pltpu.make_async_copy(
            self.block(rank, self.far[i]).at[self.halves[i]], self.other.at[s, self.halves[i]],
            self.other_sem.at[s, i],
        )

    def load_rank(self, rank):
        self.load(rank).start()
        if self.square:
            for i in range(2):
                self.load_other(rank, i).start()

    def load_all(self):
        for rank in self.ranks:
            self.load_rank(rank)

    def give(self, rank, i, which):
        me, s = self.me, self.slot(rank)
        if not self.square:
            target = lax.rem(me.p + which + 1, me.plane)
            return remote(
                self.block(rank, target), self.first.at[s, which], self.first_send.at[s, which],
                self.first_recv.at[s, which], me.at(me.z, target),
            )
        owner = (self.near[i], me.pd)[which]
        return remote(
            self.block(rank, owner).at[self.halves[i]], self.first.at[s, which, self.halves[i]],
            self.first_send.at[s, 2 * i + which], self.first_recv.at[s, 2 * i + which],
            me.at(me.z, self.near[i]),
        )

    def give_both(self, rank, i):
        s = self.slot(rank)
        return remote(
            self.other.at[s, self.halves[i]], self.second.at[s, self.halves[i]],
            self.second_send.at[s, i], self.second_recv.at[s, i], self.me.at(self.me.z, self.far[i]),
        )

    def gives(self, rank):
        if self.square:
            return [self.give(rank, i, which) for which in (1, 0) for i in range(2)]
        return [self.give(rank, 0, which) for which in range(self.me.plane - 1)]

    def begin(self, rank):
        for copy in self.gives(rank):
            copy.start()

    def middle(self, rank):
        if not self.square:
            return
        s = self.slot(rank)
        for i in range(2):
            arrival(self.first.at[s, 1, self.halves[i]], self.first_recv.at[s, 2 * i + 1])
            self.load_other(rank, i).wait()
            add_rows(
                self.other.at[s], (self.other.at[s], self.first.at[s, 1]), self.half, i * self.half
            )
            self.give_both(rank, i).start()

    def end(self, rank):
        s = self.slot(rank)
        self.load(rank).wait()
        if self.square:
            for i in range(2):
                arrival(self.first.at[s, 0, self.halves[i]], self.first_recv.at[s, 2 * i])
                arrival(self.second.at[s, self.halves[i]], self.second_recv.at[s, i])
            terms = (self.first.at[s, 0], self.second.at[s])
        else:
            for which in range(self.me.plane - 1):
                arrival(self.first.at[s, which], self.first_recv.at[s, which])
            terms = tuple(self.first.at[s, which] for which in range(self.me.plane - 1))
        add_rows(self.own.at[s], (self.own.at[s],) + terms, self.rows)

    def finish(self):
        for rank in self.ranks:
            for copy in self.gives(rank):
                copy.wait_send()
            if self.square:
                for i in range(2):
                    self.give_both(rank, i).wait_send()

    @staticmethod
    def scratch(count, rows, width, ranks=LINE):
        plane = count // LINE
        square = plane == 4
        slots = 2 if square else plane - 1
        small = (ranks, rows, width) if square else (1, 16, 128)
        return [
            pltpu.VMEM((ranks, rows, width), BF16),
            pltpu.VMEM(small, BF16),
            pltpu.VMEM((ranks, slots, rows, width), BF16),
            pltpu.VMEM(small, BF16),
        ], [
            DMA((ranks, max(4, slots))), DMA((ranks, max(4, slots))), DMA((ranks, 2)), DMA((ranks, 2)),
            DMA((ranks,)), DMA((ranks, 2)),
        ]


def dot_cols(left, right):
    return lax.dot_general(left, right, (((1,), (1,)), ((), ())), preferred_element_type=F32)


def feed_forward_kernel(
    plane, h_ref, dm_ref, gu_ref, down, down_ref, total_ref, out_ref, grad_ref, sum_ref, rows_in, weights, inner, part,
    from_pair, from_line, own, other, first, second, first_send, first_recv, second_send, second_recv,
    own_sem, other_sem, chain_send, chain_recv, pass_send, pass_recv, pair_send, pair_recv,
    line_send, line_recv, plane_send, plane_recv, load_sem, dm_sem, grad_sem, out_sem,
):
    me = Place(plane)
    rows, model = h_ref.shape
    units = inner.shape[1]
    wide = 2 * rows
    tokens = LINE * wide
    most, block, _ = down_ref.shape
    tile = 512

    def slot(z, t):
        return rows_in.at[pl.ds(pl.multiple_of((z * 2 + t) * rows, rows), rows)]

    loads = [
        copy_in(gu_ref, weights.at[:, :, pl.ds(0, 2 * units)], load_sem.at[0]),
        copy_in(down_ref, weights.at[pl.ds(0, most), :, pl.ds(2 * units, units)], load_sem.at[2]),
    ]
    late = range(LINE - LATE, LINE)
    for z in late:
        own_down = weights.at[z * plane + me.p, :, pl.ds(2 * units, units)]
        loads.append(copy_in(down.at[z], own_down, load_sem.at[3 + z]))
    for load in loads:
        load.start()
    load_dm = pltpu.make_async_copy(dm_ref, rows_in.at[pl.ds(tokens, tokens)], dm_sem)
    load_dm.start()
    keep = pltpu.make_async_copy(h_ref, slot(me.z, me.t), load_sem.at[1])
    keep.start()
    greet_all(me, plane * LINE)
    gather = PlaneGather(
        me, 0, weights.at[:, :, pl.ds(2 * units, units)], block, plane_send, plane_recv
    )
    for z in late:
        gather.start(z, down.at[z])
    summed = PlaneSum(
        me, weights, own, other, first, second,
        (first_send, first_recv, second_send, second_recv, own_sem, other_sem), range(EARLY),
    )
    chain = Chain(me, h_ref, lambda z: slot(z, me.t), chain_send, chain_recv)

    def share(z, first=None):
        src = slot(z, me.t) if first is None else first
        return remote(src, slot(z, me.t), pass_send.at[z], pass_recv.at[z], me.sibling())

    for way in range(2):
        chain.start(way, 0)
    share(me.z, h_ref).start()

    def w_rows(n, width, column):
        return weights[pl.ds(n * (width // block), width // block), :, pl.ds(column, units)].reshape(
            width, units
        )

    def compute(z):
        at = pl.ds(pl.multiple_of(z * wide, wide), wide)
        dm_at = pl.ds(pl.multiple_of(tokens + z * wide, wide), wide)

        @pl.loop(0, units // tile)
        def _(c):
            def column(job):
                return weights[:, :, pl.ds(pl.multiple_of(job * units + c * tile, tile), tile)].reshape(
                    model, tile
                )

            h = rows_in[at, :]
            gate = jnp.dot(h, column(0), preferred_element_type=F32)
            up = jnp.dot(h, column(1), preferred_element_type=F32)
            grad_hidden = jnp.dot(rows_in[dm_at, :], column(2), preferred_element_type=F32)
            sigmoid = jax.nn.sigmoid(gate)
            silu = gate * sigmoid
            here = pl.ds(pl.multiple_of(c * tile, tile), tile)
            inner[at, here] = (silu * up).astype(BF16)
            inner[pl.ds(pl.multiple_of(tokens + z * wide, wide), wide), here] = (
                grad_hidden * up * sigmoid * (1.0 + gate * (1.0 - sigmoid))
            ).astype(BF16)
            inner[pl.ds(pl.multiple_of(2 * tokens + z * wide, wide), wide), here] = (
                grad_hidden * silu
            ).astype(BF16)

        @pl.loop(0, model // tile)
        def _(n):
            here = pl.ds(pl.multiple_of(n * tile, tile), tile)
            grad = dot_cols(inner[pl.ds(pl.multiple_of(tokens + z * wide, wide), wide)], w_rows(n, tile, 0))
            grad += dot_cols(
                inner[pl.ds(pl.multiple_of(2 * tokens + z * wide, wide), wide)], w_rows(n, tile, units)
            )
            part[0, z, :, :, here] = grad.astype(BF16).reshape(2, rows, tile)

        pair(0, z).start()

        @pl.loop(0, model // tile)
        def _(n):
            here = pl.ds(pl.multiple_of(n * tile, tile), tile)
            out = dot_cols(inner[at, :], w_rows(n, tile, 2 * units))
            part[1, z, :, :, here] = out.astype(BF16).reshape(2, rows, tile)

        pair(1, z).start()

    def pair(job, z):
        return remote(
            part.at[job, z, 1 - me.t], from_pair.at[job, z], pair_send.at[job, z],
            pair_recv.at[job, z], me.sibling(),
        )

    half = rows // 2
    halves = (pl.ds(0, half), pl.ds(half, half))

    def pass_on(way, k, i):
        _, target = reach(me, 1 - way, k)
        ahead = me.z + 1 if way == 0 else me.z - 1
        return remote(
            part.at[0, target, me.t, halves[i]], from_line.at[way, k - 1, halves[i]],
            line_send.at[way, k, i], line_recv.at[way, k - 1, i], me.at(ahead, me.p),
        )

    def line(way, k, behind):
        have, z = reach(me, 1 - way, k)
        before = me.z if way == 0 else LINE - 1 - me.z

        @pl.when(jnp.logical_and(have, before == behind))
        def _():
            pair(0, z).wait_recv()
            terms = (part.at[0, z, me.t], from_pair.at[0, z])
            if behind:
                terms += (from_line.at[way, k],)
            for i in range(2):
                if behind:
                    arrival(from_line.at[way, k, halves[i]], line_recv.at[way, k, i])
                add_rows(part.at[0, z, me.t], terms, half, i * half)
                pass_on(way, k, i).start()

    def total():
        pair(0, me.z).wait_recv()
        add_rows(total_ref, (part.at[0, me.z, me.t], from_pair.at[0, me.z]), rows)
        for way in range(2):

            @pl.when(reach(me, way, 1)[0])
            def _():
                for i in range(2):
                    arrival(from_line.at[way, 0, halves[i]], line_recv.at[way, 0, i])
                    add_rows(total_ref, (total_ref, from_line.at[way, 0]), half, i * half)

    def grads(z):
        per = plane * block

        @pl.loop(0, per // tile)
        def _(n):
            column = pl.ds(pl.multiple_of(z * per + n * tile, tile), tile)
            h = rows_in[pl.ds(0, tokens), column].T
            dm = rows_in[pl.ds(tokens, tokens), column].T
            there = pl.ds((z * per + n * tile) // block, tile // block)
            for job in range(3):
                left = (h, h, dm)[job]
                start = (tokens, 2 * tokens, 0)[job]
                for c in range(units // 512):
                    grad = jnp.dot(
                        left, inner[pl.ds(start, tokens), c * 512 : (c + 1) * 512],
                        preferred_element_type=F32,
                    )
                    weights[there, :, job * units + c * 512 : job * units + (c + 1) * 512] = (
                        grad.astype(BF16).reshape(tile // block, block, 512)
                    )

        keep_grads(z).start()

    def keep_grads(z):
        return pltpu.make_async_copy(
            weights.at[pl.ds(z * plane, plane)], grad_ref.at[pl.ds(z * plane, plane)], grad_sem.at[z]
        )

    keep.wait()
    for load in loads:
        load.wait()
    load_dm.wait()
    for z in late:
        gather.forward(z)
    gather.finish(late)
    for k in range(LINE):
        for way in range(2 if k else 1):
            have, z = reach(me, way, k)

            @pl.when(have)
            def _():
                if k:
                    chain.wait_block(way, k)
                    chain.start(way, k)
                    share(z).start()
                arrival(slot(z, 1 - me.t), pass_recv.at[z])
                compute(z)

        if k:
            for way in range(2):
                line(1 - way, k, 0)
    order = [(behind, k) for behind in range(1, LINE) for k in range(1, LINE - behind)]
    order.sort(key=lambda e: (2 * e[0] + e[1], e[0]))

    def keep_out(z):
        return pltpu.make_async_copy(part.at[1, z, me.t], out_ref.at[z], out_sem.at[z])

    for i in range(LINE):
        grads(ranked(me, i))
        if i < EARLY:
            summed.load_rank(i)
        if i == 0:
            summed.begin(0)
        if i == 1:
            summed.middle(0)
            if EARLY > 1:
                summed.begin(1)
        if i < len(order):
            for way in range(2):
                line(way, order[i][1], order[i][0])
    for z in range(LINE):
        pair(1, z).wait_recv()
        add_rows(part.at[1, z, me.t], (part.at[1, z, me.t], from_pair.at[1, z]), rows)
        keep_out(z).start()
    keep_sums = [
        pltpu.make_async_copy(own.at[rank], sum_ref.at[rank], load_sem.at[rank]) for rank in range(EARLY)
    ]
    summed.end(0)
    keep_sums[0].start()
    if EARLY > 1:
        summed.middle(1)
    total()
    if EARLY > 1:
        summed.end(1)
        keep_sums[1].start()
    summed.finish()
    for copy in keep_sums:
        copy.wait()
    chain.finish()
    for z in range(LINE):
        share(z).wait_send()
        keep_grads(z).wait()
        keep_out(z).wait()
        for job in range(2):
            pair(job, z).wait_send()
    for k in range(1, LINE):
        for way in range(2):

            @pl.when(reach(me, 1 - way, k)[0])
            def _():
                for i in range(2):
                    pass_on(way, k, i).wait_send()


def feed_forward(count, h, dm_all, gu_all, down, down_all):
    rows, model = h.shape
    _, block, units = down.shape
    kinds = max(6, count // LINE - 1)
    grads = (count, block, 3 * units)
    buffers, sems = PlaneSum.scratch(count, *grads[1:], EARLY)
    tokens = LINE * 2 * rows
    vmem = pl.BlockSpec(memory_space=pltpu.VMEM)
    return pl.pallas_call(
        functools.partial(feed_forward_kernel, count // LINE),
        name="feed_forward",
        out_shape=(
            jax.ShapeDtypeStruct((rows, model), F32),
            jax.ShapeDtypeStruct((LINE, rows, model), BF16),
            jax.ShapeDtypeStruct(grads, BF16),
            jax.ShapeDtypeStruct((EARLY,) + grads[1:], BF16),
        ),
        in_specs=[ANY] * 5,
        out_specs=(vmem, ANY, ANY, ANY),
        scratch_shapes=[
            pltpu.VMEM((2 * tokens, model), BF16),
            pltpu.VMEM(grads, BF16),
            pltpu.VMEM((3 * tokens, units), BF16),
            pltpu.VMEM((2, LINE, 2, rows, model), BF16),
            pltpu.VMEM((2, LINE, rows, model), BF16),
            pltpu.VMEM((2, LINE - 1, rows, model), BF16),
            *buffers,
            *sems,
            DMA((2, LINE)), DMA((2, LINE)), DMA((LINE,)), DMA((LINE,)), DMA((2, LINE)), DMA((2, LINE)),
            DMA((2, LINE, 2)), DMA((2, LINE, 2)), DMA((1, LINE, kinds)), DMA((1, LINE, kinds)), DMA((3 + LINE,)), DMA, DMA((LINE,)), DMA((LINE,)),
        ],
        compiler_params=pltpu.CompilerParams(
            collective_id=1, has_side_effects=True, vmem_limit_bytes=60 * MB
        ),
    )(h, dm_all, gu_all, down, down_all)


def greet_plane(me):
    barrier = pltpu.get_barrier_semaphore()
    for step in range(1, me.plane):
        target = lax.rem(me.p + step, me.plane)
        pl.semaphore_signal(barrier, inc=1, device_id=me.at(me.z, target), device_id_type=MESH)
    pl.semaphore_signal(barrier, inc=1, device_id=me.sibling(), device_id_type=MESH)
    pl.semaphore_wait(barrier, me.plane)


def columns_of(weights, start, width):
    count, rows, _ = weights.shape
    return weights[:, :, pl.ds(start, width)].reshape(count * rows, width)


def rows_of(weights, n, height, start, width):
    _, rows, _ = weights.shape
    per = height // rows
    return weights[pl.ds(n * per, per), :, pl.ds(start, width)].reshape(height, width)


def attention_forward_kernel(
    plane, len_ref, seq_ref, gain_ref, cos_ref, sin_ref, tok_in, a_ref, down, x1_out, h2_out, h1_out,
    qkv_out, probs_out, o_out, down_all, weights, tok_ref, x1_ref, h2_ref, h1_ref, qkv_ref, probs_ref,
    o_ref, part, from_pair, plane_send, plane_recv, pair_send, pair_recv, load_sem, keep_sem,
):
    me = Place(plane)
    _, rows, model = tok_ref.shape
    wide = 2 * rows
    heads, _, _ = probs_ref.shape
    q_width = heads * HEAD_SIZE
    kv_width = (qkv_ref.shape[1] - q_width) // 2
    kv_heads = kv_width // HEAD_SIZE
    half = HEAD_SIZE // 2
    load_tok = copy_in(tok_in, tok_ref, load_sem.at[0])
    load_tok.start()
    load = copy_in(a_ref, weights, load_sem.at[1])
    load.start()
    keep = [
        copy_in(down.at[z], down_all.at[z * plane + me.p], load_sem.at[2 + z]) for z in range(LINE - LATE)
    ]
    for copy in keep:
        copy.start()
    outs = [
        copy_in(src, dst, keep_sem.at[i])
        for i, (src, dst) in enumerate(
            (
                (h1_ref, h1_out), (qkv_ref, qkv_out), (probs_ref, probs_out), (o_ref, o_out),
                (x1_ref, x1_out), (h2_ref, h2_out),
            )
        )
    ]
    greet_plane(me)
    gather = PlaneGather(me, 0, down_all, down.shape[1], plane_send, plane_recv)
    for z in range(LINE - LATE):
        gather.start(z, down.at[z])
    load_tok.wait()

    for t in range(2):

        def norm(at, t=t):
            x = tok_ref[t, at, :].astype(F32)
            factor = lax.rsqrt(jnp.mean(x * x, -1, keepdims=True) + EPS)
            h1_ref[pl.ds(t * rows + at.start, at.size), :] = (x * factor * gain_ref[0:1, :]).astype(BF16)

        row_loop(rows, 32, norm)
    outs[0].start()
    load.wait()

    def project(i):
        start = pl.multiple_of(i * HEAD_SIZE, HEAD_SIZE)
        return start, jnp.dot(
            h1_ref[...], columns_of(weights, start, HEAD_SIZE), preferred_element_type=F32
        )

    @pl.loop(0, heads + kv_heads)
    def _(i):
        start, values = project(i)
        first, second = values[:, :half], values[:, half:]
        cos, sin = cos_ref[...], sin_ref[...]
        qkv_ref[:, pl.ds(start, half)] = (first * cos - second * sin).astype(BF16)
        qkv_ref[:, pl.ds(start + half, half)] = (second * cos + first * sin).astype(BF16)

    @pl.loop(heads + kv_heads, heads + 2 * kv_heads)
    def _(i):
        start, values = project(i)
        qkv_ref[:, pl.ds(start, HEAD_SIZE)] = values.astype(BF16)

    outs[1].start()
    gather.forward(0)
    row = lax.broadcasted_iota(jnp.int32, (wide, wide), 0)
    key = lax.broadcasted_iota(jnp.int32, (wide, wide), 1)
    allowed = jnp.logical_and(key <= row, key < len_ref[seq_ref[0]])
    for i in range(heads):
        m = i * kv_heads // heads
        q = qkv_ref[:, i * HEAD_SIZE : (i + 1) * HEAD_SIZE]
        k = qkv_ref[:, q_width + m * HEAD_SIZE : q_width + (m + 1) * HEAD_SIZE]
        v = qkv_ref[:, q_width + kv_width + m * HEAD_SIZE : q_width + kv_width + (m + 1) * HEAD_SIZE]
        scores = dot_cols(q, k) * HEAD_SIZE ** (-0.5)
        scores = jnp.where(allowed, scores, -1e30)
        grown = jnp.exp(scores - jnp.max(scores, -1, keepdims=True))
        probs = grown / jnp.sum(grown, -1, keepdims=True)
        probs_ref[i] = probs
        o_ref[:, i * HEAD_SIZE : (i + 1) * HEAD_SIZE] = jnp.dot(
            probs.astype(BF16), v, preferred_element_type=F32
        ).astype(BF16)

    outs[2].start()
    outs[3].start()
    gather.forward(1)
    tile = 512

    @pl.loop(0, model // tile)
    def _(n):
        here = pl.ds(pl.multiple_of(n * tile, tile), tile)
        value = dot_cols(o_ref[...], rows_of(weights, n, tile, q_width + 2 * kv_width, q_width))
        part[:, :, here] = value.reshape(2, rows, tile)

    swap = remote(part.at[1 - me.t], from_pair, pair_send, pair_recv, me.sibling())
    swap.start()
    for z in range(2, LINE - LATE):
        gather.forward(z)
    swap.wait_recv()

    def add(at):
        x1 = tok_ref[me.t, at, :].astype(F32) + (part[me.t, at, :] + from_pair[at, :])
        x1_ref[at, :] = x1
        factor = lax.rsqrt(jnp.mean(x1 * x1, -1, keepdims=True) + EPS)
        h2_ref[at, :] = (x1 * factor * gain_ref[1:2, :]).astype(BF16)

    row_loop(rows, 32, add)
    outs[4].start()
    outs[5].start()
    swap.wait_send()
    gather.finish(range(LINE - LATE))
    for copy in keep + outs:
        copy.wait()


def attention_forward(count, heads, lengths, seq, gains, cos, sin, tokens_all, attn_all, down):
    _, rows, model = tokens_all.shape
    wide = 2 * rows
    q_width = heads * HEAD_SIZE
    qkv_width = attn_all.shape[2] - q_width
    plane = count // LINE
    kinds = max(6, plane - 1)
    outs = (
        jax.ShapeDtypeStruct((rows, model), F32),
        jax.ShapeDtypeStruct((rows, model), BF16),
        jax.ShapeDtypeStruct((wide, model), BF16),
        jax.ShapeDtypeStruct((wide, qkv_width), BF16),
        jax.ShapeDtypeStruct((heads, wide, wide), F32),
        jax.ShapeDtypeStruct((wide, q_width), BF16),
    )
    return pl.pallas_call(
        functools.partial(attention_forward_kernel, plane),
        name="attention_forward",
        out_shape=outs + (jax.ShapeDtypeStruct((count - LATE * plane,) + down.shape[1:], BF16),),
        in_specs=[SMEM] * 2 + [VMEM] * 3 + [ANY] * 3,
        out_specs=(ANY,) * 7,
        scratch_shapes=[
            pltpu.VMEM(attn_all.shape, BF16),
            pltpu.VMEM(tokens_all.shape, BF16),
            *[pltpu.VMEM(out.shape, out.dtype) for out in outs],
            pltpu.VMEM((2, rows, model), F32),
            pltpu.VMEM((rows, model), F32),
            DMA((1, LINE, kinds)), DMA((1, LINE, kinds)), DMA, DMA, DMA((2 + LINE,)), DMA((6,)),
        ],
        compiler_params=pltpu.CompilerParams(
            collective_id=2, has_side_effects=True, vmem_limit_bytes=60 * MB
        ),
    )(lengths, seq, gains, cos, sin, tokens_all, attn_all, down)


def attention_backward_kernel(
    plane, gain_ref, cos_ref, sin_ref, total_in, x1_in, dm_in, tok_in, h1_in, qkv_in, probs_in, o_in,
    a_ref, gw_ref, sum_ref, ga_ref, w_out, grad_tokens, gain_parts, weights, own, other, first, second,
    total_ref, x1_ref, dm_ref, tok_ref, h1_ref, qkv_ref, probs_ref, o_ref, dx, da, do, dqkv, dh1, from_pair, first_send, first_recv, second_send, second_recv, load_sem,
    other_sem, part_send, part_recv, pair_send, pair_recv, a_sem, keep_sem, grad_sem, in_sem,
):
    me = Place(plane)
    _, rows, model = tok_ref.shape
    block = weights.shape[1]
    heads, _, _ = probs_ref.shape
    q_width = heads * HEAD_SIZE
    qkv_width = qkv_ref.shape[1]
    kv_width = (qkv_width - q_width) // 2
    kv_heads = kv_width // HEAD_SIZE
    half = HEAD_SIZE // 2
    scale = HEAD_SIZE ** (-0.5)
    summed = PlaneSum(
        me, gw_ref, own, other, first, second,
        (first_send, first_recv, second_send, second_recv, load_sem, other_sem), range(EARLY, LINE),
    )
    ins = [
        copy_in(src, dst, in_sem.at[i])
        for i, (src, dst) in enumerate(
            (
                (total_in, total_ref), (x1_in, x1_ref), (dm_in.at[me.z, me.t], dm_ref), (tok_in, tok_ref),
                (h1_in, h1_ref), (qkv_in, qkv_ref), (probs_in, probs_ref), (o_in, o_ref),
            )
        )
    ]
    for copy in ins[:3]:
        copy.start()
    load = pltpu.make_async_copy(a_ref, weights, a_sem)
    load.start()
    for copy in ins[3:]:
        copy.start()
    summed.load_all()
    greet_all(me, plane * LINE)

    def part(rank):
        target = ranked(me, rank)
        way, k = way_to(me, target)
        src = own.at[summed.slot(rank)] if rank >= EARLY else sum_ref.at[rank]
        return remote(
            src, w_out.at[me.z], part_send.at[way, k], part_recv.at[way, k], me.at(target, me.p)
        )

    give_da = remote(da.at[me.t], da.at[me.t], pair_send.at[0], pair_recv.at[0], me.sibling())
    give_dh1 = remote(dh1.at[1 - me.t], from_pair, pair_send.at[1], pair_recv.at[1], me.sibling())

    def mid_norm():
        gain_parts[...] = jnp.zeros_like(gain_parts)

        def act(at):
            x, up = x1_ref[at, :], total_ref[at, :]
            factor = lax.rsqrt(jnp.mean(x * x, -1, keepdims=True) + EPS)
            scaled = up * gain_ref[1:2, :]
            grad = dm_ref[at, :].astype(F32) + (
                factor * scaled - x * factor**3 * jnp.mean(scaled * x, -1, keepdims=True)
            )
            dx[at, :] = grad
            da[me.t, at, :] = grad.astype(BF16)
            gain_parts[1:2, :] += jnp.sum(up * x * factor, 0, keepdims=True)

        row_loop(rows, 32, act)
        give_da.start()

    def grad_o():
        load.wait()
        give_da.wait_recv()

        @pl.loop(0, q_width // HEAD_SIZE)
        def _(c):
            here = pl.multiple_of(c * HEAD_SIZE, HEAD_SIZE)
            value = jnp.dot(
                da[...].reshape(2 * rows, model),
                columns_of(weights, qkv_width + here, HEAD_SIZE),
                preferred_element_type=F32,
            )
            do[:, pl.ds(here, HEAD_SIZE)] = value.astype(BF16)

    def rotate(values, start):
        first, second = values[:, :half], values[:, half:]
        cos, sin = cos_ref[...], sin_ref[...]
        dqkv[:, start : start + half] = (first * cos + second * sin).astype(BF16)
        dqkv[:, start + half : start + 2 * half] = (second * cos - first * sin).astype(BF16)

    def grad_heads():
        group = heads // kv_heads
        for m in range(kv_heads):
            at_k = q_width + m * HEAD_SIZE
            at_v = at_k + kv_width
            k = qkv_ref[:, at_k : at_k + HEAD_SIZE]
            v = qkv_ref[:, at_v : at_v + HEAD_SIZE]
            grad_k = grad_v = None
            for i in range(m * group, (m + 1) * group):
                at = slice(i * HEAD_SIZE, (i + 1) * HEAD_SIZE)
                probs = probs_ref[i]
                grad_probs = dot_cols(do[:, at], v)
                grad_scores = probs * (
                    grad_probs - jnp.sum(probs * grad_probs, -1, keepdims=True)
                )
                low = grad_scores.astype(BF16)
                rotate(jnp.dot(low, k, preferred_element_type=F32) * scale, i * HEAD_SIZE)
                more_k = dot_tn(low, qkv_ref[:, at])
                more_v = dot_tn(probs.astype(BF16), do[:, at])
                grad_k = more_k if grad_k is None else grad_k + more_k
                grad_v = more_v if grad_v is None else grad_v + more_v
            rotate(grad_k * scale, at_k)
            dqkv[:, at_v : at_v + HEAD_SIZE] = grad_v.astype(BF16)

    tile = 512

    def grad_h1():
        @pl.loop(0, model // tile)
        def _(n):
            here = pl.ds(pl.multiple_of(n * tile, tile), tile)
            value = dot_cols(dqkv[...], rows_of(weights, n, tile, 0, qkv_width))
            dh1[:, :, here] = value.reshape(2, rows, tile)

        give_dh1.start()

    def keep_grads(n):
        per = tile // block
        return pltpu.make_async_copy(
            weights.at[pl.ds(n * per, per)], ga_ref.at[pl.ds(n * per, per)], grad_sem.at[n]
        )

    def grads():
        @pl.loop(0, model // tile)
        def _(n):
            here = pl.ds(pl.multiple_of(n * tile, tile), tile)
            there = pl.ds(n * (tile // block), tile // block)
            left = h1_ref[:, here].T
            for c in range(qkv_width // tile):
                at = slice(c * tile, (c + 1) * tile)
                value = jnp.dot(left, dqkv[:, at], preferred_element_type=F32)
                weights[there, :, at] = value.astype(BF16).reshape(tile // block, block, tile)
            left = da[:, :, here].reshape(2 * rows, tile).T
            for c in range(q_width // tile):
                at = slice(c * tile, (c + 1) * tile)
                value = jnp.dot(left, o_ref[:, at], preferred_element_type=F32)
                at = slice(qkv_width + c * tile, qkv_width + (c + 1) * tile)
                weights[there, :, at] = value.astype(BF16).reshape(tile // block, block, tile)

        for n in range(model // tile):
            keep_grads(n).start()

    def in_norm():
        give_dh1.wait_recv()

        def act(at):
            x = tok_ref[me.t, at, :].astype(F32)
            up = dh1[me.t, at, :] + from_pair[at, :]
            factor = lax.rsqrt(jnp.mean(x * x, -1, keepdims=True) + EPS)
            scaled = up * gain_ref[0:1, :]
            grad_tokens[at, :] = dx[at, :] + (
                factor * scaled - x * factor**3 * jnp.mean(scaled * x, -1, keepdims=True)
            )
            gain_parts[0:1, :] += jnp.sum(up * x * factor, 0, keepdims=True)

        row_loop(rows, 32, act)

    summed.begin(EARLY)
    for rank in range(EARLY):
        part(rank).start()
    for copy in ins[:3]:
        copy.wait()
    mid_norm()
    grad_o()
    for copy in ins[3:]:
        copy.wait()
    stages = {LINE - 2: [grad_heads, grad_h1], LINE - 1: [grads, in_norm]}
    if EARLY < LINE - 2:
        stages = {1: [grad_heads, grad_h1], 2: [grads], 3: [in_norm]}
    for rank in range(EARLY, LINE):
        summed.middle(rank)
        if rank + 1 < LINE:
            summed.begin(rank + 1)
        for stage in stages[rank]:
            stage()
        summed.end(rank)
        if rank < LINE - 1:
            part(rank).start()

    keep = pltpu.make_async_copy(own.at[LINE - 1 - EARLY], w_out.at[me.z], keep_sem)
    keep.start()
    for rank in range(LINE - 1):
        part(rank).wait_send()
    for way, k in FAR_FIRST:

        @pl.when(reach(me, way, k)[0])
        def _():
            arrival(w_out.at[me.z], part_recv.at[way, k])

    summed.finish()
    give_da.wait_send()
    give_dh1.wait_send()
    for n in range(model // tile):
        keep_grads(n).wait()
    keep.wait()


def attention_backward(
    count, gains, cos, sin, total, x1, dm_all, tokens_all, h1, qkv, probs, o, attn_all, grad_mlp, first_sum
):
    _, rows, model = tokens_all.shape
    _, block, width = attn_all.shape
    wide = 2 * rows
    heads = probs.shape[0]
    q_width = heads * HEAD_SIZE
    buffers, sems = PlaneSum.scratch(count, block, width, LINE - EARLY)
    return pl.pallas_call(
        functools.partial(attention_backward_kernel, count // LINE),
        name="attention_backward",
        out_shape=(
            jax.ShapeDtypeStruct(attn_all.shape, BF16),
            jax.ShapeDtypeStruct((LINE, block, width), BF16),
            jax.ShapeDtypeStruct((rows, model), F32),
            jax.ShapeDtypeStruct((2, model), F32),
        ),
        in_specs=[VMEM] * 3 + [ANY] * 11,
        out_specs=(ANY, ANY, VMEM, VMEM),
        scratch_shapes=[
            pltpu.VMEM(attn_all.shape, BF16),
            *buffers,
            *[
                pltpu.VMEM(ref.shape, ref.dtype)
                for ref in (total, x1, dm_all[0, 0], tokens_all, h1, qkv, probs, o)
            ],
            pltpu.VMEM((rows, model), F32),
            pltpu.VMEM((2, rows, model), BF16),
            pltpu.VMEM((wide, q_width), BF16),
            pltpu.VMEM(qkv.shape, BF16),
            pltpu.VMEM((2, rows, model), F32),
            pltpu.VMEM((rows, model), F32),
            *sems,
            DMA((2, LINE)), DMA((2, LINE)), DMA((2,)), DMA((2,)), DMA, DMA, DMA((model // 512,)), DMA((8,)),
        ],
        compiler_params=pltpu.CompilerParams(
            collective_id=3, has_side_effects=True, vmem_limit_bytes=60 * MB
        ),
    )(gains, cos, sin, total, x1, dm_all, tokens_all, h1, qkv, probs, o, attn_all, grad_mlp, first_sum)


def grad_sum_kernel(
    count, gain_ref, x1_in, ga_ref, out_ref, mlp_ref, q_out, k_out, v_out, o_out, gate_out, up_out,
    down_out, output, gain_out, own, other, first, second, a_out, x1_ref, mlp, from_line, out_own, out_line, gain_in, gain_pair, first_send, first_recv, second_send, second_recv,
    load_sem, other_sem, line_send, line_recv, out_send, out_recv, load_out_sem, gain_send, gain_recv,
):
    plane = count // LINE
    me = Place(plane)
    rows = a_out.shape[0]
    summed = PlaneSum(
        me, ga_ref, own, other, first, second,
        (first_send, first_recv, second_send, second_recv, load_sem, other_sem),
    )

    class Line:
        def __init__(self, held, landing, send, recv):
            self.held, self.landing, self.send, self.recv = held, landing, send, recv

        def pass_on(self, rank):
            way, k = way_to(me, ranked(me, rank))
            ahead = jnp.where(way == 0, me.z + 1, me.z - 1)
            return remote(
                self.held(rank), self.landing.at[way, k - 1], self.send.at[way, k],
                self.recv.at[way, k - 1], me.at(ahead, me.p),
            )

        def step(self, rank):
            way, k = way_to(me, ranked(me, rank))
            before = jnp.where(way == 0, me.z, LINE - 1 - me.z)
            held = self.held(rank)

            @pl.when(before > 0)
            def _():
                arrival(self.landing.at[way, k], self.recv.at[way, k])
                add_rows(held, (held, self.landing.at[way, k]), held.shape[0])

            self.pass_on(rank).start()

        def total(self, act):
            for way in range(2):

                @pl.when(reach(me, way, 1)[0])
                def _():
                    arrival(self.landing.at[way, 0], self.recv.at[way, 0])
                    act(self.landing.at[way, 0])

        def finish(self):
            for rank in range(LINE - 1):
                self.pass_on(rank).wait_send()

    grads = Line(lambda rank: own.at[rank], from_line, line_send, line_recv)
    outs = Line(lambda rank: out_own.at[ranked(me, rank)], out_line, out_send, out_recv)
    summed.load_all()
    load_out = copy_in(out_ref, out_own, load_out_sem.at[0])
    load_out.start()
    load_x1 = copy_in(x1_in, x1_ref, load_out_sem.at[1])
    load_x1.start()
    load_mlp = copy_in(mlp_ref, mlp, load_out_sem.at[2])
    load_mlp.start()
    greet_all(me, count)

    def give_gain(step):
        target = lax.rem(me.d + step, count)
        return remote(
            gain_ref.at[target], gain_in.at[step], gain_send.at[step], gain_recv.at[step], (target, me.t)
        )

    summed.begin(0)
    for step in range(1, count):
        give_gain(step).start()
    load_out.wait()
    for rank in range(LINE - 1):

        @pl.when(jnp.logical_or(me.z == 0, me.z == LINE - 1))
        def _():
            outs.step(rank)

    at_end = jnp.logical_or(me.z == 0, me.z == LINE - 1)

    def out_start(at):
        x1_ref[at, :] = x1_ref[at, :] + out_own[me.z, at, :].astype(F32)

    def add_out(landed):
        def act(at):
            x1_ref[at, :] = x1_ref[at, :] + landed[at, :].astype(F32)

        row_loop(output.shape[0], 16, act)

    def out_end(at):
        output[at, :] = x1_ref[at, :].astype(BF16)

    units = mlp.shape[2] // 3

    def feed_forward_grads(z):
        here = slice(z * units, (z + 1) * units)
        gate_out[:, here] = mlp[z, :, :units].astype(F32)
        up_out[:, here] = mlp[z, :, units : 2 * units].astype(F32)
        down_out[here, :] = mlp[z, :, 2 * units :].astype(F32).T

    for rank in range(LINE):
        summed.middle(rank)
        if rank + 1 < LINE:
            summed.begin(rank + 1)
            if rank == 0:
                load_mlp.wait()
        else:
            load_x1.wait()
            row_loop(output.shape[0], 16, out_start)
            outs.total(add_out)
            row_loop(output.shape[0], 16, out_end)
            total = gain_ref[me.d]
            for step in range(1, count):
                give_gain(step).wait()
                total += gain_in[step]
            gain_pair[0] = total
            swap = remote(
                gain_pair.at[0], gain_pair.at[1], gain_send.at[0], gain_recv.at[0], me.sibling()
            )
            swap.start()
            swap.wait()
            gain_out[...] = gain_pair[0] + gain_pair[1]
        feed_forward_grads(rank)
        summed.end(rank)
        if rank < LINE - 1:

            @pl.when(at_end)
            def _():
                grads.step(rank)

        if 0 < rank < LINE - 1:
            @pl.when(jnp.logical_not(at_end))
            def _():
                for late in (range(rank - 1, rank) if rank < LINE - 2 else range(rank - 1, LINE - 1)):
                    outs.step(late)
                    grads.step(late)

    add_rows(a_out, (own.at[LINE - 1],), rows)
    grads.total(lambda landed: add_rows(a_out, (a_out, landed), rows))
    start = 0
    for ref in (q_out, k_out, v_out):
        ref[...] = a_out[:, start : start + ref.shape[1]]
        start += ref.shape[1]
    o_out[...] = a_out[:, start:].T
    outs.finish()
    grads.finish()
    summed.finish()


def grad_sum(count, q_width, kv_width, x1, ga, out_parts, mlp, gains):
    _, block, width = ga.shape
    _, rows, model = out_parts.shape
    hidden = LINE * (mlp.shape[2] // 3)
    buffers, sems = PlaneSum.scratch(count, block, width)
    return pl.pallas_call(
        functools.partial(grad_sum_kernel, count),
        name="grad_sum",
        out_shape=(
            jax.ShapeDtypeStruct((block, q_width), F32),
            jax.ShapeDtypeStruct((block, kv_width), F32),
            jax.ShapeDtypeStruct((block, kv_width), F32),
            jax.ShapeDtypeStruct((q_width, block), F32),
            jax.ShapeDtypeStruct((block, hidden), F32),
            jax.ShapeDtypeStruct((block, hidden), F32),
            jax.ShapeDtypeStruct((hidden, block), F32),
            jax.ShapeDtypeStruct((rows, model), BF16),
            jax.ShapeDtypeStruct(gains.shape[1:], F32),
        ),
        in_specs=[VMEM] + [ANY] * 4,
        out_specs=(VMEM,) * 9,
        scratch_shapes=[
            *buffers,
            pltpu.VMEM((block, width), F32),
            pltpu.VMEM((rows, model), F32),
            pltpu.VMEM(mlp.shape, BF16),
            pltpu.VMEM((2, LINE - 1, block, width), BF16),
            pltpu.VMEM(out_parts.shape, BF16),
            pltpu.VMEM((2, LINE - 1, rows, model), BF16),
            pltpu.VMEM(gains.shape, F32),
            pltpu.VMEM((2,) + gains.shape[1:], F32),
            *sems,
            DMA((2, LINE)), DMA((2, LINE)), DMA((2, LINE)), DMA((2, LINE)), DMA((3,)),
            DMA((count,)), DMA((count,)),
        ],
        compiler_params=pltpu.CompilerParams(
            collective_id=4, has_side_effects=True, vmem_limit_bytes=60 * MB
        ),
    )(gains, x1, ga, out_parts, mlp)


def shards(
    tokens, w_query, key_weight, value_weight, w_out, gain_attn, w_gate, w_up, w_down, gain_mlp,
    cotangent, lengths, seq_of_group,
):
    count = lax.axis_size("dp")
    rows, q_width = w_query.shape
    kv_width = key_weight.shape[1]
    model = rows * count
    cos, sin = rope_tables(tokens.shape[0] * lax.axis_size("tensor"), HEAD_SIZE)
    lanes = -rows % 128
    gains = jnp.pad(jnp.stack([gain_attn, gain_mlp]), ((0, 14), (0, lanes)))
    attn_all, gate_up_all, down, gains_all, tokens_all, dm_all = gather_all(
        count, lengths, seq_of_group,
        (w_query, key_weight, value_weight, w_out, w_gate, w_up, w_down), gains, tokens, cotangent,
    )
    gains_full = gains_all[:, :2, :rows].transpose(1, 0, 2).reshape(2, model).astype(F32)
    x1, h2, h1, qkv, probs, attended, down_all = attention_forward(
        count, q_width // HEAD_SIZE, lengths, seq_of_group, gains_full, cos, sin, tokens_all, attn_all,
        down,
    )
    grad_h2, out_parts, grad_mlp_w, first_sum = feed_forward(
        count, h2, dm_all.reshape(-1, model), gate_up_all, down, down_all
    )
    grad_attn_w, mlp_sum, grad_tokens, gain_parts = attention_backward(
        count, gains_full, cos, sin, grad_h2, x1, dm_all, tokens_all, h1, qkv, probs, attended, attn_all,
        grad_mlp_w, first_sum,
    )
    gain_parts = gain_parts.reshape(2, count, rows).transpose(1, 0, 2)
    gain_parts = jnp.pad(gain_parts, ((0, 0), (0, 6), (0, lanes)))
    (
        grad_query, grad_key, grad_value, grad_out, grad_gate, grad_up, grad_down, output, gain_sum,
    ) = grad_sum(count, q_width, kv_width, x1, grad_attn_w, out_parts, mlp_sum, gain_parts)
    return (
        output, grad_tokens, grad_query, grad_key, grad_value, grad_out, gain_sum[0, :rows],
        grad_gate, grad_up, grad_down, gain_sum[1, :rows],
    )


def solution(mesh):
    both = P(("dp", "tensor"), None)
    row = P("dp", "tensor")
    column = P("tensor", "dp")
    in_specs = (
        both, row, row, row, column, P("dp"), row, row, column, P("dp"), both, P(), P("dp"),
    )
    out_specs = (both, both, row, row, row, column, P("dp"), row, row, column, P("dp"))
    return jax.shard_map(shards, mesh=mesh, in_specs=in_specs, out_specs=out_specs, check_vma=False)
```

```python
import functools
import math

import jax
import jax.numpy as jnp
from jax import lax
from jax.experimental import pallas as pl
from jax.experimental.pallas import tpu as pltpu
from jax.sharding import PartitionSpec as P

HEAD_SIZE = 256
EPS = 1e-06
THETA = 1000042.0
LINE = 4
MESH = pl.DeviceIdType.MESH
BF16 = jnp.bfloat16
F32 = jnp.float32
MB = 1024 * 1024
SOON = 1


def rope_tables(count, head_dim):
    half = head_dim // 2
    index = jnp.arange(half, dtype=jnp.float32)
    freqs = jnp.exp(index * (-2.0 * math.log(THETA) / head_dim))
    angles = jnp.arange(count, dtype=jnp.float32)[:, None] * freqs[None, :]
    return jnp.cos(angles), jnp.sin(angles)


def dot_tn(left, right):
    return lax.dot_general(left, right, (((0,), (0,)), ((), ())), preferred_element_type=F32)


class Place:
    def __init__(self, plane):
        self.d = lax.axis_index("dp")
        self.t = lax.axis_index("tensor")
        self.plane = plane
        self.z = lax.div(self.d, plane)
        self.p = lax.rem(self.d, plane)
        if plane == 4:
            x = lax.rem(self.p, 2)
            y = lax.div(self.p, 2)
            self.px = 2 * y + 1 - x
            self.py = 2 * (1 - y) + x
            self.pd = 2 * (1 - y) + 1 - x

    def at(self, z, p):
        return (z * self.plane + p, self.t)

    def sibling(self):
        return (self.d, 1 - self.t)


def remote(src, dst, send, recv, device):
    return pltpu.make_async_remote_copy(
        src_ref=src, dst_ref=dst, send_sem=send, recv_sem=recv, device_id=device, device_id_type=MESH
    )


def arrival(ref, sem):
    pltpu.make_async_copy(ref, ref, sem).wait()


def greet_all(me, count):
    barrier = pltpu.get_barrier_semaphore()
    for step in range(1, count):
        pl.semaphore_signal(
            barrier, inc=1, device_id=(lax.rem(me.d + step, count), me.t), device_id_type=MESH
        )
    pl.semaphore_signal(barrier, inc=1, device_id=me.sibling(), device_id_type=MESH)
    pl.semaphore_wait(barrier, count)


def greet_line(me):
    barrier = pltpu.get_barrier_semaphore()
    for step in range(1, LINE):
        pl.semaphore_signal(
            barrier, inc=1, device_id=me.at(lax.rem(me.z + step, LINE), me.p), device_id_type=MESH
        )
    pl.semaphore_signal(barrier, inc=1, device_id=me.sibling(), device_id_type=MESH)
    pl.semaphore_wait(barrier, LINE)


def reach(me, way, k):
    return (me.z >= k, me.z - k) if way == 0 else (me.z + k < LINE, me.z + k)


class Chain:
    def __init__(self, me, first, held, send, recv):
        self.me, self.first, self.held, self.send, self.recv = me, first, held, send, recv

    def copy(self, way, k):
        me = self.me
        _, origin = reach(me, way, k)
        target = me.z + 1 if way == 0 else me.z - 1
        src = self.first if k == 0 else self.held(origin)
        return remote(
            src, self.held(origin), self.send.at[way, k], self.recv.at[way, k + 1], me.at(target, me.p)
        )

    def goes(self, way, k):
        have, _ = reach(self.me, way, k)
        ahead, _ = reach(self.me, 1 - way, 1)
        return jnp.logical_and(have, ahead)

    def start(self, way, k):
        if k < LINE - 1:

            @pl.when(self.goes(way, k))
            def _():
                self.copy(way, k).start()

    def wait_block(self, way, k):
        _, origin = reach(self.me, way, k)
        arrival(self.held(origin), self.recv.at[way, k])

    def finish(self):
        for way in range(2):
            for k in range(LINE - 1):

                @pl.when(self.goes(way, k))
                def _():
                    self.copy(way, k).wait_send()


class PlaneGather:
    def __init__(self, me, job, held, rows, send, recv):
        self.me, self.job, self.held, self.send, self.recv = me, job, held, send, recv
        self.half = rows // 2

    def piece(self, z, p, half):
        return self.held.at[z * self.me.plane + p, pl.ds(half * self.half, self.half)]

    def copy(self, z, kind, first=None):
        me = self.me
        if me.plane != 4:
            ref = first if first is not None else self.held.at[z * me.plane + me.p]
            target = lax.rem(me.p + kind + 1, me.plane)
            dst = self.held.at[z * me.plane + me.p]
        else:
            owner = (me.p, me.p, me.p, me.p, me.px, me.py)[kind]
            half = (0, 1, 1, 0, 0, 1)[kind]
            target = (me.px, me.px, me.py, me.py, me.py, me.px)[kind]
            dst = self.piece(z, owner, half)
            ref = dst if first is None else first.at[pl.ds(half * self.half, self.half)]
        return remote(
            ref, dst, self.send.at[self.job, z, kind], self.recv.at[self.job, z, kind], me.at(me.z, target)
        )

    def start(self, z, first=None):
        kinds = (0, 2, 1, 3) if self.me.plane == 4 else range(self.me.plane - 1)
        for kind in kinds:
            self.copy(z, kind, first).start()

    def forward(self, z):
        if self.me.plane == 4:
            self.copy(z, 0).wait_recv()
            self.copy(z, 4).start()
            self.copy(z, 2).wait_recv()
            self.copy(z, 5).start()

    def finish(self, zs=range(LINE)):
        kinds = 6 if self.me.plane == 4 else self.me.plane - 1
        for z in zs:
            for kind in range(kinds):
                copy = self.copy(z, kind)
                if self.me.plane != 4 or kind not in (0, 2):
                    copy.wait_recv()
                copy.wait_send()


def copy_in(src, dst, sem):
    return pltpu.make_async_copy(src, dst, sem)


def row_loop(rows, step, act):
    @pl.loop(0, rows // step)
    def _(i):
        act(pl.ds(pl.multiple_of(i * step, step), step))


def gather_kernel(
    count, len_ref, seq_ref, q_ref, k_ref, v_ref, o_ref, g_ref, u_ref, d_ref, gain_ref, tok_ref, cot_ref,
    a_all, gate_all, up_soon, up, down_t, gain_all, tok_all, dm_all, o_v, a_v, g_v, u_v, d_v, d_t, dm, chain_send, chain_recv,
    part_send, part_recv, plane_send, plane_recv, gain_send, gain_recv, pair_send, pair_recv, local_sem,
):
    plane = count // LINE
    me = Place(plane)
    rows, q_width = q_ref.shape
    kv_width = k_ref.shape[1]
    units = g_ref.shape[1] // LINE
    qkv_width = q_width + 2 * kv_width

    def columns(ref, z):
        return ref.at[:, pl.ds(pl.multiple_of(z * units, units), units)]

    local = [
        copy_in(o_ref, o_v, local_sem.at[0]),
        copy_in(q_ref, a_v.at[:, pl.ds(0, q_width)], local_sem.at[1]),
        copy_in(k_ref, a_v.at[:, pl.ds(q_width, kv_width)], local_sem.at[2]),
        copy_in(v_ref, a_v.at[:, pl.ds(q_width + kv_width, kv_width)], local_sem.at[3]),
        copy_in(d_ref, d_v, local_sem.at[4]),
        copy_in(cot_ref, dm, local_sem.at[5]),
        copy_in(columns(g_ref, me.z), g_v, local_sem.at[6]),
        copy_in(columns(u_ref, me.z), u_v, local_sem.at[7]),
        copy_in(gain_ref, gain_all.at[me.d], local_sem.at[8]),
        copy_in(tok_ref, tok_all.at[me.t], local_sem.at[9]),
    ]
    for copy in local[:4]:
        copy.start()
    keep_a = copy_in(a_v, a_all.at[me.d], local_sem.at[10])
    keep_down = copy_in(d_t, down_t, local_sem.at[11])
    keep_dm = copy_in(dm, dm_all.at[me.z, me.t], local_sem.at[12])
    keep_gate = copy_in(g_v, gate_all.at[me.d], local_sem.at[13])
    keep_up = copy_in(u_v, up.at[me.z], local_sem.at[14])

    attn = Chain(me, a_v, lambda z: a_all.at[z * plane + me.p], chain_send.at[0], chain_recv.at[0])
    dms = Chain(me, dm, lambda z: dm_all.at[z, me.t], chain_send.at[1], chain_recv.at[1])
    planes = (
        PlaneGather(me, 0, a_all, rows, plane_send, plane_recv),
        PlaneGather(me, 1, gate_all, rows, plane_send, plane_recv),
        PlaneGather(me, 2, up_soon, rows, plane_send, plane_recv),
    )

    def part(way, k, kind):
        _, target = reach(me, 1 - way, k)
        src = columns((g_ref, u_ref)[kind], target)
        dst = (gate_all.at[me.d], up.at[me.z])[kind]
        return remote(
            src, dst, part_send.at[way, k, kind], part_recv.at[way, k, kind], me.at(target, me.p)
        )

    def pair(z, first=None):
        src = dm_all.at[z, me.t] if first is None else first
        return remote(src, dm_all.at[z, me.t], pair_send.at[z], pair_recv.at[z], me.sibling())

    def keep_soon(soon, src):
        return copy_in(src, up_soon.at[soon * plane + me.p], local_sem.at[15 + soon])

    def start_parts(k, kinds):
        for way in range(2):

            @pl.when(reach(me, 1 - way, k)[0])
            def _():
                for kind in kinds:
                    part(way, k, kind).start()

    def each(k, act):
        for way in range(2):
            have, z = reach(me, way, k)

            @pl.when(have)
            def _():
                act(way, k, z)

    def attn_step(way, k, z):
        attn.wait_block(way, k)
        attn.start(way, k)
        planes[0].start(z)

    def part_step(way, k, z):
        arrival(gate_all.at[z * plane + me.p], part_recv.at[way, k, 0])
        planes[1].start(z)
        arrival(up.at[z], part_recv.at[way, k, 1])
        for soon in range(SOON):

            @pl.when(z == soon)
            def _():
                planes[2].start(soon, up.at[soon])
                keep_soon(soon, up.at[soon]).start()

    def dm_step(way, k, z):
        dms.wait_block(way, k)
        dms.start(way, k)
        pair(z).start()

    def give_gain(step):
        target = lax.rem(me.d + step, count)
        return remote(
            gain_ref, gain_all.at[me.d], gain_send.at[step], gain_recv.at[step], (target, me.t)
        )

    local[0].wait()
    a_v[:, qkv_width:] = o_v[...].T
    greet_all(me, count)
    for copy in local[1:4]:
        copy.wait()
    for way in range(2):
        attn.start(way, 0)
    planes[0].start(me.z, a_v)
    for copy in local[4:]:
        copy.start()
    keep_a.start()
    tokens = remote(tok_ref, tok_all.at[me.t], pair_send.at[LINE], pair_recv.at[LINE], me.sibling())
    tokens.start()
    for step in range(1, count):
        give_gain(step).start()

    local[4].wait()
    for z in range(LINE):
        d_t[z] = d_v[z * units : (z + 1) * units, :].T
    keep_down.start()
    local[5].wait()
    chosen = len_ref[seq_ref[0]]

    def mask(at):
        value = dm[at, :].astype(F32)
        row = lax.broadcasted_iota(jnp.int32, value.shape, 0) + (me.t * dm.shape[0] + at.start)
        dm[at, :] = jnp.where(row < chosen, value, 0.0).astype(BF16)

    row_loop(dm.shape[0], 32, mask)
    keep_dm.start()

    for k in range(1, LINE):
        each(k, attn_step)
        start_parts(k, (0, 1))
        if k == 1:
            planes[0].forward(me.z)
            for copy in local[6:8]:
                copy.wait()
            keep_gate.start()
            keep_up.start()
            planes[1].start(me.z, g_v)
            for soon in range(SOON):

                @pl.when(me.z == soon)
                def _():
                    planes[2].start(soon, u_v)
                    keep_soon(soon, u_v).start()

        else:
            each(k - 1, lambda way, k, z: planes[0].forward(z))
    for way in range(2):
        dms.start(way, 0)
    pair(me.z, dm).start()
    for k in range(1, LINE):
        each(k, part_step)
        if k == 1:
            each(LINE - 1, lambda way, k, z: planes[0].forward(z))
            planes[1].forward(me.z)
        else:
            each(k - 1, lambda way, k, z: planes[1].forward(z))
            each(k - 1, dm_step)
    each(LINE - 1, lambda way, k, z: planes[1].forward(z))
    for soon in range(SOON):
        planes[2].forward(soon)
    each(LINE - 1, dm_step)

    attn.finish()
    dms.finish()
    for k in range(1, LINE):
        for way in range(2):

            @pl.when(reach(me, 1 - way, k)[0])
            def _():
                for kind in range(2):
                    part(way, k, kind).wait_send()

    for step in range(1, count):
        give_gain(step).wait()
    tokens.wait()
    for z in range(LINE):
        pair(z).wait()
    for job, zs in zip(planes, (LINE, LINE, SOON)):
        job.finish(range(zs))
    for soon in range(SOON):
        keep_soon(soon, u_v).wait()
    for copy in local[8:] + [keep_a, keep_down, keep_dm, keep_gate, keep_up]:
        copy.wait()


ANY = pl.BlockSpec(memory_space=pl.ANY)
VMEM = pl.BlockSpec(memory_space=pltpu.VMEM)
SMEM = pl.BlockSpec(memory_space=pltpu.SMEM)
DMA = pltpu.SemaphoreType.DMA


def gather_all(count, lengths, seq, weights, gains, tokens, cotangent):
    w_query, key_weight, _, w_out, w_gate, _, w_down = weights
    rows, q_width = w_query.shape
    width = 2 * (q_width + key_weight.shape[1])
    units = w_gate.shape[1] // LINE
    kinds = max(6, count // LINE - 1)
    return pl.pallas_call(
        functools.partial(gather_kernel, count),
        name="gather_all",
        out_shape=(
            jax.ShapeDtypeStruct((count, rows, width), BF16),
            jax.ShapeDtypeStruct((count, rows, units), BF16),
            jax.ShapeDtypeStruct((count // LINE * SOON, rows, units), BF16),
            jax.ShapeDtypeStruct((LINE, rows, units), BF16),
            jax.ShapeDtypeStruct((LINE, rows, units), BF16),
            jax.ShapeDtypeStruct((count,) + gains.shape, gains.dtype),
            jax.ShapeDtypeStruct((2,) + tokens.shape, BF16),
            jax.ShapeDtypeStruct((LINE, 2) + cotangent.shape, BF16),
        ),
        in_specs=[SMEM] * 2 + [ANY] * 10,
        out_specs=(ANY,) * 8,
        scratch_shapes=[
            pltpu.VMEM(w_out.shape, BF16),
            pltpu.VMEM((rows, width), BF16),
            pltpu.VMEM((rows, units), BF16),
            pltpu.VMEM((rows, units), BF16),
            pltpu.VMEM(w_down.shape, BF16),
            pltpu.VMEM((LINE, rows, units), BF16),
            pltpu.VMEM(cotangent.shape, BF16),
            DMA((2, 2, LINE)), DMA((2, 2, LINE)), DMA((2, LINE, 2)), DMA((2, LINE, 2)),
            DMA((3, LINE, kinds)), DMA((3, LINE, kinds)), DMA((count,)), DMA((count,)),
            DMA((LINE + 1,)), DMA((LINE + 1,)), DMA((15 + SOON,)),
        ],
        compiler_params=pltpu.CompilerParams(
            collective_id=0, has_side_effects=True, vmem_limit_bytes=60 * MB
        ),
    )(lengths, seq, *weights, gains, tokens, cotangent)


RANKS = ((3, 2, 1, 0), (3, 0, 2, 1), (0, 3, 1, 2), (0, 1, 2, 3))
FAR_FIRST = [(way, k) for k in range(LINE - 1, 0, -1) for way in range(2)]


def ranked(me, rank):
    z = jnp.int32(RANKS[0][rank])
    for at in range(1, LINE):
        z = jnp.where(me.z == at, RANKS[at][rank], z)
    return z


def way_to(me, z):
    down = (z < me.z).astype(jnp.int32)
    return down, jnp.where(z < me.z, me.z - z, z - me.z)


def add_rows(target, terms, rows, start=0):
    step = 16

    @pl.loop(0, rows // step)
    def _(i):
        at = pl.ds(pl.multiple_of(start + i * step, step), step)
        total = terms[0][at].astype(F32)
        for term in terms[1:]:
            total += term[at].astype(F32)
        target[at] = total.astype(target.dtype)


def grad_rows(at, per, left_ref, right_ref, first, targets, there):
    tile = 512
    tokens = left_ref.shape[0]

    @pl.loop(0, per // tile)
    def _(n):
        left = left_ref[:, pl.ds(pl.multiple_of(at + n * tile, tile), tile)].T
        for job, ref, start in targets:
            block, units = ref.shape[1], right_ref.shape[1]
            rows = pl.ds(there + n * (tile // block), tile // block)
            for c in range(units // tile):
                grad = jnp.dot(
                    left, right_ref[pl.ds(first + job * tokens, tokens), c * tile : (c + 1) * tile],
                    preferred_element_type=F32,
                )
                ref[rows, :, start + c * tile : start + (c + 1) * tile] = grad.astype(BF16).reshape(
                    tile // block, block, tile
                )


class PlaneSum:
    def __init__(self, me, grad, own, other, first, second, sems, ranks=range(LINE)):
        self.me, self.grad, self.own, self.other, self.first, self.second = me, grad, own, other, first, second
        (
            self.first_send, self.first_recv, self.second_send, self.second_recv, self.load_sem, self.other_sem,
        ) = sems
        self.ranks = ranks
        self.rows = own.shape[1]
        half = self.rows // 2
        self.half = half
        self.halves = (pl.ds(0, half), pl.ds(half, half))
        self.square = me.plane == 4
        if self.square:
            self.near = (me.px, me.py)
            self.far = (me.py, me.px)

    def slot(self, rank):
        return rank - self.ranks[0]

    def block(self, rank, p):
        if callable(self.grad):
            return self.grad(rank, p)
        return self.grad.at[ranked(self.me, rank) * self.me.plane + p]

    def load(self, rank):
        s = self.slot(rank)
        return pltpu.make_async_copy(self.block(rank, self.me.p), self.own.at[s], self.load_sem.at[s])

    def load_other(self, rank, i):
        s = self.slot(rank)
        return pltpu.make_async_copy(
            self.block(rank, self.far[i]).at[self.halves[i]], self.other.at[s, self.halves[i]],
            self.other_sem.at[s, i],
        )

    def load_rank(self, rank):
        self.load(rank).start()
        if self.square:
            for i in range(2):
                self.load_other(rank, i).start()

    def load_all(self):
        for rank in self.ranks:
            self.load_rank(rank)

    def give(self, rank, i, which):
        me, s = self.me, self.slot(rank)
        if not self.square:
            target = lax.rem(me.p + which + 1, me.plane)
            return remote(
                self.block(rank, target), self.first.at[s, which], self.first_send.at[s, which],
                self.first_recv.at[s, which], me.at(me.z, target),
            )
        owner = (self.near[i], me.pd)[which]
        return remote(
            self.block(rank, owner).at[self.halves[i]], self.first.at[s, which, self.halves[i]],
            self.first_send.at[s, 2 * i + which], self.first_recv.at[s, 2 * i + which],
            me.at(me.z, self.near[i]),
        )

    def give_both(self, rank, i):
        s = self.slot(rank)
        return remote(
            self.other.at[s, self.halves[i]], self.second.at[s, self.halves[i]],
            self.second_send.at[s, i], self.second_recv.at[s, i], self.me.at(self.me.z, self.far[i]),
        )

    def gives(self, rank):
        if self.square:
            return [self.give(rank, i, which) for which in (1, 0) for i in range(2)]
        return [self.give(rank, 0, which) for which in range(self.me.plane - 1)]

    def begin(self, rank):
        for copy in self.gives(rank):
            copy.start()

    def middle(self, rank):
        if not self.square:
            return
        s = self.slot(rank)
        for i in range(2):
            arrival(self.first.at[s, 1, self.halves[i]], self.first_recv.at[s, 2 * i + 1])
            self.load_other(rank, i).wait()
            add_rows(
                self.other.at[s], (self.other.at[s], self.first.at[s, 1]), self.half, i * self.half
            )
            self.give_both(rank, i).start()

    def end(self, rank):
        s = self.slot(rank)
        self.load(rank).wait()
        if self.square:
            for i in range(2):
                arrival(self.first.at[s, 0, self.halves[i]], self.first_recv.at[s, 2 * i])
                arrival(self.second.at[s, self.halves[i]], self.second_recv.at[s, i])
            terms = (self.first.at[s, 0], self.second.at[s])
        else:
            for which in range(self.me.plane - 1):
                arrival(self.first.at[s, which], self.first_recv.at[s, which])
            terms = tuple(self.first.at[s, which] for which in range(self.me.plane - 1))
        add_rows(self.own.at[s], (self.own.at[s],) + terms, self.rows)

    def finish(self):
        for rank in self.ranks:
            for copy in self.gives(rank):
                copy.wait_send()
            if self.square:
                for i in range(2):
                    self.give_both(rank, i).wait_send()

    @staticmethod
    def scratch(count, rows, width, ranks=LINE):
        plane = count // LINE
        square = plane == 4
        slots = 2 if square else plane - 1
        small = (ranks, rows, width) if square else (1, 16, 128)
        return [
            pltpu.VMEM((ranks, rows, width), BF16),
            pltpu.VMEM(small, BF16),
            pltpu.VMEM((ranks, slots, rows, width), BF16),
            pltpu.VMEM(small, BF16),
        ], [
            DMA((ranks, max(4, slots))), DMA((ranks, max(4, slots))), DMA((ranks, 2)), DMA((ranks, 2)),
            DMA((ranks,)), DMA((ranks, 2)),
        ]


def dot_cols(left, right):
    return lax.dot_general(left, right, (((1,), (1,)), ((), ())), preferred_element_type=F32)


def feed_forward_kernel(
    plane, h_ref, dm_ref, gate_ref, up_soon, up_rest, down, total_ref, out_ref, grad_ref, sum_ref,
    h_out, inner_out, rows_in, weights, inner, down_grad, part,
    from_pair, from_line, own, other, first, second, first_send, first_recv, second_send, second_recv,
    own_sem, other_sem, chain_send, chain_recv, pass_send, pass_recv, pair_send, pair_recv,
    line_send, line_recv, plane_send, plane_recv, load_sem, dm_sem, grad_sem, out_sem, sum_sem,
):
    me = Place(plane)
    rows, model = h_ref.shape
    units = inner.shape[1]
    wide = 2 * rows
    tokens = LINE * wide
    block = down.shape[1]
    soon = up_soon.shape[0]
    tile = 512

    def slot(z, t):
        return rows_in.at[pl.ds(pl.multiple_of((z * 2 + t) * rows, rows), rows)]

    loads = [
        copy_in(gate_ref, weights.at[:, :, pl.ds(0, units)], load_sem.at[0]),
        copy_in(up_soon, weights.at[pl.ds(0, soon), :, pl.ds(units, units)], load_sem.at[2]),
        copy_in(
            up_rest, weights.at[pl.ds(soon, up_rest.shape[0]), :, pl.ds(units, units)], load_sem.at[3]
        ),
    ]
    own_down = [
        copy_in(
            down.at[z], weights.at[z * plane + me.p, :, pl.ds(2 * units, units)], load_sem.at[4 + z]
        )
        for z in range(LINE)
    ]
    for load in loads:
        load.start()
    load_dm = pltpu.make_async_copy(dm_ref, rows_in.at[pl.ds(tokens, tokens)], dm_sem)
    load_dm.start()
    keep = pltpu.make_async_copy(h_ref, slot(me.z, me.t), load_sem.at[1])
    keep.start()
    greet_all(me, plane * LINE)
    gather = PlaneGather(
        me, 0, weights.at[:, :, pl.ds(2 * units, units)], block, plane_send, plane_recv
    )
    summed = PlaneSum(
        me, down_grad, own, other, first, second,
        (first_send, first_recv, second_send, second_recv, own_sem, other_sem),
    )
    chain = Chain(me, h_ref, lambda z: slot(z, me.t), chain_send, chain_recv)

    def share(z, first=None):
        src = slot(z, me.t) if first is None else first
        return remote(src, slot(z, me.t), pass_send.at[z], pass_recv.at[z], me.sibling())

    for way in range(2):
        chain.start(way, 0)
    share(me.z, h_ref).start()
    for z in range(2):
        gather.start(z, down.at[z])
    for copy in own_down:
        copy.start()

    def w_rows(n, width, column):
        return weights[pl.ds(n * (width // block), width // block), :, pl.ds(column, units)].reshape(
            width, units
        )

    def pair_rows(z, job=0):
        return pl.ds(pl.multiple_of(job * tokens + z * wide, wide), wide)

    def columns(c, job):
        return weights[:, :, pl.ds(pl.multiple_of(job * units + c * tile, tile), tile)].reshape(model, tile)

    def project(z):
        @pl.loop(0, units // tile)
        def _(c):
            here = pl.ds(pl.multiple_of(c * tile, tile), tile)
            h = rows_in[pair_rows(z), :]
            gate = jnp.dot(h, columns(c, 0), preferred_element_type=F32)
            up = jnp.dot(h, columns(c, 1), preferred_element_type=F32)
            sigmoid = jax.nn.sigmoid(gate)
            silu = gate * sigmoid
            inner[pair_rows(z), here] = (silu * up).astype(BF16)
            inner[pair_rows(z, 1), here] = (up * sigmoid * (1.0 + gate * (1.0 - sigmoid))).astype(BF16)
            inner[pair_rows(z, 2), here] = silu.astype(BF16)

    def back(z):
        @pl.loop(0, units // tile)
        def _(c):
            here = pl.ds(pl.multiple_of(c * tile, tile), tile)
            grad_hidden = jnp.dot(rows_in[pair_rows(z, 1), :], columns(c, 2), preferred_element_type=F32)
            for job in range(1, 3):
                at = pair_rows(z, job)
                inner[at, here] = (grad_hidden * inner[at, here].astype(F32)).astype(BF16)

        @pl.loop(0, model // tile)
        def _(n):
            here = pl.ds(pl.multiple_of(n * tile, tile), tile)
            grad = dot_cols(inner[pair_rows(z, 1)], w_rows(n, tile, 0))
            grad += dot_cols(inner[pair_rows(z, 2)], w_rows(n, tile, units))
            part[0, z, :, :, here] = grad.astype(BF16).reshape(2, rows, tile)

        pair(z).start()

    def out(z):
        @pl.loop(0, model // tile)
        def _(n):
            here = pl.ds(pl.multiple_of(n * tile, tile), tile)
            value = dot_cols(inner[pair_rows(z), :], w_rows(n, tile, 2 * units))
            part[1, z, :, :, here] = value.astype(BF16).reshape(2, rows, tile)

        keep_out(z).start()

    def pair(z):
        return remote(
            part.at[0, z, 1 - me.t], from_pair.at[z], pair_send.at[z], pair_recv.at[z], me.sibling()
        )

    half = rows // 2
    halves = (pl.ds(0, half), pl.ds(half, half))

    def pass_on(way, k, i):
        _, target = reach(me, 1 - way, k)
        ahead = me.z + 1 if way == 0 else me.z - 1
        return remote(
            part.at[0, target, me.t, halves[i]], from_line.at[way, k - 1, halves[i]],
            line_send.at[way, k, i], line_recv.at[way, k - 1, i], me.at(ahead, me.p),
        )

    def line(way, k, behind):
        have, z = reach(me, 1 - way, k)
        before = me.z if way == 0 else LINE - 1 - me.z

        @pl.when(jnp.logical_and(have, before == behind))
        def _():
            pair(z).wait_recv()
            terms = (part.at[0, z, me.t], from_pair.at[z])
            if behind:
                terms += (from_line.at[way, k],)
            for i in range(2):
                if behind:
                    arrival(from_line.at[way, k, halves[i]], line_recv.at[way, k, i])
                add_rows(part.at[0, z, me.t], terms, half, i * half)
                pass_on(way, k, i).start()

    def total():
        pair(me.z).wait_recv()
        add_rows(total_ref, (part.at[0, me.z, me.t], from_pair.at[me.z]), rows)
        for way in range(2):

            @pl.when(reach(me, way, 1)[0])
            def _():
                for i in range(2):
                    arrival(from_line.at[way, 0, halves[i]], line_recv.at[way, 0, i])
                    add_rows(total_ref, (total_ref, from_line.at[way, 0]), half, i * half)

    per = plane * block

    def down_grads(rank):
        z = ranked(me, rank)
        grad_rows(
            z * per, per, rows_in.at[pl.ds(tokens, tokens)], inner, 0, [(0, down_grad, 0)], z * plane
        )
        summed.load_rank(rank)

    keeps = [
        copy_in(weights.at[pl.ds(0, plane), :, pl.ds(0, 2 * units)], grad_ref, grad_sem.at[0]),
        copy_in(rows_in.at[pl.ds(0, tokens)], h_out, grad_sem.at[1]),
        copy_in(inner.at[pl.ds(tokens, 2 * tokens)], inner_out, grad_sem.at[2]),
    ]

    def grads():
        targets = [(0, weights, 0), (1, weights, units)]
        z = ranked(me, 0)
        grad_rows(z * per, per, rows_in.at[pl.ds(0, tokens)], inner, tokens, targets, 0)

    def keep_sum(rank):
        return copy_in(own.at[rank], sum_ref.at[rank], sum_sem.at[rank])

    keep.wait()
    for load in loads:
        load.wait()
    for k in range(LINE):
        for way in range(2 if k else 1):
            have, z = reach(me, way, k)

            @pl.when(have)
            def _():
                if k:
                    chain.wait_block(way, k)
                    chain.start(way, k)
                    share(z).start()
                arrival(slot(z, 1 - me.t), pass_recv.at[z])
                project(z)

        gather.forward(k)
        if k + 2 < LINE:
            gather.start(k + 2, down.at[k + 2])
    def keep_out(z):
        return copy_in(part.at[1, z], out_ref.at[z], out_sem.at[z])

    load_dm.wait()
    keeps[1].start()
    down_grads(0)
    summed.begin(0)
    for copy in own_down:
        copy.wait()
    gather.finish()
    passing = {1: (1, 2), 2: (2, 1), 3: (1, 1)}
    for rank in range(LINE):
        if rank:
            down_grads(rank)
            if rank - 1 in passing:
                for way in range(2):
                    line(way, passing[rank - 1][1], passing[rank - 1][0])
            summed.middle(rank - 1)
            summed.begin(rank)
            if rank > 1:
                summed.end(rank - 2)
                keep_sum(rank - 2).start()
        back(ranked(me, rank))
        if rank < LINE - 1:
            out(ranked(me, rank))
            for way in range(2):
                line(way, LINE - 1 - rank, 0)
    for way in range(2):
        line(way, passing[LINE - 1][1], passing[LINE - 1][0])
    keeps[2].start()
    summed.middle(LINE - 1)
    summed.end(LINE - 2)
    keep_sum(LINE - 2).start()
    grads()
    keeps[0].start()
    out(ranked(me, LINE - 1))
    summed.end(LINE - 1)
    keep_sum(LINE - 1).start()
    total()
    summed.finish()
    chain.finish()
    for z in range(LINE):
        share(z).wait_send()
        keep_out(z).wait()
        keep_sum(z).wait()
        pair(z).wait_send()
    for copy in keeps:
        copy.wait()
    for k in range(1, LINE):
        for way in range(2):

            @pl.when(reach(me, 1 - way, k)[0])
            def _():
                for i in range(2):
                    pass_on(way, k, i).wait_send()


def feed_forward(count, h, dm_all, gate_all, up_soon, up_rest, down):
    rows, model = h.shape
    _, block, units = down.shape
    kinds = max(6, count // LINE - 1)
    buffers, sems = PlaneSum.scratch(count, block, units)
    tokens = LINE * 2 * rows
    vmem = pl.BlockSpec(memory_space=pltpu.VMEM)
    return pl.pallas_call(
        functools.partial(feed_forward_kernel, count // LINE),
        name="feed_forward",
        out_shape=(
            jax.ShapeDtypeStruct((rows, model), F32),
            jax.ShapeDtypeStruct((LINE, 2, rows, model), BF16),
            jax.ShapeDtypeStruct((count // LINE, block, 2 * units), BF16),
            jax.ShapeDtypeStruct((LINE, block, units), BF16),
            jax.ShapeDtypeStruct((tokens, model), BF16),
            jax.ShapeDtypeStruct((2 * tokens, units), BF16),
        ),
        in_specs=[ANY] * 6,
        out_specs=(vmem,) + (ANY,) * 5,
        scratch_shapes=[
            pltpu.VMEM((2 * tokens, model), BF16),
            pltpu.VMEM((count, block, 3 * units), BF16),
            pltpu.VMEM((3 * tokens, units), BF16),
            pltpu.VMEM((count, block, units), BF16),
            pltpu.VMEM((2, LINE, 2, rows, model), BF16),
            pltpu.VMEM((LINE, rows, model), BF16),
            pltpu.VMEM((2, LINE - 1, rows, model), BF16),
            *buffers,
            *sems,
            DMA((2, LINE)), DMA((2, LINE)), DMA((LINE,)), DMA((LINE,)), DMA((LINE,)), DMA((LINE,)),
            DMA((2, LINE, 2)), DMA((2, LINE, 2)), DMA((1, LINE, kinds)), DMA((1, LINE, kinds)),
            DMA((4 + LINE,)), DMA, DMA((LINE,)), DMA((LINE,)), DMA((LINE,)),
        ],
        compiler_params=pltpu.CompilerParams(
            collective_id=1, has_side_effects=True, vmem_limit_bytes=60 * MB
        ),
    )(h, dm_all, gate_all, up_soon, up_rest, down)


def greet_plane(me):
    barrier = pltpu.get_barrier_semaphore()
    for step in range(1, me.plane):
        target = lax.rem(me.p + step, me.plane)
        pl.semaphore_signal(barrier, inc=1, device_id=me.at(me.z, target), device_id_type=MESH)
    pl.semaphore_signal(barrier, inc=1, device_id=me.sibling(), device_id_type=MESH)
    pl.semaphore_wait(barrier, me.plane)


def columns_of(weights, start, width):
    count, rows, _ = weights.shape
    return weights[:, :, pl.ds(start, width)].reshape(count * rows, width)


def rows_of(weights, n, height, start, width):
    _, rows, _ = weights.shape
    per = height // rows
    return weights[pl.ds(n * per, per), :, pl.ds(start, width)].reshape(height, width)


def attention_forward_kernel(
    plane, len_ref, seq_ref, gain_ref, cos_ref, sin_ref, tok_in, a_ref, up, down_t, x1_out, h2_out, h1_out,
    qkv_out, probs_out, o_out, up_rest, down, weights, tok_ref, x1_ref, h2_ref, h1_ref, qkv_ref, probs_ref,
    o_ref, part, from_pair, plane_send, plane_recv, part_send, part_recv, pair_send, pair_recv, load_sem, keep_sem,
):
    me = Place(plane)
    _, rows, model = tok_ref.shape
    wide = 2 * rows
    heads, _, _ = probs_ref.shape
    q_width = heads * HEAD_SIZE
    kv_width = (qkv_ref.shape[1] - q_width) // 2
    kv_heads = kv_width // HEAD_SIZE
    half = HEAD_SIZE // 2
    load_tok = copy_in(tok_in, tok_ref, load_sem.at[0])
    load_tok.start()
    load = copy_in(a_ref, weights, load_sem.at[1])
    load.start()
    keep = [
        copy_in(up.at[z], up_rest.at[(z - SOON) * plane + me.p], load_sem.at[2 + z])
        for z in range(SOON, LINE)
    ]
    keep.append(copy_in(down_t.at[me.z], down.at[me.z], load_sem.at[2 + LINE]))
    for copy in keep:
        copy.start()
    outs = [
        copy_in(src, dst, keep_sem.at[i])
        for i, (src, dst) in enumerate(
            (
                (h1_ref, h1_out), (qkv_ref, qkv_out), (probs_ref, probs_out), (o_ref, o_out),
                (x1_ref, x1_out), (h2_ref, h2_out),
            )
        )
    ]
    greet_all(me, plane * LINE)
    gather = PlaneGather(me, 0, up_rest, up.shape[1], plane_send, plane_recv)
    for z in range(LINE - SOON):
        gather.start(z, up.at[z + SOON])

    def give_down(way, k):
        _, target = reach(me, 1 - way, k)
        return remote(
            down_t.at[target], down.at[me.z], part_send.at[way, k], part_recv.at[way, k],
            me.at(target, me.p),
        )

    for k in range(1, LINE):
        for way in range(2):

            @pl.when(reach(me, 1 - way, k)[0])
            def _():
                give_down(way, k).start()

    load_tok.wait()

    for t in range(2):

        def norm(at, t=t):
            x = tok_ref[t, at, :].astype(F32)
            factor = lax.rsqrt(jnp.mean(x * x, -1, keepdims=True) + EPS)
            h1_ref[pl.ds(t * rows + at.start, at.size), :] = (x * factor * gain_ref[0:1, :]).astype(BF16)

        row_loop(rows, 32, norm)
    outs[0].start()
    load.wait()

    def project(i):
        start = pl.multiple_of(i * HEAD_SIZE, HEAD_SIZE)
        return start, jnp.dot(
            h1_ref[...], columns_of(weights, start, HEAD_SIZE), preferred_element_type=F32
        )

    @pl.loop(0, heads + kv_heads)
    def _(i):
        start, values = project(i)
        first, second = values[:, :half], values[:, half:]
        cos, sin = cos_ref[...], sin_ref[...]
        qkv_ref[:, pl.ds(start, half)] = (first * cos - second * sin).astype(BF16)
        qkv_ref[:, pl.ds(start + half, half)] = (second * cos + first * sin).astype(BF16)

    @pl.loop(heads + kv_heads, heads + 2 * kv_heads)
    def _(i):
        start, values = project(i)
        qkv_ref[:, pl.ds(start, HEAD_SIZE)] = values.astype(BF16)

    outs[1].start()
    gather.forward(0)
    row = lax.broadcasted_iota(jnp.int32, (wide, wide), 0)
    key = lax.broadcasted_iota(jnp.int32, (wide, wide), 1)
    allowed = jnp.logical_and(key <= row, key < len_ref[seq_ref[0]])
    for i in range(heads):
        m = i * kv_heads // heads
        q = qkv_ref[:, i * HEAD_SIZE : (i + 1) * HEAD_SIZE]
        k = qkv_ref[:, q_width + m * HEAD_SIZE : q_width + (m + 1) * HEAD_SIZE]
        v = qkv_ref[:, q_width + kv_width + m * HEAD_SIZE : q_width + kv_width + (m + 1) * HEAD_SIZE]
        scores = dot_cols(q, k) * HEAD_SIZE ** (-0.5)
        scores = jnp.where(allowed, scores, -1e30)
        grown = jnp.exp(scores - jnp.max(scores, -1, keepdims=True))
        probs = grown / jnp.sum(grown, -1, keepdims=True)
        probs_ref[i] = probs
        o_ref[:, i * HEAD_SIZE : (i + 1) * HEAD_SIZE] = jnp.dot(
            probs.astype(BF16), v, preferred_element_type=F32
        ).astype(BF16)

    outs[2].start()
    outs[3].start()
    gather.forward(1)
    tile = 512

    @pl.loop(0, model // tile)
    def _(n):
        here = pl.ds(pl.multiple_of(n * tile, tile), tile)
        value = dot_cols(o_ref[...], rows_of(weights, n, tile, q_width + 2 * kv_width, q_width))
        part[:, :, here] = value.reshape(2, rows, tile)

    swap = remote(part.at[1 - me.t], from_pair, pair_send, pair_recv, me.sibling())
    swap.start()
    for z in range(2, LINE - SOON):
        gather.forward(z)
    swap.wait_recv()

    def add(at):
        x1 = tok_ref[me.t, at, :].astype(F32) + (part[me.t, at, :] + from_pair[at, :])
        x1_ref[at, :] = x1
        factor = lax.rsqrt(jnp.mean(x1 * x1, -1, keepdims=True) + EPS)
        h2_ref[at, :] = (x1 * factor * gain_ref[1:2, :]).astype(BF16)

    row_loop(rows, 32, add)
    outs[4].start()
    outs[5].start()
    swap.wait_send()
    gather.finish(range(LINE - SOON))
    for k in range(1, LINE):
        for way in range(2):

            @pl.when(reach(me, 1 - way, k)[0])
            def _():
                give_down(way, k).wait_send()

            @pl.when(reach(me, way, k)[0])
            def _():
                arrival(down.at[me.z], part_recv.at[way, k])

    for copy in keep + outs:
        copy.wait()


def attention_forward(count, heads, lengths, seq, gains, cos, sin, tokens_all, attn_all, up, down_t):
    _, rows, model = tokens_all.shape
    wide = 2 * rows
    q_width = heads * HEAD_SIZE
    qkv_width = attn_all.shape[2] - q_width
    plane = count // LINE
    kinds = max(6, plane - 1)
    outs = (
        jax.ShapeDtypeStruct((rows, model), F32),
        jax.ShapeDtypeStruct((rows, model), BF16),
        jax.ShapeDtypeStruct((wide, model), BF16),
        jax.ShapeDtypeStruct((wide, qkv_width), BF16),
        jax.ShapeDtypeStruct((heads, wide, wide), F32),
        jax.ShapeDtypeStruct((wide, q_width), BF16),
    )
    return pl.pallas_call(
        functools.partial(attention_forward_kernel, plane),
        name="attention_forward",
        out_shape=outs
        + (
            jax.ShapeDtypeStruct((count - SOON * plane,) + up.shape[1:], BF16),
            jax.ShapeDtypeStruct(down_t.shape, BF16),
        ),
        in_specs=[SMEM] * 2 + [VMEM] * 3 + [ANY] * 4,
        out_specs=(ANY,) * 8,
        scratch_shapes=[
            pltpu.VMEM(attn_all.shape, BF16),
            pltpu.VMEM(tokens_all.shape, BF16),
            *[pltpu.VMEM(out.shape, out.dtype) for out in outs],
            pltpu.VMEM((2, rows, model), F32),
            pltpu.VMEM((rows, model), F32),
            DMA((1, LINE, kinds)), DMA((1, LINE, kinds)), DMA((2, LINE)), DMA((2, LINE)), DMA, DMA,
            DMA((3 + LINE,)), DMA((6,)),
        ],
        compiler_params=pltpu.CompilerParams(
            collective_id=2, has_side_effects=True, vmem_limit_bytes=60 * MB
        ),
    )(lengths, seq, gains, cos, sin, tokens_all, attn_all, up, down_t)


def attention_backward_kernel(
    plane, gain_ref, cos_ref, sin_ref, total_in, x1_in, dm_in, tok_in, h1_in, qkv_in, probs_in, o_in,
    a_ref, gw_ref, sum_ref, h_in, inner_in, ga_ref, w_out, grad_tokens, gain_parts, weights, own, other, first, second,
    total_ref, x1_ref, dm_ref, tok_ref, h1_ref, qkv_ref, probs_ref, o_ref, rows_in, inner, gw, dx, da, do, dqkv, dh1, from_pair, first_send, first_recv, second_send, second_recv, load_sem,
    other_sem, part_send, part_recv, pair_send, pair_recv, a_sem, keep_sem, grad_sem, in_sem,
):
    me = Place(plane)
    _, rows, model = tok_ref.shape
    block = weights.shape[1]
    heads, _, _ = probs_ref.shape
    q_width = heads * HEAD_SIZE
    qkv_width = qkv_ref.shape[1]
    kv_width = (qkv_width - q_width) // 2
    kv_heads = kv_width // HEAD_SIZE
    half = HEAD_SIZE // 2
    scale = HEAD_SIZE ** (-0.5)
    summed = PlaneSum(
        me, lambda rank, p: gw.at[(rank - 1) * plane + p] if rank else gw_ref.at[p],
        own, other, first, second,
        (first_send, first_recv, second_send, second_recv, load_sem, other_sem),
    )
    ins = [
        copy_in(src, dst, in_sem.at[i])
        for i, (src, dst) in enumerate(
            (
                (total_in, total_ref), (x1_in, x1_ref), (dm_in.at[me.z, me.t], dm_ref), (tok_in, tok_ref),
                (h1_in, h1_ref), (qkv_in, qkv_ref), (probs_in, probs_ref), (o_in, o_ref),
                (h_in, rows_in), (inner_in, inner),
            )
        )
    ]
    for copy in ins[:3] + ins[8:]:
        copy.start()
    load = pltpu.make_async_copy(a_ref, weights, a_sem)
    load.start()
    for copy in ins[3:8]:
        copy.start()
    summed.load_rank(0)
    greet_all(me, plane * LINE)

    wide = own.shape[2]
    spans = (pl.ds(0, wide), pl.ds(wide, sum_ref.shape[2]))

    def part(rank, kind):
        target = ranked(me, rank)
        way, k = way_to(me, target)
        return remote(
            (own, sum_ref)[kind].at[rank], w_out.at[me.z, :, spans[kind]], part_send.at[way, k, kind],
            part_recv.at[way, k, kind], me.at(target, me.p),
        )

    keeps = [
        copy_in((own, sum_ref)[kind].at[LINE - 1], w_out.at[me.z, :, spans[kind]], keep_sem.at[kind])
        for kind in range(2)
    ]
    give_da = remote(da.at[me.t], da.at[me.t], pair_send.at[0], pair_recv.at[0], me.sibling())
    give_dh1 = remote(dh1.at[1 - me.t], from_pair, pair_send.at[1], pair_recv.at[1], me.sibling())

    def mid_norm():
        gain_parts[...] = jnp.zeros_like(gain_parts)

        def act(at):
            x, up = x1_ref[at, :], total_ref[at, :]
            factor = lax.rsqrt(jnp.mean(x * x, -1, keepdims=True) + EPS)
            scaled = up * gain_ref[1:2, :]
            grad = dm_ref[at, :].astype(F32) + (
                factor * scaled - x * factor**3 * jnp.mean(scaled * x, -1, keepdims=True)
            )
            dx[at, :] = grad
            da[me.t, at, :] = grad.astype(BF16)
            gain_parts[1:2, :] += jnp.sum(up * x * factor, 0, keepdims=True)

        row_loop(rows, 32, act)
        give_da.start()

    def grad_o():
        load.wait()
        give_da.wait_recv()

        @pl.loop(0, q_width // HEAD_SIZE)
        def _(c):
            here = pl.multiple_of(c * HEAD_SIZE, HEAD_SIZE)
            value = jnp.dot(
                da[...].reshape(2 * rows, model),
                columns_of(weights, qkv_width + here, HEAD_SIZE),
                preferred_element_type=F32,
            )
            do[:, pl.ds(here, HEAD_SIZE)] = value.astype(BF16)

    def rotate(values, start):
        first, second = values[:, :half], values[:, half:]
        cos, sin = cos_ref[...], sin_ref[...]
        dqkv[:, start : start + half] = (first * cos + second * sin).astype(BF16)
        dqkv[:, start + half : start + 2 * half] = (second * cos - first * sin).astype(BF16)

    def grad_heads():
        group = heads // kv_heads
        for m in range(kv_heads):
            at_k = q_width + m * HEAD_SIZE
            at_v = at_k + kv_width
            k = qkv_ref[:, at_k : at_k + HEAD_SIZE]
            v = qkv_ref[:, at_v : at_v + HEAD_SIZE]
            grad_k = grad_v = None
            for i in range(m * group, (m + 1) * group):
                at = slice(i * HEAD_SIZE, (i + 1) * HEAD_SIZE)
                probs = probs_ref[i]
                grad_probs = dot_cols(do[:, at], v)
                grad_scores = probs * (
                    grad_probs - jnp.sum(probs * grad_probs, -1, keepdims=True)
                )
                low = grad_scores.astype(BF16)
                rotate(jnp.dot(low, k, preferred_element_type=F32) * scale, i * HEAD_SIZE)
                more_k = dot_tn(low, qkv_ref[:, at])
                more_v = dot_tn(probs.astype(BF16), do[:, at])
                grad_k = more_k if grad_k is None else grad_k + more_k
                grad_v = more_v if grad_v is None else grad_v + more_v
            rotate(grad_k * scale, at_k)
            dqkv[:, at_v : at_v + HEAD_SIZE] = grad_v.astype(BF16)

    tile = 512

    def grad_h1():
        @pl.loop(0, model // tile)
        def _(n):
            here = pl.ds(pl.multiple_of(n * tile, tile), tile)
            value = dot_cols(dqkv[...], rows_of(weights, n, tile, 0, qkv_width))
            dh1[:, :, here] = value.reshape(2, rows, tile)

        give_dh1.start()

    def keep_grads(n):
        per = tile // block
        return pltpu.make_async_copy(
            weights.at[pl.ds(n * per, per)], ga_ref.at[pl.ds(n * per, per)], grad_sem.at[n]
        )

    def grads():
        @pl.loop(0, model // tile)
        def _(n):
            here = pl.ds(pl.multiple_of(n * tile, tile), tile)
            there = pl.ds(n * (tile // block), tile // block)
            left = h1_ref[:, here].T
            for c in range(qkv_width // tile):
                at = slice(c * tile, (c + 1) * tile)
                value = jnp.dot(left, dqkv[:, at], preferred_element_type=F32)
                weights[there, :, at] = value.astype(BF16).reshape(tile // block, block, tile)
            left = da[:, :, here].reshape(2 * rows, tile).T
            for c in range(q_width // tile):
                at = slice(c * tile, (c + 1) * tile)
                value = jnp.dot(left, o_ref[:, at], preferred_element_type=F32)
                at = slice(qkv_width + c * tile, qkv_width + (c + 1) * tile)
                weights[there, :, at] = value.astype(BF16).reshape(tile // block, block, tile)

        for n in range(model // tile):
            keep_grads(n).start()

    def in_norm():
        give_dh1.wait_recv()

        def act(at):
            x = tok_ref[me.t, at, :].astype(F32)
            up = dh1[me.t, at, :] + from_pair[at, :]
            factor = lax.rsqrt(jnp.mean(x * x, -1, keepdims=True) + EPS)
            scaled = up * gain_ref[0:1, :]
            grad_tokens[at, :] = dx[at, :] + (
                factor * scaled - x * factor**3 * jnp.mean(scaled * x, -1, keepdims=True)
            )
            gain_parts[0:1, :] += jnp.sum(up * x * factor, 0, keepdims=True)

        row_loop(rows, 32, act)

    summed.begin(0)
    for rank in range(LINE - 1):
        part(rank, 1).start()
    keeps[1].start()
    def mlp_grads(rank):
        per = plane * block
        targets = [(0, gw, 0), (1, gw, inner.shape[1])]
        z = ranked(me, rank)
        grad_rows(z * per, per, rows_in, inner, 0, targets, (rank - 1) * plane)
        summed.load_rank(rank)

    for copy in ins[:3]:
        copy.wait()
    mid_norm()
    for copy in ins[8:]:
        copy.wait()
    mlp_grads(1)
    grad_o()
    for copy in ins[3:8]:
        copy.wait()
    stages = (
        [grad_heads, lambda: mlp_grads(2)], [grad_h1, lambda: mlp_grads(3)], [grads], [in_norm],
    )
    for rank in range(LINE):
        summed.middle(rank)
        if rank + 1 < LINE:
            summed.begin(rank + 1)
        for stage in stages[rank]:
            stage()
        summed.end(rank)
        if rank < LINE - 1:
            part(rank, 0).start()

    keeps[0].start()
    for kind in range(2):
        for rank in range(LINE - 1):
            part(rank, kind).wait_send()
        for way, k in FAR_FIRST:

            @pl.when(reach(me, way, k)[0])
            def _():
                arrival(w_out.at[me.z, :, spans[kind]], part_recv.at[way, k, kind])

    summed.finish()
    give_da.wait_send()
    give_dh1.wait_send()
    for n in range(model // tile):
        keep_grads(n).wait()
    for copy in keeps:
        copy.wait()


def attention_backward(
    count, gains, cos, sin, total, x1, dm_all, tokens_all, h1, qkv, probs, o, attn_all, grad_mlp, first_sum, rows_in,
    inner,
):
    _, rows, model = tokens_all.shape
    _, block, width = attn_all.shape
    wide = 2 * rows
    heads = probs.shape[0]
    q_width = heads * HEAD_SIZE
    buffers, sems = PlaneSum.scratch(count, block, grad_mlp.shape[2])
    return pl.pallas_call(
        functools.partial(attention_backward_kernel, count // LINE),
        name="attention_backward",
        out_shape=(
            jax.ShapeDtypeStruct(attn_all.shape, BF16),
            jax.ShapeDtypeStruct((LINE, block, width), BF16),
            jax.ShapeDtypeStruct((rows, model), F32),
            jax.ShapeDtypeStruct((2, model), F32),
        ),
        in_specs=[VMEM] * 3 + [ANY] * 13,
        out_specs=(ANY, ANY, VMEM, VMEM),
        scratch_shapes=[
            pltpu.VMEM(attn_all.shape, BF16),
            *buffers,
            *[
                pltpu.VMEM(ref.shape, ref.dtype)
                for ref in (total, x1, dm_all[0, 0], tokens_all, h1, qkv, probs, o, rows_in, inner)
            ],
            pltpu.VMEM(((LINE - 1) * grad_mlp.shape[0],) + grad_mlp.shape[1:], BF16),
            pltpu.VMEM((rows, model), F32),
            pltpu.VMEM((2, rows, model), BF16),
            pltpu.VMEM((wide, q_width), BF16),
            pltpu.VMEM(qkv.shape, BF16),
            pltpu.VMEM((2, rows, model), F32),
            pltpu.VMEM((rows, model), F32),
            *sems,
            DMA((2, LINE, 2)), DMA((2, LINE, 2)), DMA((2,)), DMA((2,)), DMA, DMA((2,)),
            DMA((model // 512,)), DMA((10,)),
        ],
        compiler_params=pltpu.CompilerParams(
            collective_id=3, has_side_effects=True, vmem_limit_bytes=60 * MB
        ),
    )(gains, cos, sin, total, x1, dm_all, tokens_all, h1, qkv, probs, o, attn_all, grad_mlp, first_sum, rows_in, inner)


def grad_sum_kernel(
    count, gain_ref, x1_in, ga_ref, out_ref, a_out, output, gain_out, own, other, first, second, x1_ref,
    from_line, out_own, out_pair, out_line, gain_in, gain_pair, first_send, first_recv, second_send, second_recv,
    load_sem, other_sem, line_send, line_recv, out_send, out_recv, load_out_sem, pair_send, pair_recv, gain_send, gain_recv,
):
    plane = count // LINE
    me = Place(plane)
    rows = a_out.shape[0]
    summed = PlaneSum(
        me, ga_ref, own, other, first, second,
        (first_send, first_recv, second_send, second_recv, load_sem, other_sem),
    )

    class Line:
        def __init__(self, held, landing, send, recv):
            self.held, self.landing, self.send, self.recv = held, landing, send, recv

        def pass_on(self, rank):
            way, k = way_to(me, ranked(me, rank))
            ahead = jnp.where(way == 0, me.z + 1, me.z - 1)
            return remote(
                self.held(rank), self.landing.at[way, k - 1], self.send.at[way, k],
                self.recv.at[way, k - 1], me.at(ahead, me.p),
            )

        def step(self, rank):
            way, k = way_to(me, ranked(me, rank))
            before = jnp.where(way == 0, me.z, LINE - 1 - me.z)
            held = self.held(rank)

            @pl.when(before > 0)
            def _():
                arrival(self.landing.at[way, k], self.recv.at[way, k])
                add_rows(held, (held, self.landing.at[way, k]), held.shape[0])

            self.pass_on(rank).start()

        def total(self, act):
            for way in range(2):

                @pl.when(reach(me, way, 1)[0])
                def _():
                    arrival(self.landing.at[way, 0], self.recv.at[way, 0])
                    act(self.landing.at[way, 0])

        def finish(self):
            for rank in range(LINE - 1):
                self.pass_on(rank).wait_send()

    grads = Line(lambda rank: own.at[rank], from_line, line_send, line_recv)
    outs = Line(lambda rank: out_own.at[ranked(me, rank)], out_line, out_send, out_recv)
    summed.load_all()
    load_out = copy_in(out_ref.at[:, me.t], out_own, load_out_sem.at[0])
    load_out.start()
    load_x1 = copy_in(x1_in, x1_ref, load_out_sem.at[1])
    load_x1.start()
    greet_all(me, count)

    def give_gain(step):
        target = lax.rem(me.d + step, count)
        return remote(
            gain_ref.at[target], gain_in.at[step], gain_send.at[step], gain_recv.at[step], (target, me.t)
        )

    summed.begin(0)
    for step in range(1, count):
        give_gain(step).start()
    pairs = [
        remote(out_ref.at[z, 1 - me.t], out_pair.at[z], pair_send.at[z], pair_recv.at[z], me.sibling())
        for z in range(LINE)
    ]
    for copy in pairs:
        copy.start()
    load_out.wait()
    for z in range(LINE):
        pairs[z].wait_recv()
        add_rows(out_own.at[z], (out_own.at[z], out_pair.at[z]), out_own.shape[1])
    for rank in range(LINE - 1):

        @pl.when(jnp.logical_or(me.z == 0, me.z == LINE - 1))
        def _():
            outs.step(rank)

    at_end = jnp.logical_or(me.z == 0, me.z == LINE - 1)

    def out_start(at):
        x1_ref[at, :] = x1_ref[at, :] + out_own[me.z, at, :].astype(F32)

    def add_out(landed):
        def act(at):
            x1_ref[at, :] = x1_ref[at, :] + landed[at, :].astype(F32)

        row_loop(output.shape[0], 16, act)

    def out_end(at):
        output[at, :] = x1_ref[at, :].astype(BF16)

    for rank in range(LINE):
        summed.middle(rank)
        if rank + 1 < LINE:
            summed.begin(rank + 1)
        else:
            load_x1.wait()
            row_loop(output.shape[0], 16, out_start)
            outs.total(add_out)
            row_loop(output.shape[0], 16, out_end)
            total = gain_ref[me.d]
            for step in range(1, count):
                give_gain(step).wait()
                total += gain_in[step]
            gain_pair[0] = total
            swap = remote(
                gain_pair.at[0], gain_pair.at[1], gain_send.at[0], gain_recv.at[0], me.sibling()
            )
            swap.start()
            swap.wait()
            gain_out[...] = gain_pair[0] + gain_pair[1]
        summed.end(rank)
        if rank < LINE - 1:

            @pl.when(at_end)
            def _():
                grads.step(rank)

        if 0 < rank < LINE - 1:
            @pl.when(jnp.logical_not(at_end))
            def _():
                for late in (range(rank - 1, rank) if rank < LINE - 2 else range(rank - 1, LINE - 1)):
                    outs.step(late)
                    grads.step(late)

    add_rows(a_out, (own.at[LINE - 1],), rows)
    grads.total(lambda landed: add_rows(a_out, (a_out, landed), rows))
    for copy in pairs:
        copy.wait_send()
    outs.finish()
    grads.finish()
    summed.finish()


def grad_sum(count, x1, ga, out_parts, gains):
    _, block, width = ga.shape
    _, _, rows, model = out_parts.shape
    buffers, sems = PlaneSum.scratch(count, block, width)
    return pl.pallas_call(
        functools.partial(grad_sum_kernel, count),
        name="grad_sum",
        out_shape=(
            jax.ShapeDtypeStruct((block, width), F32),
            jax.ShapeDtypeStruct((rows, model), BF16),
            jax.ShapeDtypeStruct(gains.shape[1:], F32),
        ),
        in_specs=[VMEM] + [ANY] * 3,
        out_specs=(VMEM,) * 3,
        scratch_shapes=[
            *buffers,
            pltpu.VMEM((rows, model), F32),
            pltpu.VMEM((2, LINE - 1, block, width), BF16),
            pltpu.VMEM((LINE, rows, model), BF16),
            pltpu.VMEM((LINE, rows, model), BF16),
            pltpu.VMEM((2, LINE - 1, rows, model), BF16),
            pltpu.VMEM(gains.shape, F32),
            pltpu.VMEM((2,) + gains.shape[1:], F32),
            *sems,
            DMA((2, LINE)), DMA((2, LINE)), DMA((2, LINE)), DMA((2, LINE)), DMA((2,)), DMA((LINE,)),
            DMA((LINE,)), DMA((count,)), DMA((count,)),
        ],
        compiler_params=pltpu.CompilerParams(
            collective_id=4, has_side_effects=True, vmem_limit_bytes=60 * MB
        ),
    )(gains, x1, ga, out_parts)


def layouts_kernel(
    a_ref, mlp_ref, output_ref, tokens_ref, q_out, k_out, v_out, o_out, gate_out, up_out, down_out,
    output_out, tokens_out, a_v, mlp_v, output_v, tokens_v, q_v, k_v, v_v, o_v, gate_v, up_v, down_v,
    in_sem, out_sem,
):
    ins = [
        copy_in(src, dst, in_sem.at[i])
        for i, (src, dst) in enumerate(
            ((mlp_ref, mlp_v), (a_ref, a_v), (tokens_ref, tokens_v), (output_ref, output_v))
        )
    ]
    for copy in ins:
        copy.start()
    sent = []

    def give(src, dst):
        sent.append(copy_in(src, dst, out_sem.at[len(sent)]))
        sent[-1].start()

    units = mlp_v.shape[2] // 3
    ins[0].wait()
    for z in range(LINE):
        here = pl.ds(z * units, units)
        gate_v[:, here] = mlp_v[z, :, :units].astype(F32)
        give(gate_v.at[:, here], gate_out.at[:, here])
        up_v[:, here] = mlp_v[z, :, units : 2 * units].astype(F32)
        give(up_v.at[:, here], up_out.at[:, here])
        down_v[here, :] = mlp_v[z, :, 2 * units :].astype(F32).T
        give(down_v.at[here], down_out.at[here])
    for copy in ins[1:]:
        copy.wait()
    give(tokens_v, tokens_out)
    give(output_v, output_out)
    start = 0
    for src, dst in ((q_v, q_out), (k_v, k_out), (v_v, v_out)):
        src[...] = a_v[:, start : start + src.shape[1]]
        start += src.shape[1]
        give(src, dst)
    o_v[...] = a_v[:, start:].T
    give(o_v, o_out)
    for copy in sent:
        copy.wait()


def layouts(q_width, kv_width, a, mlp, output, grad_tokens):
    block = a.shape[0]
    hidden = LINE * (mlp.shape[2] // 3)
    outs = (
        jax.ShapeDtypeStruct((block, q_width), F32),
        jax.ShapeDtypeStruct((block, kv_width), F32),
        jax.ShapeDtypeStruct((block, kv_width), F32),
        jax.ShapeDtypeStruct((q_width, block), F32),
        jax.ShapeDtypeStruct((block, hidden), F32),
        jax.ShapeDtypeStruct((block, hidden), F32),
        jax.ShapeDtypeStruct((hidden, block), F32),
    )
    ins = (a, mlp, output, grad_tokens)
    return pl.pallas_call(
        layouts_kernel,
        name="layouts",
        out_shape=outs + tuple(jax.ShapeDtypeStruct(ref.shape, ref.dtype) for ref in ins[2:]),
        in_specs=[ANY] * 4,
        out_specs=(ANY,) * 9,
        scratch_shapes=[
            *[pltpu.VMEM(ref.shape, ref.dtype) for ref in ins + outs],
            DMA((4,)), DMA((3 * LINE + 6,)),
        ],
        compiler_params=pltpu.CompilerParams(vmem_limit_bytes=60 * MB),
    )(*ins)


def shards(
    tokens, w_query, key_weight, value_weight, w_out, gain_attn, w_gate, w_up, w_down, gain_mlp,
    cotangent, lengths, seq_of_group,
):
    count = lax.axis_size("dp")
    rows, q_width = w_query.shape
    kv_width = key_weight.shape[1]
    model = rows * count
    cos, sin = rope_tables(tokens.shape[0] * lax.axis_size("tensor"), HEAD_SIZE)
    lanes = -rows % 128
    gains = jnp.pad(jnp.stack([gain_attn, gain_mlp]), ((0, 14), (0, lanes)))
    attn_all, gate_all, up_soon, up, down_t, gains_all, tokens_all, dm_all = gather_all(
        count, lengths, seq_of_group,
        (w_query, key_weight, value_weight, w_out, w_gate, w_up, w_down), gains, tokens, cotangent,
    )
    gains_full = gains_all[:, :2, :rows].transpose(1, 0, 2).reshape(2, model).astype(F32)
    x1, h2, h1, qkv, probs, attended, up_rest, down = attention_forward(
        count, q_width // HEAD_SIZE, lengths, seq_of_group, gains_full, cos, sin, tokens_all, attn_all,
        up, down_t,
    )
    grad_h2, out_parts, grad_mlp_w, down_sum, rows_in, inner = feed_forward(
        count, h2, dm_all.reshape(-1, model), gate_all, up_soon, up_rest, down
    )
    grad_attn_w, mlp_sum, grad_tokens, gain_parts = attention_backward(
        count, gains_full, cos, sin, grad_h2, x1, dm_all, tokens_all, h1, qkv, probs, attended, attn_all,
        grad_mlp_w, down_sum, rows_in, inner,
    )
    gain_parts = gain_parts.reshape(2, count, rows).transpose(1, 0, 2)
    gain_parts = jnp.pad(gain_parts, ((0, 0), (0, 6), (0, lanes)))
    attn_sum, output, gain_sum = grad_sum(count, x1, grad_attn_w, out_parts, gain_parts)
    (
        grad_query, grad_key, grad_value, grad_out, grad_gate, grad_up, grad_down, output, grad_tokens,
    ) = layouts(q_width, kv_width, attn_sum, mlp_sum, output, grad_tokens)
    return (
        output, grad_tokens, grad_query, grad_key, grad_value, grad_out, gain_sum[0, :rows],
        grad_gate, grad_up, grad_down, gain_sum[1, :rows],
    )


def solution(mesh):
    both = P(("dp", "tensor"), None)
    row = P("dp", "tensor")
    column = P("tensor", "dp")
    in_specs = (
        both, row, row, row, column, P("dp"), row, row, column, P("dp"), both, P(), P("dp"),
    )
    out_specs = (both, both, row, row, row, column, P("dp"), row, row, column, P("dp"))
    return jax.shard_map(shards, mesh=mesh, in_specs=in_specs, out_specs=out_specs, check_vma=False)
```

```python
import functools
import math

import jax
import jax.numpy as jnp
from jax import lax
from jax.experimental import pallas as pl
from jax.experimental.pallas import tpu as pltpu
from jax.sharding import PartitionSpec as P

HEAD_SIZE = 256
EPS = 1e-06
THETA = 1000042.0
LINE = 4
MESH = pl.DeviceIdType.MESH
BF16 = jnp.bfloat16
F32 = jnp.float32
MB = 1024 * 1024
SOON = 2


def rope_tables(count, head_dim):
    half = head_dim // 2
    index = jnp.arange(half, dtype=jnp.float32)
    freqs = jnp.exp(index * (-2.0 * math.log(THETA) / head_dim))
    angles = jnp.arange(count, dtype=jnp.float32)[:, None] * freqs[None, :]
    return jnp.cos(angles), jnp.sin(angles)


def dot_tn(left, right):
    return lax.dot_general(left, right, (((0,), (0,)), ((), ())), preferred_element_type=F32)


class Place:
    def __init__(self, plane):
        self.d = lax.axis_index("dp")
        self.t = lax.axis_index("tensor")
        self.plane = plane
        self.z = lax.div(self.d, plane)
        self.p = lax.rem(self.d, plane)
        self.h = lax.rem(self.z, 2)
        if plane == 4:
            x = lax.rem(self.p, 2)
            y = lax.div(self.p, 2)
            self.px = 2 * y + 1 - x
            self.py = 2 * (1 - y) + x
            self.pd = 2 * (1 - y) + 1 - x

    def at(self, z, p):
        return (z * self.plane + p, self.t)

    def sibling(self):
        return (self.d, 1 - self.t)

    def mate(self):
        return self.at(self.z + 1 - 2 * self.h, self.p)


def remote(src, dst, send, recv, device):
    return pltpu.make_async_remote_copy(
        src_ref=src, dst_ref=dst, send_sem=send, recv_sem=recv, device_id=device, device_id_type=MESH
    )


def arrival(ref, sem):
    pltpu.make_async_copy(ref, ref, sem).wait()


def greet_all(me, count):
    barrier = pltpu.get_barrier_semaphore()
    for step in range(1, count):
        pl.semaphore_signal(
            barrier, inc=1, device_id=(lax.rem(me.d + step, count), me.t), device_id_type=MESH
        )
    pl.semaphore_signal(barrier, inc=1, device_id=me.sibling(), device_id_type=MESH)
    pl.semaphore_wait(barrier, count)


def greet_line(me):
    barrier = pltpu.get_barrier_semaphore()
    for step in range(1, LINE):
        pl.semaphore_signal(
            barrier, inc=1, device_id=me.at(lax.rem(me.z + step, LINE), me.p), device_id_type=MESH
        )
    pl.semaphore_signal(barrier, inc=1, device_id=me.sibling(), device_id_type=MESH)
    pl.semaphore_wait(barrier, LINE)


def reach(me, way, k):
    return (me.z >= k, me.z - k) if way == 0 else (me.z + k < LINE, me.z + k)


class Chain:
    def __init__(self, me, first, held, send, recv):
        self.me, self.first, self.held, self.send, self.recv = me, first, held, send, recv

    def copy(self, way, k):
        me = self.me
        _, origin = reach(me, way, k)
        target = me.z + 1 if way == 0 else me.z - 1
        src = self.first if k == 0 else self.held(origin)
        return remote(
            src, self.held(origin), self.send.at[way, k], self.recv.at[way, k + 1], me.at(target, me.p)
        )

    def goes(self, way, k):
        have, _ = reach(self.me, way, k)
        ahead, _ = reach(self.me, 1 - way, 1)
        return jnp.logical_and(have, ahead)

    def start(self, way, k):
        if k < LINE - 1:

            @pl.when(self.goes(way, k))
            def _():
                self.copy(way, k).start()

    def wait_block(self, way, k):
        _, origin = reach(self.me, way, k)
        arrival(self.held(origin), self.recv.at[way, k])

    def finish(self):
        for way in range(2):
            for k in range(LINE - 1):

                @pl.when(self.goes(way, k))
                def _():
                    self.copy(way, k).wait_send()


class PlaneGather:
    def __init__(self, me, job, held, rows, send, recv):
        self.me, self.job, self.held, self.send, self.recv = me, job, held, send, recv
        self.half = rows // 2

    def piece(self, z, p, half):
        return self.held.at[z * self.me.plane + p, pl.ds(half * self.half, self.half)]

    def copy(self, z, kind, first=None):
        me = self.me
        if me.plane != 4:
            ref = first if first is not None else self.held.at[z * me.plane + me.p]
            target = lax.rem(me.p + kind + 1, me.plane)
            dst = self.held.at[z * me.plane + me.p]
        else:
            owner = (me.p, me.p, me.p, me.p, me.px, me.py)[kind]
            half = (0, 1, 1, 0, 0, 1)[kind]
            target = (me.px, me.px, me.py, me.py, me.py, me.px)[kind]
            dst = self.piece(z, owner, half)
            ref = dst if first is None else first.at[pl.ds(half * self.half, self.half)]
        return remote(
            ref, dst, self.send.at[self.job, z, kind], self.recv.at[self.job, z, kind], me.at(me.z, target)
        )

    def start(self, z, first=None):
        kinds = (0, 2, 1, 3) if self.me.plane == 4 else range(self.me.plane - 1)
        for kind in kinds:
            self.copy(z, kind, first).start()

    def forward(self, z):
        if self.me.plane == 4:
            self.copy(z, 0).wait_recv()
            self.copy(z, 4).start()
            self.copy(z, 2).wait_recv()
            self.copy(z, 5).start()

    def finish(self, zs=range(LINE)):
        kinds = 6 if self.me.plane == 4 else self.me.plane - 1
        for z in zs:
            for kind in range(kinds):
                copy = self.copy(z, kind)
                if self.me.plane != 4 or kind not in (0, 2):
                    copy.wait_recv()
                copy.wait_send()


class Quad:
    def __init__(self, me, blocks, send, recv):
        self.me, self.blocks, self.send, self.recv = me, blocks, send, recv

    def copy(self, i, first=None):
        me = self.me
        dst = self.blocks.at[me.h if i < 2 else 1 - me.h, me.t]
        device = me.mate() if i == 1 else me.sibling()
        return remote(dst if first is None else first, dst, self.send.at[i], self.recv.at[i], device)

    def start(self, first=None):
        for i in (1, 0):
            self.copy(i, first).start()

    def forward(self):
        arrival(self.blocks.at[1 - self.me.h, self.me.t], self.recv.at[1])
        self.copy(2).start()

    def finish(self):
        me = self.me
        arrival(self.blocks.at[me.h, 1 - me.t], self.recv.at[0])
        arrival(self.blocks.at[1 - me.h, 1 - me.t], self.recv.at[2])

    def finish_sends(self):
        for i in range(3):
            self.copy(i).wait_send()


class QuadSum:
    def __init__(self, me, part, from_pair, low, from_mate, send, recv):
        self.me, self.part, self.from_pair, self.low, self.from_mate = me, part, from_pair, low, from_mate
        self.pair = remote(part.at[:, 1 - me.t], from_pair, send.at[0], recv.at[0], me.sibling())
        self.mate = remote(low, from_mate, send.at[1], recv.at[1], me.mate())

    def start(self):
        self.pair.start()

    def to_mate(self):
        me = self.me
        self.pair.wait_recv()

        def act(at):
            total = self.part[1 - me.h, me.t, at, :] + self.from_pair[1 - me.h, at, :]
            self.low[at, :] = total.astype(BF16)

        row_loop(self.low.shape[0], 32, act)
        self.mate.start()

    def wait(self):
        self.mate.wait_recv()

    def rows(self, at):
        me = self.me
        total = self.part[me.h, me.t, at, :] + self.from_pair[me.h, at, :]
        return total + self.from_mate[at, :].astype(F32)

    def finish_sends(self):
        self.pair.wait_send()
        self.mate.wait_send()


def copy_in(src, dst, sem):
    return pltpu.make_async_copy(src, dst, sem)


def row_loop(rows, step, act):
    @pl.loop(0, rows // step)
    def _(i):
        act(pl.ds(pl.multiple_of(i * step, step), step))


def gather_kernel(
    count, len_ref, seq_ref, gain_ref, q_ref, k_ref, v_ref, o_ref, g_ref, u_ref, d_ref, tok_ref, cot_ref,
    a_all, gate_all, up_soon, up, down_t, gain_all, tok_all, dm_all, o_v, a_v, g_v, u_v, d_v, d_t, dm,
    gain_v, chain_send, chain_recv, part_send, part_recv, plane_send, plane_recv, gain_send, gain_recv,
    pair_send, pair_recv, tok_send, tok_recv, local_sem,
):
    plane = count // LINE
    me = Place(plane)
    rows = q_ref.shape[0]
    units = g_ref.shape[1] // LINE
    q_half, kv_half = q_ref.shape[1] // 2, k_ref.shape[1] // 2
    qkv_half = q_half + 2 * kv_half

    def columns(ref, z):
        return ref.at[:, pl.ds(pl.multiple_of(z * units, units), units)]

    local = [copy_in(o_ref, o_v, local_sem.at[0])]
    for h in range(2):
        start = 0
        for ref, width in ((q_ref, q_half), (k_ref, kv_half), (v_ref, kv_half)):
            src = ref.at[:, pl.ds(h * width, width)]
            local.append(copy_in(src, a_v.at[h, :, pl.ds(start, width)], local_sem.at[len(local)]))
            start += width
    early = len(local)
    for src, dst in (
        (d_ref, d_v), (cot_ref, dm), (columns(g_ref, me.z), g_v), (columns(u_ref, me.z), u_v),
        (tok_ref, tok_all.at[me.h, me.t]),
    ):
        local.append(copy_in(src, dst, local_sem.at[len(local)]))
    for copy in local[:early]:
        copy.start()
    keep_a = copy_in(a_v.at[me.h], a_all.at[me.d], local_sem.at[12])
    keep_down = copy_in(d_t, down_t, local_sem.at[13])
    keep_dm = copy_in(dm, dm_all.at[me.z, me.t], local_sem.at[14])
    keep_gate = copy_in(g_v, gate_all.at[me.d], local_sem.at[15])
    keep_up = copy_in(u_v, up.at[me.z], local_sem.at[16])
    keep_gain = copy_in(gain_v, gain_all.at[me.d], local_sem.at[17])

    dms = Chain(me, dm, lambda z: dm_all.at[z, me.t], chain_send, chain_recv)
    planes = (
        PlaneGather(me, 0, a_all, rows, plane_send, plane_recv),
        PlaneGather(me, 1, gate_all, rows, plane_send, plane_recv),
        PlaneGather(me, 2, up_soon, rows, plane_send, plane_recv),
    )

    def part(way, k, kind):
        _, target = reach(me, 1 - way, k)
        src = columns((g_ref, u_ref)[kind - 1], target) if kind else a_v.at[lax.rem(target, 2)]
        dst = (a_all.at[me.d], gate_all.at[me.d], up.at[me.z])[kind]
        return remote(
            src, dst, part_send.at[way, k, kind], part_recv.at[way, k, kind], me.at(target, me.p)
        )

    def pair(z, first=None):
        src = dm_all.at[z, me.t] if first is None else first
        return remote(src, dm_all.at[z, me.t], pair_send.at[z], pair_recv.at[z], me.sibling())

    def keep_soon(soon, src):
        return copy_in(src, up_soon.at[soon * plane + me.p], local_sem.at[18 + soon])

    def start_parts(k, kinds):
        for way in range(2):

            @pl.when(reach(me, 1 - way, k)[0])
            def _():
                for kind in kinds:
                    part(way, k, kind).start()

    def each(k, act):
        for way in range(2):
            have, z = reach(me, way, k)

            @pl.when(have)
            def _():
                act(way, k, z)

    def attn_step(way, k, z):
        arrival(a_all.at[z * plane + me.p], part_recv.at[way, k, 0])
        planes[0].start(z)

    def part_step(way, k, z):
        arrival(gate_all.at[z * plane + me.p], part_recv.at[way, k, 1])
        planes[1].start(z)
        arrival(up.at[z], part_recv.at[way, k, 2])
        for soon in range(SOON):

            @pl.when(z == soon)
            def _():
                planes[2].start(soon, up.at[soon])
                keep_soon(soon, up.at[soon]).start()

    def dm_step(way, k, z):
        dms.wait_block(way, k)
        dms.start(way, k)
        pair(z).start()

    def give_gain(step):
        target = lax.rem(me.d + step, count)
        return remote(
            gain_v, gain_all.at[me.d], gain_send.at[step], gain_recv.at[step], (target, me.t)
        )

    chosen = len_ref[seq_ref[0]]
    kind_of = lax.broadcasted_iota(jnp.int32, gain_ref.shape, 0)
    gain_v[...] = jnp.where(kind_of == 2, chosen.astype(F32), gain_ref[...].astype(F32)).astype(BF16)
    local[0].wait()
    for h in range(2):
        a_v[h, :, qkv_half:] = o_v[h * q_half : (h + 1) * q_half, :].T
    greet_all(me, count)
    for copy in local[1:early]:
        copy.wait()
    toks = Quad(me, tok_all, tok_send, tok_recv)
    for k in range(1, LINE):
        start_parts(k, (0,))
    planes[0].start(me.z, a_v.at[me.h])
    toks.start(tok_ref)
    for step in range(1, count):
        give_gain(step).start()
    for copy in local[early:]:
        copy.start()
    keep_a.start()
    keep_gain.start()

    local[early].wait()
    for z in range(LINE):
        d_t[z] = d_v[z * units : (z + 1) * units, :].T
    keep_down.start()
    local[early + 1].wait()

    def mask(at):
        value = dm[at, :].astype(F32)
        row = lax.broadcasted_iota(jnp.int32, value.shape, 0) + (me.t * dm.shape[0] + at.start)
        dm[at, :] = jnp.where(row < chosen, value, 0.0).astype(BF16)

    row_loop(dm.shape[0], 32, mask)
    keep_dm.start()

    for k in range(1, LINE):
        each(k, attn_step)
        start_parts(k, (1,))
        if k == 1:
            toks.forward()
            planes[0].forward(me.z)
            for copy in local[early + 2 : early + 4]:
                copy.wait()
            keep_gate.start()
            keep_up.start()
            planes[1].start(me.z, g_v)
            for soon in range(SOON):

                @pl.when(me.z == soon)
                def _():
                    planes[2].start(soon, u_v)
                    keep_soon(soon, u_v).start()

        else:
            each(k - 1, lambda way, k, z: planes[0].forward(z))
    for k in range(1, LINE):
        start_parts(k, (2,))
    for way in range(2):
        dms.start(way, 0)
    pair(me.z, dm).start()
    for k in range(1, LINE):
        each(k, part_step)
        if k == 1:
            each(LINE - 1, lambda way, k, z: planes[0].forward(z))
            planes[1].forward(me.z)
        else:
            each(k - 1, lambda way, k, z: planes[1].forward(z))
            each(k - 1, dm_step)
    each(LINE - 1, lambda way, k, z: planes[1].forward(z))
    for soon in range(SOON):
        planes[2].forward(soon)
    each(LINE - 1, dm_step)

    dms.finish()
    for k in range(1, LINE):
        for way in range(2):

            @pl.when(reach(me, 1 - way, k)[0])
            def _():
                for kind in range(3):
                    part(way, k, kind).wait_send()

    for step in range(1, count):
        give_gain(step).wait()
    toks.finish()
    toks.finish_sends()
    for z in range(LINE):
        pair(z).wait()
    for job, zs in zip(planes, (LINE, LINE, SOON)):
        job.finish(range(zs))
    for soon in range(SOON):
        keep_soon(soon, u_v).wait()
    for copy in local[early + 4 :] + [keep_a, keep_down, keep_dm, keep_gate, keep_up, keep_gain]:
        copy.wait()


ANY = pl.BlockSpec(memory_space=pl.ANY)
VMEM = pl.BlockSpec(memory_space=pltpu.VMEM)
SMEM = pl.BlockSpec(memory_space=pltpu.SMEM)
DMA = pltpu.SemaphoreType.DMA


def gather_all(count, lengths, seq, gains, weights, tokens, cotangent):
    w_query, key_weight, _, w_out, w_gate, _, w_down = weights
    rows, q_width = w_query.shape
    width = q_width + key_weight.shape[1]
    units = w_gate.shape[1] // LINE
    plane = count // LINE
    kinds = max(6, plane - 1)
    return pl.pallas_call(
        functools.partial(gather_kernel, count),
        name="gather_all",
        out_shape=(
            jax.ShapeDtypeStruct((count, rows, width), BF16),
            jax.ShapeDtypeStruct((count, rows, units), BF16),
            jax.ShapeDtypeStruct((plane * SOON, rows, units), BF16),
            jax.ShapeDtypeStruct((LINE, rows, units), BF16),
            jax.ShapeDtypeStruct((LINE, rows, units), BF16),
            jax.ShapeDtypeStruct((count,) + gains.shape, gains.dtype),
            jax.ShapeDtypeStruct((2, 2) + tokens.shape, BF16),
            jax.ShapeDtypeStruct((LINE, 2) + cotangent.shape, BF16),
        ),
        in_specs=[SMEM] * 2 + [VMEM] + [ANY] * 9,
        out_specs=(ANY,) * 8,
        scratch_shapes=[
            pltpu.VMEM(w_out.shape, BF16),
            pltpu.VMEM((2, rows, width), BF16),
            pltpu.VMEM((rows, units), BF16),
            pltpu.VMEM((rows, units), BF16),
            pltpu.VMEM(w_down.shape, BF16),
            pltpu.VMEM((LINE, rows, units), BF16),
            pltpu.VMEM(cotangent.shape, BF16),
            pltpu.VMEM(gains.shape, BF16),
            DMA((2, LINE)), DMA((2, LINE)), DMA((2, LINE, 3)), DMA((2, LINE, 3)),
            DMA((3, LINE, kinds)), DMA((3, LINE, kinds)), DMA((count,)), DMA((count,)),
            DMA((LINE,)), DMA((LINE,)), DMA((3,)), DMA((3,)), DMA((18 + SOON,)),
        ],
        compiler_params=pltpu.CompilerParams(
            collective_id=0, has_side_effects=True, vmem_limit_bytes=60 * MB
        ),
    )(lengths, seq, gains, *weights, tokens, cotangent)


RANKS = ((3, 2, 1, 0), (3, 0, 2, 1), (0, 3, 1, 2), (0, 1, 2, 3))
FAR_FIRST = [(way, k) for k in range(LINE - 1, 0, -1) for way in range(2)]


def ranked(me, rank):
    z = jnp.int32(RANKS[0][rank])
    for at in range(1, LINE):
        z = jnp.where(me.z == at, RANKS[at][rank], z)
    return z


def way_to(me, z):
    down = (z < me.z).astype(jnp.int32)
    return down, jnp.where(z < me.z, me.z - z, z - me.z)


def add_rows(target, terms, rows, start=0):
    step = 16

    @pl.loop(0, rows // step)
    def _(i):
        at = pl.ds(pl.multiple_of(start + i * step, step), step)
        total = terms[0][at].astype(F32)
        for term in terms[1:]:
            total += term[at].astype(F32)
        target[at] = total.astype(target.dtype)


def grad_rows(at, per, left_ref, right_ref, first, targets, there):
    tile = 512
    tokens = left_ref.shape[0]

    @pl.loop(0, per // tile)
    def _(n):
        left = left_ref[:, pl.ds(pl.multiple_of(at + n * tile, tile), tile)].T
        for job, ref, start in targets:
            block, units = ref.shape[1], right_ref.shape[1]
            rows = pl.ds(there + n * (tile // block), tile // block)
            for c in range(units // tile):
                grad = jnp.dot(
                    left, right_ref[pl.ds(first + job * tokens, tokens), c * tile : (c + 1) * tile],
                    preferred_element_type=F32,
                )
                ref[rows, :, start + c * tile : start + (c + 1) * tile] = grad.astype(BF16).reshape(
                    tile // block, block, tile
                )


class PlaneSum:
    def __init__(self, me, grad, own, other, first, second, sems, ranks=range(LINE)):
        self.me, self.grad, self.own, self.other, self.first, self.second = me, grad, own, other, first, second
        (
            self.first_send, self.first_recv, self.second_send, self.second_recv, self.load_sem, self.other_sem,
        ) = sems
        self.ranks = ranks
        self.rows = own.shape[1]
        half = self.rows // 2
        self.half = half
        self.halves = (pl.ds(0, half), pl.ds(half, half))
        self.square = me.plane == 4
        if self.square:
            self.near = (me.px, me.py)
            self.far = (me.py, me.px)

    def slot(self, rank):
        return rank - self.ranks[0]

    def block(self, rank, p):
        if callable(self.grad):
            return self.grad(rank, p)
        return self.grad.at[ranked(self.me, rank) * self.me.plane + p]

    def load(self, rank):
        s = self.slot(rank)
        return pltpu.make_async_copy(self.block(rank, self.me.p), self.own.at[s], self.load_sem.at[s])

    def load_other(self, rank, i):
        s = self.slot(rank)
        return pltpu.make_async_copy(
            self.block(rank, self.far[i]).at[self.halves[i]], self.other.at[s, self.halves[i]],
            self.other_sem.at[s, i],
        )

    def load_rank(self, rank):
        self.load(rank).start()
        if self.square:
            for i in range(2):
                self.load_other(rank, i).start()

    def load_all(self):
        for rank in self.ranks:
            self.load_rank(rank)

    def give(self, rank, i, which):
        me, s = self.me, self.slot(rank)
        if not self.square:
            target = lax.rem(me.p + which + 1, me.plane)
            return remote(
                self.block(rank, target), self.first.at[s, which], self.first_send.at[s, which],
                self.first_recv.at[s, which], me.at(me.z, target),
            )
        owner = (self.near[i], me.pd)[which]
        return remote(
            self.block(rank, owner).at[self.halves[i]], self.first.at[s, which, self.halves[i]],
            self.first_send.at[s, 2 * i + which], self.first_recv.at[s, 2 * i + which],
            me.at(me.z, self.near[i]),
        )

    def give_both(self, rank, i):
        s = self.slot(rank)
        return remote(
            self.other.at[s, self.halves[i]], self.second.at[s, self.halves[i]],
            self.second_send.at[s, i], self.second_recv.at[s, i], self.me.at(self.me.z, self.far[i]),
        )

    def gives(self, rank):
        if self.square:
            return [self.give(rank, i, which) for which in (1, 0) for i in range(2)]
        return [self.give(rank, 0, which) for which in range(self.me.plane - 1)]

    def begin(self, rank):
        for copy in self.gives(rank):
            copy.start()

    def middle(self, rank):
        if not self.square:
            return
        s = self.slot(rank)
        for i in range(2):
            arrival(self.first.at[s, 1, self.halves[i]], self.first_recv.at[s, 2 * i + 1])
            self.load_other(rank, i).wait()
            add_rows(
                self.other.at[s], (self.other.at[s], self.first.at[s, 1]), self.half, i * self.half
            )
            self.give_both(rank, i).start()

    def end(self, rank):
        s = self.slot(rank)
        self.load(rank).wait()
        if self.square:
            for i in range(2):
                arrival(self.first.at[s, 0, self.halves[i]], self.first_recv.at[s, 2 * i])
                arrival(self.second.at[s, self.halves[i]], self.second_recv.at[s, i])
            terms = (self.first.at[s, 0], self.second.at[s])
        else:
            for which in range(self.me.plane - 1):
                arrival(self.first.at[s, which], self.first_recv.at[s, which])
            terms = tuple(self.first.at[s, which] for which in range(self.me.plane - 1))
        add_rows(self.own.at[s], (self.own.at[s],) + terms, self.rows)

    def finish(self):
        for rank in self.ranks:
            for copy in self.gives(rank):
                copy.wait_send()
            if self.square:
                for i in range(2):
                    self.give_both(rank, i).wait_send()

    @staticmethod
    def scratch(count, rows, width, ranks=LINE):
        plane = count // LINE
        square = plane == 4
        slots = 2 if square else plane - 1
        small = (ranks, rows, width) if square else (1, 16, 128)
        return [
            pltpu.VMEM((ranks, rows, width), BF16),
            pltpu.VMEM(small, BF16),
            pltpu.VMEM((ranks, slots, rows, width), BF16),
            pltpu.VMEM(small, BF16),
        ], [
            DMA((ranks, max(4, slots))), DMA((ranks, max(4, slots))), DMA((ranks, 2)), DMA((ranks, 2)),
            DMA((ranks,)), DMA((ranks, 2)),
        ]


def dot_cols(left, right):
    return lax.dot_general(left, right, (((1,), (1,)), ((), ())), preferred_element_type=F32)


def feed_forward_kernel(
    plane, h_ref, dm_ref, gate_ref, up_soon, up_rest, down, total_ref, out_ref, grad_ref, sum_ref,
    h_out, inner_out, rows_in, weights, inner, down_grad, part,
    from_pair, from_line, own, other, first, second, first_send, first_recv, second_send, second_recv,
    own_sem, other_sem, chain_send, chain_recv, pass_send, pass_recv, pair_send, pair_recv,
    line_send, line_recv, plane_send, plane_recv, load_sem, dm_sem, grad_sem, out_sem, sum_sem,
):
    me = Place(plane)
    rows, model = h_ref.shape
    units = inner.shape[1]
    wide = 2 * rows
    tokens = LINE * wide
    block = down.shape[1]
    soon = up_soon.shape[0]
    tile = 512

    def slot(z, t):
        return rows_in.at[pl.ds(pl.multiple_of((z * 2 + t) * rows, rows), rows)]

    loads = [
        copy_in(gate_ref, weights.at[:, :, pl.ds(0, units)], load_sem.at[0]),
        copy_in(up_soon, weights.at[pl.ds(0, soon), :, pl.ds(units, units)], load_sem.at[2]),
        copy_in(
            up_rest, weights.at[pl.ds(soon, up_rest.shape[0]), :, pl.ds(units, units)], load_sem.at[3]
        ),
    ]
    own_down = [
        copy_in(
            down.at[z], weights.at[z * plane + me.p, :, pl.ds(2 * units, units)], load_sem.at[4 + z]
        )
        for z in range(LINE)
    ]
    for load in loads:
        load.start()
    load_dm = pltpu.make_async_copy(dm_ref, rows_in.at[pl.ds(tokens, tokens)], dm_sem)
    load_dm.start()
    keep = pltpu.make_async_copy(h_ref, slot(me.z, me.t), load_sem.at[1])
    keep.start()
    greet_all(me, plane * LINE)
    gather = PlaneGather(
        me, 0, weights.at[:, :, pl.ds(2 * units, units)], block, plane_send, plane_recv
    )
    summed = PlaneSum(
        me, down_grad, own, other, first, second,
        (first_send, first_recv, second_send, second_recv, own_sem, other_sem),
    )
    chain = Chain(me, h_ref, lambda z: slot(z, me.t), chain_send, chain_recv)

    def share(z, first=None):
        src = slot(z, me.t) if first is None else first
        return remote(src, slot(z, me.t), pass_send.at[z], pass_recv.at[z], me.sibling())

    for way in range(2):
        chain.start(way, 0)
    share(me.z, h_ref).start()
    for z in range(2):
        gather.start(z, down.at[z])
    for copy in own_down:
        copy.start()

    def w_rows(n, width, column):
        return weights[pl.ds(n * (width // block), width // block), :, pl.ds(column, units)].reshape(
            width, units
        )

    def pair_rows(z, job=0):
        return pl.ds(pl.multiple_of(job * tokens + z * wide, wide), wide)

    def columns(c, job):
        return weights[:, :, pl.ds(pl.multiple_of(job * units + c * tile, tile), tile)].reshape(model, tile)

    def project(z):
        @pl.loop(0, units // tile)
        def _(c):
            here = pl.ds(pl.multiple_of(c * tile, tile), tile)
            h = rows_in[pair_rows(z), :]
            gate = jnp.dot(h, columns(c, 0), preferred_element_type=F32)
            up = jnp.dot(h, columns(c, 1), preferred_element_type=F32)
            sigmoid = jax.nn.sigmoid(gate)
            silu = gate * sigmoid
            inner[pair_rows(z), here] = (silu * up).astype(BF16)
            inner[pair_rows(z, 1), here] = (up * sigmoid * (1.0 + gate * (1.0 - sigmoid))).astype(BF16)
            inner[pair_rows(z, 2), here] = silu.astype(BF16)

    def back(z):
        @pl.loop(0, units // tile)
        def _(c):
            here = pl.ds(pl.multiple_of(c * tile, tile), tile)
            grad_hidden = jnp.dot(rows_in[pair_rows(z, 1), :], columns(c, 2), preferred_element_type=F32)
            for job in range(1, 3):
                at = pair_rows(z, job)
                inner[at, here] = (grad_hidden * inner[at, here].astype(F32)).astype(BF16)

        @pl.loop(0, model // tile)
        def _(n):
            here = pl.ds(pl.multiple_of(n * tile, tile), tile)
            grad = dot_cols(inner[pair_rows(z, 1)], w_rows(n, tile, 0))
            grad += dot_cols(inner[pair_rows(z, 2)], w_rows(n, tile, units))
            part[0, z, :, :, here] = grad.astype(BF16).reshape(2, rows, tile)

        pair(z).start()

    def out(z):
        @pl.loop(0, model // tile)
        def _(n):
            here = pl.ds(pl.multiple_of(n * tile, tile), tile)
            value = dot_cols(inner[pair_rows(z), :], w_rows(n, tile, 2 * units))
            part[1, z, :, :, here] = value.astype(BF16).reshape(2, rows, tile)

        keep_out(z).start()

    def pair(z):
        return remote(
            part.at[0, z, 1 - me.t], from_pair.at[z], pair_send.at[z], pair_recv.at[z], me.sibling()
        )

    half = rows // 2
    halves = (pl.ds(0, half), pl.ds(half, half))

    def pass_on(way, k, i):
        _, target = reach(me, 1 - way, k)
        ahead = me.z + 1 if way == 0 else me.z - 1
        return remote(
            part.at[0, target, me.t, halves[i]], from_line.at[way, k - 1, halves[i]],
            line_send.at[way, k, i], line_recv.at[way, k - 1, i], me.at(ahead, me.p),
        )

    def line(way, k, behind):
        have, z = reach(me, 1 - way, k)
        before = me.z if way == 0 else LINE - 1 - me.z

        @pl.when(jnp.logical_and(have, before == behind))
        def _():
            pair(z).wait_recv()
            terms = (part.at[0, z, me.t], from_pair.at[z])
            if behind:
                terms += (from_line.at[way, k],)
            for i in range(2):
                if behind:
                    arrival(from_line.at[way, k, halves[i]], line_recv.at[way, k, i])
                add_rows(part.at[0, z, me.t], terms, half, i * half)
                pass_on(way, k, i).start()

    def total():
        pair(me.z).wait_recv()
        add_rows(total_ref, (part.at[0, me.z, me.t], from_pair.at[me.z]), rows)
        for way in range(2):

            @pl.when(reach(me, way, 1)[0])
            def _():
                for i in range(2):
                    arrival(from_line.at[way, 0, halves[i]], line_recv.at[way, 0, i])
                    add_rows(total_ref, (total_ref, from_line.at[way, 0]), half, i * half)

    per = plane * block

    def down_grads(rank):
        z = ranked(me, rank)
        grad_rows(
            z * per, per, rows_in.at[pl.ds(tokens, tokens)], inner, 0, [(0, down_grad, 0)], z * plane
        )
        summed.load_rank(rank)

    keeps = [
        copy_in(weights.at[pl.ds(0, plane), :, pl.ds(0, 2 * units)], grad_ref, grad_sem.at[0]),
        copy_in(rows_in.at[pl.ds(0, tokens)], h_out, grad_sem.at[1]),
        copy_in(inner.at[pl.ds(tokens, 2 * tokens)], inner_out, grad_sem.at[2]),
    ]

    def grads():
        targets = [(0, weights, 0), (1, weights, units)]
        z = ranked(me, 0)
        grad_rows(z * per, per, rows_in.at[pl.ds(0, tokens)], inner, tokens, targets, 0)

    def keep_sum(rank):
        return copy_in(own.at[rank], sum_ref.at[rank], sum_sem.at[rank])

    keep.wait()
    for load in loads:
        load.wait()
    for k in range(LINE):
        for way in range(2 if k else 1):
            have, z = reach(me, way, k)

            @pl.when(have)
            def _():
                if k:
                    chain.wait_block(way, k)
                    chain.start(way, k)
                    share(z).start()
                arrival(slot(z, 1 - me.t), pass_recv.at[z])
                project(z)

        gather.forward(k)
        if k + 2 < LINE:
            gather.start(k + 2, down.at[k + 2])
    def keep_out(z):
        return copy_in(part.at[1, z], out_ref.at[z], out_sem.at[z])

    load_dm.wait()
    keeps[1].start()
    down_grads(0)
    summed.begin(0)
    for copy in own_down:
        copy.wait()
    gather.finish()
    passing = {1: (1, 2), 2: (2, 1), 3: (1, 1)}
    for rank in range(LINE):
        if rank:
            down_grads(rank)
            if rank - 1 in passing:
                for way in range(2):
                    line(way, passing[rank - 1][1], passing[rank - 1][0])
            summed.middle(rank - 1)
            summed.begin(rank)
            if rank > 1:
                summed.end(rank - 2)
                keep_sum(rank - 2).start()
        back(ranked(me, rank))
        if rank < LINE - 1:
            out(ranked(me, rank))
            for way in range(2):
                line(way, LINE - 1 - rank, 0)
    for way in range(2):
        line(way, passing[LINE - 1][1], passing[LINE - 1][0])
    keeps[2].start()
    summed.middle(LINE - 1)
    summed.end(LINE - 2)
    keep_sum(LINE - 2).start()
    grads()
    keeps[0].start()
    out(ranked(me, LINE - 1))
    summed.end(LINE - 1)
    keep_sum(LINE - 1).start()
    total()
    summed.finish()
    chain.finish()
    for z in range(LINE):
        share(z).wait_send()
        keep_out(z).wait()
        keep_sum(z).wait()
        pair(z).wait_send()
    for copy in keeps:
        copy.wait()
    for k in range(1, LINE):
        for way in range(2):

            @pl.when(reach(me, 1 - way, k)[0])
            def _():
                for i in range(2):
                    pass_on(way, k, i).wait_send()


def feed_forward(count, h, dm_all, gate_all, up_soon, up_rest, down):
    rows, model = h.shape
    _, block, units = down.shape
    kinds = max(6, count // LINE - 1)
    buffers, sems = PlaneSum.scratch(count, block, units)
    tokens = LINE * 2 * rows
    vmem = pl.BlockSpec(memory_space=pltpu.VMEM)
    return pl.pallas_call(
        functools.partial(feed_forward_kernel, count // LINE),
        name="feed_forward",
        out_shape=(
            jax.ShapeDtypeStruct((rows, model), F32),
            jax.ShapeDtypeStruct((LINE, 2, rows, model), BF16),
            jax.ShapeDtypeStruct((count // LINE, block, 2 * units), BF16),
            jax.ShapeDtypeStruct((LINE, block, units), BF16),
            jax.ShapeDtypeStruct((tokens, model), BF16),
            jax.ShapeDtypeStruct((2 * tokens, units), BF16),
        ),
        in_specs=[ANY] * 6,
        out_specs=(vmem,) + (ANY,) * 5,
        scratch_shapes=[
            pltpu.VMEM((2 * tokens, model), BF16),
            pltpu.VMEM((count, block, 3 * units), BF16),
            pltpu.VMEM((3 * tokens, units), BF16),
            pltpu.VMEM((count, block, units), BF16),
            pltpu.VMEM((2, LINE, 2, rows, model), BF16),
            pltpu.VMEM((LINE, rows, model), BF16),
            pltpu.VMEM((2, LINE - 1, rows, model), BF16),
            *buffers,
            *sems,
            DMA((2, LINE)), DMA((2, LINE)), DMA((LINE,)), DMA((LINE,)), DMA((LINE,)), DMA((LINE,)),
            DMA((2, LINE, 2)), DMA((2, LINE, 2)), DMA((1, LINE, kinds)), DMA((1, LINE, kinds)),
            DMA((4 + LINE,)), DMA, DMA((LINE,)), DMA((LINE,)), DMA((LINE,)),
        ],
        compiler_params=pltpu.CompilerParams(
            collective_id=1, has_side_effects=True, vmem_limit_bytes=60 * MB
        ),
    )(h, dm_all, gate_all, up_soon, up_rest, down)


def greet_plane(me):
    barrier = pltpu.get_barrier_semaphore()
    for step in range(1, me.plane):
        target = lax.rem(me.p + step, me.plane)
        pl.semaphore_signal(barrier, inc=1, device_id=me.at(me.z, target), device_id_type=MESH)
    pl.semaphore_signal(barrier, inc=1, device_id=me.sibling(), device_id_type=MESH)
    pl.semaphore_wait(barrier, me.plane)


def columns_of(weights, start, width):
    count, rows, _ = weights.shape
    return weights[:, :, pl.ds(start, width)].reshape(count * rows, width)


def rows_of(weights, n, height, start, width):
    _, rows, _ = weights.shape
    per = height // rows
    return weights[pl.ds(n * per, per), :, pl.ds(start, width)].reshape(height, width)


def attention_forward_kernel(
    plane, gain_ref, lens_ref, cos_ref, sin_ref, tok_in, a_ref, up, down_t, x1_out, h2_out, h1_out,
    qkv_out, probs_out, o_out, up_rest, down, weights, tok_ref, x1_ref, h2_ref, h1_ref, qkv_ref, probs_ref,
    o_ref, part, from_pair, low, from_mate, plane_send, plane_recv, part_send, part_recv, sum_send,
    sum_recv, load_sem, keep_sem,
):
    me = Place(plane)
    _, _, rows, model = tok_ref.shape
    wide = 2 * rows
    q_width = o_ref.shape[1]
    heads = q_width // HEAD_SIZE
    kv_width = (qkv_ref.shape[1] - q_width) // 2
    kv_heads = kv_width // HEAD_SIZE
    half = HEAD_SIZE // 2
    load_tok = copy_in(tok_in, tok_ref, load_sem.at[0])
    load_tok.start()
    load = copy_in(a_ref, weights, load_sem.at[1])
    load.start()
    keep = [
        copy_in(up.at[z], up_rest.at[(z - SOON) * plane + me.p], load_sem.at[2 + z])
        for z in range(SOON, LINE)
    ]
    keep.append(copy_in(down_t.at[me.z], down.at[me.z], load_sem.at[2 + LINE]))
    for copy in keep:
        copy.start()
    outs = [
        copy_in(src, dst, keep_sem.at[i])
        for i, (src, dst) in enumerate(
            (
                (h1_ref, h1_out), (qkv_ref, qkv_out), (probs_ref, probs_out), (o_ref, o_out),
                (x1_ref, x1_out), (h2_ref, h2_out),
            )
        )
    ]
    greet_all(me, plane * LINE)
    gather = PlaneGather(me, 0, up_rest, up.shape[1], plane_send, plane_recv)
    for z in range(LINE - SOON):
        gather.start(z, up.at[z + SOON])

    def give_down(way, k):
        _, target = reach(me, 1 - way, k)
        return remote(
            down_t.at[target], down.at[me.z], part_send.at[way, k], part_recv.at[way, k],
            me.at(target, me.p),
        )

    for k in range(1, LINE):
        for way in range(2):

            @pl.when(reach(me, 1 - way, k)[0])
            def _():
                give_down(way, k).start()

    load_tok.wait()

    for n in range(4):

        def norm(at, n=n):
            x = tok_ref[n // 2, n % 2, at, :].astype(F32)
            factor = lax.rsqrt(jnp.mean(x * x, -1, keepdims=True) + EPS)
            h1_ref[pl.ds(n * rows + at.start, at.size), :] = (x * factor * gain_ref[0:1, :]).astype(BF16)

        row_loop(rows, 32, norm)
    outs[0].start()
    load.wait()

    def project(i):
        start = pl.multiple_of(i * HEAD_SIZE, HEAD_SIZE)
        return start, jnp.dot(
            h1_ref[...], columns_of(weights, start, HEAD_SIZE), preferred_element_type=F32
        )

    @pl.loop(0, heads + kv_heads)
    def _(i):
        start, values = project(i)
        cos, sin = cos_ref[...], sin_ref[...]
        for n in range(2):
            at = slice(n * wide, (n + 1) * wide)
            first, second = values[at, :half], values[at, half:]
            qkv_ref[at, pl.ds(start, half)] = (first * cos - second * sin).astype(BF16)
            qkv_ref[at, pl.ds(start + half, half)] = (second * cos + first * sin).astype(BF16)

    @pl.loop(heads + kv_heads, heads + 2 * kv_heads)
    def _(i):
        start, values = project(i)
        qkv_ref[:, pl.ds(start, HEAD_SIZE)] = values.astype(BF16)

    outs[1].start()
    gather.forward(0)
    row = lax.broadcasted_iota(jnp.int32, (wide, wide), 0)
    key = lax.broadcasted_iota(jnp.int32, (wide, wide), 1)
    for n in range(2):
        length = lens_ref[me.d - me.h * plane + n * plane, 2:3, 0:1].astype(F32)
        allowed = jnp.logical_and(key <= row, key.astype(F32) < length)
        at = slice(n * wide, (n + 1) * wide)
        for i in range(heads):
            m = i * kv_heads // heads
            q = qkv_ref[at, i * HEAD_SIZE : (i + 1) * HEAD_SIZE]
            k = qkv_ref[at, q_width + m * HEAD_SIZE : q_width + (m + 1) * HEAD_SIZE]
            v_start = q_width + kv_width + m * HEAD_SIZE
            v = qkv_ref[at, v_start : v_start + HEAD_SIZE]
            scores = dot_cols(q, k) * HEAD_SIZE ** (-0.5)
            scores = jnp.where(allowed, scores, -1e30)
            grown = jnp.exp(scores - jnp.max(scores, -1, keepdims=True))
            probs = grown / jnp.sum(grown, -1, keepdims=True)
            probs_ref[n * heads + i] = probs
            o_ref[at, i * HEAD_SIZE : (i + 1) * HEAD_SIZE] = jnp.dot(
                probs.astype(BF16), v, preferred_element_type=F32
            ).astype(BF16)

    outs[2].start()
    outs[3].start()
    tile = 512

    @pl.loop(0, model // tile)
    def _(n):
        here = pl.ds(pl.multiple_of(n * tile, tile), tile)
        value = dot_cols(o_ref[...], rows_of(weights, n, tile, q_width + 2 * kv_width, q_width))
        part[:, :, :, here] = value.reshape(2, 2, rows, tile)

    total = QuadSum(me, part, from_pair, low, from_mate, sum_send, sum_recv)
    total.start()
    for z in range(1, LINE - SOON):
        gather.forward(z)
    total.to_mate()
    total.wait()

    def add(at):
        x1 = tok_ref[me.h, me.t, at, :].astype(F32) + total.rows(at)
        x1_ref[at, :] = x1
        factor = lax.rsqrt(jnp.mean(x1 * x1, -1, keepdims=True) + EPS)
        h2_ref[at, :] = (x1 * factor * gain_ref[1:2, :]).astype(BF16)

    row_loop(rows, 32, add)
    outs[4].start()
    outs[5].start()
    total.finish_sends()
    gather.finish(range(LINE - SOON))
    for k in range(1, LINE):
        for way in range(2):

            @pl.when(reach(me, 1 - way, k)[0])
            def _():
                give_down(way, k).wait_send()

            @pl.when(reach(me, way, k)[0])
            def _():
                arrival(down.at[me.z], part_recv.at[way, k])

    for copy in keep + outs:
        copy.wait()


def attention_forward(count, q_width, kv_width, gains, lens, cos, sin, tokens_all, attn_all, up, down_t):
    _, _, rows, model = tokens_all.shape
    wide = 2 * rows
    plane = count // LINE
    kinds = max(6, plane - 1)
    outs = (
        jax.ShapeDtypeStruct((rows, model), F32),
        jax.ShapeDtypeStruct((rows, model), BF16),
        jax.ShapeDtypeStruct((2 * wide, model), BF16),
        jax.ShapeDtypeStruct((2 * wide, q_width + 2 * kv_width), BF16),
        jax.ShapeDtypeStruct((2 * q_width // HEAD_SIZE, wide, wide), F32),
        jax.ShapeDtypeStruct((2 * wide, q_width), BF16),
    )
    return pl.pallas_call(
        functools.partial(attention_forward_kernel, plane),
        name="attention_forward",
        out_shape=outs
        + (
            jax.ShapeDtypeStruct((count - SOON * plane,) + up.shape[1:], BF16),
            jax.ShapeDtypeStruct(down_t.shape, BF16),
        ),
        in_specs=[VMEM] * 4 + [ANY] * 4,
        out_specs=(ANY,) * 8,
        scratch_shapes=[
            pltpu.VMEM(attn_all.shape, BF16),
            pltpu.VMEM(tokens_all.shape, BF16),
            *[pltpu.VMEM(out.shape, out.dtype) for out in outs],
            pltpu.VMEM((2, 2, rows, model), F32),
            pltpu.VMEM((2, rows, model), F32),
            pltpu.VMEM((rows, model), BF16),
            pltpu.VMEM((rows, model), BF16),
            DMA((1, LINE, kinds)), DMA((1, LINE, kinds)), DMA((2, LINE)), DMA((2, LINE)), DMA((2,)),
            DMA((2,)), DMA((3 + LINE,)), DMA((6,)),
        ],
        compiler_params=pltpu.CompilerParams(
            collective_id=2, has_side_effects=True, vmem_limit_bytes=60 * MB
        ),
    )(gains, lens, cos, sin, tokens_all, attn_all, up, down_t)


def attention_backward_kernel(
    plane, gain_ref, cos_ref, sin_ref, total_in, x1_in, dm_in, tok_in, h1_in, qkv_in, probs_in, o_in,
    a_ref, gw_ref, sum_ref, h_in, inner_in, ga_ref, w_out, grad_tokens, gain_parts, weights, own, other, first, second,
    total_ref, x1_ref, dm_ref, tok_ref, h1_ref, qkv_ref, probs_ref, o_ref, rows_in, inner, gw, dx, da, do,
    dqkv, dh1, from_pair, low, from_mate, first_send, first_recv, second_send, second_recv, load_sem,
    other_sem, part_send, part_recv, da_send, da_recv, sum_send, sum_recv, a_sem, keep_sem, grad_sem, in_sem,
):
    me = Place(plane)
    rows, model = tok_ref.shape
    block = weights.shape[1]
    q_width = o_ref.shape[1]
    heads = q_width // HEAD_SIZE
    seq = 2 * rows
    qkv_width = qkv_ref.shape[1]
    kv_width = (qkv_width - q_width) // 2
    kv_heads = kv_width // HEAD_SIZE
    half = HEAD_SIZE // 2
    scale = HEAD_SIZE ** (-0.5)
    summed = PlaneSum(
        me, lambda rank, p: gw.at[(rank - 1) * plane + p] if rank else gw_ref.at[p],
        own, other, first, second,
        (first_send, first_recv, second_send, second_recv, load_sem, other_sem),
    )
    ins = [
        copy_in(src, dst, in_sem.at[i])
        for i, (src, dst) in enumerate(
            (
                (total_in, total_ref), (x1_in, x1_ref), (dm_in.at[me.z, me.t], dm_ref),
                (tok_in.at[me.h, me.t], tok_ref),
                (h1_in, h1_ref), (qkv_in, qkv_ref), (probs_in, probs_ref), (o_in, o_ref),
                (h_in, rows_in), (inner_in, inner),
            )
        )
    ]
    for copy in ins[:3] + ins[8:]:
        copy.start()
    load = pltpu.make_async_copy(a_ref, weights, a_sem)
    load.start()
    for copy in ins[3:8]:
        copy.start()
    summed.load_rank(0)
    greet_all(me, plane * LINE)

    wide = own.shape[2]
    spans = (pl.ds(0, wide), pl.ds(wide, sum_ref.shape[2]))

    def part(rank, kind):
        target = ranked(me, rank)
        way, k = way_to(me, target)
        return remote(
            (own, sum_ref)[kind].at[rank], w_out.at[me.z, :, spans[kind]], part_send.at[way, k, kind],
            part_recv.at[way, k, kind], me.at(target, me.p),
        )

    keeps = [
        copy_in((own, sum_ref)[kind].at[LINE - 1], w_out.at[me.z, :, spans[kind]], keep_sem.at[kind])
        for kind in range(2)
    ]
    das = Quad(me, da, da_send, da_recv)
    dh1_sum = QuadSum(me, dh1, from_pair, low, from_mate, sum_send, sum_recv)

    def mid_norm():
        gain_parts[...] = jnp.zeros_like(gain_parts)

        def act(at):
            x, up = x1_ref[at, :], total_ref[at, :]
            factor = lax.rsqrt(jnp.mean(x * x, -1, keepdims=True) + EPS)
            scaled = up * gain_ref[1:2, :]
            grad = dm_ref[at, :].astype(F32) + (
                factor * scaled - x * factor**3 * jnp.mean(scaled * x, -1, keepdims=True)
            )
            dx[at, :] = grad
            da[me.h, me.t, at, :] = grad.astype(BF16)
            gain_parts[1:2, :] += jnp.sum(up * x * factor, 0, keepdims=True)

        row_loop(rows, 32, act)
        das.start()

    def grad_o():
        load.wait()
        das.finish()

        @pl.loop(0, q_width // HEAD_SIZE)
        def _(c):
            here = pl.multiple_of(c * HEAD_SIZE, HEAD_SIZE)
            value = jnp.dot(
                da[...].reshape(2 * seq, model),
                columns_of(weights, qkv_width + here, HEAD_SIZE),
                preferred_element_type=F32,
            )
            do[:, pl.ds(here, HEAD_SIZE)] = value.astype(BF16)

    def rotate(values, rows_at, start):
        first, second = values[:, :half], values[:, half:]
        cos, sin = cos_ref[...], sin_ref[...]
        dqkv[rows_at, start : start + half] = (first * cos + second * sin).astype(BF16)
        dqkv[rows_at, start + half : start + 2 * half] = (second * cos - first * sin).astype(BF16)

    def grad_heads(n):
        group = heads // kv_heads
        here = slice(n * seq, (n + 1) * seq)
        for m in range(kv_heads):
            at_k = q_width + m * HEAD_SIZE
            at_v = at_k + kv_width
            k = qkv_ref[here, at_k : at_k + HEAD_SIZE]
            v = qkv_ref[here, at_v : at_v + HEAD_SIZE]
            grad_k = grad_v = None
            for i in range(m * group, (m + 1) * group):
                at = slice(i * HEAD_SIZE, (i + 1) * HEAD_SIZE)
                probs = probs_ref[n * heads + i]
                grad_probs = dot_cols(do[here, at], v)
                grad_scores = probs * (
                    grad_probs - jnp.sum(probs * grad_probs, -1, keepdims=True)
                )
                low_scores = grad_scores.astype(BF16)
                rotate(
                    jnp.dot(low_scores, k, preferred_element_type=F32) * scale, here, i * HEAD_SIZE
                )
                more_k = dot_tn(low_scores, qkv_ref[here, at])
                more_v = dot_tn(probs.astype(BF16), do[here, at])
                grad_k = more_k if grad_k is None else grad_k + more_k
                grad_v = more_v if grad_v is None else grad_v + more_v
            rotate(grad_k * scale, here, at_k)
            dqkv[here, at_v : at_v + HEAD_SIZE] = grad_v.astype(BF16)

    tile = 512

    def grad_h1():
        @pl.loop(0, model // tile)
        def _(n):
            here = pl.ds(pl.multiple_of(n * tile, tile), tile)
            value = dot_cols(dqkv[...], rows_of(weights, n, tile, 0, qkv_width))
            dh1[:, :, :, here] = value.reshape(2, 2, rows, tile)

        dh1_sum.start()

    def keep_grads(n):
        per = tile // block
        return pltpu.make_async_copy(
            weights.at[pl.ds(n * per, per)], ga_ref.at[pl.ds(n * per, per)], grad_sem.at[n]
        )

    def grads():
        @pl.loop(0, model // tile)
        def _(n):
            here = pl.ds(pl.multiple_of(n * tile, tile), tile)
            there = pl.ds(n * (tile // block), tile // block)
            left = h1_ref[:, here].T
            for c in range(qkv_width // tile):
                at = slice(c * tile, (c + 1) * tile)
                value = jnp.dot(left, dqkv[:, at], preferred_element_type=F32)
                weights[there, :, at] = value.astype(BF16).reshape(tile // block, block, tile)
            left = da[:, :, :, here].reshape(2 * seq, tile).T
            for c in range(q_width // tile):
                at = slice(c * tile, (c + 1) * tile)
                value = jnp.dot(left, o_ref[:, at], preferred_element_type=F32)
                at = slice(qkv_width + c * tile, qkv_width + (c + 1) * tile)
                weights[there, :, at] = value.astype(BF16).reshape(tile // block, block, tile)

        for n in range(model // tile):
            keep_grads(n).start()

    def in_norm():
        dh1_sum.wait()

        def act(at):
            x = tok_ref[at, :].astype(F32)
            up = dh1_sum.rows(at)
            factor = lax.rsqrt(jnp.mean(x * x, -1, keepdims=True) + EPS)
            scaled = up * gain_ref[0:1, :]
            grad_tokens[at, :] = dx[at, :] + (
                factor * scaled - x * factor**3 * jnp.mean(scaled * x, -1, keepdims=True)
            )
            gain_parts[0:1, :] += jnp.sum(up * x * factor, 0, keepdims=True)

        row_loop(rows, 32, act)

    summed.begin(0)
    for rank in range(LINE - 1):
        part(rank, 1).start()
    keeps[1].start()
    def mlp_grads(rank):
        per = plane * block
        targets = [(0, gw, 0), (1, gw, inner.shape[1])]
        z = ranked(me, rank)
        grad_rows(z * per, per, rows_in, inner, 0, targets, (rank - 1) * plane)
        summed.load_rank(rank)

    for copy in ins[:3]:
        copy.wait()
    mid_norm()
    for copy in ins[8:]:
        copy.wait()
    mlp_grads(1)
    summed.middle(0)
    summed.begin(1)
    das.forward()
    mlp_grads(2)
    for copy in ins[3:8]:
        copy.wait()
    grad_o()
    grad_heads(0)
    grad_heads(1)
    summed.end(0)
    part(0, 0).start()
    grad_h1()
    summed.middle(1)
    summed.begin(2)
    dh1_sum.to_mate()
    mlp_grads(3)
    summed.end(1)
    part(1, 0).start()
    grads()
    summed.middle(2)
    summed.begin(3)
    in_norm()
    summed.end(2)
    part(2, 0).start()
    summed.middle(3)
    summed.end(3)

    keeps[0].start()
    for kind in range(2):
        for rank in range(LINE - 1):
            part(rank, kind).wait_send()
        for way, k in FAR_FIRST:

            @pl.when(reach(me, way, k)[0])
            def _():
                arrival(w_out.at[me.z, :, spans[kind]], part_recv.at[way, k, kind])

    summed.finish()
    das.finish_sends()
    dh1_sum.finish_sends()
    for n in range(model // tile):
        keep_grads(n).wait()
    for copy in keeps:
        copy.wait()


def attention_backward(
    count, gains, cos, sin, total, x1, dm_all, tokens_all, h1, qkv, probs, o, attn_all, grad_mlp, first_sum, rows_in,
    inner,
):
    _, _, rows, model = tokens_all.shape
    _, block, _ = attn_all.shape
    buffers, sems = PlaneSum.scratch(count, block, grad_mlp.shape[2])
    return pl.pallas_call(
        functools.partial(attention_backward_kernel, count // LINE),
        name="attention_backward",
        out_shape=(
            jax.ShapeDtypeStruct(attn_all.shape, BF16),
            jax.ShapeDtypeStruct((LINE, block, grad_mlp.shape[2] + first_sum.shape[2]), BF16),
            jax.ShapeDtypeStruct((rows, model), F32),
            jax.ShapeDtypeStruct((2, model), F32),
        ),
        in_specs=[VMEM] * 3 + [ANY] * 13,
        out_specs=(ANY, ANY, VMEM, VMEM),
        scratch_shapes=[
            pltpu.VMEM(attn_all.shape, BF16),
            *buffers,
            *[
                pltpu.VMEM(ref.shape, ref.dtype)
                for ref in (total, x1, dm_all[0, 0], dm_all[0, 0], h1, qkv, probs, o, rows_in, inner)
            ],
            pltpu.VMEM(((LINE - 1) * grad_mlp.shape[0],) + grad_mlp.shape[1:], BF16),
            pltpu.VMEM((rows, model), F32),
            pltpu.VMEM((2, 2, rows, model), BF16),
            pltpu.VMEM(o.shape, BF16),
            pltpu.VMEM(qkv.shape, BF16),
            pltpu.VMEM((2, 2, rows, model), F32),
            pltpu.VMEM((2, rows, model), F32),
            pltpu.VMEM((rows, model), BF16),
            pltpu.VMEM((rows, model), BF16),
            *sems,
            DMA((2, LINE, 2)), DMA((2, LINE, 2)), DMA((3,)), DMA((3,)), DMA((2,)), DMA((2,)), DMA, DMA((2,)),
            DMA((model // 512,)), DMA((10,)),
        ],
        compiler_params=pltpu.CompilerParams(
            collective_id=3, has_side_effects=True, vmem_limit_bytes=60 * MB
        ),
    )(gains, cos, sin, total, x1, dm_all, tokens_all, h1, qkv, probs, o, attn_all, grad_mlp, first_sum, rows_in, inner)


def grad_sum_kernel(
    count, gain_ref, x1_in, ga_ref, out_ref, a_out, output, gain_out, own, other, first, second, x1_ref,
    landed, out_own, out_pair, out_line, gain_in, gain_pair, first_send, first_recv, second_send, second_recv,
    load_sem, other_sem, part_send, part_recv, out_send, out_recv, load_out_sem, pair_send, pair_recv, gain_send, gain_recv,
):
    plane = count // LINE
    me = Place(plane)
    rows = a_out.shape[1]
    summed = PlaneSum(
        me, ga_ref, own, other, first, second,
        (first_send, first_recv, second_send, second_recv, load_sem, other_sem),
    )

    class Line:
        def __init__(self, held, landing, send, recv):
            self.held, self.landing, self.send, self.recv = held, landing, send, recv

        def pass_on(self, rank):
            way, k = way_to(me, ranked(me, rank))
            ahead = jnp.where(way == 0, me.z + 1, me.z - 1)
            return remote(
                self.held(rank), self.landing.at[way, k - 1], self.send.at[way, k],
                self.recv.at[way, k - 1], me.at(ahead, me.p),
            )

        def step(self, rank):
            way, k = way_to(me, ranked(me, rank))
            before = jnp.where(way == 0, me.z, LINE - 1 - me.z)
            held = self.held(rank)

            @pl.when(before > 0)
            def _():
                arrival(self.landing.at[way, k], self.recv.at[way, k])
                add_rows(held, (held, self.landing.at[way, k]), held.shape[0])

            self.pass_on(rank).start()

        def total(self, act):
            for way in range(2):

                @pl.when(reach(me, way, 1)[0])
                def _():
                    arrival(self.landing.at[way, 0], self.recv.at[way, 0])
                    act(self.landing.at[way, 0])

        def finish(self):
            for rank in range(LINE - 1):
                self.pass_on(rank).wait_send()

    def part(rank):
        target = ranked(me, rank)
        way, k = way_to(me, target)
        return remote(
            own.at[rank], landed.at[me.z], part_send.at[way, k], part_recv.at[way, k],
            me.at(target, me.p),
        )

    outs = Line(lambda rank: out_own.at[ranked(me, rank)], out_line, out_send, out_recv)
    summed.load_all()
    load_out = copy_in(out_ref.at[:, me.t], out_own, load_out_sem.at[0])
    load_out.start()
    load_x1 = copy_in(x1_in, x1_ref, load_out_sem.at[1])
    load_x1.start()
    greet_all(me, count)

    def give_gain(step):
        target = lax.rem(me.d + step, count)
        return remote(
            gain_ref.at[target], gain_in.at[step], gain_send.at[step], gain_recv.at[step], (target, me.t)
        )

    summed.begin(0)
    for step in range(1, count):
        give_gain(step).start()
    pairs = [
        remote(out_ref.at[z, 1 - me.t], out_pair.at[z], pair_send.at[z], pair_recv.at[z], me.sibling())
        for z in range(LINE)
    ]
    for copy in pairs:
        copy.start()
    load_out.wait()
    for z in range(LINE):
        pairs[z].wait_recv()
        add_rows(out_own.at[z], (out_own.at[z], out_pair.at[z]), out_own.shape[1])
    for rank in range(LINE - 1):

        @pl.when(jnp.logical_or(me.z == 0, me.z == LINE - 1))
        def _():
            outs.step(rank)

    at_end = jnp.logical_or(me.z == 0, me.z == LINE - 1)

    def out_start(at):
        x1_ref[at, :] = x1_ref[at, :] + out_own[me.z, at, :].astype(F32)

    def add_out(landed):
        def act(at):
            x1_ref[at, :] = x1_ref[at, :] + landed[at, :].astype(F32)

        row_loop(output.shape[0], 16, act)

    def out_end(at):
        output[at, :] = x1_ref[at, :].astype(BF16)

    for rank in range(LINE):
        summed.middle(rank)
        if rank + 1 < LINE:
            summed.begin(rank + 1)
        else:
            load_x1.wait()
            row_loop(output.shape[0], 16, out_start)
            outs.total(add_out)
            row_loop(output.shape[0], 16, out_end)
            total = gain_ref[me.d]
            for step in range(1, count):
                give_gain(step).wait()
                total += gain_in[step]
            gain_pair[0] = total
            swap = remote(
                gain_pair.at[0], gain_pair.at[1], gain_send.at[0], gain_recv.at[0], me.sibling()
            )
            swap.start()
            swap.wait()
            gain_out[...] = gain_pair[0] + gain_pair[1]
        summed.end(rank)
        if rank < LINE - 1:
            part(rank).start()
        if 0 < rank < LINE - 1:
            @pl.when(jnp.logical_not(at_end))
            def _():
                for late in (range(rank - 1, rank) if rank < LINE - 2 else range(rank - 1, LINE - 1)):
                    outs.step(late)

    keep = copy_in(own.at[LINE - 1], landed.at[me.z], load_out_sem.at[2])
    keep.start()
    for way, k in FAR_FIRST:
        have, z = reach(me, way, k)

        @pl.when(have)
        def _():
            arrival(landed.at[z], part_recv.at[way, k])

    keep.wait()
    for h in range(2):
        add_rows(a_out.at[h], tuple(landed.at[z] for z in range(h, LINE, 2)), rows)
    for rank in range(LINE - 1):
        part(rank).wait_send()
    for copy in pairs:
        copy.wait_send()
    outs.finish()
    summed.finish()


def grad_sum(count, x1, ga, out_parts, gains):
    _, block, width = ga.shape
    _, _, rows, model = out_parts.shape
    buffers, sems = PlaneSum.scratch(count, block, width)
    return pl.pallas_call(
        functools.partial(grad_sum_kernel, count),
        name="grad_sum",
        out_shape=(
            jax.ShapeDtypeStruct((2, block, width), F32),
            jax.ShapeDtypeStruct((rows, model), BF16),
            jax.ShapeDtypeStruct(gains.shape[1:], F32),
        ),
        in_specs=[VMEM] + [ANY] * 3,
        out_specs=(VMEM,) * 3,
        scratch_shapes=[
            *buffers,
            pltpu.VMEM((rows, model), F32),
            pltpu.VMEM((LINE, block, width), BF16),
            pltpu.VMEM((LINE, rows, model), BF16),
            pltpu.VMEM((LINE, rows, model), BF16),
            pltpu.VMEM((2, LINE - 1, rows, model), BF16),
            pltpu.VMEM(gains.shape, F32),
            pltpu.VMEM((2,) + gains.shape[1:], F32),
            *sems,
            DMA((2, LINE)), DMA((2, LINE)), DMA((2, LINE)), DMA((2, LINE)), DMA((3,)), DMA((LINE,)),
            DMA((LINE,)), DMA((count,)), DMA((count,)),
        ],
        compiler_params=pltpu.CompilerParams(
            collective_id=4, has_side_effects=True, vmem_limit_bytes=60 * MB
        ),
    )(gains, x1, ga, out_parts)


def layouts_kernel(
    a_ref, mlp_ref, output_ref, tokens_ref, q_out, k_out, v_out, o_out, gate_out, up_out, down_out,
    output_out, tokens_out, a_v, mlp_v, output_v, tokens_v, q_v, k_v, v_v, o_v, gate_v, up_v, down_v,
    in_sem, out_sem,
):
    ins = [
        copy_in(src, dst, in_sem.at[i])
        for i, (src, dst) in enumerate(
            ((mlp_ref, mlp_v), (a_ref, a_v), (tokens_ref, tokens_v), (output_ref, output_v))
        )
    ]
    for copy in ins:
        copy.start()
    sent = []

    def give(src, dst):
        sent.append(copy_in(src, dst, out_sem.at[len(sent)]))
        sent[-1].start()

    units = mlp_v.shape[2] // 3
    ins[0].wait()
    for z in range(LINE):
        here = pl.ds(z * units, units)
        gate_v[:, here] = mlp_v[z, :, :units].astype(F32)
        give(gate_v.at[:, here], gate_out.at[:, here])
        up_v[:, here] = mlp_v[z, :, units : 2 * units].astype(F32)
        give(up_v.at[:, here], up_out.at[:, here])
        down_v[here, :] = mlp_v[z, :, 2 * units :].astype(F32).T
        give(down_v.at[here], down_out.at[here])
    for copy in ins[1:]:
        copy.wait()
    give(tokens_v, tokens_out)
    give(output_v, output_out)
    start = 0
    for src, dst in ((q_v, q_out), (k_v, k_out), (v_v, v_out)):
        half = src.shape[1] // 2
        for h in range(2):
            src[:, h * half : (h + 1) * half] = a_v[h, :, start : start + half]
        start += half
        give(src, dst)
    half = o_v.shape[0] // 2
    for h in range(2):
        o_v[h * half : (h + 1) * half, :] = a_v[h, :, start:].T
    give(o_v, o_out)
    for copy in sent:
        copy.wait()


def layouts(q_width, kv_width, a, mlp, output, grad_tokens):
    block = a.shape[1]
    hidden = LINE * (mlp.shape[2] // 3)
    outs = (
        jax.ShapeDtypeStruct((block, q_width), F32),
        jax.ShapeDtypeStruct((block, kv_width), F32),
        jax.ShapeDtypeStruct((block, kv_width), F32),
        jax.ShapeDtypeStruct((q_width, block), F32),
        jax.ShapeDtypeStruct((block, hidden), F32),
        jax.ShapeDtypeStruct((block, hidden), F32),
        jax.ShapeDtypeStruct((hidden, block), F32),
    )
    ins = (a, mlp, output, grad_tokens)
    return pl.pallas_call(
        layouts_kernel,
        name="layouts",
        out_shape=outs + tuple(jax.ShapeDtypeStruct(ref.shape, ref.dtype) for ref in ins[2:]),
        in_specs=[ANY] * 4,
        out_specs=(ANY,) * 9,
        scratch_shapes=[
            *[pltpu.VMEM(ref.shape, ref.dtype) for ref in ins + outs],
            DMA((4,)), DMA((3 * LINE + 6,)),
        ],
        compiler_params=pltpu.CompilerParams(vmem_limit_bytes=60 * MB),
    )(*ins)


def shards(
    tokens, w_query, key_weight, value_weight, w_out, gain_attn, w_gate, w_up, w_down, gain_mlp,
    cotangent, lengths, seq_of_group,
):
    count = lax.axis_size("dp")
    rows, q_width = w_query.shape
    kv_width = key_weight.shape[1]
    model = rows * count
    cos, sin = rope_tables(tokens.shape[0] * lax.axis_size("tensor"), HEAD_SIZE)
    lanes = -rows % 128
    gains = jnp.pad(jnp.stack([gain_attn, gain_mlp]), ((0, 14), (0, lanes)))
    attn_all, gate_all, up_soon, up, down_t, gains_all, tokens_all, dm_all = gather_all(
        count, lengths, seq_of_group, gains,
        (w_query, key_weight, value_weight, w_out, w_gate, w_up, w_down), tokens, cotangent,
    )
    gains_full = gains_all[:, :2, :rows].transpose(1, 0, 2).reshape(2, model).astype(F32)
    x1, h2, h1, qkv, probs, attended, up_rest, down = attention_forward(
        count, q_width // 2, kv_width // 2, gains_full, gains_all, cos, sin, tokens_all, attn_all, up,
        down_t,
    )
    grad_h2, out_parts, grad_mlp_w, down_sum, rows_in, inner = feed_forward(
        count, h2, dm_all.reshape(-1, model), gate_all, up_soon, up_rest, down
    )
    grad_attn_w, mlp_sum, grad_tokens, gain_parts = attention_backward(
        count, gains_full, cos, sin, grad_h2, x1, dm_all, tokens_all, h1, qkv, probs, attended, attn_all,
        grad_mlp_w, down_sum, rows_in, inner,
    )
    gain_parts = gain_parts.reshape(2, count, rows).transpose(1, 0, 2)
    gain_parts = jnp.pad(gain_parts, ((0, 0), (0, 6), (0, lanes)))
    attn_sum, output, gain_sum = grad_sum(count, x1, grad_attn_w, out_parts, gain_parts)
    (
        grad_query, grad_key, grad_value, grad_out, grad_gate, grad_up, grad_down, output, grad_tokens,
    ) = layouts(q_width, kv_width, attn_sum, mlp_sum, output, grad_tokens)
    return (
        output, grad_tokens, grad_query, grad_key, grad_value, grad_out, gain_sum[0, :rows],
        grad_gate, grad_up, grad_down, gain_sum[1, :rows],
    )


def solution(mesh):
    both = P(("dp", "tensor"), None)
    row = P("dp", "tensor")
    column = P("tensor", "dp")
    in_specs = (
        both, row, row, row, column, P("dp"), row, row, column, P("dp"), both, P(), P("dp"),
    )
    out_specs = (both, both, row, row, row, column, P("dp"), row, row, column, P("dp"))
    return jax.shard_map(shards, mesh=mesh, in_specs=in_specs, out_specs=out_specs, check_vma=False)
```

```python
import functools
import math

import jax
import jax.numpy as jnp
import numpy as np
from jax import lax
from jax.experimental import pallas as pl
from jax.experimental.pallas import tpu as pltpu
from jax.sharding import PartitionSpec as P

HEAD_SIZE = 256
EPS = 1e-06
THETA = 1000042.0
LINE = 4
MESH = pl.DeviceIdType.MESH
BF16 = jnp.bfloat16
F32 = jnp.float32
MB = 1024 * 1024
AHEAD = 4
SOON = 2


def rope_tables(count, head_dim):
    half = head_dim // 2
    index = np.arange(half, dtype=np.float32)
    freqs = np.exp(index * np.float32(-2.0 * math.log(THETA) / head_dim))
    angles = np.arange(count, dtype=np.float32)[:, None] * freqs[None, :]
    return np.cos(angles), np.sin(angles)


def dot_tn(left, right):
    return lax.dot_general(left, right, (((0,), (0,)), ((), ())), preferred_element_type=F32)


class Place:
    def __init__(self, plane):
        self.d = lax.axis_index("dp")
        self.t = lax.axis_index("tensor")
        self.plane = plane
        self.z = lax.div(self.d, plane)
        self.p = lax.rem(self.d, plane)
        self.h = lax.rem(self.z, 2)
        if plane == 4:
            x = lax.rem(self.p, 2)
            y = lax.div(self.p, 2)
            self.px = 2 * y + 1 - x
            self.py = 2 * (1 - y) + x
            self.pd = 2 * (1 - y) + 1 - x

    def at(self, z, p):
        return (z * self.plane + p, self.t)

    def sibling(self):
        return (self.d, 1 - self.t)

    def mate(self):
        return self.at(self.z + 1 - 2 * self.h, self.p)


def remote(src, dst, send, recv, device):
    return pltpu.make_async_remote_copy(
        src_ref=src, dst_ref=dst, send_sem=send, recv_sem=recv, device_id=device, device_id_type=MESH
    )


def arrival(ref, sem):
    pltpu.make_async_copy(ref, ref, sem).wait()


def greet_all(me, count):
    barrier = pltpu.get_barrier_semaphore()
    for step in range(1, count):
        pl.semaphore_signal(
            barrier, inc=1, device_id=(lax.rem(me.d + step, count), me.t), device_id_type=MESH
        )
    pl.semaphore_signal(barrier, inc=1, device_id=me.sibling(), device_id_type=MESH)
    pl.semaphore_wait(barrier, count)


def greet_line(me):
    barrier = pltpu.get_barrier_semaphore()
    for step in range(1, LINE):
        pl.semaphore_signal(
            barrier, inc=1, device_id=me.at(lax.rem(me.z + step, LINE), me.p), device_id_type=MESH
        )
    pl.semaphore_signal(barrier, inc=1, device_id=me.sibling(), device_id_type=MESH)
    pl.semaphore_wait(barrier, LINE)


def reach(me, way, k):
    return (me.z >= k, me.z - k) if way == 0 else (me.z + k < LINE, me.z + k)


class Chain:
    def __init__(self, me, first, held, send, recv):
        self.me, self.first, self.held, self.send, self.recv = me, first, held, send, recv

    def copy(self, way, k):
        me = self.me
        _, origin = reach(me, way, k)
        target = me.z + 1 if way == 0 else me.z - 1
        src = self.first if k == 0 else self.held(origin)
        return remote(
            src, self.held(origin), self.send.at[way, k], self.recv.at[way, k + 1], me.at(target, me.p)
        )

    def goes(self, way, k):
        have, _ = reach(self.me, way, k)
        ahead, _ = reach(self.me, 1 - way, 1)
        return jnp.logical_and(have, ahead)

    def start(self, way, k):
        if k < LINE - 1:

            @pl.when(self.goes(way, k))
            def _():
                self.copy(way, k).start()

    def wait_block(self, way, k):
        _, origin = reach(self.me, way, k)
        arrival(self.held(origin), self.recv.at[way, k])

    def finish(self):
        for way in range(2):
            for k in range(LINE - 1):

                @pl.when(self.goes(way, k))
                def _():
                    self.copy(way, k).wait_send()


class PlaneGather:
    def __init__(self, me, job, held, rows, send, recv):
        self.me, self.job, self.held, self.send, self.recv = me, job, held, send, recv
        self.half = rows // 2

    def piece(self, z, p, half):
        return self.held.at[z * self.me.plane + p, pl.ds(half * self.half, self.half)]

    def copy(self, z, kind, first=None):
        me = self.me
        if me.plane != 4:
            ref = first if first is not None else self.held.at[z * me.plane + me.p]
            target = lax.rem(me.p + kind + 1, me.plane)
            dst = self.held.at[z * me.plane + me.p]
        else:
            owner = (me.p, me.p, me.p, me.p, me.px, me.py)[kind]
            half = (0, 1, 1, 0, 0, 1)[kind]
            target = (me.px, me.px, me.py, me.py, me.py, me.px)[kind]
            dst = self.piece(z, owner, half)
            ref = dst if first is None else first.at[pl.ds(half * self.half, self.half)]
        return remote(
            ref, dst, self.send.at[self.job, z, kind], self.recv.at[self.job, z, kind], me.at(me.z, target)
        )

    def start(self, z, first=None):
        kinds = (0, 2, 1, 3) if self.me.plane == 4 else range(self.me.plane - 1)
        for kind in kinds:
            self.copy(z, kind, first).start()

    def forward(self, z):
        if self.me.plane == 4:
            self.copy(z, 0).wait_recv()
            self.copy(z, 4).start()
            self.copy(z, 2).wait_recv()
            self.copy(z, 5).start()

    def finish(self, zs=range(LINE)):
        kinds = 6 if self.me.plane == 4 else self.me.plane - 1
        for z in zs:
            for kind in range(kinds):
                copy = self.copy(z, kind)
                if self.me.plane != 4 or kind not in (0, 2):
                    copy.wait_recv()
                copy.wait_send()


class Quad:
    def __init__(self, me, blocks, send, recv):
        self.me, self.blocks, self.send, self.recv = me, blocks, send, recv

    def copy(self, i, first=None):
        me = self.me
        dst = self.blocks.at[me.h if i < 2 else 1 - me.h, me.t]
        device = me.mate() if i == 1 else me.sibling()
        return remote(dst if first is None else first, dst, self.send.at[i], self.recv.at[i], device)

    def start(self, first=None):
        for i in (1, 0):
            self.copy(i, first).start()

    def forward(self):
        arrival(self.blocks.at[1 - self.me.h, self.me.t], self.recv.at[1])
        self.copy(2).start()

    def finish(self):
        me = self.me
        arrival(self.blocks.at[me.h, 1 - me.t], self.recv.at[0])
        arrival(self.blocks.at[1 - me.h, 1 - me.t], self.recv.at[2])

    def finish_sends(self):
        for i in range(3):
            self.copy(i).wait_send()


class QuadSum:
    def __init__(self, me, part, from_pair, low, from_mate, send, recv):
        self.me, self.part, self.from_pair, self.low, self.from_mate = me, part, from_pair, low, from_mate
        self.send, self.recv = send, recv
        self.mate = remote(low, from_mate, send.at[2], recv.at[2], me.mate())

    def pair(self, h):
        me = self.me
        return remote(
            self.part.at[h, 1 - me.t], self.from_pair.at[h], self.send.at[h], self.recv.at[h], me.sibling()
        )

    def start(self, h):
        self.pair(h).start()

    def to_mate(self):
        me = self.me
        self.pair(1 - me.h).wait_recv()

        def act(at):
            total = self.part[1 - me.h, me.t, at, :] + self.from_pair[1 - me.h, at, :]
            self.low[at, :] = total.astype(BF16)

        row_loop(self.low.shape[0], 32, act)
        self.mate.start()

    def wait(self):
        self.pair(self.me.h).wait_recv()
        self.mate.wait_recv()

    def rows(self, at):
        me = self.me
        total = self.part[me.h, me.t, at, :] + self.from_pair[me.h, at, :]
        return total + self.from_mate[at, :].astype(F32)

    def finish_sends(self):
        for h in range(2):
            self.pair(h).wait_send()
        self.mate.wait_send()


def copy_in(src, dst, sem):
    return pltpu.make_async_copy(src, dst, sem)


def row_loop(rows, step, act):
    @pl.loop(0, rows // step)
    def _(i):
        act(pl.ds(pl.multiple_of(i * step, step), step))


def gather_kernel(
    count, len_ref, seq_ref, gain_ref, q_ref, k_ref, v_ref, o_ref, g_ref, u_ref, d_ref, tok_ref, cot_ref,
    a_all, gate_all, up_soon, up, down_t, gain_all, tok_all, dm_all, o_v, a_v, g_v, u_v, d_v, d_t, dm,
    gain_v, chain_send, chain_recv, part_send, part_recv, plane_send, plane_recv, gain_send, gain_recv,
    pair_send, pair_recv, tok_send, tok_recv, local_sem,
):
    plane = count // LINE
    me = Place(plane)
    rows = q_ref.shape[0]
    units = g_ref.shape[1] // LINE
    q_half, kv_half = q_ref.shape[1] // 2, k_ref.shape[1] // 2
    qkv_half = q_half + 2 * kv_half

    def columns(ref, z):
        return ref.at[:, pl.ds(pl.multiple_of(z * units, units), units)]

    local = [copy_in(o_ref, o_v, local_sem.at[0])]
    for h in range(2):
        start = 0
        for ref, width in ((q_ref, q_half), (k_ref, kv_half), (v_ref, kv_half)):
            src = ref.at[:, pl.ds(h * width, width)]
            local.append(copy_in(src, a_v.at[h, :, pl.ds(start, width)], local_sem.at[len(local)]))
            start += width
    early = len(local)
    for src, dst in (
        (d_ref, d_v), (cot_ref, dm), (columns(g_ref, me.z), g_v), (columns(u_ref, me.z), u_v),
        (tok_ref, tok_all.at[me.h, me.t]),
    ):
        local.append(copy_in(src, dst, local_sem.at[len(local)]))
    for copy in local[:early]:
        copy.start()
    keep_a = copy_in(a_v.at[me.h], a_all.at[me.d], local_sem.at[12])
    keep_down = copy_in(d_t, down_t, local_sem.at[13])
    keep_dm = copy_in(dm, dm_all.at[me.z, me.t], local_sem.at[14])
    keep_gate = copy_in(g_v, gate_all.at[me.d], local_sem.at[15])
    keep_up = copy_in(u_v, up.at[me.z], local_sem.at[16])
    keep_gain = copy_in(gain_v, gain_all.at[me.d], local_sem.at[17])

    dms = Chain(me, dm, lambda z: dm_all.at[z, me.t], chain_send, chain_recv)
    planes = (
        PlaneGather(me, 0, a_all, rows, plane_send, plane_recv),
        PlaneGather(me, 1, gate_all, rows, plane_send, plane_recv),
        PlaneGather(me, 2, up_soon, rows, plane_send, plane_recv),
    )

    def part(way, k, kind):
        _, target = reach(me, 1 - way, k)
        src = columns((g_ref, u_ref)[kind - 1], target) if kind else a_v.at[lax.rem(target, 2)]
        dst = (a_all.at[me.d], gate_all.at[me.d], up.at[me.z])[kind]
        return remote(
            src, dst, part_send.at[way, k, kind], part_recv.at[way, k, kind], me.at(target, me.p)
        )

    def pair(z, first=None):
        src = dm_all.at[z, me.t] if first is None else first
        return remote(src, dm_all.at[z, me.t], pair_send.at[z], pair_recv.at[z], me.sibling())

    def keep_soon(soon, src):
        return copy_in(src, up_soon.at[soon * plane + me.p], local_sem.at[18 + soon])

    def start_parts(k, kinds):
        for way in range(2):

            @pl.when(reach(me, 1 - way, k)[0])
            def _():
                for kind in kinds:
                    part(way, k, kind).start()

    def each(k, act):
        for way in range(2):
            have, z = reach(me, way, k)

            @pl.when(have)
            def _():
                act(way, k, z)

    def attn_step(way, k, z):
        arrival(a_all.at[z * plane + me.p], part_recv.at[way, k, 0])
        planes[0].start(z)

    def gate_step(way, k, z):
        arrival(gate_all.at[z * plane + me.p], part_recv.at[way, k, 1])
        planes[1].start(z)

    def up_step(way, k, z):
        arrival(up.at[z], part_recv.at[way, k, 2])

        @pl.when(z == me.z + 1 - 2 * me.h)
        def _():
            planes[2].start(1 - me.h, up.at[z])
            keep_soon(1 - me.h, up.at[z]).start()

    def dm_step(way, k, z):
        dms.wait_block(way, k)
        pair(z).start()

    def give_gain(step):
        target = lax.rem(me.d + step, count)
        return remote(
            gain_v, gain_all.at[me.d], gain_send.at[step], gain_recv.at[step], (target, me.t)
        )

    chosen = len_ref[seq_ref[0]]
    kind_of = lax.broadcasted_iota(jnp.int32, gain_ref.shape, 0)
    gain_v[...] = jnp.where(kind_of == 2, chosen.astype(F32), gain_ref[...].astype(F32)).astype(BF16)
    local[0].wait()
    for h in range(2):
        a_v[h, :, qkv_half:] = o_v[h * q_half : (h + 1) * q_half, :].T
    greet_all(me, count)
    for copy in local[1:early]:
        copy.wait()
    toks = Quad(me, tok_all, tok_send, tok_recv)
    levels = [(0, 1), (0, 2), (0, 3), (3, 1), (1, 1), (1, 2), (1, 3), (3, 2), (2, 1), (2, 2), (2, 3), (3, 3)]

    def start_level(kind, k):
        if kind < 3:
            start_parts(k, (kind,))
        elif k == 1:
            for way in range(2):
                dms.start(way, 0)
            pair(me.z, dm).start()
        else:
            each(k - 1, lambda way, k, z: dms.start(way, k))

    def finish_level(kind, k):
        each(k, (attn_step, gate_step, up_step, dm_step)[kind])

    def forward_level(kind, k):
        if kind < 2:
            each(k, lambda way, k, z: planes[kind].forward(z))

    for level in levels[:2]:
        start_level(*level)
    planes[0].start(me.z, a_v.at[me.h])
    toks.start(tok_ref)
    for step in range(1, count):
        give_gain(step).start()
    for copy in local[early:]:
        copy.start()
    keep_a.start()
    keep_gain.start()

    local[early].wait()
    for z in range(LINE):
        d_t[z] = d_v[z * units : (z + 1) * units, :].T
    keep_down.start()
    local[early + 1].wait()

    def mask(at):
        value = dm[at, :].astype(F32)
        row = lax.broadcasted_iota(jnp.int32, value.shape, 0) + (me.t * dm.shape[0] + at.start)
        dm[at, :] = jnp.where(row < chosen, value, 0.0).astype(BF16)

    row_loop(dm.shape[0], 32, mask)
    keep_dm.start()

    for i, level in enumerate(levels):
        if i == 0:
            for more in levels[2:AHEAD]:
                start_level(*more)
        finish_level(*level)
        if i + AHEAD < len(levels):
            start_level(*levels[i + AHEAD])
        if level == (0, 1):
            toks.forward()
            planes[0].forward(me.z)
            for copy in local[early + 2 : early + 4]:
                copy.wait()
            keep_gate.start()
            keep_up.start()
            planes[1].start(me.z, g_v)
        if level == (0, 3):
            planes[1].forward(me.z)
        if level == (1, 3):
            planes[2].start(me.h, u_v)
            keep_soon(me.h, u_v).start()
        if level == (3, 3):
            planes[2].forward(me.h)
        if i:
            forward_level(*levels[i - 1])
    planes[2].forward(1 - me.h)

    dms.finish()
    for k in range(1, LINE):
        for way in range(2):

            @pl.when(reach(me, 1 - way, k)[0])
            def _():
                for kind in range(3):
                    part(way, k, kind).wait_send()

    for step in range(1, count):
        give_gain(step).wait()
    toks.finish()
    toks.finish_sends()
    for z in range(LINE):
        pair(z).wait()
    for job, zs in zip(planes, (LINE, LINE, SOON)):
        job.finish(range(zs))
    for soon in range(SOON):
        keep_soon(soon, u_v).wait()
    for copy in local[early + 4 :] + [keep_a, keep_down, keep_dm, keep_gate, keep_up, keep_gain]:
        copy.wait()


ANY = pl.BlockSpec(memory_space=pl.ANY)
VMEM = pl.BlockSpec(memory_space=pltpu.VMEM)
SMEM = pl.BlockSpec(memory_space=pltpu.SMEM)
DMA = pltpu.SemaphoreType.DMA


def gather_all(count, lengths, seq, gains, weights, tokens, cotangent):
    w_query, key_weight, _, w_out, w_gate, _, w_down = weights
    rows, q_width = w_query.shape
    width = q_width + key_weight.shape[1]
    units = w_gate.shape[1] // LINE
    plane = count // LINE
    kinds = max(6, plane - 1)
    return pl.pallas_call(
        functools.partial(gather_kernel, count),
        name="gather_all",
        out_shape=(
            jax.ShapeDtypeStruct((count, rows, width), BF16),
            jax.ShapeDtypeStruct((count, rows, units), BF16),
            jax.ShapeDtypeStruct((plane * SOON, rows, units), BF16),
            jax.ShapeDtypeStruct((LINE, rows, units), BF16),
            jax.ShapeDtypeStruct((LINE, rows, units), BF16),
            jax.ShapeDtypeStruct((count,) + gains.shape, gains.dtype),
            jax.ShapeDtypeStruct((2, 2) + tokens.shape, BF16),
            jax.ShapeDtypeStruct((LINE, 2) + cotangent.shape, BF16),
        ),
        in_specs=[SMEM] * 2 + [VMEM] + [ANY] * 9,
        out_specs=(ANY,) * 8,
        scratch_shapes=[
            pltpu.VMEM(w_out.shape, BF16),
            pltpu.VMEM((2, rows, width), BF16),
            pltpu.VMEM((rows, units), BF16),
            pltpu.VMEM((rows, units), BF16),
            pltpu.VMEM(w_down.shape, BF16),
            pltpu.VMEM((LINE, rows, units), BF16),
            pltpu.VMEM(cotangent.shape, BF16),
            pltpu.VMEM(gains.shape, BF16),
            DMA((2, LINE)), DMA((2, LINE)), DMA((2, LINE, 3)), DMA((2, LINE, 3)),
            DMA((3, LINE, kinds)), DMA((3, LINE, kinds)), DMA((count,)), DMA((count,)),
            DMA((LINE,)), DMA((LINE,)), DMA((3,)), DMA((3,)), DMA((18 + SOON,)),
        ],
        compiler_params=pltpu.CompilerParams(
            collective_id=0, has_side_effects=True, vmem_limit_bytes=60 * MB
        ),
    )(lengths, seq, gains, *weights, tokens, cotangent)


RANKS = ((3, 2, 1, 0), (3, 0, 2, 1), (0, 3, 1, 2), (0, 1, 2, 3))
FAR_FIRST = [(way, k) for k in range(LINE - 1, 0, -1) for way in range(2)]


def ranked(me, rank):
    z = jnp.int32(RANKS[0][rank])
    for at in range(1, LINE):
        z = jnp.where(me.z == at, RANKS[at][rank], z)
    return z


def way_to(me, z):
    down = (z < me.z).astype(jnp.int32)
    return down, jnp.where(z < me.z, me.z - z, z - me.z)


def add_rows(target, terms, rows, start=0):
    step = 16

    @pl.loop(0, rows // step)
    def _(i):
        at = pl.ds(pl.multiple_of(start + i * step, step), step)
        total = terms[0][at].astype(F32)
        for term in terms[1:]:
            total += term[at].astype(F32)
        target[at] = total.astype(target.dtype)


def grad_rows(at, per, left_ref, right_ref, first, targets, there):
    tile = 512
    tokens = left_ref.shape[0]

    @pl.loop(0, per // tile)
    def _(n):
        left = left_ref[:, pl.ds(pl.multiple_of(at + n * tile, tile), tile)].T
        for job, ref, start in targets:
            block, units = ref.shape[1], right_ref.shape[1]
            rows = pl.ds(there + n * (tile // block), tile // block)
            for c in range(units // tile):
                grad = jnp.dot(
                    left, right_ref[pl.ds(first + job * tokens, tokens), c * tile : (c + 1) * tile],
                    preferred_element_type=F32,
                )
                ref[rows, :, start + c * tile : start + (c + 1) * tile] = grad.astype(BF16).reshape(
                    tile // block, block, tile
                )


class PlaneSum:
    def __init__(self, me, grad, own, other, first, second, sems, ranks=range(LINE)):
        self.me, self.grad, self.own, self.other, self.first, self.second = me, grad, own, other, first, second
        (
            self.first_send, self.first_recv, self.second_send, self.second_recv, self.load_sem, self.other_sem,
        ) = sems
        self.ranks = ranks
        self.rows = own.shape[1]
        half = self.rows // 2
        self.half = half
        self.halves = (pl.ds(0, half), pl.ds(half, half))
        self.square = me.plane == 4
        if self.square:
            self.near = (me.px, me.py)
            self.far = (me.py, me.px)

    def slot(self, rank):
        return rank - self.ranks[0]

    def block(self, rank, p):
        if callable(self.grad):
            return self.grad(rank, p)
        return self.grad.at[ranked(self.me, rank) * self.me.plane + p]

    def load(self, rank):
        s = self.slot(rank)
        return pltpu.make_async_copy(self.block(rank, self.me.p), self.own.at[s], self.load_sem.at[s])

    def load_other(self, rank, i):
        s = self.slot(rank)
        return pltpu.make_async_copy(
            self.block(rank, self.far[i]).at[self.halves[i]], self.other.at[s, self.halves[i]],
            self.other_sem.at[s, i],
        )

    def load_rank(self, rank):
        self.load(rank).start()
        if self.square:
            for i in range(2):
                self.load_other(rank, i).start()

    def load_all(self):
        for rank in self.ranks:
            self.load_rank(rank)

    def give(self, rank, i, which):
        me, s = self.me, self.slot(rank)
        if not self.square:
            target = lax.rem(me.p + which + 1, me.plane)
            return remote(
                self.block(rank, target), self.first.at[s, which], self.first_send.at[s, which],
                self.first_recv.at[s, which], me.at(me.z, target),
            )
        owner = (self.near[i], me.pd)[which]
        return remote(
            self.block(rank, owner).at[self.halves[i]], self.first.at[s, which, self.halves[i]],
            self.first_send.at[s, 2 * i + which], self.first_recv.at[s, 2 * i + which],
            me.at(me.z, self.near[i]),
        )

    def give_both(self, rank, i):
        s = self.slot(rank)
        return remote(
            self.other.at[s, self.halves[i]], self.second.at[s, self.halves[i]],
            self.second_send.at[s, i], self.second_recv.at[s, i], self.me.at(self.me.z, self.far[i]),
        )

    def gives(self, rank):
        if self.square:
            return [self.give(rank, i, which) for which in (1, 0) for i in range(2)]
        return [self.give(rank, 0, which) for which in range(self.me.plane - 1)]

    def begin(self, rank):
        for copy in self.gives(rank):
            copy.start()

    def middle(self, rank):
        if not self.square:
            return
        s = self.slot(rank)
        for i in range(2):
            arrival(self.first.at[s, 1, self.halves[i]], self.first_recv.at[s, 2 * i + 1])
            self.load_other(rank, i).wait()
            add_rows(
                self.other.at[s], (self.other.at[s], self.first.at[s, 1]), self.half, i * self.half
            )
            self.give_both(rank, i).start()

    def end(self, rank):
        s = self.slot(rank)
        self.load(rank).wait()
        if self.square:
            for i in range(2):
                arrival(self.first.at[s, 0, self.halves[i]], self.first_recv.at[s, 2 * i])
                arrival(self.second.at[s, self.halves[i]], self.second_recv.at[s, i])
            terms = (self.first.at[s, 0], self.second.at[s])
        else:
            for which in range(self.me.plane - 1):
                arrival(self.first.at[s, which], self.first_recv.at[s, which])
            terms = tuple(self.first.at[s, which] for which in range(self.me.plane - 1))
        add_rows(self.own.at[s], (self.own.at[s],) + terms, self.rows)

    def finish(self):
        for rank in self.ranks:
            for copy in self.gives(rank):
                copy.wait_send()
            if self.square:
                for i in range(2):
                    self.give_both(rank, i).wait_send()

    @staticmethod
    def scratch(count, rows, width, ranks=LINE):
        plane = count // LINE
        square = plane == 4
        slots = 2 if square else plane - 1
        small = (ranks, rows, width) if square else (1, 16, 128)
        return [
            pltpu.VMEM((ranks, rows, width), BF16),
            pltpu.VMEM(small, BF16),
            pltpu.VMEM((ranks, slots, rows, width), BF16),
            pltpu.VMEM(small, BF16),
        ], [
            DMA((ranks, max(4, slots))), DMA((ranks, max(4, slots))), DMA((ranks, 2)), DMA((ranks, 2)),
            DMA((ranks,)), DMA((ranks, 2)),
        ]


def dot_cols(left, right):
    return lax.dot_general(left, right, (((1,), (1,)), ((), ())), preferred_element_type=F32)


def feed_forward_kernel(
    plane, h_ref, dm_ref, gate_ref, up_soon, up_rest, down, total_ref, out_ref, grad_ref, sum_ref,
    h_out, inner_out, rows_in, weights, inner, down_grad, part,
    from_pair, from_line, own, other, first, second, first_send, first_recv, second_send, second_recv,
    own_sem, other_sem, chain_send, chain_recv, pass_send, pass_recv, pair_send, pair_recv,
    line_send, line_recv, plane_send, plane_recv, load_sem, dm_sem, grad_sem, out_sem, sum_sem,
):
    me = Place(plane)
    rows, model = h_ref.shape
    units = inner.shape[1]
    wide = 2 * rows
    tokens = LINE * wide
    block = down.shape[1]
    soon = up_soon.shape[0]
    tile = 512

    def slot(z, t):
        return rows_in.at[pl.ds(pl.multiple_of((z * 2 + t) * rows, rows), rows)]

    loads = [
        copy_in(gate_ref, weights.at[:, :, pl.ds(0, units)], load_sem.at[0]),
        copy_in(
            up_soon, weights.at[pl.ds((me.z - me.h) * plane, soon), :, pl.ds(units, units)], load_sem.at[2]
        ),
        copy_in(
            up_rest, weights.at[pl.ds((SOON - me.z + me.h) * plane, soon), :, pl.ds(units, units)],
            load_sem.at[3],
        ),
    ]
    own_down = [
        copy_in(
            down.at[z], weights.at[z * plane + me.p, :, pl.ds(2 * units, units)], load_sem.at[4 + z]
        )
        for z in range(LINE)
    ]
    for load in loads:
        load.start()
    load_dm = pltpu.make_async_copy(dm_ref, rows_in.at[pl.ds(tokens, tokens)], dm_sem)
    load_dm.start()
    keep = pltpu.make_async_copy(h_ref, slot(me.z, me.t), load_sem.at[1])
    keep.start()
    greet_all(me, plane * LINE)
    gather = PlaneGather(
        me, 0, weights.at[:, :, pl.ds(2 * units, units)], block, plane_send, plane_recv
    )
    summed = PlaneSum(
        me, down_grad, own, other, first, second,
        (first_send, first_recv, second_send, second_recv, own_sem, other_sem),
    )
    chain = Chain(me, h_ref, lambda z: slot(z, me.t), chain_send, chain_recv)

    def share(z, first=None):
        src = slot(z, me.t) if first is None else first
        return remote(src, slot(z, me.t), pass_send.at[z], pass_recv.at[z], me.sibling())

    for way in range(2):
        chain.start(way, 0)
    share(me.z, h_ref).start()
    for z in range(2):
        gather.start(z, down.at[z])
    for copy in own_down:
        copy.start()

    def w_rows(n, width, column):
        return weights[pl.ds(n * (width // block), width // block), :, pl.ds(column, units)].reshape(
            width, units
        )

    def pair_rows(z, job=0):
        return pl.ds(pl.multiple_of(job * tokens + z * wide, wide), wide)

    def columns(c, job):
        return weights[:, :, pl.ds(pl.multiple_of(job * units + c * tile, tile), tile)].reshape(model, tile)

    def project(z):
        @pl.loop(0, units // tile)
        def _(c):
            here = pl.ds(pl.multiple_of(c * tile, tile), tile)
            h = rows_in[pair_rows(z), :]
            gate = jnp.dot(h, columns(c, 0), preferred_element_type=F32)
            up = jnp.dot(h, columns(c, 1), preferred_element_type=F32)
            sigmoid = jax.nn.sigmoid(gate)
            silu = gate * sigmoid
            inner[pair_rows(z), here] = (silu * up).astype(BF16)
            inner[pair_rows(z, 1), here] = (up * sigmoid * (1.0 + gate * (1.0 - sigmoid))).astype(BF16)
            inner[pair_rows(z, 2), here] = silu.astype(BF16)

    def back(z):
        @pl.loop(0, units // tile)
        def _(c):
            here = pl.ds(pl.multiple_of(c * tile, tile), tile)
            grad_hidden = jnp.dot(rows_in[pair_rows(z, 1), :], columns(c, 2), preferred_element_type=F32)
            for job in range(1, 3):
                at = pair_rows(z, job)
                inner[at, here] = (grad_hidden * inner[at, here].astype(F32)).astype(BF16)

        @pl.loop(0, model // tile)
        def _(n):
            here = pl.ds(pl.multiple_of(n * tile, tile), tile)
            grad = dot_cols(inner[pair_rows(z, 1)], w_rows(n, tile, 0))
            grad += dot_cols(inner[pair_rows(z, 2)], w_rows(n, tile, units))
            part[0, z, :, :, here] = grad.astype(BF16).reshape(2, rows, tile)

        pair(z).start()

    def out(z):
        @pl.loop(0, model // tile)
        def _(n):
            here = pl.ds(pl.multiple_of(n * tile, tile), tile)
            value = dot_cols(inner[pair_rows(z), :], w_rows(n, tile, 2 * units))
            part[1, z, :, :, here] = value.astype(BF16).reshape(2, rows, tile)

        keep_out(z).start()

    def pair(z):
        return remote(
            part.at[0, z, 1 - me.t], from_pair.at[z], pair_send.at[z], pair_recv.at[z], me.sibling()
        )

    half = rows // 2
    halves = (pl.ds(0, half), pl.ds(half, half))

    def pass_on(way, k, i):
        _, target = reach(me, 1 - way, k)
        ahead = me.z + 1 if way == 0 else me.z - 1
        return remote(
            part.at[0, target, me.t, halves[i]], from_line.at[way, k - 1, halves[i]],
            line_send.at[way, k, i], line_recv.at[way, k - 1, i], me.at(ahead, me.p),
        )

    def line(way, k, behind):
        have, z = reach(me, 1 - way, k)
        before = me.z if way == 0 else LINE - 1 - me.z

        @pl.when(jnp.logical_and(have, before == behind))
        def _():
            pair(z).wait_recv()
            terms = (part.at[0, z, me.t], from_pair.at[z])
            if behind:
                terms += (from_line.at[way, k],)
            for i in range(2):
                if behind:
                    arrival(from_line.at[way, k, halves[i]], line_recv.at[way, k, i])
                add_rows(part.at[0, z, me.t], terms, half, i * half)
                pass_on(way, k, i).start()

    def total():
        pair(me.z).wait_recv()
        add_rows(total_ref, (part.at[0, me.z, me.t], from_pair.at[me.z]), rows)
        for way in range(2):

            @pl.when(reach(me, way, 1)[0])
            def _():
                for i in range(2):
                    arrival(from_line.at[way, 0, halves[i]], line_recv.at[way, 0, i])
                    add_rows(total_ref, (total_ref, from_line.at[way, 0]), half, i * half)

    per = plane * block

    def down_grads(rank):
        z = ranked(me, rank)
        grad_rows(
            z * per, per, rows_in.at[pl.ds(tokens, tokens)], inner, 0, [(0, down_grad, 0)], z * plane
        )
        summed.load_rank(rank)

    keeps = [
        copy_in(weights.at[pl.ds(0, plane), :, pl.ds(0, 2 * units)], grad_ref, grad_sem.at[0]),
        copy_in(rows_in.at[pl.ds(0, tokens)], h_out, grad_sem.at[1]),
        copy_in(inner.at[pl.ds(tokens, 2 * tokens)], inner_out, grad_sem.at[2]),
    ]

    def grads():
        targets = [(0, weights, 0), (1, weights, units)]
        z = ranked(me, 0)
        grad_rows(z * per, per, rows_in.at[pl.ds(0, tokens)], inner, tokens, targets, 0)

    def keep_sum(rank):
        return copy_in(own.at[rank], sum_ref.at[rank], sum_sem.at[rank])

    keep.wait()
    for load in loads:
        load.wait()
    for k in range(LINE):
        for way in range(2 if k else 1):
            have, z = reach(me, way, k)

            @pl.when(have)
            def _():
                if k:
                    chain.wait_block(way, k)
                    chain.start(way, k)
                    share(z).start()
                arrival(slot(z, 1 - me.t), pass_recv.at[z])
                project(z)

        gather.forward(k)
        if k + 2 < LINE:
            gather.start(k + 2, down.at[k + 2])
    def keep_out(z):
        return copy_in(part.at[1, z], out_ref.at[z], out_sem.at[z])

    load_dm.wait()
    keeps[1].start()
    down_grads(0)
    summed.begin(0)
    for copy in own_down:
        copy.wait()
    gather.finish()
    passing = {1: (1, 2), 2: (2, 1), 3: (1, 1)}
    for rank in range(LINE):
        if rank:
            down_grads(rank)
            if rank - 1 in passing:
                for way in range(2):
                    line(way, passing[rank - 1][1], passing[rank - 1][0])
            summed.middle(rank - 1)
            summed.begin(rank)
            if rank > 1:
                summed.end(rank - 2)
                keep_sum(rank - 2).start()
        back(ranked(me, rank))
        if rank < LINE - 1:
            out(ranked(me, rank))
            for way in range(2):
                line(way, LINE - 1 - rank, 0)
    for way in range(2):
        line(way, passing[LINE - 1][1], passing[LINE - 1][0])
    keeps[2].start()
    summed.middle(LINE - 1)
    summed.end(LINE - 2)
    keep_sum(LINE - 2).start()
    grads()
    keeps[0].start()
    out(ranked(me, LINE - 1))
    summed.end(LINE - 1)
    keep_sum(LINE - 1).start()
    total()
    summed.finish()
    chain.finish()
    for z in range(LINE):
        share(z).wait_send()
        keep_out(z).wait()
        keep_sum(z).wait()
        pair(z).wait_send()
    for copy in keeps:
        copy.wait()
    for k in range(1, LINE):
        for way in range(2):

            @pl.when(reach(me, 1 - way, k)[0])
            def _():
                for i in range(2):
                    pass_on(way, k, i).wait_send()


def feed_forward(count, h, dm_all, gate_all, up_soon, up_rest, down):
    rows, model = h.shape
    _, block, units = down.shape
    kinds = max(6, count // LINE - 1)
    buffers, sems = PlaneSum.scratch(count, block, units)
    tokens = LINE * 2 * rows
    vmem = pl.BlockSpec(memory_space=pltpu.VMEM)
    return pl.pallas_call(
        functools.partial(feed_forward_kernel, count // LINE),
        name="feed_forward",
        out_shape=(
            jax.ShapeDtypeStruct((rows, model), F32),
            jax.ShapeDtypeStruct((LINE, 2, rows, model), BF16),
            jax.ShapeDtypeStruct((count // LINE, block, 2 * units), BF16),
            jax.ShapeDtypeStruct((LINE, block, units), BF16),
            jax.ShapeDtypeStruct((tokens, model), BF16),
            jax.ShapeDtypeStruct((2 * tokens, units), BF16),
        ),
        in_specs=[ANY] * 6,
        out_specs=(vmem,) + (ANY,) * 5,
        scratch_shapes=[
            pltpu.VMEM((2 * tokens, model), BF16),
            pltpu.VMEM((count, block, 3 * units), BF16),
            pltpu.VMEM((3 * tokens, units), BF16),
            pltpu.VMEM((count, block, units), BF16),
            pltpu.VMEM((2, LINE, 2, rows, model), BF16),
            pltpu.VMEM((LINE, rows, model), BF16),
            pltpu.VMEM((2, LINE - 1, rows, model), BF16),
            *buffers,
            *sems,
            DMA((2, LINE)), DMA((2, LINE)), DMA((LINE,)), DMA((LINE,)), DMA((LINE,)), DMA((LINE,)),
            DMA((2, LINE, 2)), DMA((2, LINE, 2)), DMA((1, LINE, kinds)), DMA((1, LINE, kinds)),
            DMA((4 + LINE,)), DMA, DMA((LINE,)), DMA((LINE,)), DMA((LINE,)),
        ],
        compiler_params=pltpu.CompilerParams(
            collective_id=1, has_side_effects=True, vmem_limit_bytes=60 * MB
        ),
    )(h, dm_all, gate_all, up_soon, up_rest, down)


def greet_plane(me):
    barrier = pltpu.get_barrier_semaphore()
    for step in range(1, me.plane):
        target = lax.rem(me.p + step, me.plane)
        pl.semaphore_signal(barrier, inc=1, device_id=me.at(me.z, target), device_id_type=MESH)
    pl.semaphore_signal(barrier, inc=1, device_id=me.sibling(), device_id_type=MESH)
    pl.semaphore_wait(barrier, me.plane)


def columns_of(weights, start, width):
    count, rows, _ = weights.shape
    return weights[:, :, pl.ds(start, width)].reshape(count * rows, width)


def rows_of(weights, n, height, start, width):
    _, rows, _ = weights.shape
    per = height // rows
    return weights[pl.ds(n * per, per), :, pl.ds(start, width)].reshape(height, width)


def attention_forward_kernel(
    plane, lens_ref, cos_ref, sin_ref, tok_in, a_ref, up, down_t, gain_ref, x1_out, h2_out, h1_out,
    qkv_out, probs_out, o_out, up_rest, down, weights, tok_ref, x1_ref, h2_ref, h1_ref, qkv_ref, probs_ref,
    o_ref, part, from_pair, low, from_mate, plane_send, plane_recv, part_send, part_recv, sum_send,
    sum_recv, load_sem, keep_sem,
):
    me = Place(plane)
    _, _, rows, model = tok_ref.shape
    wide = 2 * rows
    q_width = o_ref.shape[1]
    heads = q_width // HEAD_SIZE
    kv_width = (qkv_ref.shape[1] - q_width) // 2
    kv_heads = kv_width // HEAD_SIZE
    half = HEAD_SIZE // 2
    load_tok = copy_in(tok_in, tok_ref, load_sem.at[0])
    load_tok.start()
    load = copy_in(a_ref, weights, load_sem.at[1])
    load.start()
    far = SOON - (me.z - me.h)
    keep = [
        copy_in(up.at[far + z], up_rest.at[z * plane + me.p], load_sem.at[2 + z])
        for z in range(LINE - SOON)
    ]
    keep.append(copy_in(down_t.at[me.z], down.at[me.z], load_sem.at[2 + LINE]))
    for copy in keep:
        copy.start()
    outs = [
        copy_in(src, dst, keep_sem.at[i])
        for i, (src, dst) in enumerate(
            (
                (h1_ref, h1_out), (qkv_ref, qkv_out), (probs_ref, probs_out), (o_ref, o_out),
                (x1_ref, x1_out), (h2_ref, h2_out),
            )
        )
    ]
    greet_all(me, plane * LINE)
    gather = PlaneGather(me, 0, up_rest, up.shape[1], plane_send, plane_recv)
    for z in range(LINE - SOON):
        gather.start(z, up.at[far + z])

    def give_down(way, k):
        _, target = reach(me, 1 - way, k)
        return remote(
            down_t.at[target], down.at[me.z], part_send.at[way, k], part_recv.at[way, k],
            me.at(target, me.p),
        )

    for k in range(1, LINE):
        for way in range(2):

            @pl.when(reach(me, 1 - way, k)[0])
            def _():
                give_down(way, k).start()

    span = model // (plane * LINE)
    for d in range(plane * LINE):
        gain_ref[:, d * span : (d + 1) * span] = lens_ref[d, 0:2, :span].astype(F32)
    load_tok.wait()

    for n in range(4):

        def norm(at, n=n):
            x = tok_ref[n // 2, n % 2, at, :].astype(F32)
            factor = lax.rsqrt(jnp.mean(x * x, -1, keepdims=True) + EPS)
            h1_ref[pl.ds(n * rows + at.start, at.size), :] = (x * factor * gain_ref[0:1, :]).astype(BF16)

        row_loop(rows, 32, norm)
    outs[0].start()
    load.wait()

    def project(i):
        start = pl.multiple_of(i * HEAD_SIZE, HEAD_SIZE)
        return start, jnp.dot(
            h1_ref[...], columns_of(weights, start, HEAD_SIZE), preferred_element_type=F32
        )

    @pl.loop(0, heads + kv_heads)
    def _(i):
        start, values = project(i)
        cos, sin = cos_ref[...], sin_ref[...]
        for n in range(2):
            at = slice(n * wide, (n + 1) * wide)
            first, second = values[at, :half], values[at, half:]
            qkv_ref[at, pl.ds(start, half)] = (first * cos - second * sin).astype(BF16)
            qkv_ref[at, pl.ds(start + half, half)] = (second * cos + first * sin).astype(BF16)

    @pl.loop(heads + kv_heads, heads + 2 * kv_heads)
    def _(i):
        start, values = project(i)
        qkv_ref[:, pl.ds(start, HEAD_SIZE)] = values.astype(BF16)

    outs[1].start()
    gather.forward(0)
    row = lax.broadcasted_iota(jnp.int32, (wide, wide), 0)
    key = lax.broadcasted_iota(jnp.int32, (wide, wide), 1)
    tile = 512
    total = QuadSum(me, part, from_pair, low, from_mate, sum_send, sum_recv)

    def attend(n):
        length = lens_ref[me.d + (n - me.h) * plane, 2:3, 0:1].astype(F32)
        allowed = jnp.logical_and(key <= row, key.astype(F32) < length)
        at = pl.ds(pl.multiple_of(n * wide, wide), wide)
        for i in range(heads):
            m = i * kv_heads // heads
            q = qkv_ref[at, i * HEAD_SIZE : (i + 1) * HEAD_SIZE]
            k = qkv_ref[at, q_width + m * HEAD_SIZE : q_width + (m + 1) * HEAD_SIZE]
            v_start = q_width + kv_width + m * HEAD_SIZE
            v = qkv_ref[at, v_start : v_start + HEAD_SIZE]
            scores = dot_cols(q, k) * HEAD_SIZE ** (-0.5)
            scores = jnp.where(allowed, scores, -1e30)
            grown = jnp.exp(scores - jnp.max(scores, -1, keepdims=True))
            probs = grown / jnp.sum(grown, -1, keepdims=True)
            probs_ref[n * heads + i] = probs
            o_ref[at, i * HEAD_SIZE : (i + 1) * HEAD_SIZE] = jnp.dot(
                probs.astype(BF16), v, preferred_element_type=F32
            ).astype(BF16)

        @pl.loop(0, model // tile)
        def _(c):
            here = pl.ds(pl.multiple_of(c * tile, tile), tile)
            value = dot_cols(o_ref[at, :], rows_of(weights, c, tile, q_width + 2 * kv_width, q_width))
            part[n, :, :, here] = value.reshape(2, rows, tile)

        total.start(n)

    attend(1 - me.h)
    total.to_mate()
    attend(me.h)
    outs[2].start()
    outs[3].start()
    for z in range(1, LINE - SOON):
        gather.forward(z)
    total.wait()

    def add(at):
        x1 = tok_ref[me.h, me.t, at, :].astype(F32) + total.rows(at)
        x1_ref[at, :] = x1
        factor = lax.rsqrt(jnp.mean(x1 * x1, -1, keepdims=True) + EPS)
        h2_ref[at, :] = (x1 * factor * gain_ref[1:2, :]).astype(BF16)

    row_loop(rows, 32, add)
    outs[4].start()
    outs[5].start()
    total.finish_sends()
    gather.finish(range(LINE - SOON))
    for k in range(1, LINE):
        for way in range(2):

            @pl.when(reach(me, 1 - way, k)[0])
            def _():
                give_down(way, k).wait_send()

            @pl.when(reach(me, way, k)[0])
            def _():
                arrival(down.at[me.z], part_recv.at[way, k])

    for copy in keep + outs:
        copy.wait()


def attention_forward(count, q_width, kv_width, lens, cos, sin, tokens_all, attn_all, up, down_t):
    _, _, rows, model = tokens_all.shape
    wide = 2 * rows
    plane = count // LINE
    kinds = max(6, plane - 1)
    outs = (
        jax.ShapeDtypeStruct((rows, model), F32),
        jax.ShapeDtypeStruct((rows, model), BF16),
        jax.ShapeDtypeStruct((2 * wide, model), BF16),
        jax.ShapeDtypeStruct((2 * wide, q_width + 2 * kv_width), BF16),
        jax.ShapeDtypeStruct((2 * q_width // HEAD_SIZE, wide, wide), F32),
        jax.ShapeDtypeStruct((2 * wide, q_width), BF16),
    )
    return pl.pallas_call(
        functools.partial(attention_forward_kernel, plane),
        name="attention_forward",
        out_shape=(jax.ShapeDtypeStruct((2, model), F32),)
        + outs
        + (
            jax.ShapeDtypeStruct((count - SOON * plane,) + up.shape[1:], BF16),
            jax.ShapeDtypeStruct(down_t.shape, BF16),
        ),
        in_specs=[VMEM] * 3 + [ANY] * 4,
        out_specs=(VMEM,) + (ANY,) * 8,
        scratch_shapes=[
            pltpu.VMEM(attn_all.shape, BF16),
            pltpu.VMEM(tokens_all.shape, BF16),
            *[pltpu.VMEM(out.shape, out.dtype) for out in outs],
            pltpu.VMEM((2, 2, rows, model), F32),
            pltpu.VMEM((2, rows, model), F32),
            pltpu.VMEM((rows, model), BF16),
            pltpu.VMEM((rows, model), BF16),
            DMA((1, LINE, kinds)), DMA((1, LINE, kinds)), DMA((2, LINE)), DMA((2, LINE)), DMA((3,)),
            DMA((3,)), DMA((3 + LINE,)), DMA((6,)),
        ],
        compiler_params=pltpu.CompilerParams(
            collective_id=2, has_side_effects=True, vmem_limit_bytes=60 * MB
        ),
    )(lens, cos, sin, tokens_all, attn_all, up, down_t)


def attention_backward_kernel(
    plane, gain_ref, cos_ref, sin_ref, total_in, x1_in, dm_in, tok_in, h1_in, qkv_in, probs_in, o_in,
    a_ref, gw_ref, sum_ref, h_in, inner_in, ga_ref, w_out, grad_tokens, gain_blocks, gain_parts, weights, own, other, first, second,
    total_ref, x1_ref, dm_ref, tok_ref, h1_ref, qkv_ref, probs_ref, o_ref, rows_in, inner, gw, dx, da, do,
    dqkv, dh1, from_pair, low, from_mate, first_send, first_recv, second_send, second_recv, load_sem,
    other_sem, part_send, part_recv, da_send, da_recv, sum_send, sum_recv, a_sem, keep_sem, grad_sem, in_sem,
):
    me = Place(plane)
    rows, model = tok_ref.shape
    block = weights.shape[1]
    q_width = o_ref.shape[1]
    heads = q_width // HEAD_SIZE
    seq = 2 * rows
    qkv_width = qkv_ref.shape[1]
    kv_width = (qkv_width - q_width) // 2
    kv_heads = kv_width // HEAD_SIZE
    half = HEAD_SIZE // 2
    scale = HEAD_SIZE ** (-0.5)
    summed = PlaneSum(
        me, lambda rank, p: gw.at[(rank - 1) * plane + p] if rank else gw_ref.at[p],
        own, other, first, second,
        (first_send, first_recv, second_send, second_recv, load_sem, other_sem),
    )
    ins = [
        copy_in(src, dst, in_sem.at[i])
        for i, (src, dst) in enumerate(
            (
                (total_in, total_ref), (x1_in, x1_ref), (dm_in.at[me.z, me.t], dm_ref),
                (tok_in.at[me.h, me.t], tok_ref),
                (h1_in, h1_ref), (qkv_in, qkv_ref), (probs_in, probs_ref), (o_in, o_ref),
                (h_in, rows_in), (inner_in, inner),
            )
        )
    ]
    for copy in ins[:3] + ins[8:]:
        copy.start()
    load = pltpu.make_async_copy(a_ref, weights, a_sem)
    load.start()
    for copy in ins[3:8]:
        copy.start()
    summed.load_rank(0)
    greet_all(me, plane * LINE)

    wide = own.shape[2]
    spans = (pl.ds(0, wide), pl.ds(wide, sum_ref.shape[2]))

    def part(rank, kind):
        target = ranked(me, rank)
        way, k = way_to(me, target)
        return remote(
            (own, sum_ref)[kind].at[rank], w_out.at[me.z, :, spans[kind]], part_send.at[way, k, kind],
            part_recv.at[way, k, kind], me.at(target, me.p),
        )

    keeps = [
        copy_in((own, sum_ref)[kind].at[LINE - 1], w_out.at[me.z, :, spans[kind]], keep_sem.at[kind])
        for kind in range(2)
    ]
    das = Quad(me, da, da_send, da_recv)
    dh1_sum = QuadSum(me, dh1, from_pair, low, from_mate, sum_send, sum_recv)

    def mid_norm():
        gain_parts[...] = jnp.zeros_like(gain_parts)

        def act(at):
            x, up = x1_ref[at, :], total_ref[at, :]
            factor = lax.rsqrt(jnp.mean(x * x, -1, keepdims=True) + EPS)
            scaled = up * gain_ref[1:2, :]
            grad = dm_ref[at, :].astype(F32) + (
                factor * scaled - x * factor**3 * jnp.mean(scaled * x, -1, keepdims=True)
            )
            dx[at, :] = grad
            da[me.h, me.t, at, :] = grad.astype(BF16)
            gain_parts[1:2, :] += jnp.sum(up * x * factor, 0, keepdims=True)

        row_loop(rows, 32, act)
        das.start()

    def grad_o():
        load.wait()
        das.finish()

        @pl.loop(0, q_width // HEAD_SIZE)
        def _(c):
            here = pl.multiple_of(c * HEAD_SIZE, HEAD_SIZE)
            value = jnp.dot(
                da[...].reshape(2 * seq, model),
                columns_of(weights, qkv_width + here, HEAD_SIZE),
                preferred_element_type=F32,
            )
            do[:, pl.ds(here, HEAD_SIZE)] = value.astype(BF16)

    def rotate(values, rows_at, start):
        first, second = values[:, :half], values[:, half:]
        cos, sin = cos_ref[...], sin_ref[...]
        dqkv[rows_at, start : start + half] = (first * cos + second * sin).astype(BF16)
        dqkv[rows_at, start + half : start + 2 * half] = (second * cos - first * sin).astype(BF16)

    def grad_heads(n):
        group = heads // kv_heads
        here = slice(n * seq, (n + 1) * seq)
        for m in range(kv_heads):
            at_k = q_width + m * HEAD_SIZE
            at_v = at_k + kv_width
            k = qkv_ref[here, at_k : at_k + HEAD_SIZE]
            v = qkv_ref[here, at_v : at_v + HEAD_SIZE]
            grad_k = grad_v = None
            for i in range(m * group, (m + 1) * group):
                at = slice(i * HEAD_SIZE, (i + 1) * HEAD_SIZE)
                probs = probs_ref[n * heads + i]
                grad_probs = dot_cols(do[here, at], v)
                grad_scores = probs * (
                    grad_probs - jnp.sum(probs * grad_probs, -1, keepdims=True)
                )
                low_scores = grad_scores.astype(BF16)
                rotate(
                    jnp.dot(low_scores, k, preferred_element_type=F32) * scale, here, i * HEAD_SIZE
                )
                more_k = dot_tn(low_scores, qkv_ref[here, at])
                more_v = dot_tn(probs.astype(BF16), do[here, at])
                grad_k = more_k if grad_k is None else grad_k + more_k
                grad_v = more_v if grad_v is None else grad_v + more_v
            rotate(grad_k * scale, here, at_k)
            dqkv[here, at_v : at_v + HEAD_SIZE] = grad_v.astype(BF16)

    tile = 512

    def grad_h1():
        @pl.loop(0, model // tile)
        def _(n):
            here = pl.ds(pl.multiple_of(n * tile, tile), tile)
            value = dot_cols(dqkv[...], rows_of(weights, n, tile, 0, qkv_width))
            dh1[:, :, :, here] = value.reshape(2, 2, rows, tile)

        for h in range(2):
            dh1_sum.start(h)

    def keep_grads(n):
        per = tile // block
        return pltpu.make_async_copy(
            weights.at[pl.ds(n * per, per)], ga_ref.at[pl.ds(n * per, per)], grad_sem.at[n]
        )

    def grads():
        @pl.loop(0, model // tile)
        def _(n):
            here = pl.ds(pl.multiple_of(n * tile, tile), tile)
            there = pl.ds(n * (tile // block), tile // block)
            left = h1_ref[:, here].T
            for c in range(qkv_width // tile):
                at = slice(c * tile, (c + 1) * tile)
                value = jnp.dot(left, dqkv[:, at], preferred_element_type=F32)
                weights[there, :, at] = value.astype(BF16).reshape(tile // block, block, tile)
            left = da[:, :, :, here].reshape(2 * seq, tile).T
            for c in range(q_width // tile):
                at = slice(c * tile, (c + 1) * tile)
                value = jnp.dot(left, o_ref[:, at], preferred_element_type=F32)
                at = slice(qkv_width + c * tile, qkv_width + (c + 1) * tile)
                weights[there, :, at] = value.astype(BF16).reshape(tile // block, block, tile)

        for n in range(model // tile):
            keep_grads(n).start()

    def in_norm():
        dh1_sum.wait()

        def act(at):
            x = tok_ref[at, :].astype(F32)
            up = dh1_sum.rows(at)
            factor = lax.rsqrt(jnp.mean(x * x, -1, keepdims=True) + EPS)
            scaled = up * gain_ref[0:1, :]
            grad_tokens[at, :] = dx[at, :] + (
                factor * scaled - x * factor**3 * jnp.mean(scaled * x, -1, keepdims=True)
            )
            gain_parts[0:1, :] += jnp.sum(up * x * factor, 0, keepdims=True)

        row_loop(rows, 32, act)

    summed.begin(0)
    for rank in range(LINE - 1):
        part(rank, 1).start()
    keeps[1].start()
    def mlp_grads(rank):
        per = plane * block
        targets = [(0, gw, 0), (1, gw, inner.shape[1])]
        z = ranked(me, rank)
        grad_rows(z * per, per, rows_in, inner, 0, targets, (rank - 1) * plane)
        summed.load_rank(rank)

    for copy in ins[:3]:
        copy.wait()
    mid_norm()
    for copy in ins[8:]:
        copy.wait()
    mlp_grads(1)
    summed.middle(0)
    summed.begin(1)
    mlp_grads(2)
    das.forward()
    for copy in ins[3:8]:
        copy.wait()
    summed.end(0)
    part(0, 0).start()
    grad_o()
    summed.middle(1)
    summed.begin(2)
    grad_heads(0)
    grad_heads(1)
    mlp_grads(3)
    summed.end(1)
    part(1, 0).start()
    grad_h1()
    summed.middle(2)
    summed.begin(3)
    dh1_sum.to_mate()
    grads()
    summed.end(2)
    part(2, 0).start()
    summed.middle(3)
    in_norm()
    summed.end(3)

    span = model // gain_blocks.shape[0]
    gain_blocks[...] = jnp.zeros_like(gain_blocks)
    for d in range(gain_blocks.shape[0]):
        gain_blocks[d, 0:2, :span] = gain_parts[:, d * span : (d + 1) * span]
    keeps[0].start()
    for kind in range(2):
        for rank in range(LINE - 1):
            part(rank, kind).wait_send()
        for way, k in FAR_FIRST:

            @pl.when(reach(me, way, k)[0])
            def _():
                arrival(w_out.at[me.z, :, spans[kind]], part_recv.at[way, k, kind])

    summed.finish()
    das.finish_sends()
    dh1_sum.finish_sends()
    for n in range(model // tile):
        keep_grads(n).wait()
    for copy in keeps:
        copy.wait()


def attention_backward(
    count, gains, cos, sin, total, x1, dm_all, tokens_all, h1, qkv, probs, o, attn_all, grad_mlp, first_sum, rows_in,
    inner,
):
    _, _, rows, model = tokens_all.shape
    _, block, _ = attn_all.shape
    buffers, sems = PlaneSum.scratch(count, block, grad_mlp.shape[2])
    return pl.pallas_call(
        functools.partial(attention_backward_kernel, count // LINE),
        name="attention_backward",
        out_shape=(
            jax.ShapeDtypeStruct(attn_all.shape, BF16),
            jax.ShapeDtypeStruct((LINE, block, grad_mlp.shape[2] + first_sum.shape[2]), BF16),
            jax.ShapeDtypeStruct((rows, model), F32),
            jax.ShapeDtypeStruct((count, 8, max(128, model // count)), F32),
        ),
        in_specs=[VMEM] * 3 + [ANY] * 13,
        out_specs=(ANY, ANY, VMEM, VMEM),
        scratch_shapes=[
            pltpu.VMEM((2, model), F32),
            pltpu.VMEM(attn_all.shape, BF16),
            *buffers,
            *[
                pltpu.VMEM(ref.shape, ref.dtype)
                for ref in (total, x1, dm_all[0, 0], dm_all[0, 0], h1, qkv, probs, o, rows_in, inner)
            ],
            pltpu.VMEM(((LINE - 1) * grad_mlp.shape[0],) + grad_mlp.shape[1:], BF16),
            pltpu.VMEM((rows, model), F32),
            pltpu.VMEM((2, 2, rows, model), BF16),
            pltpu.VMEM(o.shape, BF16),
            pltpu.VMEM(qkv.shape, BF16),
            pltpu.VMEM((2, 2, rows, model), F32),
            pltpu.VMEM((2, rows, model), F32),
            pltpu.VMEM((rows, model), BF16),
            pltpu.VMEM((rows, model), BF16),
            *sems,
            DMA((2, LINE, 2)), DMA((2, LINE, 2)), DMA((3,)), DMA((3,)), DMA((3,)), DMA((3,)), DMA, DMA((2,)),
            DMA((model // 512,)), DMA((10,)),
        ],
        compiler_params=pltpu.CompilerParams(
            collective_id=3, has_side_effects=True, vmem_limit_bytes=60 * MB
        ),
    )(gains, cos, sin, total, x1, dm_all, tokens_all, h1, qkv, probs, o, attn_all, grad_mlp, first_sum, rows_in, inner)


def grad_sum_kernel(
    count, gain_ref, x1_in, ga_ref, out_ref, a_out, output, gain_out, own, other, first, second, x1_ref,
    landed, out_own, out_pair, out_line, gain_in, gain_pair, first_send, first_recv, second_send, second_recv,
    load_sem, other_sem, part_send, part_recv, out_send, out_recv, load_out_sem, pair_send, pair_recv, gain_send, gain_recv,
):
    plane = count // LINE
    me = Place(plane)
    rows = a_out.shape[1]
    summed = PlaneSum(
        me, ga_ref, own, other, first, second,
        (first_send, first_recv, second_send, second_recv, load_sem, other_sem),
    )

    class Line:
        def __init__(self, held, landing, send, recv):
            self.held, self.landing, self.send, self.recv = held, landing, send, recv

        def pass_on(self, rank):
            way, k = way_to(me, ranked(me, rank))
            ahead = jnp.where(way == 0, me.z + 1, me.z - 1)
            return remote(
                self.held(rank), self.landing.at[way, k - 1], self.send.at[way, k],
                self.recv.at[way, k - 1], me.at(ahead, me.p),
            )

        def step(self, rank):
            way, k = way_to(me, ranked(me, rank))
            before = jnp.where(way == 0, me.z, LINE - 1 - me.z)
            held = self.held(rank)

            @pl.when(before > 0)
            def _():
                arrival(self.landing.at[way, k], self.recv.at[way, k])
                add_rows(held, (held, self.landing.at[way, k]), held.shape[0])

            self.pass_on(rank).start()

        def total(self, act):
            for way in range(2):

                @pl.when(reach(me, way, 1)[0])
                def _():
                    arrival(self.landing.at[way, 0], self.recv.at[way, 0])
                    act(self.landing.at[way, 0])

        def finish(self):
            for rank in range(LINE - 1):
                self.pass_on(rank).wait_send()

    def part(rank):
        target = ranked(me, rank)
        way, k = way_to(me, target)
        return remote(
            own.at[rank], landed.at[me.z], part_send.at[way, k], part_recv.at[way, k],
            me.at(target, me.p),
        )

    outs = Line(lambda rank: out_own.at[ranked(me, rank)], out_line, out_send, out_recv)
    summed.load_all()
    load_out = copy_in(out_ref.at[:, me.t], out_own, load_out_sem.at[0])
    load_out.start()
    load_x1 = copy_in(x1_in, x1_ref, load_out_sem.at[1])
    load_x1.start()
    greet_all(me, count)

    def give_gain(step):
        target = lax.rem(me.d + step, count)
        return remote(
            gain_ref.at[target], gain_in.at[step], gain_send.at[step], gain_recv.at[step], (target, me.t)
        )

    summed.begin(0)
    for step in range(1, count):
        give_gain(step).start()
    pairs = [
        remote(
            out_ref.at[ranked(me, rank), 1 - me.t], out_pair.at[ranked(me, rank)], pair_send.at[rank],
            pair_recv.at[rank], me.sibling(),
        )
        for rank in range(LINE)
    ]
    for copy in pairs:
        copy.start()
    load_out.wait()
    def out_step(rank):
        z = ranked(me, rank)
        pairs[rank].wait_recv()
        add_rows(out_own.at[z], (out_own.at[z], out_pair.at[z]), out_own.shape[1])
        if rank < LINE - 1:

            @pl.when(jnp.logical_or(me.z == 0, me.z == LINE - 1))
            def _():
                outs.step(rank)

    out_step(0)
    at_end = jnp.logical_or(me.z == 0, me.z == LINE - 1)

    def out_start(at):
        x1_ref[at, :] = x1_ref[at, :] + out_own[me.z, at, :].astype(F32)

    def add_out(landed):
        def act(at):
            x1_ref[at, :] = x1_ref[at, :] + landed[at, :].astype(F32)

        row_loop(output.shape[0], 16, act)

    def out_end(at):
        output[at, :] = x1_ref[at, :].astype(BF16)

    for rank in range(LINE):
        summed.middle(rank)
        if rank + 1 < LINE:
            summed.begin(rank + 1)
            out_step(rank + 1)
        else:
            load_x1.wait()
            total = gain_ref[me.d]
            for step in range(1, count):
                give_gain(step).wait()
                total += gain_in[step]
            gain_pair[0] = total
            swap = remote(
                gain_pair.at[0], gain_pair.at[1], gain_send.at[0], gain_recv.at[0], me.sibling()
            )
            swap.start()
            swap.wait()
            gain_out[...] = gain_pair[0] + gain_pair[1]
        summed.end(rank)
        if rank < LINE - 1:
            part(rank).start()
        if 0 < rank < LINE - 1:
            @pl.when(jnp.logical_not(at_end))
            def _():
                for late in (range(rank - 1, rank) if rank < LINE - 2 else range(rank - 1, LINE - 1)):
                    outs.step(late)

    row_loop(output.shape[0], 16, out_start)
    outs.total(add_out)
    row_loop(output.shape[0], 16, out_end)
    keep = copy_in(own.at[LINE - 1], landed.at[me.z], load_out_sem.at[2])
    keep.start()
    for way, k in FAR_FIRST:
        have, z = reach(me, way, k)

        @pl.when(have)
        def _():
            arrival(landed.at[z], part_recv.at[way, k])

    keep.wait()
    for h in range(2):
        add_rows(a_out.at[h], tuple(landed.at[z] for z in range(h, LINE, 2)), rows)
    for rank in range(LINE - 1):
        part(rank).wait_send()
    for copy in pairs:
        copy.wait_send()
    outs.finish()
    summed.finish()


def grad_sum(count, x1, ga, out_parts, gains):
    _, block, width = ga.shape
    _, _, rows, model = out_parts.shape
    buffers, sems = PlaneSum.scratch(count, block, width)
    return pl.pallas_call(
        functools.partial(grad_sum_kernel, count),
        name="grad_sum",
        out_shape=(
            jax.ShapeDtypeStruct((2, block, width), F32),
            jax.ShapeDtypeStruct((rows, model), BF16),
            jax.ShapeDtypeStruct(gains.shape[1:], F32),
        ),
        in_specs=[VMEM] + [ANY] * 3,
        out_specs=(VMEM,) * 3,
        scratch_shapes=[
            *buffers,
            pltpu.VMEM((rows, model), F32),
            pltpu.VMEM((LINE, block, width), BF16),
            pltpu.VMEM((LINE, rows, model), BF16),
            pltpu.VMEM((LINE, rows, model), BF16),
            pltpu.VMEM((2, LINE - 1, rows, model), BF16),
            pltpu.VMEM(gains.shape, F32),
            pltpu.VMEM((2,) + gains.shape[1:], F32),
            *sems,
            DMA((2, LINE)), DMA((2, LINE)), DMA((2, LINE)), DMA((2, LINE)), DMA((3,)), DMA((LINE,)),
            DMA((LINE,)), DMA((count,)), DMA((count,)),
        ],
        compiler_params=pltpu.CompilerParams(
            collective_id=4, has_side_effects=True, vmem_limit_bytes=60 * MB
        ),
    )(gains, x1, ga, out_parts)


def layouts_kernel(
    gain_ref, a_ref, mlp_ref, output_ref, tokens_ref, gain_attn, gain_mlp, q_out, k_out, v_out, o_out, gate_out, up_out, down_out,
    output_out, tokens_out, a_v, mlp_v, output_v, tokens_v, q_v, k_v, v_v, o_v, gate_v, up_v, down_v,
    in_sem, out_sem,
):
    ins = [
        copy_in(src, dst, in_sem.at[i])
        for i, (src, dst) in enumerate(
            ((mlp_ref, mlp_v), (a_ref, a_v), (tokens_ref, tokens_v), (output_ref, output_v))
        )
    ]
    for copy in ins:
        copy.start()
    sent = []

    def give(src, dst):
        sent.append(copy_in(src, dst, out_sem.at[len(sent)]))
        sent[-1].start()

    span = gain_attn.shape[1]
    gain_attn[...] = gain_ref[0:1, :span]
    gain_mlp[...] = gain_ref[1:2, :span]
    units = mlp_v.shape[2] // 3
    ins[0].wait()
    for z in range(LINE):
        here = pl.ds(z * units, units)
        gate_v[:, here] = mlp_v[z, :, :units].astype(F32)
        give(gate_v.at[:, here], gate_out.at[:, here])
        up_v[:, here] = mlp_v[z, :, units : 2 * units].astype(F32)
        give(up_v.at[:, here], up_out.at[:, here])
        down_v[here, :] = mlp_v[z, :, 2 * units :].astype(F32).T
        give(down_v.at[here], down_out.at[here])
    for copy in ins[1:]:
        copy.wait()
    give(tokens_v, tokens_out)
    give(output_v, output_out)
    start = 0
    for src, dst in ((q_v, q_out), (k_v, k_out), (v_v, v_out)):
        half = src.shape[1] // 2
        for h in range(2):
            src[:, h * half : (h + 1) * half] = a_v[h, :, start : start + half]
        start += half
        give(src, dst)
    half = o_v.shape[0] // 2
    for h in range(2):
        o_v[h * half : (h + 1) * half, :] = a_v[h, :, start:].T
    give(o_v, o_out)
    for copy in sent:
        copy.wait()


def layouts(q_width, kv_width, gain_sum, a, mlp, output, grad_tokens):
    block = a.shape[1]
    hidden = LINE * (mlp.shape[2] // 3)
    outs = (
        jax.ShapeDtypeStruct((block, q_width), F32),
        jax.ShapeDtypeStruct((block, kv_width), F32),
        jax.ShapeDtypeStruct((block, kv_width), F32),
        jax.ShapeDtypeStruct((q_width, block), F32),
        jax.ShapeDtypeStruct((block, hidden), F32),
        jax.ShapeDtypeStruct((block, hidden), F32),
        jax.ShapeDtypeStruct((hidden, block), F32),
    )
    ins = (a, mlp, output, grad_tokens)
    return pl.pallas_call(
        layouts_kernel,
        name="layouts",
        out_shape=(jax.ShapeDtypeStruct((1, block), F32),) * 2
        + outs
        + tuple(jax.ShapeDtypeStruct(ref.shape, ref.dtype) for ref in ins[2:]),
        in_specs=[VMEM] + [ANY] * 4,
        out_specs=(VMEM,) * 2 + (ANY,) * 9,
        scratch_shapes=[
            *[pltpu.VMEM(ref.shape, ref.dtype) for ref in ins + outs],
            DMA((4,)), DMA((3 * LINE + 6,)),
        ],
        compiler_params=pltpu.CompilerParams(vmem_limit_bytes=60 * MB),
    )(gain_sum, *ins)


def shards(
    tokens, w_query, key_weight, value_weight, w_out, gain_attn, w_gate, w_up, w_down, gain_mlp,
    cotangent, lengths, seq_of_group,
):
    count = lax.axis_size("dp")
    rows, q_width = w_query.shape
    kv_width = key_weight.shape[1]
    model = rows * count
    cos, sin = rope_tables(tokens.shape[0] * lax.axis_size("tensor"), HEAD_SIZE)
    lanes = -rows % 128
    gains = jnp.pad(jnp.stack([gain_attn, gain_mlp]), ((0, 14), (0, lanes)))
    attn_all, gate_all, up_soon, up, down_t, gains_all, tokens_all, dm_all = gather_all(
        count, lengths, seq_of_group, gains,
        (w_query, key_weight, value_weight, w_out, w_gate, w_up, w_down), tokens, cotangent,
    )
    gains_full, x1, h2, h1, qkv, probs, attended, up_rest, down = attention_forward(
        count, q_width // 2, kv_width // 2, gains_all, cos, sin, tokens_all, attn_all, up, down_t
    )
    grad_h2, out_parts, grad_mlp_w, down_sum, rows_in, inner = feed_forward(
        count, h2, dm_all.reshape(-1, model), gate_all, up_soon, up_rest, down
    )
    grad_attn_w, mlp_sum, grad_tokens, gain_parts = attention_backward(
        count, gains_full, cos, sin, grad_h2, x1, dm_all, tokens_all, h1, qkv, probs, attended, attn_all,
        grad_mlp_w, down_sum, rows_in, inner,
    )
    attn_sum, output, gain_sum = grad_sum(count, x1, grad_attn_w, out_parts, gain_parts)
    (
        grad_gain_attn, grad_gain_mlp, grad_query, grad_key, grad_value, grad_out, grad_gate, grad_up,
        grad_down, output, grad_tokens,
    ) = layouts(q_width, kv_width, gain_sum, attn_sum, mlp_sum, output, grad_tokens)
    return (
        output, grad_tokens, grad_query, grad_key, grad_value, grad_out, grad_gain_attn.reshape(rows),
        grad_gate, grad_up, grad_down, grad_gain_mlp.reshape(rows),
    )


def solution(mesh):
    both = P(("dp", "tensor"), None)
    row = P("dp", "tensor")
    column = P("tensor", "dp")
    in_specs = (
        both, row, row, row, column, P("dp"), row, row, column, P("dp"), both, P(), P("dp"),
    )
    out_specs = (both, both, row, row, row, column, P("dp"), row, row, column, P("dp"))
    return jax.shard_map(shards, mesh=mesh, in_specs=in_specs, out_specs=out_specs, check_vma=False)
```

```python
import functools
import math

import jax
import jax.numpy as jnp
import numpy as np
from jax import lax
from jax.experimental import pallas as pl
from jax.experimental.pallas import tpu as pltpu
from jax.sharding import PartitionSpec as P

HEAD_SIZE = 256
EPS = 1e-06
THETA = 1000042.0
LINE = 4
MESH = pl.DeviceIdType.MESH
BF16 = jnp.bfloat16
F32 = jnp.float32
MB = 1024 * 1024
AHEAD = 4
SOON = 2


def rope_tables(count, head_dim):
    half = head_dim // 2
    index = np.arange(half, dtype=np.float32)
    freqs = np.exp(index * np.float32(-2.0 * math.log(THETA) / head_dim))
    angles = np.arange(count, dtype=np.float32)[:, None] * freqs[None, :]
    return np.cos(angles), np.sin(angles)


def dot_tn(left, right):
    return lax.dot_general(left, right, (((0,), (0,)), ((), ())), preferred_element_type=F32)


class Place:
    def __init__(self, plane):
        self.d = lax.axis_index("dp")
        self.t = lax.axis_index("tensor")
        self.plane = plane
        self.z = lax.div(self.d, plane)
        self.p = lax.rem(self.d, plane)
        self.h = lax.rem(self.z, 2)
        if plane == 4:
            x = lax.rem(self.p, 2)
            y = lax.div(self.p, 2)
            self.px = 2 * y + 1 - x
            self.py = 2 * (1 - y) + x
            self.pd = 2 * (1 - y) + 1 - x

    def at(self, z, p):
        return (z * self.plane + p, self.t)

    def sibling(self):
        return (self.d, 1 - self.t)

    def mate(self):
        return self.at(self.z + 1 - 2 * self.h, self.p)


def remote(src, dst, send, recv, device):
    return pltpu.make_async_remote_copy(
        src_ref=src, dst_ref=dst, send_sem=send, recv_sem=recv, device_id=device, device_id_type=MESH
    )


def arrival(ref, sem):
    pltpu.make_async_copy(ref, ref, sem).wait()


def greet_all(me, count):
    barrier = pltpu.get_barrier_semaphore()
    for step in range(1, count):
        pl.semaphore_signal(
            barrier, inc=1, device_id=(lax.rem(me.d + step, count), me.t), device_id_type=MESH
        )
    pl.semaphore_signal(barrier, inc=1, device_id=me.sibling(), device_id_type=MESH)
    pl.semaphore_wait(barrier, count)


def greet_line(me):
    barrier = pltpu.get_barrier_semaphore()
    for step in range(1, LINE):
        pl.semaphore_signal(
            barrier, inc=1, device_id=me.at(lax.rem(me.z + step, LINE), me.p), device_id_type=MESH
        )
    pl.semaphore_signal(barrier, inc=1, device_id=me.sibling(), device_id_type=MESH)
    pl.semaphore_wait(barrier, LINE)


def reach(me, way, k):
    return (me.z >= k, me.z - k) if way == 0 else (me.z + k < LINE, me.z + k)


class Chain:
    def __init__(self, me, first, held, send, recv):
        self.me, self.first, self.held, self.send, self.recv = me, first, held, send, recv

    def copy(self, way, k):
        me = self.me
        _, origin = reach(me, way, k)
        target = me.z + 1 if way == 0 else me.z - 1
        src = self.first if k == 0 else self.held(origin)
        return remote(
            src, self.held(origin), self.send.at[way, k], self.recv.at[way, k + 1], me.at(target, me.p)
        )

    def goes(self, way, k):
        have, _ = reach(self.me, way, k)
        ahead, _ = reach(self.me, 1 - way, 1)
        return jnp.logical_and(have, ahead)

    def start(self, way, k):
        if k < LINE - 1:

            @pl.when(self.goes(way, k))
            def _():
                self.copy(way, k).start()

    def wait_block(self, way, k):
        _, origin = reach(self.me, way, k)
        arrival(self.held(origin), self.recv.at[way, k])

    def finish(self):
        for way in range(2):
            for k in range(LINE - 1):

                @pl.when(self.goes(way, k))
                def _():
                    self.copy(way, k).wait_send()


class PlaneGather:
    def __init__(self, me, job, held, rows, send, recv):
        self.me, self.job, self.held, self.send, self.recv = me, job, held, send, recv
        self.half = rows // 2

    def piece(self, z, p, half):
        return self.held.at[z * self.me.plane + p, pl.ds(half * self.half, self.half)]

    def copy(self, z, kind, first=None):
        me = self.me
        if me.plane != 4:
            ref = first if first is not None else self.held.at[z * me.plane + me.p]
            target = lax.rem(me.p + kind + 1, me.plane)
            dst = self.held.at[z * me.plane + me.p]
        else:
            owner = (me.p, me.p, me.p, me.p, me.px, me.py)[kind]
            half = (0, 1, 1, 0, 0, 1)[kind]
            target = (me.px, me.px, me.py, me.py, me.py, me.px)[kind]
            dst = self.piece(z, owner, half)
            ref = dst if first is None else first.at[pl.ds(half * self.half, self.half)]
        return remote(
            ref, dst, self.send.at[self.job, z, kind], self.recv.at[self.job, z, kind], me.at(me.z, target)
        )

    def start(self, z, first=None):
        kinds = (0, 2, 1, 3) if self.me.plane == 4 else range(self.me.plane - 1)
        for kind in kinds:
            self.copy(z, kind, first).start()

    def forward(self, z):
        if self.me.plane == 4:
            self.copy(z, 0).wait_recv()
            self.copy(z, 4).start()
            self.copy(z, 2).wait_recv()
            self.copy(z, 5).start()

    def finish(self, zs=range(LINE)):
        kinds = 6 if self.me.plane == 4 else self.me.plane - 1
        for z in zs:
            for kind in range(kinds):
                copy = self.copy(z, kind)
                if self.me.plane != 4 or kind not in (0, 2):
                    copy.wait_recv()
                copy.wait_send()


class Quad:
    def __init__(self, me, blocks, send, recv):
        self.me, self.blocks, self.send, self.recv = me, blocks, send, recv

    def copy(self, i, first=None):
        me = self.me
        dst = self.blocks.at[me.h if i < 2 else 1 - me.h, me.t]
        device = me.mate() if i == 1 else me.sibling()
        return remote(dst if first is None else first, dst, self.send.at[i], self.recv.at[i], device)

    def start(self, first=None):
        for i in (1, 0):
            self.copy(i, first).start()

    def forward(self):
        arrival(self.blocks.at[1 - self.me.h, self.me.t], self.recv.at[1])
        self.copy(2).start()

    def finish(self):
        me = self.me
        arrival(self.blocks.at[me.h, 1 - me.t], self.recv.at[0])
        arrival(self.blocks.at[1 - me.h, 1 - me.t], self.recv.at[2])

    def finish_sends(self):
        for i in range(3):
            self.copy(i).wait_send()


class QuadSum:
    def __init__(self, me, part, from_pair, low, from_mate, send, recv):
        self.me, self.part, self.from_pair, self.low, self.from_mate = me, part, from_pair, low, from_mate
        self.send, self.recv = send, recv
        self.mate = remote(low, from_mate, send.at[2], recv.at[2], me.mate())

    def pair(self, h):
        me = self.me
        return remote(
            self.part.at[h, 1 - me.t], self.from_pair.at[h], self.send.at[h], self.recv.at[h], me.sibling()
        )

    def start(self, h):
        self.pair(h).start()

    def to_mate(self):
        me = self.me
        self.pair(1 - me.h).wait_recv()

        def act(at):
            total = self.part[1 - me.h, me.t, at, :] + self.from_pair[1 - me.h, at, :]
            self.low[at, :] = total.astype(BF16)

        row_loop(self.low.shape[0], 32, act)
        self.mate.start()

    def wait(self):
        self.pair(self.me.h).wait_recv()
        self.mate.wait_recv()

    def rows(self, at):
        me = self.me
        total = self.part[me.h, me.t, at, :] + self.from_pair[me.h, at, :]
        return total + self.from_mate[at, :].astype(F32)

    def finish_sends(self):
        for h in range(2):
            self.pair(h).wait_send()
        self.mate.wait_send()


def copy_in(src, dst, sem):
    return pltpu.make_async_copy(src, dst, sem)


def row_loop(rows, step, act):
    @pl.loop(0, rows // step)
    def _(i):
        act(pl.ds(pl.multiple_of(i * step, step), step))


def gather_kernel(
    count, len_ref, seq_ref, gain_ref, q_ref, k_ref, v_ref, o_ref, g_ref, u_ref, d_ref, tok_ref, cot_ref,
    a_all, gate_all, up_soon, up, down_t, gain_all, tok_all, dm_all, o_v, a_v, g_v, u_v, d_v, d_t, dm,
    gain_v, chain_send, chain_recv, part_send, part_recv, plane_send, plane_recv, gain_send, gain_recv,
    pair_send, pair_recv, tok_send, tok_recv, local_sem,
):
    plane = count // LINE
    me = Place(plane)
    rows = q_ref.shape[0]
    units = g_ref.shape[1] // LINE
    q_half, kv_half = q_ref.shape[1] // 2, k_ref.shape[1] // 2
    qkv_half = q_half + 2 * kv_half

    def columns(ref, z):
        return ref.at[:, pl.ds(pl.multiple_of(z * units, units), units)]

    local = [copy_in(o_ref, o_v, local_sem.at[0])]
    for h in range(2):
        start = 0
        for ref, width in ((q_ref, q_half), (k_ref, kv_half), (v_ref, kv_half)):
            src = ref.at[:, pl.ds(h * width, width)]
            local.append(copy_in(src, a_v.at[h, :, pl.ds(start, width)], local_sem.at[len(local)]))
            start += width
    early = len(local)
    for src, dst in (
        (d_ref, d_v), (cot_ref, dm), (columns(g_ref, me.z), g_v), (columns(u_ref, me.z), u_v),
        (tok_ref, tok_all.at[me.h, me.t]),
    ):
        local.append(copy_in(src, dst, local_sem.at[len(local)]))
    for copy in local[:early]:
        copy.start()
    keep_a = copy_in(a_v.at[me.h], a_all.at[me.d], local_sem.at[12])
    keep_down = copy_in(d_t, down_t, local_sem.at[13])
    keep_dm = copy_in(dm, dm_all.at[me.z, me.t], local_sem.at[14])
    keep_gate = copy_in(g_v, gate_all.at[me.d], local_sem.at[15])
    keep_up = copy_in(u_v, up.at[me.z], local_sem.at[16])
    keep_gain = copy_in(gain_v, gain_all.at[me.d], local_sem.at[17])

    dms = Chain(me, dm, lambda z: dm_all.at[z, me.t], chain_send, chain_recv)
    planes = (
        PlaneGather(me, 0, a_all, rows, plane_send, plane_recv),
        PlaneGather(me, 1, gate_all, rows, plane_send, plane_recv),
        PlaneGather(me, 2, up_soon, rows, plane_send, plane_recv),
    )

    def part(way, k, kind):
        _, target = reach(me, 1 - way, k)
        src = columns((g_ref, u_ref)[kind - 1], target) if kind else a_v.at[lax.rem(target, 2)]
        dst = (a_all.at[me.d], gate_all.at[me.d], up.at[me.z])[kind]
        return remote(
            src, dst, part_send.at[way, k, kind], part_recv.at[way, k, kind], me.at(target, me.p)
        )

    def pair(z, first=None):
        src = dm_all.at[z, me.t] if first is None else first
        return remote(src, dm_all.at[z, me.t], pair_send.at[z], pair_recv.at[z], me.sibling())

    def keep_soon(soon, src):
        return copy_in(src, up_soon.at[soon * plane + me.p], local_sem.at[18 + soon])

    def start_parts(k, kinds):
        for way in range(2):

            @pl.when(reach(me, 1 - way, k)[0])
            def _():
                for kind in kinds:
                    part(way, k, kind).start()

    def each(k, act):
        for way in range(2):
            have, z = reach(me, way, k)

            @pl.when(have)
            def _():
                act(way, k, z)

    def attn_step(way, k, z):
        arrival(a_all.at[z * plane + me.p], part_recv.at[way, k, 0])
        planes[0].start(z)

    def gate_step(way, k, z):
        arrival(gate_all.at[z * plane + me.p], part_recv.at[way, k, 1])
        planes[1].start(z)

    def up_step(way, k, z):
        arrival(up.at[z], part_recv.at[way, k, 2])

        @pl.when(z == me.z + 1 - 2 * me.h)
        def _():
            planes[2].start(1 - me.h, up.at[z])
            keep_soon(1 - me.h, up.at[z]).start()

    def dm_step(way, k, z):
        dms.wait_block(way, k)
        pair(z).start()

    def give_gain(step):
        target = lax.rem(me.d + step, count)
        return remote(
            gain_v, gain_all.at[me.d], gain_send.at[step], gain_recv.at[step], (target, me.t)
        )

    chosen = len_ref[seq_ref[0]]
    kind_of = lax.broadcasted_iota(jnp.int32, gain_ref.shape, 0)
    gain_v[...] = jnp.where(kind_of == 2, chosen.astype(F32), gain_ref[...].astype(F32)).astype(BF16)
    local[0].wait()
    for h in range(2):
        a_v[h, :, qkv_half:] = o_v[h * q_half : (h + 1) * q_half, :].T
    greet_all(me, count)
    for copy in local[1:early]:
        copy.wait()
    toks = Quad(me, tok_all, tok_send, tok_recv)
    levels = [(0, 1), (0, 2), (0, 3), (3, 1), (1, 1), (1, 2), (1, 3), (3, 2), (2, 1), (2, 2), (2, 3), (3, 3)]

    def start_level(kind, k):
        if kind < 3:
            start_parts(k, (kind,))
        elif k == 1:
            for way in range(2):
                dms.start(way, 0)
            pair(me.z, dm).start()
        else:
            each(k - 1, lambda way, k, z: dms.start(way, k))

    def finish_level(kind, k):
        each(k, (attn_step, gate_step, up_step, dm_step)[kind])

    def forward_level(kind, k):
        if kind < 2:
            each(k, lambda way, k, z: planes[kind].forward(z))

    for level in levels[:2]:
        start_level(*level)
    planes[0].start(me.z, a_v.at[me.h])
    toks.start(tok_ref)
    for step in range(1, count):
        give_gain(step).start()
    for copy in local[early:]:
        copy.start()
    keep_a.start()
    keep_gain.start()

    local[early].wait()
    for z in range(LINE):
        d_t[z] = d_v[z * units : (z + 1) * units, :].T
    keep_down.start()
    local[early + 1].wait()

    def mask(at):
        value = dm[at, :].astype(F32)
        row = lax.broadcasted_iota(jnp.int32, value.shape, 0) + (me.t * dm.shape[0] + at.start)
        dm[at, :] = jnp.where(row < chosen, value, 0.0).astype(BF16)

    row_loop(dm.shape[0], 32, mask)
    keep_dm.start()

    for i, level in enumerate(levels):
        if i == 0:
            for more in levels[2:AHEAD]:
                start_level(*more)
        finish_level(*level)
        if i + AHEAD < len(levels):
            start_level(*levels[i + AHEAD])
        if level == (0, 1):
            toks.forward()
            planes[0].forward(me.z)
            for copy in local[early + 2 : early + 4]:
                copy.wait()
            keep_gate.start()
            keep_up.start()
            planes[1].start(me.z, g_v)
        if level == (0, 3):
            planes[1].forward(me.z)
        if level == (1, 3):
            planes[2].start(me.h, u_v)
            keep_soon(me.h, u_v).start()
        if level == (3, 3):
            planes[2].forward(me.h)
        if i:
            forward_level(*levels[i - 1])
    planes[2].forward(1 - me.h)

    dms.finish()
    for k in range(1, LINE):
        for way in range(2):

            @pl.when(reach(me, 1 - way, k)[0])
            def _():
                for kind in range(3):
                    part(way, k, kind).wait_send()

    for step in range(1, count):
        give_gain(step).wait()
    toks.finish()
    toks.finish_sends()
    for z in range(LINE):
        pair(z).wait()
    for job, zs in zip(planes, (LINE, LINE, SOON)):
        job.finish(range(zs))
    for soon in range(SOON):
        keep_soon(soon, u_v).wait()
    for copy in local[early + 4 :] + [keep_a, keep_down, keep_dm, keep_gate, keep_up, keep_gain]:
        copy.wait()


ANY = pl.BlockSpec(memory_space=pl.ANY)
VMEM = pl.BlockSpec(memory_space=pltpu.VMEM)
SMEM = pl.BlockSpec(memory_space=pltpu.SMEM)
DMA = pltpu.SemaphoreType.DMA


def gather_all(count, lengths, seq, gains, weights, tokens, cotangent):
    w_query, key_weight, _, w_out, w_gate, _, w_down = weights
    rows, q_width = w_query.shape
    width = q_width + key_weight.shape[1]
    units = w_gate.shape[1] // LINE
    plane = count // LINE
    kinds = max(6, plane - 1)
    return pl.pallas_call(
        functools.partial(gather_kernel, count),
        name="gather_all",
        out_shape=(
            jax.ShapeDtypeStruct((count, rows, width), BF16),
            jax.ShapeDtypeStruct((count, rows, units), BF16),
            jax.ShapeDtypeStruct((plane * SOON, rows, units), BF16),
            jax.ShapeDtypeStruct((LINE, rows, units), BF16),
            jax.ShapeDtypeStruct((LINE, rows, units), BF16),
            jax.ShapeDtypeStruct((count,) + gains.shape, gains.dtype),
            jax.ShapeDtypeStruct((2, 2) + tokens.shape, BF16),
            jax.ShapeDtypeStruct((LINE, 2) + cotangent.shape, BF16),
        ),
        in_specs=[SMEM] * 2 + [VMEM] + [ANY] * 9,
        out_specs=(ANY,) * 8,
        scratch_shapes=[
            pltpu.VMEM(w_out.shape, BF16),
            pltpu.VMEM((2, rows, width), BF16),
            pltpu.VMEM((rows, units), BF16),
            pltpu.VMEM((rows, units), BF16),
            pltpu.VMEM(w_down.shape, BF16),
            pltpu.VMEM((LINE, rows, units), BF16),
            pltpu.VMEM(cotangent.shape, BF16),
            pltpu.VMEM(gains.shape, BF16),
            DMA((2, LINE)), DMA((2, LINE)), DMA((2, LINE, 3)), DMA((2, LINE, 3)),
            DMA((3, LINE, kinds)), DMA((3, LINE, kinds)), DMA((count,)), DMA((count,)),
            DMA((LINE,)), DMA((LINE,)), DMA((3,)), DMA((3,)), DMA((18 + SOON,)),
        ],
        compiler_params=pltpu.CompilerParams(
            collective_id=0, has_side_effects=True, vmem_limit_bytes=60 * MB
        ),
    )(lengths, seq, gains, *weights, tokens, cotangent)


RANKS = ((3, 2, 1, 0), (3, 0, 2, 1), (0, 3, 1, 2), (0, 1, 2, 3))
FAR_FIRST = [(way, k) for k in range(LINE - 1, 0, -1) for way in range(2)]


def ranked(me, rank):
    z = jnp.int32(RANKS[0][rank])
    for at in range(1, LINE):
        z = jnp.where(me.z == at, RANKS[at][rank], z)
    return z


def way_to(me, z):
    down = (z < me.z).astype(jnp.int32)
    return down, jnp.where(z < me.z, me.z - z, z - me.z)


def add_rows(target, terms, rows, start=0):
    step = 16

    @pl.loop(0, rows // step)
    def _(i):
        at = pl.ds(pl.multiple_of(start + i * step, step), step)
        total = terms[0][at].astype(F32)
        for term in terms[1:]:
            total += term[at].astype(F32)
        target[at] = total.astype(target.dtype)


def grad_rows(at, per, left_ref, right_ref, first, targets, there):
    tile = 512
    tokens = left_ref.shape[0]

    @pl.loop(0, per // tile)
    def _(n):
        left = left_ref[:, pl.ds(pl.multiple_of(at + n * tile, tile), tile)].T
        for job, ref, start in targets:
            block, units = ref.shape[1], right_ref.shape[1]
            rows = pl.ds(there + n * (tile // block), tile // block)
            for c in range(units // tile):
                grad = jnp.dot(
                    left, right_ref[pl.ds(first + job * tokens, tokens), c * tile : (c + 1) * tile],
                    preferred_element_type=F32,
                )
                ref[rows, :, start + c * tile : start + (c + 1) * tile] = grad.astype(BF16).reshape(
                    tile // block, block, tile
                )


class PlaneSum:
    def __init__(self, me, grad, own, other, first, second, sems, ranks=range(LINE)):
        self.me, self.grad, self.own, self.other, self.first, self.second = me, grad, own, other, first, second
        (
            self.first_send, self.first_recv, self.second_send, self.second_recv, self.load_sem, self.other_sem,
        ) = sems
        self.ranks = ranks
        self.rows = own.shape[1]
        half = self.rows // 2
        self.half = half
        self.halves = (pl.ds(0, half), pl.ds(half, half))
        self.square = me.plane == 4
        if self.square:
            self.near = (me.px, me.py)
            self.far = (me.py, me.px)

    def slot(self, rank):
        return rank - self.ranks[0]

    def block(self, rank, p):
        if callable(self.grad):
            return self.grad(rank, p)
        return self.grad.at[ranked(self.me, rank) * self.me.plane + p]

    def load(self, rank):
        s = self.slot(rank)
        return pltpu.make_async_copy(self.block(rank, self.me.p), self.own.at[s], self.load_sem.at[s])

    def load_other(self, rank, i):
        s = self.slot(rank)
        return pltpu.make_async_copy(
            self.block(rank, self.far[i]).at[self.halves[i]], self.other.at[s, self.halves[i]],
            self.other_sem.at[s, i],
        )

    def load_rank(self, rank):
        self.load(rank).start()
        if self.square:
            for i in range(2):
                self.load_other(rank, i).start()

    def load_all(self):
        for rank in self.ranks:
            self.load_rank(rank)

    def give(self, rank, i, which):
        me, s = self.me, self.slot(rank)
        if not self.square:
            target = lax.rem(me.p + which + 1, me.plane)
            return remote(
                self.block(rank, target), self.first.at[s, which], self.first_send.at[s, which],
                self.first_recv.at[s, which], me.at(me.z, target),
            )
        owner = (self.near[i], me.pd)[which]
        return remote(
            self.block(rank, owner).at[self.halves[i]], self.first.at[s, which, self.halves[i]],
            self.first_send.at[s, 2 * i + which], self.first_recv.at[s, 2 * i + which],
            me.at(me.z, self.near[i]),
        )

    def give_both(self, rank, i):
        s = self.slot(rank)
        return remote(
            self.other.at[s, self.halves[i]], self.second.at[s, self.halves[i]],
            self.second_send.at[s, i], self.second_recv.at[s, i], self.me.at(self.me.z, self.far[i]),
        )

    def gives(self, rank):
        if self.square:
            return [self.give(rank, i, which) for which in (1, 0) for i in range(2)]
        return [self.give(rank, 0, which) for which in range(self.me.plane - 1)]

    def begin(self, rank):
        for copy in self.gives(rank):
            copy.start()

    def middle(self, rank):
        if not self.square:
            return
        s = self.slot(rank)
        for i in range(2):
            arrival(self.first.at[s, 1, self.halves[i]], self.first_recv.at[s, 2 * i + 1])
            self.load_other(rank, i).wait()
            add_rows(
                self.other.at[s], (self.other.at[s], self.first.at[s, 1]), self.half, i * self.half
            )
            self.give_both(rank, i).start()

    def end(self, rank):
        s = self.slot(rank)
        self.load(rank).wait()
        if self.square:
            for i in range(2):
                arrival(self.first.at[s, 0, self.halves[i]], self.first_recv.at[s, 2 * i])
                arrival(self.second.at[s, self.halves[i]], self.second_recv.at[s, i])
            terms = (self.first.at[s, 0], self.second.at[s])
        else:
            for which in range(self.me.plane - 1):
                arrival(self.first.at[s, which], self.first_recv.at[s, which])
            terms = tuple(self.first.at[s, which] for which in range(self.me.plane - 1))
        add_rows(self.own.at[s], (self.own.at[s],) + terms, self.rows)

    def finish(self):
        for rank in self.ranks:
            for copy in self.gives(rank):
                copy.wait_send()
            if self.square:
                for i in range(2):
                    self.give_both(rank, i).wait_send()

    @staticmethod
    def scratch(count, rows, width, ranks=LINE):
        plane = count // LINE
        square = plane == 4
        slots = 2 if square else plane - 1
        small = (ranks, rows, width) if square else (1, 16, 128)
        return [
            pltpu.VMEM((ranks, rows, width), BF16),
            pltpu.VMEM(small, BF16),
            pltpu.VMEM((ranks, slots, rows, width), BF16),
            pltpu.VMEM(small, BF16),
        ], [
            DMA((ranks, max(4, slots))), DMA((ranks, max(4, slots))), DMA((ranks, 2)), DMA((ranks, 2)),
            DMA((ranks,)), DMA((ranks, 2)),
        ]


def dot_cols(left, right):
    return lax.dot_general(left, right, (((1,), (1,)), ((), ())), preferred_element_type=F32)


def feed_forward_kernel(
    plane, h_ref, dm_ref, gate_ref, up_soon, up_rest, down, total_ref, out_ref, grad_ref, sum_ref,
    h_out, inner_out, rows_in, weights, inner, down_grad, part,
    from_pair, from_line, own, other, first, second, first_send, first_recv, second_send, second_recv,
    own_sem, other_sem, chain_send, chain_recv, pass_send, pass_recv, pair_send, pair_recv,
    line_send, line_recv, plane_send, plane_recv, load_sem, dm_sem, grad_sem, out_sem, sum_sem,
):
    me = Place(plane)
    rows, model = h_ref.shape
    units = inner.shape[1]
    wide = 2 * rows
    tokens = LINE * wide
    block = down.shape[1]
    soon = up_soon.shape[0]
    tile = 512

    def slot(z, t):
        return rows_in.at[pl.ds(pl.multiple_of((z * 2 + t) * rows, rows), rows)]

    loads = [
        copy_in(gate_ref, weights.at[:, :, pl.ds(0, units)], load_sem.at[0]),
        copy_in(
            up_soon, weights.at[pl.ds((me.z - me.h) * plane, soon), :, pl.ds(units, units)], load_sem.at[2]
        ),
        copy_in(
            up_rest, weights.at[pl.ds((SOON - me.z + me.h) * plane, soon), :, pl.ds(units, units)],
            load_sem.at[3],
        ),
    ]
    own_down = [
        copy_in(
            down.at[z], weights.at[z * plane + me.p, :, pl.ds(2 * units, units)], load_sem.at[4 + z]
        )
        for z in range(LINE)
    ]
    for load in loads:
        load.start()
    load_dm = pltpu.make_async_copy(dm_ref, rows_in.at[pl.ds(tokens, tokens)], dm_sem)
    load_dm.start()
    keep = pltpu.make_async_copy(h_ref, slot(me.z, me.t), load_sem.at[1])
    keep.start()
    greet_all(me, plane * LINE)
    gather = PlaneGather(
        me, 0, weights.at[:, :, pl.ds(2 * units, units)], block, plane_send, plane_recv
    )
    summed = PlaneSum(
        me, down_grad, own, other, first, second,
        (first_send, first_recv, second_send, second_recv, own_sem, other_sem),
    )
    chain = Chain(me, h_ref, lambda z: slot(z, me.t), chain_send, chain_recv)

    def share(z, first=None):
        src = slot(z, me.t) if first is None else first
        return remote(src, slot(z, me.t), pass_send.at[z], pass_recv.at[z], me.sibling())

    for way in range(2):
        chain.start(way, 0)
    share(me.z, h_ref).start()
    for z in range(2):
        gather.start(z, down.at[z])
    for copy in own_down:
        copy.start()

    def w_rows(n, width, column):
        return weights[pl.ds(n * (width // block), width // block), :, pl.ds(column, units)].reshape(
            width, units
        )

    def pair_rows(z, job=0):
        return pl.ds(pl.multiple_of(job * tokens + z * wide, wide), wide)

    def columns(c, job):
        return weights[:, :, pl.ds(pl.multiple_of(job * units + c * tile, tile), tile)].reshape(model, tile)

    def project(z):
        @pl.loop(0, units // tile)
        def _(c):
            here = pl.ds(pl.multiple_of(c * tile, tile), tile)
            h = rows_in[pair_rows(z), :]
            gate = jnp.dot(h, columns(c, 0), preferred_element_type=F32)
            up = jnp.dot(h, columns(c, 1), preferred_element_type=F32)
            sigmoid = jax.nn.sigmoid(gate)
            silu = gate * sigmoid
            inner[pair_rows(z), here] = (silu * up).astype(BF16)
            inner[pair_rows(z, 1), here] = (up * sigmoid * (1.0 + gate * (1.0 - sigmoid))).astype(BF16)
            inner[pair_rows(z, 2), here] = silu.astype(BF16)

    def back(z):
        @pl.loop(0, units // tile)
        def _(c):
            here = pl.ds(pl.multiple_of(c * tile, tile), tile)
            grad_hidden = jnp.dot(rows_in[pair_rows(z, 1), :], columns(c, 2), preferred_element_type=F32)
            for job in range(1, 3):
                at = pair_rows(z, job)
                inner[at, here] = (grad_hidden * inner[at, here].astype(F32)).astype(BF16)

        @pl.loop(0, model // tile)
        def _(n):
            here = pl.ds(pl.multiple_of(n * tile, tile), tile)
            grad = dot_cols(inner[pair_rows(z, 1)], w_rows(n, tile, 0))
            grad += dot_cols(inner[pair_rows(z, 2)], w_rows(n, tile, units))
            part[0, z, :, :, here] = grad.astype(BF16).reshape(2, rows, tile)

        pair(z).start()

    def out(z):
        @pl.loop(0, model // tile)
        def _(n):
            here = pl.ds(pl.multiple_of(n * tile, tile), tile)
            value = dot_cols(inner[pair_rows(z), :], w_rows(n, tile, 2 * units))
            part[1, z, :, :, here] = value.astype(BF16).reshape(2, rows, tile)

        keep_out(z).start()

    def pair(z):
        return remote(
            part.at[0, z, 1 - me.t], from_pair.at[z], pair_send.at[z], pair_recv.at[z], me.sibling()
        )

    half = rows // 2
    halves = (pl.ds(0, half), pl.ds(half, half))

    def pass_on(way, k, i):
        _, target = reach(me, 1 - way, k)
        ahead = me.z + 1 if way == 0 else me.z - 1
        return remote(
            part.at[0, target, me.t, halves[i]], from_line.at[way, k - 1, halves[i]],
            line_send.at[way, k, i], line_recv.at[way, k - 1, i], me.at(ahead, me.p),
        )

    def line(way, k, behind):
        have, z = reach(me, 1 - way, k)
        before = me.z if way == 0 else LINE - 1 - me.z

        @pl.when(jnp.logical_and(have, before == behind))
        def _():
            pair(z).wait_recv()
            terms = (part.at[0, z, me.t], from_pair.at[z])
            if behind:
                terms += (from_line.at[way, k],)
            for i in range(2):
                if behind:
                    arrival(from_line.at[way, k, halves[i]], line_recv.at[way, k, i])
                add_rows(part.at[0, z, me.t], terms, half, i * half)
                pass_on(way, k, i).start()

    def total():
        pair(me.z).wait_recv()
        add_rows(total_ref, (part.at[0, me.z, me.t], from_pair.at[me.z]), rows)
        for way in range(2):

            @pl.when(reach(me, way, 1)[0])
            def _():
                for i in range(2):
                    arrival(from_line.at[way, 0, halves[i]], line_recv.at[way, 0, i])
                    add_rows(total_ref, (total_ref, from_line.at[way, 0]), half, i * half)

    per = plane * block

    def down_grads(rank):
        z = ranked(me, rank)
        grad_rows(
            z * per, per, rows_in.at[pl.ds(tokens, tokens)], inner, 0, [(0, down_grad, 0)], z * plane
        )
        summed.load_rank(rank)

    keeps = [
        copy_in(weights.at[pl.ds(0, plane), :, pl.ds(0, 2 * units)], grad_ref, grad_sem.at[0]),
        copy_in(rows_in.at[pl.ds(0, tokens)], h_out, grad_sem.at[1]),
        copy_in(inner.at[pl.ds(tokens, 2 * tokens)], inner_out, grad_sem.at[2]),
    ]

    def grads():
        targets = [(0, weights, 0), (1, weights, units)]
        z = ranked(me, 0)
        grad_rows(z * per, per, rows_in.at[pl.ds(0, tokens)], inner, tokens, targets, 0)

    def keep_sum(rank):
        return copy_in(own.at[rank], sum_ref.at[rank], sum_sem.at[rank])

    keep.wait()
    for load in loads:
        load.wait()
    for k in range(LINE):
        for way in range(2 if k else 1):
            have, z = reach(me, way, k)

            @pl.when(have)
            def _():
                if k:
                    chain.wait_block(way, k)
                    chain.start(way, k)
                    share(z).start()
                arrival(slot(z, 1 - me.t), pass_recv.at[z])
                project(z)

        gather.forward(k)
        if k + 2 < LINE:
            gather.start(k + 2, down.at[k + 2])
    def keep_out(z):
        return copy_in(part.at[1, z], out_ref.at[z], out_sem.at[z])

    load_dm.wait()
    keeps[1].start()
    down_grads(0)
    summed.begin(0)
    for copy in own_down:
        copy.wait()
    gather.finish()
    passing = {1: (1, 2), 2: (2, 1), 3: (1, 1)}
    for rank in range(LINE):
        if rank:
            down_grads(rank)
            if rank - 1 in passing:
                for way in range(2):
                    line(way, passing[rank - 1][1], passing[rank - 1][0])
            summed.middle(rank - 1)
            summed.begin(rank)
            if rank > 1:
                summed.end(rank - 2)
                keep_sum(rank - 2).start()
        back(ranked(me, rank))
        if rank < LINE - 1:
            out(ranked(me, rank))
            for way in range(2):
                line(way, LINE - 1 - rank, 0)
    for way in range(2):
        line(way, passing[LINE - 1][1], passing[LINE - 1][0])
    keeps[2].start()
    summed.middle(LINE - 1)
    summed.end(LINE - 2)
    keep_sum(LINE - 2).start()
    grads()
    keeps[0].start()
    out(ranked(me, LINE - 1))
    summed.end(LINE - 1)
    keep_sum(LINE - 1).start()
    total()
    summed.finish()
    chain.finish()
    for z in range(LINE):
        share(z).wait_send()
        keep_out(z).wait()
        keep_sum(z).wait()
        pair(z).wait_send()
    for copy in keeps:
        copy.wait()
    for k in range(1, LINE):
        for way in range(2):

            @pl.when(reach(me, 1 - way, k)[0])
            def _():
                for i in range(2):
                    pass_on(way, k, i).wait_send()


def feed_forward(count, h, dm_all, gate_all, up_soon, up_rest, down):
    rows, model = h.shape
    _, block, units = down.shape
    kinds = max(6, count // LINE - 1)
    buffers, sems = PlaneSum.scratch(count, block, units)
    tokens = LINE * 2 * rows
    vmem = pl.BlockSpec(memory_space=pltpu.VMEM)
    return pl.pallas_call(
        functools.partial(feed_forward_kernel, count // LINE),
        name="feed_forward",
        out_shape=(
            jax.ShapeDtypeStruct((rows, model), F32),
            jax.ShapeDtypeStruct((LINE, 2, rows, model), BF16),
            jax.ShapeDtypeStruct((count // LINE, block, 2 * units), BF16),
            jax.ShapeDtypeStruct((LINE, block, units), BF16),
            jax.ShapeDtypeStruct((tokens, model), BF16),
            jax.ShapeDtypeStruct((2 * tokens, units), BF16),
        ),
        in_specs=[ANY] * 6,
        out_specs=(vmem,) + (ANY,) * 5,
        scratch_shapes=[
            pltpu.VMEM((2 * tokens, model), BF16),
            pltpu.VMEM((count, block, 3 * units), BF16),
            pltpu.VMEM((3 * tokens, units), BF16),
            pltpu.VMEM((count, block, units), BF16),
            pltpu.VMEM((2, LINE, 2, rows, model), BF16),
            pltpu.VMEM((LINE, rows, model), BF16),
            pltpu.VMEM((2, LINE - 1, rows, model), BF16),
            *buffers,
            *sems,
            DMA((2, LINE)), DMA((2, LINE)), DMA((LINE,)), DMA((LINE,)), DMA((LINE,)), DMA((LINE,)),
            DMA((2, LINE, 2)), DMA((2, LINE, 2)), DMA((1, LINE, kinds)), DMA((1, LINE, kinds)),
            DMA((4 + LINE,)), DMA, DMA((LINE,)), DMA((LINE,)), DMA((LINE,)),
        ],
        compiler_params=pltpu.CompilerParams(
            collective_id=1, has_side_effects=True, vmem_limit_bytes=60 * MB
        ),
    )(h, dm_all, gate_all, up_soon, up_rest, down)


def greet_plane(me):
    barrier = pltpu.get_barrier_semaphore()
    for step in range(1, me.plane):
        target = lax.rem(me.p + step, me.plane)
        pl.semaphore_signal(barrier, inc=1, device_id=me.at(me.z, target), device_id_type=MESH)
    pl.semaphore_signal(barrier, inc=1, device_id=me.sibling(), device_id_type=MESH)
    pl.semaphore_wait(barrier, me.plane)


def columns_of(weights, start, width):
    count, rows, _ = weights.shape
    return weights[:, :, pl.ds(start, width)].reshape(count * rows, width)


def rows_of(weights, n, height, start, width):
    _, rows, _ = weights.shape
    per = height // rows
    return weights[pl.ds(n * per, per), :, pl.ds(start, width)].reshape(height, width)


def attention_forward_kernel(
    plane, lens_ref, cos_ref, sin_ref, tok_in, a_ref, up, down_t, gain_ref, x1_out, h2_out, h1_out,
    qkv_out, probs_out, o_out, up_rest, down, weights, tok_ref, x1_ref, h2_ref, h1_ref, qkv_ref, probs_ref,
    o_ref, part, from_pair, low, from_mate, plane_send, plane_recv, part_send, part_recv, sum_send,
    sum_recv, load_sem, keep_sem,
):
    me = Place(plane)
    _, _, rows, model = tok_ref.shape
    wide = 2 * rows
    q_width = o_ref.shape[1]
    heads = q_width // HEAD_SIZE
    kv_width = (qkv_ref.shape[1] - q_width) // 2
    kv_heads = kv_width // HEAD_SIZE
    half = HEAD_SIZE // 2
    load_tok = copy_in(tok_in, tok_ref, load_sem.at[0])
    load_tok.start()
    load = copy_in(a_ref, weights, load_sem.at[1])
    load.start()
    far = SOON - (me.z - me.h)
    keep = [
        copy_in(up.at[far + z], up_rest.at[z * plane + me.p], load_sem.at[2 + z])
        for z in range(LINE - SOON)
    ]
    keep.append(copy_in(down_t.at[me.z], down.at[me.z], load_sem.at[2 + LINE]))
    for copy in keep:
        copy.start()
    outs = [
        copy_in(src, dst, keep_sem.at[i])
        for i, (src, dst) in enumerate(
            (
                (h1_ref, h1_out), (qkv_ref, qkv_out), (probs_ref, probs_out), (o_ref, o_out),
                (x1_ref, x1_out), (h2_ref, h2_out),
            )
        )
    ]
    greet_all(me, plane * LINE)
    gather = PlaneGather(me, 0, up_rest, up.shape[1], plane_send, plane_recv)
    for z in range(LINE - SOON):
        gather.start(z, up.at[far + z])

    def give_down(way, k):
        _, target = reach(me, 1 - way, k)
        return remote(
            down_t.at[target], down.at[me.z], part_send.at[way, k], part_recv.at[way, k],
            me.at(target, me.p),
        )

    for k in range(1, LINE):
        for way in range(2):

            @pl.when(reach(me, 1 - way, k)[0])
            def _():
                give_down(way, k).start()

    span = model // (plane * LINE)
    for d in range(plane * LINE):
        gain_ref[:, d * span : (d + 1) * span] = lens_ref[d].astype(F32)[0:2, :span]
    load_tok.wait()

    for n in range(4):

        def norm(at, n=n):
            x = tok_ref[n // 2, n % 2, at, :].astype(F32)
            factor = lax.rsqrt(jnp.mean(x * x, -1, keepdims=True) + EPS)
            h1_ref[pl.ds(n * rows + at.start, at.size), :] = (x * factor * gain_ref[0:1, :]).astype(BF16)

        row_loop(rows, 32, norm)
    outs[0].start()
    load.wait()

    def project(i):
        start = pl.multiple_of(i * HEAD_SIZE, HEAD_SIZE)
        return start, jnp.dot(
            h1_ref[...], columns_of(weights, start, HEAD_SIZE), preferred_element_type=F32
        )

    @pl.loop(0, heads + kv_heads)
    def _(i):
        start, values = project(i)
        cos, sin = cos_ref[...], sin_ref[...]
        for n in range(2):
            at = slice(n * wide, (n + 1) * wide)
            first, second = values[at, :half], values[at, half:]
            qkv_ref[at, pl.ds(start, half)] = (first * cos - second * sin).astype(BF16)
            qkv_ref[at, pl.ds(start + half, half)] = (second * cos + first * sin).astype(BF16)

    @pl.loop(heads + kv_heads, heads + 2 * kv_heads)
    def _(i):
        start, values = project(i)
        qkv_ref[:, pl.ds(start, HEAD_SIZE)] = values.astype(BF16)

    outs[1].start()
    gather.forward(0)
    row = lax.broadcasted_iota(jnp.int32, (wide, wide), 0)
    key = lax.broadcasted_iota(jnp.int32, (wide, wide), 1)
    tile = 512
    total = QuadSum(me, part, from_pair, low, from_mate, sum_send, sum_recv)

    def attend(n):
        length = lens_ref[me.d + (n - me.h) * plane].astype(F32)[2:3, 0:1]
        allowed = jnp.logical_and(key <= row, key.astype(F32) < length)
        at = pl.ds(pl.multiple_of(n * wide, wide), wide)
        for i in range(heads):
            m = i * kv_heads // heads
            q = qkv_ref[at, i * HEAD_SIZE : (i + 1) * HEAD_SIZE]
            k = qkv_ref[at, q_width + m * HEAD_SIZE : q_width + (m + 1) * HEAD_SIZE]
            v_start = q_width + kv_width + m * HEAD_SIZE
            v = qkv_ref[at, v_start : v_start + HEAD_SIZE]
            scores = dot_cols(q, k) * HEAD_SIZE ** (-0.5)
            scores = jnp.where(allowed, scores, -1e30)
            grown = jnp.exp(scores - jnp.max(scores, -1, keepdims=True))
            probs = grown / jnp.sum(grown, -1, keepdims=True)
            probs_ref[n * heads + i] = probs
            o_ref[at, i * HEAD_SIZE : (i + 1) * HEAD_SIZE] = jnp.dot(
                probs.astype(BF16), v, preferred_element_type=F32
            ).astype(BF16)

        @pl.loop(0, model // tile)
        def _(c):
            here = pl.ds(pl.multiple_of(c * tile, tile), tile)
            value = dot_cols(o_ref[at, :], rows_of(weights, c, tile, q_width + 2 * kv_width, q_width))
            part[n, :, :, here] = value.reshape(2, rows, tile)

        total.start(n)

    attend(1 - me.h)
    total.to_mate()
    attend(me.h)
    outs[2].start()
    outs[3].start()
    for z in range(1, LINE - SOON):
        gather.forward(z)
    total.wait()

    def add(at):
        x1 = tok_ref[me.h, me.t, at, :].astype(F32) + total.rows(at)
        x1_ref[at, :] = x1
        factor = lax.rsqrt(jnp.mean(x1 * x1, -1, keepdims=True) + EPS)
        h2_ref[at, :] = (x1 * factor * gain_ref[1:2, :]).astype(BF16)

    row_loop(rows, 32, add)
    outs[4].start()
    outs[5].start()
    total.finish_sends()
    gather.finish(range(LINE - SOON))
    for k in range(1, LINE):
        for way in range(2):

            @pl.when(reach(me, 1 - way, k)[0])
            def _():
                give_down(way, k).wait_send()

            @pl.when(reach(me, way, k)[0])
            def _():
                arrival(down.at[me.z], part_recv.at[way, k])

    for copy in keep + outs:
        copy.wait()


def attention_forward(count, q_width, kv_width, lens, cos, sin, tokens_all, attn_all, up, down_t):
    _, _, rows, model = tokens_all.shape
    wide = 2 * rows
    plane = count // LINE
    kinds = max(6, plane - 1)
    outs = (
        jax.ShapeDtypeStruct((rows, model), F32),
        jax.ShapeDtypeStruct((rows, model), BF16),
        jax.ShapeDtypeStruct((2 * wide, model), BF16),
        jax.ShapeDtypeStruct((2 * wide, q_width + 2 * kv_width), BF16),
        jax.ShapeDtypeStruct((2 * q_width // HEAD_SIZE, wide, wide), F32),
        jax.ShapeDtypeStruct((2 * wide, q_width), BF16),
    )
    return pl.pallas_call(
        functools.partial(attention_forward_kernel, plane),
        name="attention_forward",
        out_shape=(jax.ShapeDtypeStruct((2, model), F32),)
        + outs
        + (
            jax.ShapeDtypeStruct((count - SOON * plane,) + up.shape[1:], BF16),
            jax.ShapeDtypeStruct(down_t.shape, BF16),
        ),
        in_specs=[VMEM] * 3 + [ANY] * 4,
        out_specs=(VMEM,) + (ANY,) * 8,
        scratch_shapes=[
            pltpu.VMEM(attn_all.shape, BF16),
            pltpu.VMEM(tokens_all.shape, BF16),
            *[pltpu.VMEM(out.shape, out.dtype) for out in outs],
            pltpu.VMEM((2, 2, rows, model), F32),
            pltpu.VMEM((2, rows, model), F32),
            pltpu.VMEM((rows, model), BF16),
            pltpu.VMEM((rows, model), BF16),
            DMA((1, LINE, kinds)), DMA((1, LINE, kinds)), DMA((2, LINE)), DMA((2, LINE)), DMA((3,)),
            DMA((3,)), DMA((3 + LINE,)), DMA((6,)),
        ],
        compiler_params=pltpu.CompilerParams(
            collective_id=2, has_side_effects=True, vmem_limit_bytes=60 * MB
        ),
    )(lens, cos, sin, tokens_all, attn_all, up, down_t)


def attention_backward_kernel(
    plane, gain_ref, cos_ref, sin_ref, total_in, x1_in, dm_in, tok_in, h1_in, qkv_in, probs_in, o_in,
    a_ref, gw_ref, sum_ref, h_in, inner_in, ga_ref, w_out, grad_tokens, gain_blocks, gain_parts, weights, own, other, first, second,
    total_ref, x1_ref, dm_ref, tok_ref, h1_ref, qkv_ref, probs_ref, o_ref, rows_in, inner, gw, dx, da, do,
    dqkv, dh1, from_pair, low, from_mate, first_send, first_recv, second_send, second_recv, load_sem,
    other_sem, part_send, part_recv, da_send, da_recv, sum_send, sum_recv, a_sem, keep_sem, grad_sem, in_sem,
):
    me = Place(plane)
    rows, model = tok_ref.shape
    block = weights.shape[1]
    q_width = o_ref.shape[1]
    heads = q_width // HEAD_SIZE
    seq = 2 * rows
    qkv_width = qkv_ref.shape[1]
    kv_width = (qkv_width - q_width) // 2
    kv_heads = kv_width // HEAD_SIZE
    half = HEAD_SIZE // 2
    scale = HEAD_SIZE ** (-0.5)
    summed = PlaneSum(
        me, lambda rank, p: gw.at[(rank - 1) * plane + p] if rank else gw_ref.at[p],
        own, other, first, second,
        (first_send, first_recv, second_send, second_recv, load_sem, other_sem),
    )
    ins = [
        copy_in(src, dst, in_sem.at[i])
        for i, (src, dst) in enumerate(
            (
                (total_in, total_ref), (x1_in, x1_ref), (dm_in.at[me.z, me.t], dm_ref),
                (tok_in.at[me.h, me.t], tok_ref),
                (h1_in, h1_ref), (qkv_in, qkv_ref), (probs_in, probs_ref), (o_in, o_ref),
                (h_in, rows_in), (inner_in, inner),
            )
        )
    ]
    for copy in ins[:3] + ins[8:]:
        copy.start()
    load = pltpu.make_async_copy(a_ref, weights, a_sem)
    load.start()
    for copy in ins[3:8]:
        copy.start()
    summed.load_rank(0)
    greet_all(me, plane * LINE)

    wide = own.shape[2]
    spans = (pl.ds(0, wide), pl.ds(wide, sum_ref.shape[2]))

    def part(rank, kind):
        target = ranked(me, rank)
        way, k = way_to(me, target)
        return remote(
            (own, sum_ref)[kind].at[rank], w_out.at[me.z, :, spans[kind]], part_send.at[way, k, kind],
            part_recv.at[way, k, kind], me.at(target, me.p),
        )

    keeps = [
        copy_in((own, sum_ref)[kind].at[LINE - 1], w_out.at[me.z, :, spans[kind]], keep_sem.at[kind])
        for kind in range(2)
    ]
    das = Quad(me, da, da_send, da_recv)
    dh1_sum = QuadSum(me, dh1, from_pair, low, from_mate, sum_send, sum_recv)

    def mid_norm():
        gain_parts[...] = jnp.zeros_like(gain_parts)

        def act(at):
            x, up = x1_ref[at, :], total_ref[at, :]
            factor = lax.rsqrt(jnp.mean(x * x, -1, keepdims=True) + EPS)
            scaled = up * gain_ref[1:2, :]
            grad = dm_ref[at, :].astype(F32) + (
                factor * scaled - x * factor**3 * jnp.mean(scaled * x, -1, keepdims=True)
            )
            dx[at, :] = grad
            da[me.h, me.t, at, :] = grad.astype(BF16)
            gain_parts[1:2, :] += jnp.sum(up * x * factor, 0, keepdims=True)

        row_loop(rows, 32, act)
        das.start()

    def grad_o():
        load.wait()
        das.finish()

        @pl.loop(0, q_width // HEAD_SIZE)
        def _(c):
            here = pl.multiple_of(c * HEAD_SIZE, HEAD_SIZE)
            value = jnp.dot(
                da[...].reshape(2 * seq, model),
                columns_of(weights, qkv_width + here, HEAD_SIZE),
                preferred_element_type=F32,
            )
            do[:, pl.ds(here, HEAD_SIZE)] = value.astype(BF16)

    def rotate(values, rows_at, start):
        first, second = values[:, :half], values[:, half:]
        cos, sin = cos_ref[...], sin_ref[...]
        dqkv[rows_at, start : start + half] = (first * cos + second * sin).astype(BF16)
        dqkv[rows_at, start + half : start + 2 * half] = (second * cos - first * sin).astype(BF16)

    def grad_heads(n):
        group = heads // kv_heads
        here = slice(n * seq, (n + 1) * seq)
        for m in range(kv_heads):
            at_k = q_width + m * HEAD_SIZE
            at_v = at_k + kv_width
            k = qkv_ref[here, at_k : at_k + HEAD_SIZE]
            v = qkv_ref[here, at_v : at_v + HEAD_SIZE]
            grad_k = grad_v = None
            for i in range(m * group, (m + 1) * group):
                at = slice(i * HEAD_SIZE, (i + 1) * HEAD_SIZE)
                probs = probs_ref[n * heads + i]
                grad_probs = dot_cols(do[here, at], v)
                grad_scores = probs * (
                    grad_probs - jnp.sum(probs * grad_probs, -1, keepdims=True)
                )
                low_scores = grad_scores.astype(BF16)
                rotate(
                    jnp.dot(low_scores, k, preferred_element_type=F32) * scale, here, i * HEAD_SIZE
                )
                more_k = dot_tn(low_scores, qkv_ref[here, at])
                more_v = dot_tn(probs.astype(BF16), do[here, at])
                grad_k = more_k if grad_k is None else grad_k + more_k
                grad_v = more_v if grad_v is None else grad_v + more_v
            rotate(grad_k * scale, here, at_k)
            dqkv[here, at_v : at_v + HEAD_SIZE] = grad_v.astype(BF16)

    tile = 512

    def grad_h1():
        @pl.loop(0, model // tile)
        def _(n):
            here = pl.ds(pl.multiple_of(n * tile, tile), tile)
            value = dot_cols(dqkv[...], rows_of(weights, n, tile, 0, qkv_width))
            dh1[:, :, :, here] = value.reshape(2, 2, rows, tile)

        for h in range(2):
            dh1_sum.start(h)

    def keep_grads(n):
        per = tile // block
        return pltpu.make_async_copy(
            weights.at[pl.ds(n * per, per)], ga_ref.at[pl.ds(n * per, per)], grad_sem.at[n]
        )

    def grads():
        @pl.loop(0, model // tile)
        def _(n):
            here = pl.ds(pl.multiple_of(n * tile, tile), tile)
            there = pl.ds(n * (tile // block), tile // block)
            left = h1_ref[:, here].T
            for c in range(qkv_width // tile):
                at = slice(c * tile, (c + 1) * tile)
                value = jnp.dot(left, dqkv[:, at], preferred_element_type=F32)
                weights[there, :, at] = value.astype(BF16).reshape(tile // block, block, tile)
            left = da[:, :, :, here].reshape(2 * seq, tile).T
            for c in range(q_width // tile):
                at = slice(c * tile, (c + 1) * tile)
                value = jnp.dot(left, o_ref[:, at], preferred_element_type=F32)
                at = slice(qkv_width + c * tile, qkv_width + (c + 1) * tile)
                weights[there, :, at] = value.astype(BF16).reshape(tile // block, block, tile)

        for n in range(model // tile):
            keep_grads(n).start()

    def in_norm():
        dh1_sum.wait()

        def act(at):
            x = tok_ref[at, :].astype(F32)
            up = dh1_sum.rows(at)
            factor = lax.rsqrt(jnp.mean(x * x, -1, keepdims=True) + EPS)
            scaled = up * gain_ref[0:1, :]
            grad_tokens[at, :] = dx[at, :] + (
                factor * scaled - x * factor**3 * jnp.mean(scaled * x, -1, keepdims=True)
            )
            gain_parts[0:1, :] += jnp.sum(up * x * factor, 0, keepdims=True)

        row_loop(rows, 32, act)

    summed.begin(0)
    for rank in range(LINE - 1):
        part(rank, 1).start()
    keeps[1].start()
    def mlp_grads(rank):
        per = plane * block
        targets = [(0, gw, 0), (1, gw, inner.shape[1])]
        z = ranked(me, rank)
        grad_rows(z * per, per, rows_in, inner, 0, targets, (rank - 1) * plane)
        summed.load_rank(rank)

    for copy in ins[:3]:
        copy.wait()
    mid_norm()
    for copy in ins[8:]:
        copy.wait()
    mlp_grads(1)
    summed.middle(0)
    summed.begin(1)
    mlp_grads(2)
    das.forward()
    for copy in ins[3:8]:
        copy.wait()
    summed.end(0)
    part(0, 0).start()
    grad_o()
    summed.middle(1)
    summed.begin(2)
    grad_heads(0)
    grad_heads(1)
    mlp_grads(3)
    summed.end(1)
    part(1, 0).start()
    grad_h1()
    summed.middle(2)
    summed.begin(3)
    dh1_sum.to_mate()
    grads()
    summed.end(2)
    part(2, 0).start()
    summed.middle(3)
    in_norm()
    summed.end(3)

    span = model // gain_blocks.shape[0]
    gain_blocks[...] = jnp.zeros_like(gain_blocks)
    for d in range(gain_blocks.shape[0]):
        gain_blocks[d, 0:2, :span] = gain_parts[:, d * span : (d + 1) * span]
    keeps[0].start()
    for kind in range(2):
        for rank in range(LINE - 1):
            part(rank, kind).wait_send()
        for way, k in FAR_FIRST:

            @pl.when(reach(me, way, k)[0])
            def _():
                arrival(w_out.at[me.z, :, spans[kind]], part_recv.at[way, k, kind])

    summed.finish()
    das.finish_sends()
    dh1_sum.finish_sends()
    for n in range(model // tile):
        keep_grads(n).wait()
    for copy in keeps:
        copy.wait()


def attention_backward(
    count, gains, cos, sin, total, x1, dm_all, tokens_all, h1, qkv, probs, o, attn_all, grad_mlp, first_sum, rows_in,
    inner,
):
    _, _, rows, model = tokens_all.shape
    _, block, _ = attn_all.shape
    buffers, sems = PlaneSum.scratch(count, block, grad_mlp.shape[2])
    return pl.pallas_call(
        functools.partial(attention_backward_kernel, count // LINE),
        name="attention_backward",
        out_shape=(
            jax.ShapeDtypeStruct(attn_all.shape, BF16),
            jax.ShapeDtypeStruct((LINE, block, grad_mlp.shape[2] + first_sum.shape[2]), BF16),
            jax.ShapeDtypeStruct((rows, model), F32),
            jax.ShapeDtypeStruct((count, 8, max(128, model // count)), F32),
        ),
        in_specs=[VMEM] * 3 + [ANY] * 13,
        out_specs=(ANY, ANY, VMEM, VMEM),
        scratch_shapes=[
            pltpu.VMEM((2, model), F32),
            pltpu.VMEM(attn_all.shape, BF16),
            *buffers,
            *[
                pltpu.VMEM(ref.shape, ref.dtype)
                for ref in (total, x1, dm_all[0, 0], dm_all[0, 0], h1, qkv, probs, o, rows_in, inner)
            ],
            pltpu.VMEM(((LINE - 1) * grad_mlp.shape[0],) + grad_mlp.shape[1:], BF16),
            pltpu.VMEM((rows, model), F32),
            pltpu.VMEM((2, 2, rows, model), BF16),
            pltpu.VMEM(o.shape, BF16),
            pltpu.VMEM(qkv.shape, BF16),
            pltpu.VMEM((2, 2, rows, model), F32),
            pltpu.VMEM((2, rows, model), F32),
            pltpu.VMEM((rows, model), BF16),
            pltpu.VMEM((rows, model), BF16),
            *sems,
            DMA((2, LINE, 2)), DMA((2, LINE, 2)), DMA((3,)), DMA((3,)), DMA((3,)), DMA((3,)), DMA, DMA((2,)),
            DMA((model // 512,)), DMA((10,)),
        ],
        compiler_params=pltpu.CompilerParams(
            collective_id=3, has_side_effects=True, vmem_limit_bytes=60 * MB
        ),
    )(gains, cos, sin, total, x1, dm_all, tokens_all, h1, qkv, probs, o, attn_all, grad_mlp, first_sum, rows_in, inner)


def grad_sum_kernel(
    count, gain_ref, x1_in, ga_ref, out_ref, a_out, output, gain_out, own, other, first, second, x1_ref,
    landed, out_own, out_pair, out_line, gain_in, gain_pair, first_send, first_recv, second_send, second_recv,
    load_sem, other_sem, part_send, part_recv, out_send, out_recv, load_out_sem, pair_send, pair_recv, gain_send, gain_recv,
):
    plane = count // LINE
    me = Place(plane)
    rows = a_out.shape[1]
    summed = PlaneSum(
        me, ga_ref, own, other, first, second,
        (first_send, first_recv, second_send, second_recv, load_sem, other_sem),
    )

    class Line:
        def __init__(self, held, landing, send, recv):
            self.held, self.landing, self.send, self.recv = held, landing, send, recv

        def pass_on(self, rank):
            way, k = way_to(me, ranked(me, rank))
            ahead = jnp.where(way == 0, me.z + 1, me.z - 1)
            return remote(
                self.held(rank), self.landing.at[way, k - 1], self.send.at[way, k],
                self.recv.at[way, k - 1], me.at(ahead, me.p),
            )

        def step(self, rank):
            way, k = way_to(me, ranked(me, rank))
            before = jnp.where(way == 0, me.z, LINE - 1 - me.z)
            held = self.held(rank)

            @pl.when(before > 0)
            def _():
                arrival(self.landing.at[way, k], self.recv.at[way, k])
                add_rows(held, (held, self.landing.at[way, k]), held.shape[0])

            self.pass_on(rank).start()

        def total(self, act):
            for way in range(2):

                @pl.when(reach(me, way, 1)[0])
                def _():
                    arrival(self.landing.at[way, 0], self.recv.at[way, 0])
                    act(self.landing.at[way, 0])

        def finish(self):
            for rank in range(LINE - 1):
                self.pass_on(rank).wait_send()

    def part(rank):
        target = ranked(me, rank)
        way, k = way_to(me, target)
        return remote(
            own.at[rank], landed.at[me.z], part_send.at[way, k], part_recv.at[way, k],
            me.at(target, me.p),
        )

    outs = Line(lambda rank: out_own.at[ranked(me, rank)], out_line, out_send, out_recv)
    summed.load_all()
    load_out = copy_in(out_ref.at[:, me.t], out_own, load_out_sem.at[0])
    load_out.start()
    load_x1 = copy_in(x1_in, x1_ref, load_out_sem.at[1])
    load_x1.start()
    greet_all(me, count)

    def give_gain(step):
        target = lax.rem(me.d + step, count)
        return remote(
            gain_ref.at[target], gain_in.at[step], gain_send.at[step], gain_recv.at[step], (target, me.t)
        )

    summed.begin(0)
    for step in range(1, count):
        give_gain(step).start()
    pairs = [
        remote(
            out_ref.at[ranked(me, rank), 1 - me.t], out_pair.at[ranked(me, rank)], pair_send.at[rank],
            pair_recv.at[rank], me.sibling(),
        )
        for rank in range(LINE)
    ]
    for copy in pairs:
        copy.start()
    load_out.wait()
    def out_step(rank):
        z = ranked(me, rank)
        pairs[rank].wait_recv()
        add_rows(out_own.at[z], (out_own.at[z], out_pair.at[z]), out_own.shape[1])
        if rank < LINE - 1:

            @pl.when(jnp.logical_or(me.z == 0, me.z == LINE - 1))
            def _():
                outs.step(rank)

    out_step(0)
    at_end = jnp.logical_or(me.z == 0, me.z == LINE - 1)

    def out_start(at):
        x1_ref[at, :] = x1_ref[at, :] + out_own[me.z, at, :].astype(F32)

    def add_out(landed):
        def act(at):
            x1_ref[at, :] = x1_ref[at, :] + landed[at, :].astype(F32)

        row_loop(output.shape[0], 16, act)

    def out_end(at):
        output[at, :] = x1_ref[at, :].astype(BF16)

    for rank in range(LINE):
        summed.middle(rank)
        if rank + 1 < LINE:
            summed.begin(rank + 1)
            out_step(rank + 1)
        else:
            load_x1.wait()
            total = gain_ref[me.d]
            for step in range(1, count):
                give_gain(step).wait()
                total += gain_in[step]
            gain_pair[0] = total
            swap = remote(
                gain_pair.at[0], gain_pair.at[1], gain_send.at[0], gain_recv.at[0], me.sibling()
            )
            swap.start()
            swap.wait()
            gain_out[...] = gain_pair[0] + gain_pair[1]
        summed.end(rank)
        if rank < LINE - 1:
            part(rank).start()
        for late in {0: (0,), 1: (2, 1)}.get(rank, ()):
            @pl.when(jnp.logical_not(at_end))
            def _():
                outs.step(late)


    row_loop(output.shape[0], 16, out_start)
    outs.total(add_out)
    row_loop(output.shape[0], 16, out_end)
    keep = copy_in(own.at[LINE - 1], landed.at[me.z], load_out_sem.at[2])
    keep.start()
    for way, k in FAR_FIRST:
        have, z = reach(me, way, k)

        @pl.when(have)
        def _():
            arrival(landed.at[z], part_recv.at[way, k])

    keep.wait()
    for h in range(2):
        add_rows(a_out.at[h], tuple(landed.at[z] for z in range(h, LINE, 2)), rows)
    for rank in range(LINE - 1):
        part(rank).wait_send()
    for copy in pairs:
        copy.wait_send()
    outs.finish()
    summed.finish()


def grad_sum(count, x1, ga, out_parts, gains):
    _, block, width = ga.shape
    _, _, rows, model = out_parts.shape
    buffers, sems = PlaneSum.scratch(count, block, width)
    return pl.pallas_call(
        functools.partial(grad_sum_kernel, count),
        name="grad_sum",
        out_shape=(
            jax.ShapeDtypeStruct((2, block, width), F32),
            jax.ShapeDtypeStruct((rows, model), BF16),
            jax.ShapeDtypeStruct(gains.shape[1:], F32),
        ),
        in_specs=[VMEM] + [ANY] * 3,
        out_specs=(VMEM,) * 3,
        scratch_shapes=[
            *buffers,
            pltpu.VMEM((rows, model), F32),
            pltpu.VMEM((LINE, block, width), BF16),
            pltpu.VMEM((LINE, rows, model), BF16),
            pltpu.VMEM((LINE, rows, model), BF16),
            pltpu.VMEM((2, LINE - 1, rows, model), BF16),
            pltpu.VMEM(gains.shape, F32),
            pltpu.VMEM((2,) + gains.shape[1:], F32),
            *sems,
            DMA((2, LINE)), DMA((2, LINE)), DMA((2, LINE)), DMA((2, LINE)), DMA((3,)), DMA((LINE,)),
            DMA((LINE,)), DMA((count,)), DMA((count,)),
        ],
        compiler_params=pltpu.CompilerParams(
            collective_id=4, has_side_effects=True, vmem_limit_bytes=60 * MB
        ),
    )(gains, x1, ga, out_parts)


def layouts_kernel(
    gain_ref, a_ref, mlp_ref, output_ref, tokens_ref, gain_attn, gain_mlp, q_out, k_out, v_out, o_out, gate_out, up_out, down_out,
    output_out, tokens_out, a_v, mlp_v, output_v, tokens_v, q_v, k_v, v_v, o_v, gate_v, up_v, down_v,
    in_sem, out_sem,
):
    ins = [
        copy_in(src, dst, in_sem.at[i])
        for i, (src, dst) in enumerate(
            ((mlp_ref, mlp_v), (a_ref, a_v), (tokens_ref, tokens_v), (output_ref, output_v))
        )
    ]
    for copy in ins:
        copy.start()
    sent = []

    def give(src, dst):
        sent.append(copy_in(src, dst, out_sem.at[len(sent)]))
        sent[-1].start()

    span = gain_attn.shape[1]
    gain_attn[...] = gain_ref[0:1, :span]
    gain_mlp[...] = gain_ref[1:2, :span]
    units = mlp_v.shape[2] // 3
    ins[0].wait()
    for z in range(LINE):
        here = pl.ds(z * units, units)
        gate_v[:, here] = mlp_v[z, :, :units].astype(F32)
        give(gate_v.at[:, here], gate_out.at[:, here])
        up_v[:, here] = mlp_v[z, :, units : 2 * units].astype(F32)
        give(up_v.at[:, here], up_out.at[:, here])
        down_v[here, :] = mlp_v[z, :, 2 * units :].astype(F32).T
        give(down_v.at[here], down_out.at[here])
    for copy in ins[1:]:
        copy.wait()
    give(tokens_v, tokens_out)
    give(output_v, output_out)
    start = 0
    for src, dst in ((q_v, q_out), (k_v, k_out), (v_v, v_out)):
        half = src.shape[1] // 2
        for h in range(2):
            src[:, h * half : (h + 1) * half] = a_v[h, :, start : start + half]
        start += half
        give(src, dst)
    half = o_v.shape[0] // 2
    for h in range(2):
        o_v[h * half : (h + 1) * half, :] = a_v[h, :, start:].T
    give(o_v, o_out)
    for copy in sent:
        copy.wait()


def layouts(q_width, kv_width, gain_sum, a, mlp, output, grad_tokens):
    block = a.shape[1]
    hidden = LINE * (mlp.shape[2] // 3)
    outs = (
        jax.ShapeDtypeStruct((block, q_width), F32),
        jax.ShapeDtypeStruct((block, kv_width), F32),
        jax.ShapeDtypeStruct((block, kv_width), F32),
        jax.ShapeDtypeStruct((q_width, block), F32),
        jax.ShapeDtypeStruct((block, hidden), F32),
        jax.ShapeDtypeStruct((block, hidden), F32),
        jax.ShapeDtypeStruct((hidden, block), F32),
    )
    ins = (a, mlp, output, grad_tokens)
    return pl.pallas_call(
        layouts_kernel,
        name="layouts",
        out_shape=(jax.ShapeDtypeStruct((1, block), F32),) * 2
        + outs
        + tuple(jax.ShapeDtypeStruct(ref.shape, ref.dtype) for ref in ins[2:]),
        in_specs=[VMEM] + [ANY] * 4,
        out_specs=(VMEM,) * 2 + (ANY,) * 9,
        scratch_shapes=[
            *[pltpu.VMEM(ref.shape, ref.dtype) for ref in ins + outs],
            DMA((4,)), DMA((3 * LINE + 6,)),
        ],
        compiler_params=pltpu.CompilerParams(vmem_limit_bytes=60 * MB),
    )(gain_sum, *ins)


def shards(
    tokens, w_query, key_weight, value_weight, w_out, gain_attn, w_gate, w_up, w_down, gain_mlp,
    cotangent, lengths, seq_of_group,
):
    count = lax.axis_size("dp")
    rows, q_width = w_query.shape
    kv_width = key_weight.shape[1]
    model = rows * count
    cos, sin = rope_tables(tokens.shape[0] * lax.axis_size("tensor"), HEAD_SIZE)
    lanes = -rows % 128
    gains = jnp.pad(jnp.stack([gain_attn, gain_mlp]), ((0, 14), (0, lanes)))
    attn_all, gate_all, up_soon, up, down_t, gains_all, tokens_all, dm_all = gather_all(
        count, lengths, seq_of_group, gains,
        (w_query, key_weight, value_weight, w_out, w_gate, w_up, w_down), tokens, cotangent,
    )
    gains_full, x1, h2, h1, qkv, probs, attended, up_rest, down = attention_forward(
        count, q_width // 2, kv_width // 2, gains_all, cos, sin, tokens_all, attn_all, up, down_t
    )
    grad_h2, out_parts, grad_mlp_w, down_sum, rows_in, inner = feed_forward(
        count, h2, dm_all.reshape(-1, model), gate_all, up_soon, up_rest, down
    )
    grad_attn_w, mlp_sum, grad_tokens, gain_parts = attention_backward(
        count, gains_full, cos, sin, grad_h2, x1, dm_all, tokens_all, h1, qkv, probs, attended, attn_all,
        grad_mlp_w, down_sum, rows_in, inner,
    )
    attn_sum, output, gain_sum = grad_sum(count, x1, grad_attn_w, out_parts, gain_parts)
    (
        grad_gain_attn, grad_gain_mlp, grad_query, grad_key, grad_value, grad_out, grad_gate, grad_up,
        grad_down, output, grad_tokens,
    ) = layouts(q_width, kv_width, gain_sum, attn_sum, mlp_sum, output, grad_tokens)
    return (
        output, grad_tokens, grad_query, grad_key, grad_value, grad_out, grad_gain_attn.reshape(rows),
        grad_gate, grad_up, grad_down, grad_gain_mlp.reshape(rows),
    )


def solution(mesh):
    both = P(("dp", "tensor"), None)
    row = P("dp", "tensor")
    column = P("tensor", "dp")
    in_specs = (
        both, row, row, row, column, P("dp"), row, row, column, P("dp"), both, P(), P("dp"),
    )
    out_specs = (both, both, row, row, row, column, P("dp"), row, row, column, P("dp"))
    return jax.shard_map(shards, mesh=mesh, in_specs=in_specs, out_specs=out_specs, check_vma=False)
```

```python
import functools
import math

import jax
import jax.numpy as jnp
import numpy as np
from jax import lax
from jax.experimental import pallas as pl
from jax.experimental.pallas import tpu as pltpu
from jax.sharding import PartitionSpec as P

HEAD_SIZE = 256
EPS = 1e-06
THETA = 1000042.0
LINE = 4
MESH = pl.DeviceIdType.MESH
BF16 = jnp.bfloat16
F32 = jnp.float32
MB = 1024 * 1024
AHEAD = 4
SOON = 2


def rope_tables(count, head_dim):
    half = head_dim // 2
    index = np.arange(half, dtype=np.float32)
    freqs = np.exp(index * np.float32(-2.0 * math.log(THETA) / head_dim))
    angles = np.arange(count, dtype=np.float32)[:, None] * freqs[None, :]
    return np.cos(angles), np.sin(angles)


def dot_tn(left, right):
    return lax.dot_general(left, right, (((0,), (0,)), ((), ())), preferred_element_type=F32)


class Place:
    def __init__(self, plane):
        self.d = lax.axis_index("dp")
        self.t = lax.axis_index("tensor")
        self.plane = plane
        self.z = lax.div(self.d, plane)
        self.p = lax.rem(self.d, plane)
        self.h = lax.rem(self.z, 2)
        if plane == 4:
            x = lax.rem(self.p, 2)
            y = lax.div(self.p, 2)
            self.px = 2 * y + 1 - x
            self.py = 2 * (1 - y) + x
            self.pd = 2 * (1 - y) + 1 - x

    def at(self, z, p):
        return (z * self.plane + p, self.t)

    def sibling(self):
        return (self.d, 1 - self.t)

    def mate(self):
        return self.at(self.z + 1 - 2 * self.h, self.p)


def remote(src, dst, send, recv, device):
    return pltpu.make_async_remote_copy(
        src_ref=src, dst_ref=dst, send_sem=send, recv_sem=recv, device_id=device, device_id_type=MESH
    )


def arrival(ref, sem):
    pltpu.make_async_copy(ref, ref, sem).wait()


def greet_all(me, count):
    barrier = pltpu.get_barrier_semaphore()
    for step in range(1, count):
        pl.semaphore_signal(
            barrier, inc=1, device_id=(lax.rem(me.d + step, count), me.t), device_id_type=MESH
        )
    pl.semaphore_signal(barrier, inc=1, device_id=me.sibling(), device_id_type=MESH)
    pl.semaphore_wait(barrier, count)


def greet_near(me):
    barrier = pltpu.get_barrier_semaphore()
    for step in range(1, me.plane):
        target = lax.rem(me.p + step, me.plane)
        pl.semaphore_signal(barrier, inc=1, device_id=me.at(me.z, target), device_id_type=MESH)
    for step in range(1, LINE):
        target = lax.rem(me.z + step, LINE)
        pl.semaphore_signal(barrier, inc=1, device_id=me.at(target, me.p), device_id_type=MESH)
    pl.semaphore_signal(barrier, inc=1, device_id=me.sibling(), device_id_type=MESH)
    pl.semaphore_wait(barrier, me.plane + LINE - 1)


def reach(me, way, k):
    return (me.z >= k, me.z - k) if way == 0 else (me.z + k < LINE, me.z + k)


class Chain:
    def __init__(self, me, first, held, send, recv):
        self.me, self.first, self.held, self.send, self.recv = me, first, held, send, recv

    def copy(self, way, k):
        me = self.me
        _, origin = reach(me, way, k)
        target = me.z + 1 if way == 0 else me.z - 1
        src = self.first if k == 0 else self.held(origin)
        return remote(
            src, self.held(origin), self.send.at[way, k], self.recv.at[way, k + 1], me.at(target, me.p)
        )

    def goes(self, way, k):
        have, _ = reach(self.me, way, k)
        ahead, _ = reach(self.me, 1 - way, 1)
        return jnp.logical_and(have, ahead)

    def start(self, way, k):
        if k < LINE - 1:

            @pl.when(self.goes(way, k))
            def _():
                self.copy(way, k).start()

    def wait_block(self, way, k):
        _, origin = reach(self.me, way, k)
        arrival(self.held(origin), self.recv.at[way, k])

    def finish(self):
        for way in range(2):
            for k in range(LINE - 1):

                @pl.when(self.goes(way, k))
                def _():
                    self.copy(way, k).wait_send()


class PlaneGather:
    def __init__(self, me, job, held, rows, send, recv):
        self.me, self.job, self.held, self.send, self.recv = me, job, held, send, recv
        self.half = rows // 2

    def piece(self, z, p, half):
        return self.held.at[z * self.me.plane + p, pl.ds(half * self.half, self.half)]

    def copy(self, z, kind, first=None):
        me = self.me
        if me.plane != 4:
            ref = first if first is not None else self.held.at[z * me.plane + me.p]
            target = lax.rem(me.p + kind + 1, me.plane)
            dst = self.held.at[z * me.plane + me.p]
        else:
            owner = (me.p, me.p, me.p, me.p, me.px, me.py)[kind]
            half = (0, 1, 1, 0, 0, 1)[kind]
            target = (me.px, me.px, me.py, me.py, me.py, me.px)[kind]
            dst = self.piece(z, owner, half)
            ref = dst if first is None else first.at[pl.ds(half * self.half, self.half)]
        return remote(
            ref, dst, self.send.at[self.job, z, kind], self.recv.at[self.job, z, kind], me.at(me.z, target)
        )

    def start(self, z, first=None):
        kinds = (0, 2, 1, 3) if self.me.plane == 4 else range(self.me.plane - 1)
        for kind in kinds:
            self.copy(z, kind, first).start()

    def forward(self, z):
        if self.me.plane == 4:
            self.copy(z, 0).wait_recv()
            self.copy(z, 4).start()
            self.copy(z, 2).wait_recv()
            self.copy(z, 5).start()

    def finish(self, zs=range(LINE)):
        kinds = 6 if self.me.plane == 4 else self.me.plane - 1
        for z in zs:
            for kind in range(kinds):
                copy = self.copy(z, kind)
                if self.me.plane != 4 or kind not in (0, 2):
                    copy.wait_recv()
                copy.wait_send()


class Quad:
    def __init__(self, me, blocks, send, recv):
        self.me, self.blocks, self.send, self.recv = me, blocks, send, recv

    def copy(self, i, first=None):
        me = self.me
        dst = self.blocks.at[me.h if i < 2 else 1 - me.h, me.t]
        device = me.mate() if i == 1 else me.sibling()
        return remote(dst if first is None else first, dst, self.send.at[i], self.recv.at[i], device)

    def start(self, first=None):
        for i in (1, 0):
            self.copy(i, first).start()

    def forward(self):
        arrival(self.blocks.at[1 - self.me.h, self.me.t], self.recv.at[1])
        self.copy(2).start()

    def finish(self):
        me = self.me
        arrival(self.blocks.at[me.h, 1 - me.t], self.recv.at[0])
        arrival(self.blocks.at[1 - me.h, 1 - me.t], self.recv.at[2])

    def finish_sends(self):
        for i in range(3):
            self.copy(i).wait_send()


class QuadSum:
    def __init__(self, me, part, from_pair, low, from_mate, send, recv):
        self.me, self.part, self.from_pair, self.low, self.from_mate = me, part, from_pair, low, from_mate
        self.send, self.recv = send, recv
        self.mate = remote(low, from_mate, send.at[2], recv.at[2], me.mate())

    def pair(self, h):
        me = self.me
        return remote(
            self.part.at[h, 1 - me.t], self.from_pair.at[h], self.send.at[h], self.recv.at[h], me.sibling()
        )

    def start(self, h):
        self.pair(h).start()

    def to_mate(self):
        me = self.me
        self.pair(1 - me.h).wait_recv()

        def act(at):
            total = self.part[1 - me.h, me.t, at, :] + self.from_pair[1 - me.h, at, :]
            self.low[at, :] = total.astype(BF16)

        row_loop(self.low.shape[0], 32, act)
        self.mate.start()

    def wait(self):
        self.pair(self.me.h).wait_recv()
        self.mate.wait_recv()

    def rows(self, at):
        me = self.me
        total = self.part[me.h, me.t, at, :] + self.from_pair[me.h, at, :]
        return total + self.from_mate[at, :].astype(F32)

    def finish_sends(self):
        for h in range(2):
            self.pair(h).wait_send()
        self.mate.wait_send()


def copy_in(src, dst, sem):
    return pltpu.make_async_copy(src, dst, sem)


def row_loop(rows, step, act):
    @pl.loop(0, rows // step)
    def _(i):
        act(pl.ds(pl.multiple_of(i * step, step), step))


def gather_kernel(
    count, len_ref, seq_ref, gain_ref, q_ref, k_ref, v_ref, o_ref, g_ref, u_ref, d_ref, tok_ref, cot_ref,
    a_all, gate_all, up_soon, up, down_t, gain_all, tok_all, dm_all, o_v, a_v, g_v, u_v, d_v, d_t, dm,
    gain_v, chain_send, chain_recv, part_send, part_recv, plane_send, plane_recv, gain_send, gain_recv,
    pair_send, pair_recv, tok_send, tok_recv, local_sem,
):
    plane = count // LINE
    me = Place(plane)
    rows = q_ref.shape[0]
    units = g_ref.shape[1] // LINE
    q_half, kv_half = q_ref.shape[1] // 2, k_ref.shape[1] // 2
    qkv_half = q_half + 2 * kv_half

    def columns(ref, z):
        return ref.at[:, pl.ds(pl.multiple_of(z * units, units), units)]

    local = [copy_in(o_ref, o_v, local_sem.at[0])]
    for h in range(2):
        start = 0
        for ref, width in ((q_ref, q_half), (k_ref, kv_half), (v_ref, kv_half)):
            src = ref.at[:, pl.ds(h * width, width)]
            local.append(copy_in(src, a_v.at[h, :, pl.ds(start, width)], local_sem.at[len(local)]))
            start += width
    early = len(local)
    for src, dst in (
        (d_ref, d_v), (cot_ref, dm), (columns(g_ref, me.z), g_v), (columns(u_ref, me.z), u_v),
        (tok_ref, tok_all.at[me.h, me.t]),
    ):
        local.append(copy_in(src, dst, local_sem.at[len(local)]))
    for copy in local[:early]:
        copy.start()
    keep_a = copy_in(a_v.at[me.h], a_all.at[me.d], local_sem.at[12])
    keep_down = copy_in(d_t, down_t, local_sem.at[13])
    keep_dm = copy_in(dm, dm_all.at[me.z, me.t], local_sem.at[14])
    keep_gate = copy_in(g_v, gate_all.at[me.d], local_sem.at[15])
    keep_up = copy_in(u_v, up.at[me.z], local_sem.at[16])
    keep_gain = copy_in(gain_v, gain_all.at[me.d], local_sem.at[17])

    dms = Chain(me, dm, lambda z: dm_all.at[z, me.t], chain_send, chain_recv)
    planes = (
        PlaneGather(me, 0, a_all, rows, plane_send, plane_recv),
        PlaneGather(me, 1, gate_all, rows, plane_send, plane_recv),
        PlaneGather(me, 2, up_soon, rows, plane_send, plane_recv),
    )

    def part(way, k, kind):
        _, target = reach(me, 1 - way, k)
        src = columns((g_ref, u_ref)[kind - 1], target) if kind else a_v.at[lax.rem(target, 2)]
        dst = (a_all.at[me.d], gate_all.at[me.d], up.at[me.z])[kind]
        return remote(
            src, dst, part_send.at[way, k, kind], part_recv.at[way, k, kind], me.at(target, me.p)
        )

    def pair(z, first=None):
        src = dm_all.at[z, me.t] if first is None else first
        return remote(src, dm_all.at[z, me.t], pair_send.at[z], pair_recv.at[z], me.sibling())

    def keep_soon(soon, src):
        return copy_in(src, up_soon.at[soon * plane + me.p], local_sem.at[18 + soon])

    def start_parts(k, kinds):
        for way in range(2):

            @pl.when(reach(me, 1 - way, k)[0])
            def _():
                for kind in kinds:
                    part(way, k, kind).start()

    def each(k, act):
        for way in range(2):
            have, z = reach(me, way, k)

            @pl.when(have)
            def _():
                act(way, k, z)

    def attn_step(way, k, z):
        arrival(a_all.at[z * plane + me.p], part_recv.at[way, k, 0])
        planes[0].start(z)

    def gate_step(way, k, z):
        arrival(gate_all.at[z * plane + me.p], part_recv.at[way, k, 1])
        planes[1].start(z)

    def up_step(way, k, z):
        arrival(up.at[z], part_recv.at[way, k, 2])

        @pl.when(z == me.z + 1 - 2 * me.h)
        def _():
            planes[2].start(1 - me.h, up.at[z])
            keep_soon(1 - me.h, up.at[z]).start()

    def dm_step(way, k, z):
        dms.wait_block(way, k)
        pair(z).start()

    def give_gain(step):
        target = lax.rem(me.d + step, count)
        return remote(
            gain_v, gain_all.at[me.d], gain_send.at[step], gain_recv.at[step], (target, me.t)
        )

    chosen = len_ref[seq_ref[0]]
    kind_of = lax.broadcasted_iota(jnp.int32, gain_ref.shape, 0)
    gain_v[...] = jnp.where(kind_of == 2, chosen.astype(F32), gain_ref[...].astype(F32)).astype(BF16)
    local[0].wait()
    for h in range(2):
        a_v[h, :, qkv_half:] = o_v[h * q_half : (h + 1) * q_half, :].T
    greet_all(me, count)
    for copy in local[1:early]:
        copy.wait()
    toks = Quad(me, tok_all, tok_send, tok_recv)
    levels = [(0, 1), (0, 2), (0, 3), (3, 1), (1, 1), (1, 2), (1, 3), (3, 2), (2, 1), (2, 2), (2, 3), (3, 3)]

    def start_level(kind, k):
        if kind < 3:
            start_parts(k, (kind,))
        elif k == 1:
            for way in range(2):
                dms.start(way, 0)
            pair(me.z, dm).start()
        else:
            each(k - 1, lambda way, k, z: dms.start(way, k))

    def finish_level(kind, k):
        each(k, (attn_step, gate_step, up_step, dm_step)[kind])

    def forward_level(kind, k):
        if kind < 2:
            each(k, lambda way, k, z: planes[kind].forward(z))

    for level in levels[:2]:
        start_level(*level)
    planes[0].start(me.z, a_v.at[me.h])
    toks.start(tok_ref)
    for step in range(1, count):
        give_gain(step).start()
    for copy in local[early:]:
        copy.start()
    keep_a.start()
    keep_gain.start()

    local[early].wait()
    for z in range(LINE):
        d_t[z] = d_v[z * units : (z + 1) * units, :].T
    keep_down.start()
    local[early + 1].wait()

    def mask(at):
        value = dm[at, :].astype(F32)
        row = lax.broadcasted_iota(jnp.int32, value.shape, 0) + (me.t * dm.shape[0] + at.start)
        dm[at, :] = jnp.where(row < chosen, value, 0.0).astype(BF16)

    row_loop(dm.shape[0], 32, mask)
    keep_dm.start()

    for i, level in enumerate(levels):
        if i == 0:
            for more in levels[2:AHEAD]:
                start_level(*more)
        finish_level(*level)
        if i + AHEAD < len(levels):
            start_level(*levels[i + AHEAD])
        if level == (0, 1):
            toks.forward()
            planes[0].forward(me.z)
            for copy in local[early + 2 : early + 4]:
                copy.wait()
            keep_gate.start()
            keep_up.start()
            planes[1].start(me.z, g_v)
        if level == (0, 3):
            planes[1].forward(me.z)
        if level == (1, 3):
            planes[2].start(me.h, u_v)
            keep_soon(me.h, u_v).start()
        if level == (3, 3):
            planes[2].forward(me.h)
        if i:
            forward_level(*levels[i - 1])
    planes[2].forward(1 - me.h)

    dms.finish()
    for k in range(1, LINE):
        for way in range(2):

            @pl.when(reach(me, 1 - way, k)[0])
            def _():
                for kind in range(3):
                    part(way, k, kind).wait_send()

    for step in range(1, count):
        give_gain(step).wait()
    toks.finish()
    toks.finish_sends()
    for z in range(LINE):
        pair(z).wait()
    for job, zs in zip(planes, (LINE, LINE, SOON)):
        job.finish(range(zs))
    for soon in range(SOON):
        keep_soon(soon, u_v).wait()
    for copy in local[early + 4 :] + [keep_a, keep_down, keep_dm, keep_gate, keep_up, keep_gain]:
        copy.wait()


ANY = pl.BlockSpec(memory_space=pl.ANY)
VMEM = pl.BlockSpec(memory_space=pltpu.VMEM)
SMEM = pl.BlockSpec(memory_space=pltpu.SMEM)
DMA = pltpu.SemaphoreType.DMA


def gather_all(count, lengths, seq, gains, weights, tokens, cotangent):
    w_query, key_weight, _, w_out, w_gate, _, w_down = weights
    rows, q_width = w_query.shape
    width = q_width + key_weight.shape[1]
    units = w_gate.shape[1] // LINE
    plane = count // LINE
    kinds = max(6, plane - 1)
    return pl.pallas_call(
        functools.partial(gather_kernel, count),
        name="gather_all",
        out_shape=(
            jax.ShapeDtypeStruct((count, rows, width), BF16),
            jax.ShapeDtypeStruct((count, rows, units), BF16),
            jax.ShapeDtypeStruct((plane * SOON, rows, units), BF16),
            jax.ShapeDtypeStruct((LINE, rows, units), BF16),
            jax.ShapeDtypeStruct((LINE, rows, units), BF16),
            jax.ShapeDtypeStruct((count,) + gains.shape, gains.dtype),
            jax.ShapeDtypeStruct((2, 2) + tokens.shape, BF16),
            jax.ShapeDtypeStruct((LINE, 2) + cotangent.shape, BF16),
        ),
        in_specs=[SMEM] * 2 + [VMEM] + [ANY] * 9,
        out_specs=(ANY,) * 8,
        scratch_shapes=[
            pltpu.VMEM(w_out.shape, BF16),
            pltpu.VMEM((2, rows, width), BF16),
            pltpu.VMEM((rows, units), BF16),
            pltpu.VMEM((rows, units), BF16),
            pltpu.VMEM(w_down.shape, BF16),
            pltpu.VMEM((LINE, rows, units), BF16),
            pltpu.VMEM(cotangent.shape, BF16),
            pltpu.VMEM(gains.shape, BF16),
            DMA((2, LINE)), DMA((2, LINE)), DMA((2, LINE, 3)), DMA((2, LINE, 3)),
            DMA((3, LINE, kinds)), DMA((3, LINE, kinds)), DMA((count,)), DMA((count,)),
            DMA((LINE,)), DMA((LINE,)), DMA((3,)), DMA((3,)), DMA((18 + SOON,)),
        ],
        compiler_params=pltpu.CompilerParams(
            collective_id=0, has_side_effects=True, vmem_limit_bytes=60 * MB
        ),
    )(lengths, seq, gains, *weights, tokens, cotangent)


RANKS = ((3, 2, 1, 0), (3, 0, 2, 1), (0, 3, 1, 2), (0, 1, 2, 3))
FAR_FIRST = [(way, k) for k in range(LINE - 1, 0, -1) for way in range(2)]


def ranked(me, rank):
    z = jnp.int32(RANKS[0][rank])
    for at in range(1, LINE):
        z = jnp.where(me.z == at, RANKS[at][rank], z)
    return z


def way_to(me, z):
    down = (z < me.z).astype(jnp.int32)
    return down, jnp.where(z < me.z, me.z - z, z - me.z)


def add_rows(target, terms, rows, start=0):
    step = 16

    @pl.loop(0, rows // step)
    def _(i):
        at = pl.ds(pl.multiple_of(start + i * step, step), step)
        total = terms[0][at].astype(F32)
        for term in terms[1:]:
            total += term[at].astype(F32)
        target[at] = total.astype(target.dtype)


def grad_rows(at, per, left_ref, right_ref, first, targets, there):
    tile = 512
    tokens = left_ref.shape[0]

    @pl.loop(0, per // tile)
    def _(n):
        left = left_ref[:, pl.ds(pl.multiple_of(at + n * tile, tile), tile)].T
        for job, ref, start in targets:
            block, units = ref.shape[1], right_ref.shape[1]
            rows = pl.ds(there + n * (tile // block), tile // block)
            for c in range(units // tile):
                grad = jnp.dot(
                    left, right_ref[pl.ds(first + job * tokens, tokens), c * tile : (c + 1) * tile],
                    preferred_element_type=F32,
                )
                ref[rows, :, start + c * tile : start + (c + 1) * tile] = grad.astype(BF16).reshape(
                    tile // block, block, tile
                )


class PlaneSum:
    def __init__(self, me, grad, own, other, first, second, sems, ranks=range(LINE)):
        self.me, self.grad, self.own, self.other, self.first, self.second = me, grad, own, other, first, second
        (
            self.first_send, self.first_recv, self.second_send, self.second_recv, self.load_sem, self.other_sem,
        ) = sems
        self.ranks = ranks
        self.rows = own.shape[1]
        half = self.rows // 2
        self.half = half
        self.halves = (pl.ds(0, half), pl.ds(half, half))
        self.square = me.plane == 4
        if self.square:
            self.near = (me.px, me.py)
            self.far = (me.py, me.px)

    def slot(self, rank):
        return rank - self.ranks[0]

    def block(self, rank, p):
        if callable(self.grad):
            return self.grad(rank, p)
        return self.grad.at[ranked(self.me, rank) * self.me.plane + p]

    def load(self, rank):
        s = self.slot(rank)
        return pltpu.make_async_copy(self.block(rank, self.me.p), self.own.at[s], self.load_sem.at[s])

    def load_other(self, rank, i):
        s = self.slot(rank)
        return pltpu.make_async_copy(
            self.block(rank, self.far[i]).at[self.halves[i]], self.other.at[s, self.halves[i]],
            self.other_sem.at[s, i],
        )

    def load_rank(self, rank):
        self.load(rank).start()
        if self.square:
            for i in range(2):
                self.load_other(rank, i).start()

    def load_all(self):
        for rank in self.ranks:
            self.load_rank(rank)

    def give(self, rank, i, which):
        me, s = self.me, self.slot(rank)
        if not self.square:
            target = lax.rem(me.p + which + 1, me.plane)
            return remote(
                self.block(rank, target), self.first.at[s, which], self.first_send.at[s, which],
                self.first_recv.at[s, which], me.at(me.z, target),
            )
        owner = (self.near[i], me.pd)[which]
        return remote(
            self.block(rank, owner).at[self.halves[i]], self.first.at[s, which, self.halves[i]],
            self.first_send.at[s, 2 * i + which], self.first_recv.at[s, 2 * i + which],
            me.at(me.z, self.near[i]),
        )

    def give_both(self, rank, i):
        s = self.slot(rank)
        return remote(
            self.other.at[s, self.halves[i]], self.second.at[s, self.halves[i]],
            self.second_send.at[s, i], self.second_recv.at[s, i], self.me.at(self.me.z, self.far[i]),
        )

    def gives(self, rank):
        if self.square:
            return [self.give(rank, i, which) for which in (1, 0) for i in range(2)]
        return [self.give(rank, 0, which) for which in range(self.me.plane - 1)]

    def begin(self, rank):
        for copy in self.gives(rank):
            copy.start()

    def middle(self, rank):
        if not self.square:
            return
        s = self.slot(rank)
        for i in range(2):
            arrival(self.first.at[s, 1, self.halves[i]], self.first_recv.at[s, 2 * i + 1])
            self.load_other(rank, i).wait()
            add_rows(
                self.other.at[s], (self.other.at[s], self.first.at[s, 1]), self.half, i * self.half
            )
            self.give_both(rank, i).start()

    def end(self, rank):
        s = self.slot(rank)
        self.load(rank).wait()
        if self.square:
            for i in range(2):
                arrival(self.first.at[s, 0, self.halves[i]], self.first_recv.at[s, 2 * i])
                arrival(self.second.at[s, self.halves[i]], self.second_recv.at[s, i])
            terms = (self.first.at[s, 0], self.second.at[s])
        else:
            for which in range(self.me.plane - 1):
                arrival(self.first.at[s, which], self.first_recv.at[s, which])
            terms = tuple(self.first.at[s, which] for which in range(self.me.plane - 1))
        add_rows(self.own.at[s], (self.own.at[s],) + terms, self.rows)

    def finish(self):
        for rank in self.ranks:
            for copy in self.gives(rank):
                copy.wait_send()
            if self.square:
                for i in range(2):
                    self.give_both(rank, i).wait_send()

    @staticmethod
    def scratch(count, rows, width, ranks=LINE):
        plane = count // LINE
        square = plane == 4
        slots = 2 if square else plane - 1
        small = (ranks, rows, width) if square else (1, 16, 128)
        return [
            pltpu.VMEM((ranks, rows, width), BF16),
            pltpu.VMEM(small, BF16),
            pltpu.VMEM((ranks, slots, rows, width), BF16),
            pltpu.VMEM(small, BF16),
        ], [
            DMA((ranks, max(4, slots))), DMA((ranks, max(4, slots))), DMA((ranks, 2)), DMA((ranks, 2)),
            DMA((ranks,)), DMA((ranks, 2)),
        ]


def dot_cols(left, right):
    return lax.dot_general(left, right, (((1,), (1,)), ((), ())), preferred_element_type=F32)


def feed_forward_kernel(
    plane, h_ref, dm_ref, gate_ref, up_soon, up_rest, down, total_ref, out_ref, grad_ref, sum_ref,
    h_out, inner_out, rows_in, weights, inner, down_grad, part,
    from_pair, from_line, own, other, first, second, first_send, first_recv, second_send, second_recv,
    own_sem, other_sem, chain_send, chain_recv, pass_send, pass_recv, pair_send, pair_recv,
    line_send, line_recv, plane_send, plane_recv, load_sem, dm_sem, grad_sem, out_sem, sum_sem,
):
    me = Place(plane)
    rows, model = h_ref.shape
    units = inner.shape[1]
    wide = 2 * rows
    tokens = LINE * wide
    block = down.shape[1]
    soon = up_soon.shape[0]
    tile = 512

    def slot(z, t):
        return rows_in.at[pl.ds(pl.multiple_of((z * 2 + t) * rows, rows), rows)]

    loads = [
        copy_in(gate_ref, weights.at[:, :, pl.ds(0, units)], load_sem.at[0]),
        copy_in(
            up_soon, weights.at[pl.ds((me.z - me.h) * plane, soon), :, pl.ds(units, units)], load_sem.at[2]
        ),
        copy_in(
            up_rest, weights.at[pl.ds((SOON - me.z + me.h) * plane, soon), :, pl.ds(units, units)],
            load_sem.at[3],
        ),
    ]
    own_down = [
        copy_in(
            down.at[z], weights.at[z * plane + me.p, :, pl.ds(2 * units, units)], load_sem.at[4 + z]
        )
        for z in range(LINE)
    ]
    for load in loads:
        load.start()
    load_dm = pltpu.make_async_copy(dm_ref, rows_in.at[pl.ds(tokens, tokens)], dm_sem)
    load_dm.start()
    keep = pltpu.make_async_copy(h_ref, slot(me.z, me.t), load_sem.at[1])
    keep.start()
    greet_near(me)
    gather = PlaneGather(
        me, 0, weights.at[:, :, pl.ds(2 * units, units)], block, plane_send, plane_recv
    )
    summed = PlaneSum(
        me, down_grad, own, other, first, second,
        (first_send, first_recv, second_send, second_recv, own_sem, other_sem),
    )
    chain = Chain(me, h_ref, lambda z: slot(z, me.t), chain_send, chain_recv)

    def share(z, first=None):
        src = slot(z, me.t) if first is None else first
        return remote(src, slot(z, me.t), pass_send.at[z], pass_recv.at[z], me.sibling())

    for way in range(2):
        chain.start(way, 0)
    share(me.z, h_ref).start()
    for z in range(2):
        gather.start(z, down.at[z])
    for copy in own_down:
        copy.start()

    def w_rows(n, width, column):
        return weights[pl.ds(n * (width // block), width // block), :, pl.ds(column, units)].reshape(
            width, units
        )

    def pair_rows(z, job=0):
        return pl.ds(pl.multiple_of(job * tokens + z * wide, wide), wide)

    def columns(c, job):
        return weights[:, :, pl.ds(pl.multiple_of(job * units + c * tile, tile), tile)].reshape(model, tile)

    def project(z):
        @pl.loop(0, units // tile)
        def _(c):
            here = pl.ds(pl.multiple_of(c * tile, tile), tile)
            h = rows_in[pair_rows(z), :]
            gate = jnp.dot(h, columns(c, 0), preferred_element_type=F32)
            up = jnp.dot(h, columns(c, 1), preferred_element_type=F32)
            sigmoid = jax.nn.sigmoid(gate)
            silu = gate * sigmoid
            inner[pair_rows(z), here] = (silu * up).astype(BF16)
            inner[pair_rows(z, 1), here] = (up * sigmoid * (1.0 + gate * (1.0 - sigmoid))).astype(BF16)
            inner[pair_rows(z, 2), here] = silu.astype(BF16)

    def back(z):
        @pl.loop(0, units // tile)
        def _(c):
            here = pl.ds(pl.multiple_of(c * tile, tile), tile)
            grad_hidden = jnp.dot(rows_in[pair_rows(z, 1), :], columns(c, 2), preferred_element_type=F32)
            for job in range(1, 3):
                at = pair_rows(z, job)
                inner[at, here] = (grad_hidden * inner[at, here].astype(F32)).astype(BF16)

        @pl.loop(0, model // tile)
        def _(n):
            here = pl.ds(pl.multiple_of(n * tile, tile), tile)
            grad = dot_cols(inner[pair_rows(z, 1)], w_rows(n, tile, 0))
            grad += dot_cols(inner[pair_rows(z, 2)], w_rows(n, tile, units))
            part[0, z, :, :, here] = grad.astype(BF16).reshape(2, rows, tile)

        pair(z).start()

    def out(z):
        @pl.loop(0, model // tile)
        def _(n):
            here = pl.ds(pl.multiple_of(n * tile, tile), tile)
            value = dot_cols(inner[pair_rows(z), :], w_rows(n, tile, 2 * units))
            part[1, z, :, :, here] = value.astype(BF16).reshape(2, rows, tile)

        keep_out(z).start()

    def pair(z):
        return remote(
            part.at[0, z, 1 - me.t], from_pair.at[z], pair_send.at[z], pair_recv.at[z], me.sibling()
        )

    half = rows // 2
    halves = (pl.ds(0, half), pl.ds(half, half))

    def pass_on(way, k, i):
        _, target = reach(me, 1 - way, k)
        ahead = me.z + 1 if way == 0 else me.z - 1
        return remote(
            part.at[0, target, me.t, halves[i]], from_line.at[way, k - 1, halves[i]],
            line_send.at[way, k, i], line_recv.at[way, k - 1, i], me.at(ahead, me.p),
        )

    def line(way, k, behind):
        have, z = reach(me, 1 - way, k)
        before = me.z if way == 0 else LINE - 1 - me.z

        @pl.when(jnp.logical_and(have, before == behind))
        def _():
            pair(z).wait_recv()
            terms = (part.at[0, z, me.t], from_pair.at[z])
            if behind:
                terms += (from_line.at[way, k],)
            for i in range(2):
                if behind:
                    arrival(from_line.at[way, k, halves[i]], line_recv.at[way, k, i])
                add_rows(part.at[0, z, me.t], terms, half, i * half)
                pass_on(way, k, i).start()

    def total():
        pair(me.z).wait_recv()
        add_rows(total_ref, (part.at[0, me.z, me.t], from_pair.at[me.z]), rows)
        for way in range(2):

            @pl.when(reach(me, way, 1)[0])
            def _():
                for i in range(2):
                    arrival(from_line.at[way, 0, halves[i]], line_recv.at[way, 0, i])
                    add_rows(total_ref, (total_ref, from_line.at[way, 0]), half, i * half)

    per = plane * block

    def down_grads(rank):
        z = ranked(me, rank)
        grad_rows(
            z * per, per, rows_in.at[pl.ds(tokens, tokens)], inner, 0, [(0, down_grad, 0)], z * plane
        )
        summed.load_rank(rank)

    keeps = [
        copy_in(weights.at[pl.ds(0, plane), :, pl.ds(0, 2 * units)], grad_ref, grad_sem.at[0]),
        copy_in(rows_in.at[pl.ds(0, tokens)], h_out, grad_sem.at[1]),
        copy_in(inner.at[pl.ds(tokens, 2 * tokens)], inner_out, grad_sem.at[2]),
    ]

    def grads():
        targets = [(0, weights, 0), (1, weights, units)]
        z = ranked(me, 0)
        grad_rows(z * per, per, rows_in.at[pl.ds(0, tokens)], inner, tokens, targets, 0)

    def keep_sum(rank):
        return copy_in(own.at[rank], sum_ref.at[rank], sum_sem.at[rank])

    keep.wait()
    for load in loads:
        load.wait()
    for k in range(LINE):
        for way in range(2 if k else 1):
            have, z = reach(me, way, k)

            @pl.when(have)
            def _():
                if k:
                    chain.wait_block(way, k)
                    chain.start(way, k)
                    share(z).start()
                arrival(slot(z, 1 - me.t), pass_recv.at[z])
                project(z)

        gather.forward(k)
        if k + 2 < LINE:
            gather.start(k + 2, down.at[k + 2])
    def keep_out(z):
        return copy_in(part.at[1, z], out_ref.at[z], out_sem.at[z])

    load_dm.wait()
    keeps[1].start()
    down_grads(0)
    summed.begin(0)
    for copy in own_down:
        copy.wait()
    gather.finish()
    passing = {1: (1, 2), 2: (2, 1), 3: (1, 1)}
    for rank in range(LINE):
        if rank:
            down_grads(rank)
            if rank - 1 in passing:
                for way in range(2):
                    line(way, passing[rank - 1][1], passing[rank - 1][0])
            summed.middle(rank - 1)
            summed.begin(rank)
            if rank > 1:
                summed.end(rank - 2)
                keep_sum(rank - 2).start()
        back(ranked(me, rank))
        if rank < LINE - 1:
            out(ranked(me, rank))
            for way in range(2):
                line(way, LINE - 1 - rank, 0)
    for way in range(2):
        line(way, passing[LINE - 1][1], passing[LINE - 1][0])
    keeps[2].start()
    summed.middle(LINE - 1)
    summed.end(LINE - 2)
    keep_sum(LINE - 2).start()
    grads()
    keeps[0].start()
    out(ranked(me, LINE - 1))
    summed.end(LINE - 1)
    keep_sum(LINE - 1).start()
    total()
    summed.finish()
    chain.finish()
    for z in range(LINE):
        share(z).wait_send()
        keep_out(z).wait()
        keep_sum(z).wait()
        pair(z).wait_send()
    for copy in keeps:
        copy.wait()
    for k in range(1, LINE):
        for way in range(2):

            @pl.when(reach(me, 1 - way, k)[0])
            def _():
                for i in range(2):
                    pass_on(way, k, i).wait_send()


def feed_forward(count, h, dm_all, gate_all, up_soon, up_rest, down):
    rows, model = h.shape
    _, block, units = down.shape
    kinds = max(6, count // LINE - 1)
    buffers, sems = PlaneSum.scratch(count, block, units)
    tokens = LINE * 2 * rows
    vmem = pl.BlockSpec(memory_space=pltpu.VMEM)
    return pl.pallas_call(
        functools.partial(feed_forward_kernel, count // LINE),
        name="feed_forward",
        out_shape=(
            jax.ShapeDtypeStruct((rows, model), F32),
            jax.ShapeDtypeStruct((LINE, 2, rows, model), BF16),
            jax.ShapeDtypeStruct((count // LINE, block, 2 * units), BF16),
            jax.ShapeDtypeStruct((LINE, block, units), BF16),
            jax.ShapeDtypeStruct((tokens, model), BF16),
            jax.ShapeDtypeStruct((2 * tokens, units), BF16),
        ),
        in_specs=[ANY] * 6,
        out_specs=(vmem,) + (ANY,) * 5,
        scratch_shapes=[
            pltpu.VMEM((2 * tokens, model), BF16),
            pltpu.VMEM((count, block, 3 * units), BF16),
            pltpu.VMEM((3 * tokens, units), BF16),
            pltpu.VMEM((count, block, units), BF16),
            pltpu.VMEM((2, LINE, 2, rows, model), BF16),
            pltpu.VMEM((LINE, rows, model), BF16),
            pltpu.VMEM((2, LINE - 1, rows, model), BF16),
            *buffers,
            *sems,
            DMA((2, LINE)), DMA((2, LINE)), DMA((LINE,)), DMA((LINE,)), DMA((LINE,)), DMA((LINE,)),
            DMA((2, LINE, 2)), DMA((2, LINE, 2)), DMA((1, LINE, kinds)), DMA((1, LINE, kinds)),
            DMA((4 + LINE,)), DMA, DMA((LINE,)), DMA((LINE,)), DMA((LINE,)),
        ],
        compiler_params=pltpu.CompilerParams(
            collective_id=1, has_side_effects=True, vmem_limit_bytes=60 * MB
        ),
    )(h, dm_all, gate_all, up_soon, up_rest, down)


def columns_of(weights, start, width):
    count, rows, _ = weights.shape
    return weights[:, :, pl.ds(start, width)].reshape(count * rows, width)


def rows_of(weights, n, height, start, width):
    _, rows, _ = weights.shape
    per = height // rows
    return weights[pl.ds(n * per, per), :, pl.ds(start, width)].reshape(height, width)


def attention_forward_kernel(
    plane, lens_ref, cos_ref, sin_ref, tok_in, a_ref, up, down_t, gain_ref, x1_out, h2_out, h1_out,
    qkv_out, probs_out, o_out, up_rest, down, weights, tok_ref, x1_ref, h2_ref, h1_ref, qkv_ref, probs_ref,
    o_ref, part, from_pair, low, from_mate, plane_send, plane_recv, part_send, part_recv, sum_send,
    sum_recv, load_sem, keep_sem,
):
    me = Place(plane)
    _, _, rows, model = tok_ref.shape
    wide = 2 * rows
    q_width = o_ref.shape[1]
    heads = q_width // HEAD_SIZE
    kv_width = (qkv_ref.shape[1] - q_width) // 2
    kv_heads = kv_width // HEAD_SIZE
    half = HEAD_SIZE // 2
    load_tok = copy_in(tok_in, tok_ref, load_sem.at[0])
    load_tok.start()
    load = copy_in(a_ref, weights, load_sem.at[1])
    load.start()
    far = SOON - (me.z - me.h)
    keep = [
        copy_in(up.at[far + z], up_rest.at[z * plane + me.p], load_sem.at[2 + z])
        for z in range(LINE - SOON)
    ]
    keep.append(copy_in(down_t.at[me.z], down.at[me.z], load_sem.at[2 + LINE]))
    for copy in keep:
        copy.start()
    outs = [
        copy_in(src, dst, keep_sem.at[i])
        for i, (src, dst) in enumerate(
            (
                (h1_ref, h1_out), (qkv_ref, qkv_out), (probs_ref, probs_out), (o_ref, o_out),
                (x1_ref, x1_out), (h2_ref, h2_out),
            )
        )
    ]
    greet_near(me)
    gather = PlaneGather(me, 0, up_rest, up.shape[1], plane_send, plane_recv)
    for z in range(LINE - SOON):
        gather.start(z, up.at[far + z])

    def give_down(way, k):
        _, target = reach(me, 1 - way, k)
        return remote(
            down_t.at[target], down.at[me.z], part_send.at[way, k], part_recv.at[way, k],
            me.at(target, me.p),
        )

    for k in range(1, LINE):
        for way in range(2):

            @pl.when(reach(me, 1 - way, k)[0])
            def _():
                give_down(way, k).start()

    span = model // (plane * LINE)
    for d in range(plane * LINE):
        gain_ref[:, d * span : (d + 1) * span] = lens_ref[d].astype(F32)[0:2, :span]
    load_tok.wait()

    for n in range(4):

        def norm(at, n=n):
            x = tok_ref[n // 2, n % 2, at, :].astype(F32)
            factor = lax.rsqrt(jnp.mean(x * x, -1, keepdims=True) + EPS)
            h1_ref[pl.ds(n * rows + at.start, at.size), :] = (x * factor * gain_ref[0:1, :]).astype(BF16)

        row_loop(rows, 32, norm)
    outs[0].start()
    load.wait()

    def project(i):
        start = pl.multiple_of(i * HEAD_SIZE, HEAD_SIZE)
        return start, jnp.dot(
            h1_ref[...], columns_of(weights, start, HEAD_SIZE), preferred_element_type=F32
        )

    @pl.loop(0, heads + kv_heads)
    def _(i):
        start, values = project(i)
        cos, sin = cos_ref[...], sin_ref[...]
        for n in range(2):
            at = slice(n * wide, (n + 1) * wide)
            first, second = values[at, :half], values[at, half:]
            qkv_ref[at, pl.ds(start, half)] = (first * cos - second * sin).astype(BF16)
            qkv_ref[at, pl.ds(start + half, half)] = (second * cos + first * sin).astype(BF16)

    @pl.loop(heads + kv_heads, heads + 2 * kv_heads)
    def _(i):
        start, values = project(i)
        qkv_ref[:, pl.ds(start, HEAD_SIZE)] = values.astype(BF16)

    outs[1].start()
    gather.forward(0)
    row = lax.broadcasted_iota(jnp.int32, (wide, wide), 0)
    key = lax.broadcasted_iota(jnp.int32, (wide, wide), 1)
    tile = 512
    total = QuadSum(me, part, from_pair, low, from_mate, sum_send, sum_recv)

    def attend(n):
        length = lens_ref[me.d + (n - me.h) * plane].astype(F32)[2:3, 0:1]
        allowed = jnp.logical_and(key <= row, key.astype(F32) < length)
        at = pl.ds(pl.multiple_of(n * wide, wide), wide)
        for i in range(heads):
            m = i * kv_heads // heads
            q = qkv_ref[at, i * HEAD_SIZE : (i + 1) * HEAD_SIZE]
            k = qkv_ref[at, q_width + m * HEAD_SIZE : q_width + (m + 1) * HEAD_SIZE]
            v_start = q_width + kv_width + m * HEAD_SIZE
            v = qkv_ref[at, v_start : v_start + HEAD_SIZE]
            scores = dot_cols(q, k) * HEAD_SIZE ** (-0.5)
            scores = jnp.where(allowed, scores, -1e30)
            grown = jnp.exp(scores - jnp.max(scores, -1, keepdims=True))
            probs = grown / jnp.sum(grown, -1, keepdims=True)
            probs_ref[n * heads + i] = probs
            o_ref[at, i * HEAD_SIZE : (i + 1) * HEAD_SIZE] = jnp.dot(
                probs.astype(BF16), v, preferred_element_type=F32
            ).astype(BF16)

        @pl.loop(0, model // tile)
        def _(c):
            here = pl.ds(pl.multiple_of(c * tile, tile), tile)
            value = dot_cols(o_ref[at, :], rows_of(weights, c, tile, q_width + 2 * kv_width, q_width))
            part[n, :, :, here] = value.reshape(2, rows, tile)

        total.start(n)

    attend(1 - me.h)
    total.to_mate()
    attend(me.h)
    outs[2].start()
    outs[3].start()
    for z in range(1, LINE - SOON):
        gather.forward(z)
    total.wait()

    def add(at):
        x1 = tok_ref[me.h, me.t, at, :].astype(F32) + total.rows(at)
        x1_ref[at, :] = x1
        factor = lax.rsqrt(jnp.mean(x1 * x1, -1, keepdims=True) + EPS)
        h2_ref[at, :] = (x1 * factor * gain_ref[1:2, :]).astype(BF16)

    row_loop(rows, 32, add)
    outs[4].start()
    outs[5].start()
    total.finish_sends()
    gather.finish(range(LINE - SOON))
    for k in range(1, LINE):
        for way in range(2):

            @pl.when(reach(me, 1 - way, k)[0])
            def _():
                give_down(way, k).wait_send()

            @pl.when(reach(me, way, k)[0])
            def _():
                arrival(down.at[me.z], part_recv.at[way, k])

    for copy in keep + outs:
        copy.wait()


def attention_forward(count, q_width, kv_width, lens, cos, sin, tokens_all, attn_all, up, down_t):
    _, _, rows, model = tokens_all.shape
    wide = 2 * rows
    plane = count // LINE
    kinds = max(6, plane - 1)
    outs = (
        jax.ShapeDtypeStruct((rows, model), F32),
        jax.ShapeDtypeStruct((rows, model), BF16),
        jax.ShapeDtypeStruct((2 * wide, model), BF16),
        jax.ShapeDtypeStruct((2 * wide, q_width + 2 * kv_width), BF16),
        jax.ShapeDtypeStruct((2 * q_width // HEAD_SIZE, wide, wide), F32),
        jax.ShapeDtypeStruct((2 * wide, q_width), BF16),
    )
    return pl.pallas_call(
        functools.partial(attention_forward_kernel, plane),
        name="attention_forward",
        out_shape=(jax.ShapeDtypeStruct((2, model), F32),)
        + outs
        + (
            jax.ShapeDtypeStruct((count - SOON * plane,) + up.shape[1:], BF16),
            jax.ShapeDtypeStruct(down_t.shape, BF16),
        ),
        in_specs=[VMEM] * 3 + [ANY] * 4,
        out_specs=(VMEM,) + (ANY,) * 8,
        scratch_shapes=[
            pltpu.VMEM(attn_all.shape, BF16),
            pltpu.VMEM(tokens_all.shape, BF16),
            *[pltpu.VMEM(out.shape, out.dtype) for out in outs],
            pltpu.VMEM((2, 2, rows, model), F32),
            pltpu.VMEM((2, rows, model), F32),
            pltpu.VMEM((rows, model), BF16),
            pltpu.VMEM((rows, model), BF16),
            DMA((1, LINE, kinds)), DMA((1, LINE, kinds)), DMA((2, LINE)), DMA((2, LINE)), DMA((3,)),
            DMA((3,)), DMA((3 + LINE,)), DMA((6,)),
        ],
        compiler_params=pltpu.CompilerParams(
            collective_id=2, has_side_effects=True, vmem_limit_bytes=60 * MB
        ),
    )(lens, cos, sin, tokens_all, attn_all, up, down_t)


def attention_backward_kernel(
    plane, gain_ref, cos_ref, sin_ref, total_in, x1_in, dm_in, tok_in, h1_in, qkv_in, probs_in, o_in,
    a_ref, gw_ref, sum_ref, h_in, inner_in, ga_ref, w_out, grad_tokens, gain_blocks, gain_parts, weights, own, other, first, second,
    total_ref, x1_ref, dm_ref, tok_ref, h1_ref, qkv_ref, probs_ref, o_ref, rows_in, inner, gw, dx, da, do,
    dqkv, dh1, from_pair, low, from_mate, first_send, first_recv, second_send, second_recv, load_sem,
    other_sem, part_send, part_recv, da_send, da_recv, sum_send, sum_recv, a_sem, keep_sem, grad_sem, in_sem,
):
    me = Place(plane)
    rows, model = tok_ref.shape
    block = weights.shape[1]
    q_width = o_ref.shape[1]
    heads = q_width // HEAD_SIZE
    seq = 2 * rows
    qkv_width = qkv_ref.shape[1]
    kv_width = (qkv_width - q_width) // 2
    kv_heads = kv_width // HEAD_SIZE
    half = HEAD_SIZE // 2
    scale = HEAD_SIZE ** (-0.5)
    summed = PlaneSum(
        me, lambda rank, p: gw.at[(rank - 1) * plane + p] if rank else gw_ref.at[p],
        own, other, first, second,
        (first_send, first_recv, second_send, second_recv, load_sem, other_sem),
    )
    ins = [
        copy_in(src, dst, in_sem.at[i])
        for i, (src, dst) in enumerate(
            (
                (total_in, total_ref), (x1_in, x1_ref), (dm_in.at[me.z, me.t], dm_ref),
                (tok_in.at[me.h, me.t], tok_ref),
                (h1_in, h1_ref), (qkv_in, qkv_ref), (probs_in, probs_ref), (o_in, o_ref),
                (h_in, rows_in), (inner_in, inner),
            )
        )
    ]
    for copy in ins[:3] + ins[8:]:
        copy.start()
    load = pltpu.make_async_copy(a_ref, weights, a_sem)
    load.start()
    for copy in ins[3:8]:
        copy.start()
    summed.load_rank(0)
    greet_near(me)

    wide = own.shape[2]
    spans = (pl.ds(0, wide), pl.ds(wide, sum_ref.shape[2]))

    def part(rank, kind):
        target = ranked(me, rank)
        way, k = way_to(me, target)
        return remote(
            (own, sum_ref)[kind].at[rank], w_out.at[me.z, :, spans[kind]], part_send.at[way, k, kind],
            part_recv.at[way, k, kind], me.at(target, me.p),
        )

    keeps = [
        copy_in((own, sum_ref)[kind].at[LINE - 1], w_out.at[me.z, :, spans[kind]], keep_sem.at[kind])
        for kind in range(2)
    ]
    das = Quad(me, da, da_send, da_recv)
    dh1_sum = QuadSum(me, dh1, from_pair, low, from_mate, sum_send, sum_recv)

    def mid_norm():
        gain_parts[...] = jnp.zeros_like(gain_parts)

        def act(at):
            x, up = x1_ref[at, :], total_ref[at, :]
            factor = lax.rsqrt(jnp.mean(x * x, -1, keepdims=True) + EPS)
            scaled = up * gain_ref[1:2, :]
            grad = dm_ref[at, :].astype(F32) + (
                factor * scaled - x * factor**3 * jnp.mean(scaled * x, -1, keepdims=True)
            )
            dx[at, :] = grad
            da[me.h, me.t, at, :] = grad.astype(BF16)
            gain_parts[1:2, :] += jnp.sum(up * x * factor, 0, keepdims=True)

        row_loop(rows, 32, act)
        das.start()

    def grad_o():
        load.wait()
        das.finish()

        @pl.loop(0, q_width // HEAD_SIZE)
        def _(c):
            here = pl.multiple_of(c * HEAD_SIZE, HEAD_SIZE)
            value = jnp.dot(
                da[...].reshape(2 * seq, model),
                columns_of(weights, qkv_width + here, HEAD_SIZE),
                preferred_element_type=F32,
            )
            do[:, pl.ds(here, HEAD_SIZE)] = value.astype(BF16)

    def rotate(values, rows_at, start):
        first, second = values[:, :half], values[:, half:]
        cos, sin = cos_ref[...], sin_ref[...]
        dqkv[rows_at, start : start + half] = (first * cos + second * sin).astype(BF16)
        dqkv[rows_at, start + half : start + 2 * half] = (second * cos - first * sin).astype(BF16)

    def grad_heads(n):
        group = heads // kv_heads
        here = slice(n * seq, (n + 1) * seq)
        for m in range(kv_heads):
            at_k = q_width + m * HEAD_SIZE
            at_v = at_k + kv_width
            k = qkv_ref[here, at_k : at_k + HEAD_SIZE]
            v = qkv_ref[here, at_v : at_v + HEAD_SIZE]
            grad_k = grad_v = None
            for i in range(m * group, (m + 1) * group):
                at = slice(i * HEAD_SIZE, (i + 1) * HEAD_SIZE)
                probs = probs_ref[n * heads + i]
                grad_probs = dot_cols(do[here, at], v)
                grad_scores = probs * (
                    grad_probs - jnp.sum(probs * grad_probs, -1, keepdims=True)
                )
                low_scores = grad_scores.astype(BF16)
                rotate(
                    jnp.dot(low_scores, k, preferred_element_type=F32) * scale, here, i * HEAD_SIZE
                )
                more_k = dot_tn(low_scores, qkv_ref[here, at])
                more_v = dot_tn(probs.astype(BF16), do[here, at])
                grad_k = more_k if grad_k is None else grad_k + more_k
                grad_v = more_v if grad_v is None else grad_v + more_v
            rotate(grad_k * scale, here, at_k)
            dqkv[here, at_v : at_v + HEAD_SIZE] = grad_v.astype(BF16)

    tile = 512

    def grad_h1():
        @pl.loop(0, model // tile)
        def _(n):
            here = pl.ds(pl.multiple_of(n * tile, tile), tile)
            value = dot_cols(dqkv[...], rows_of(weights, n, tile, 0, qkv_width))
            dh1[:, :, :, here] = value.reshape(2, 2, rows, tile)

        for h in range(2):
            dh1_sum.start(h)

    def keep_grads(n):
        per = tile // block
        return pltpu.make_async_copy(
            weights.at[pl.ds(n * per, per)], ga_ref.at[pl.ds(n * per, per)], grad_sem.at[n]
        )

    def grads():
        @pl.loop(0, model // tile)
        def _(n):
            here = pl.ds(pl.multiple_of(n * tile, tile), tile)
            there = pl.ds(n * (tile // block), tile // block)
            left = h1_ref[:, here].T
            for c in range(qkv_width // tile):
                at = slice(c * tile, (c + 1) * tile)
                value = jnp.dot(left, dqkv[:, at], preferred_element_type=F32)
                weights[there, :, at] = value.astype(BF16).reshape(tile // block, block, tile)
            left = da[:, :, :, here].reshape(2 * seq, tile).T
            for c in range(q_width // tile):
                at = slice(c * tile, (c + 1) * tile)
                value = jnp.dot(left, o_ref[:, at], preferred_element_type=F32)
                at = slice(qkv_width + c * tile, qkv_width + (c + 1) * tile)
                weights[there, :, at] = value.astype(BF16).reshape(tile // block, block, tile)

        for n in range(model // tile):
            keep_grads(n).start()

    def in_norm():
        dh1_sum.wait()

        def act(at):
            x = tok_ref[at, :].astype(F32)
            up = dh1_sum.rows(at)
            factor = lax.rsqrt(jnp.mean(x * x, -1, keepdims=True) + EPS)
            scaled = up * gain_ref[0:1, :]
            grad_tokens[at, :] = dx[at, :] + (
                factor * scaled - x * factor**3 * jnp.mean(scaled * x, -1, keepdims=True)
            )
            gain_parts[0:1, :] += jnp.sum(up * x * factor, 0, keepdims=True)

        row_loop(rows, 32, act)

    summed.begin(0)
    for rank in range(LINE - 1):
        part(rank, 1).start()
    keeps[1].start()
    def mlp_grads(rank):
        per = plane * block
        targets = [(0, gw, 0), (1, gw, inner.shape[1])]
        z = ranked(me, rank)
        grad_rows(z * per, per, rows_in, inner, 0, targets, (rank - 1) * plane)
        summed.load_rank(rank)

    for copy in ins[:3]:
        copy.wait()
    mid_norm()
    for copy in ins[8:]:
        copy.wait()
    mlp_grads(1)
    summed.middle(0)
    summed.begin(1)
    mlp_grads(2)
    das.forward()
    for copy in ins[3:8]:
        copy.wait()
    summed.end(0)
    part(0, 0).start()
    grad_o()
    summed.middle(1)
    summed.begin(2)
    grad_heads(0)
    grad_heads(1)
    mlp_grads(3)
    summed.end(1)
    part(1, 0).start()
    grad_h1()
    summed.middle(2)
    summed.begin(3)
    dh1_sum.to_mate()
    grads()
    summed.end(2)
    part(2, 0).start()
    summed.middle(3)
    in_norm()
    summed.end(3)

    span = model // gain_blocks.shape[0]
    gain_blocks[...] = jnp.zeros_like(gain_blocks)
    for d in range(gain_blocks.shape[0]):
        gain_blocks[d, 0:2, :span] = gain_parts[:, d * span : (d + 1) * span]
    keeps[0].start()
    for kind in range(2):
        for rank in range(LINE - 1):
            part(rank, kind).wait_send()
        for way, k in FAR_FIRST:

            @pl.when(reach(me, way, k)[0])
            def _():
                arrival(w_out.at[me.z, :, spans[kind]], part_recv.at[way, k, kind])

    summed.finish()
    das.finish_sends()
    dh1_sum.finish_sends()
    for n in range(model // tile):
        keep_grads(n).wait()
    for copy in keeps:
        copy.wait()


def attention_backward(
    count, gains, cos, sin, total, x1, dm_all, tokens_all, h1, qkv, probs, o, attn_all, grad_mlp, first_sum, rows_in,
    inner,
):
    _, _, rows, model = tokens_all.shape
    _, block, _ = attn_all.shape
    buffers, sems = PlaneSum.scratch(count, block, grad_mlp.shape[2])
    return pl.pallas_call(
        functools.partial(attention_backward_kernel, count // LINE),
        name="attention_backward",
        out_shape=(
            jax.ShapeDtypeStruct(attn_all.shape, BF16),
            jax.ShapeDtypeStruct((LINE, block, grad_mlp.shape[2] + first_sum.shape[2]), BF16),
            jax.ShapeDtypeStruct((rows, model), F32),
            jax.ShapeDtypeStruct((count, 8, max(128, model // count)), F32),
        ),
        in_specs=[VMEM] * 3 + [ANY] * 13,
        out_specs=(ANY, ANY, VMEM, VMEM),
        scratch_shapes=[
            pltpu.VMEM((2, model), F32),
            pltpu.VMEM(attn_all.shape, BF16),
            *buffers,
            *[
                pltpu.VMEM(ref.shape, ref.dtype)
                for ref in (total, x1, dm_all[0, 0], dm_all[0, 0], h1, qkv, probs, o, rows_in, inner)
            ],
            pltpu.VMEM(((LINE - 1) * grad_mlp.shape[0],) + grad_mlp.shape[1:], BF16),
            pltpu.VMEM((rows, model), F32),
            pltpu.VMEM((2, 2, rows, model), BF16),
            pltpu.VMEM(o.shape, BF16),
            pltpu.VMEM(qkv.shape, BF16),
            pltpu.VMEM((2, 2, rows, model), F32),
            pltpu.VMEM((2, rows, model), F32),
            pltpu.VMEM((rows, model), BF16),
            pltpu.VMEM((rows, model), BF16),
            *sems,
            DMA((2, LINE, 2)), DMA((2, LINE, 2)), DMA((3,)), DMA((3,)), DMA((3,)), DMA((3,)), DMA, DMA((2,)),
            DMA((model // 512,)), DMA((10,)),
        ],
        compiler_params=pltpu.CompilerParams(
            collective_id=3, has_side_effects=True, vmem_limit_bytes=60 * MB
        ),
    )(gains, cos, sin, total, x1, dm_all, tokens_all, h1, qkv, probs, o, attn_all, grad_mlp, first_sum, rows_in, inner)


def grad_sum_kernel(
    count, gain_ref, x1_in, ga_ref, out_ref, a_out, output, gain_out, own, other, first, second, x1_ref,
    landed, out_own, out_pair, out_line, gain_in, gain_pair, first_send, first_recv, second_send, second_recv,
    load_sem, other_sem, part_send, part_recv, out_send, out_recv, load_out_sem, pair_send, pair_recv, gain_send, gain_recv,
):
    plane = count // LINE
    me = Place(plane)
    rows = a_out.shape[1]
    summed = PlaneSum(
        me, ga_ref, own, other, first, second,
        (first_send, first_recv, second_send, second_recv, load_sem, other_sem),
    )

    class Line:
        def __init__(self, held, landing, send, recv):
            self.held, self.landing, self.send, self.recv = held, landing, send, recv

        def pass_on(self, rank):
            way, k = way_to(me, ranked(me, rank))
            ahead = jnp.where(way == 0, me.z + 1, me.z - 1)
            return remote(
                self.held(rank), self.landing.at[way, k - 1], self.send.at[way, k],
                self.recv.at[way, k - 1], me.at(ahead, me.p),
            )

        def step(self, rank):
            way, k = way_to(me, ranked(me, rank))
            before = jnp.where(way == 0, me.z, LINE - 1 - me.z)
            held = self.held(rank)

            @pl.when(before > 0)
            def _():
                arrival(self.landing.at[way, k], self.recv.at[way, k])
                add_rows(held, (held, self.landing.at[way, k]), held.shape[0])

            self.pass_on(rank).start()

        def total(self, act):
            for way in range(2):

                @pl.when(reach(me, way, 1)[0])
                def _():
                    arrival(self.landing.at[way, 0], self.recv.at[way, 0])
                    act(self.landing.at[way, 0])

        def finish(self):
            for rank in range(LINE - 1):
                self.pass_on(rank).wait_send()

    def part(rank):
        target = ranked(me, rank)
        way, k = way_to(me, target)
        return remote(
            own.at[rank], landed.at[me.z], part_send.at[way, k], part_recv.at[way, k],
            me.at(target, me.p),
        )

    outs = Line(lambda rank: out_own.at[ranked(me, rank)], out_line, out_send, out_recv)
    summed.load_all()
    load_out = copy_in(out_ref.at[:, me.t], out_own, load_out_sem.at[0])
    load_out.start()
    load_x1 = copy_in(x1_in, x1_ref, load_out_sem.at[1])
    load_x1.start()
    greet_all(me, count)

    def give_gain(step):
        target = lax.rem(me.d + step, count)
        return remote(
            gain_ref.at[target], gain_in.at[step], gain_send.at[step], gain_recv.at[step], (target, me.t)
        )

    summed.begin(0)
    for step in range(1, count):
        give_gain(step).start()
    pairs = [
        remote(
            out_ref.at[ranked(me, rank), 1 - me.t], out_pair.at[ranked(me, rank)], pair_send.at[rank],
            pair_recv.at[rank], me.sibling(),
        )
        for rank in range(LINE)
    ]
    for copy in pairs:
        copy.start()
    load_out.wait()
    def out_step(rank):
        z = ranked(me, rank)
        pairs[rank].wait_recv()
        add_rows(out_own.at[z], (out_own.at[z], out_pair.at[z]), out_own.shape[1])
        if rank < LINE - 1:

            @pl.when(jnp.logical_or(me.z == 0, me.z == LINE - 1))
            def _():
                outs.step(rank)

    out_step(0)
    at_end = jnp.logical_or(me.z == 0, me.z == LINE - 1)

    def out_start(at):
        x1_ref[at, :] = x1_ref[at, :] + out_own[me.z, at, :].astype(F32)

    def add_out(landed):
        def act(at):
            x1_ref[at, :] = x1_ref[at, :] + landed[at, :].astype(F32)

        row_loop(output.shape[0], 16, act)

    def out_end(at):
        output[at, :] = x1_ref[at, :].astype(BF16)

    for rank in range(LINE):
        summed.middle(rank)
        if rank + 1 < LINE:
            summed.begin(rank + 1)
            out_step(rank + 1)
        else:
            load_x1.wait()
            total = gain_ref[me.d]
            for step in range(1, count):
                give_gain(step).wait()
                total += gain_in[step]
            gain_pair[0] = total
            swap = remote(
                gain_pair.at[0], gain_pair.at[1], gain_send.at[0], gain_recv.at[0], me.sibling()
            )
            swap.start()
            swap.wait()
            gain_out[...] = gain_pair[0] + gain_pair[1]
        summed.end(rank)
        if rank < LINE - 1:
            part(rank).start()
        for late in {0: (0,), 1: (2, 1)}.get(rank, ()):
            @pl.when(jnp.logical_not(at_end))
            def _():
                outs.step(late)


    row_loop(output.shape[0], 16, out_start)
    outs.total(add_out)
    row_loop(output.shape[0], 16, out_end)
    keep = copy_in(own.at[LINE - 1], landed.at[me.z], load_out_sem.at[2])
    keep.start()
    for way, k in FAR_FIRST:
        have, z = reach(me, way, k)

        @pl.when(have)
        def _():
            arrival(landed.at[z], part_recv.at[way, k])

    keep.wait()
    for h in range(2):
        add_rows(a_out.at[h], tuple(landed.at[z] for z in range(h, LINE, 2)), rows)
    for rank in range(LINE - 1):
        part(rank).wait_send()
    for copy in pairs:
        copy.wait_send()
    outs.finish()
    summed.finish()


def grad_sum(count, x1, ga, out_parts, gains):
    _, block, width = ga.shape
    _, _, rows, model = out_parts.shape
    buffers, sems = PlaneSum.scratch(count, block, width)
    return pl.pallas_call(
        functools.partial(grad_sum_kernel, count),
        name="grad_sum",
        out_shape=(
            jax.ShapeDtypeStruct((2, block, width), F32),
            jax.ShapeDtypeStruct((rows, model), BF16),
            jax.ShapeDtypeStruct(gains.shape[1:], F32),
        ),
        in_specs=[VMEM] + [ANY] * 3,
        out_specs=(VMEM,) * 3,
        scratch_shapes=[
            *buffers,
            pltpu.VMEM((rows, model), F32),
            pltpu.VMEM((LINE, block, width), BF16),
            pltpu.VMEM((LINE, rows, model), BF16),
            pltpu.VMEM((LINE, rows, model), BF16),
            pltpu.VMEM((2, LINE - 1, rows, model), BF16),
            pltpu.VMEM(gains.shape, F32),
            pltpu.VMEM((2,) + gains.shape[1:], F32),
            *sems,
            DMA((2, LINE)), DMA((2, LINE)), DMA((2, LINE)), DMA((2, LINE)), DMA((3,)), DMA((LINE,)),
            DMA((LINE,)), DMA((count,)), DMA((count,)),
        ],
        compiler_params=pltpu.CompilerParams(
            collective_id=4, has_side_effects=True, vmem_limit_bytes=60 * MB
        ),
    )(gains, x1, ga, out_parts)


def layouts_kernel(
    gain_ref, a_ref, mlp_ref, output_ref, tokens_ref, gain_attn, gain_mlp, q_out, k_out, v_out, o_out, gate_out, up_out, down_out,
    output_out, tokens_out, a_v, mlp_v, output_v, tokens_v, q_v, k_v, v_v, o_v, gate_v, up_v, down_v,
    in_sem, out_sem,
):
    ins = [
        copy_in(src, dst, in_sem.at[i])
        for i, (src, dst) in enumerate(
            ((mlp_ref, mlp_v), (a_ref, a_v), (tokens_ref, tokens_v), (output_ref, output_v))
        )
    ]
    for copy in ins:
        copy.start()
    sent = []

    def give(src, dst):
        sent.append(copy_in(src, dst, out_sem.at[len(sent)]))
        sent[-1].start()

    span = gain_attn.shape[1]
    gain_attn[...] = gain_ref[0:1, :span]
    gain_mlp[...] = gain_ref[1:2, :span]
    units = mlp_v.shape[2] // 3
    ins[0].wait()
    for z in range(LINE):
        here = pl.ds(z * units, units)
        gate_v[:, here] = mlp_v[z, :, :units].astype(F32)
        give(gate_v.at[:, here], gate_out.at[:, here])
        up_v[:, here] = mlp_v[z, :, units : 2 * units].astype(F32)
        give(up_v.at[:, here], up_out.at[:, here])
        down_v[here, :] = mlp_v[z, :, 2 * units :].astype(F32).T
        give(down_v.at[here], down_out.at[here])
    for copy in ins[1:]:
        copy.wait()
    give(tokens_v, tokens_out)
    give(output_v, output_out)
    start = 0
    for src, dst in ((q_v, q_out), (k_v, k_out), (v_v, v_out)):
        half = src.shape[1] // 2
        for h in range(2):
            src[:, h * half : (h + 1) * half] = a_v[h, :, start : start + half]
        start += half
        give(src, dst)
    half = o_v.shape[0] // 2
    for h in range(2):
        o_v[h * half : (h + 1) * half, :] = a_v[h, :, start:].T
    give(o_v, o_out)
    for copy in sent:
        copy.wait()


def layouts(q_width, kv_width, gain_sum, a, mlp, output, grad_tokens):
    block = a.shape[1]
    hidden = LINE * (mlp.shape[2] // 3)
    outs = (
        jax.ShapeDtypeStruct((block, q_width), F32),
        jax.ShapeDtypeStruct((block, kv_width), F32),
        jax.ShapeDtypeStruct((block, kv_width), F32),
        jax.ShapeDtypeStruct((q_width, block), F32),
        jax.ShapeDtypeStruct((block, hidden), F32),
        jax.ShapeDtypeStruct((block, hidden), F32),
        jax.ShapeDtypeStruct((hidden, block), F32),
    )
    ins = (a, mlp, output, grad_tokens)
    return pl.pallas_call(
        layouts_kernel,
        name="layouts",
        out_shape=(jax.ShapeDtypeStruct((1, block), F32),) * 2
        + outs
        + tuple(jax.ShapeDtypeStruct(ref.shape, ref.dtype) for ref in ins[2:]),
        in_specs=[VMEM] + [ANY] * 4,
        out_specs=(VMEM,) * 2 + (ANY,) * 9,
        scratch_shapes=[
            *[pltpu.VMEM(ref.shape, ref.dtype) for ref in ins + outs],
            DMA((4,)), DMA((3 * LINE + 6,)),
        ],
        compiler_params=pltpu.CompilerParams(vmem_limit_bytes=60 * MB),
    )(gain_sum, *ins)


def shards(
    tokens, w_query, key_weight, value_weight, w_out, gain_attn, w_gate, w_up, w_down, gain_mlp,
    cotangent, lengths, seq_of_group,
):
    count = lax.axis_size("dp")
    rows, q_width = w_query.shape
    kv_width = key_weight.shape[1]
    model = rows * count
    cos, sin = rope_tables(tokens.shape[0] * lax.axis_size("tensor"), HEAD_SIZE)
    lanes = -rows % 128
    gains = jnp.pad(jnp.stack([gain_attn, gain_mlp]), ((0, 14), (0, lanes)))
    attn_all, gate_all, up_soon, up, down_t, gains_all, tokens_all, dm_all = gather_all(
        count, lengths, seq_of_group, gains,
        (w_query, key_weight, value_weight, w_out, w_gate, w_up, w_down), tokens, cotangent,
    )
    gains_full, x1, h2, h1, qkv, probs, attended, up_rest, down = attention_forward(
        count, q_width // 2, kv_width // 2, gains_all, cos, sin, tokens_all, attn_all, up, down_t
    )
    grad_h2, out_parts, grad_mlp_w, down_sum, rows_in, inner = feed_forward(
        count, h2, dm_all.reshape(-1, model), gate_all, up_soon, up_rest, down
    )
    grad_attn_w, mlp_sum, grad_tokens, gain_parts = attention_backward(
        count, gains_full, cos, sin, grad_h2, x1, dm_all, tokens_all, h1, qkv, probs, attended, attn_all,
        grad_mlp_w, down_sum, rows_in, inner,
    )
    attn_sum, output, gain_sum = grad_sum(count, x1, grad_attn_w, out_parts, gain_parts)
    (
        grad_gain_attn, grad_gain_mlp, grad_query, grad_key, grad_value, grad_out, grad_gate, grad_up,
        grad_down, output, grad_tokens,
    ) = layouts(q_width, kv_width, gain_sum, attn_sum, mlp_sum, output, grad_tokens)
    return (
        output, grad_tokens, grad_query, grad_key, grad_value, grad_out, grad_gain_attn.reshape(rows),
        grad_gate, grad_up, grad_down, grad_gain_mlp.reshape(rows),
    )


def solution(mesh):
    both = P(("dp", "tensor"), None)
    row = P("dp", "tensor")
    column = P("tensor", "dp")
    in_specs = (
        both, row, row, row, column, P("dp"), row, row, column, P("dp"), both, P(), P("dp"),
    )
    out_specs = (both, both, row, row, row, column, P("dp"), row, row, column, P("dp"))
    return jax.shard_map(shards, mesh=mesh, in_specs=in_specs, out_specs=out_specs, check_vma=False)
```

```python
import functools
import math

import jax
import jax.numpy as jnp
import numpy as np
from jax import lax
from jax.experimental import pallas as pl
from jax.experimental.pallas import tpu as pltpu
from jax.sharding import PartitionSpec as P

HEAD_SIZE = 256
EPS = 1e-06
THETA = 1000042.0
LINE = 4
MESH = pl.DeviceIdType.MESH
BF16 = jnp.bfloat16
F32 = jnp.float32
MB = 1024 * 1024
AHEAD = 4
SOON = 2


def rope_tables(count, head_dim):
    half = head_dim // 2
    index = np.arange(half, dtype=np.float32)
    freqs = np.exp(index * np.float32(-2.0 * math.log(THETA) / head_dim))
    angles = np.arange(count, dtype=np.float32)[:, None] * freqs[None, :]
    return np.cos(angles), np.sin(angles)


def dot_tn(left, right):
    return lax.dot_general(left, right, (((0,), (0,)), ((), ())), preferred_element_type=F32)


class Place:
    def __init__(self, plane):
        self.d = lax.axis_index("dp")
        self.t = lax.axis_index("tensor")
        self.plane = plane
        self.z = lax.div(self.d, plane)
        self.p = lax.rem(self.d, plane)
        self.h = lax.rem(self.z, 2)
        if plane == 4:
            x = lax.rem(self.p, 2)
            y = lax.div(self.p, 2)
            self.px = 2 * y + 1 - x
            self.py = 2 * (1 - y) + x
            self.pd = 2 * (1 - y) + 1 - x

    def at(self, z, p):
        return (z * self.plane + p, self.t)

    def sibling(self):
        return (self.d, 1 - self.t)

    def mate(self):
        return self.at(self.z + 1 - 2 * self.h, self.p)


def remote(src, dst, send, recv, device):
    return pltpu.make_async_remote_copy(
        src_ref=src, dst_ref=dst, send_sem=send, recv_sem=recv, device_id=device, device_id_type=MESH
    )


def arrival(ref, sem):
    pltpu.make_async_copy(ref, ref, sem).wait()


def greet_all(me, count):
    barrier = pltpu.get_barrier_semaphore()
    for step in range(1, count):
        pl.semaphore_signal(
            barrier, inc=1, device_id=(lax.rem(me.d + step, count), me.t), device_id_type=MESH
        )
    pl.semaphore_signal(barrier, inc=1, device_id=me.sibling(), device_id_type=MESH)
    pl.semaphore_wait(barrier, count)


def greet_near(me):
    barrier = pltpu.get_barrier_semaphore()
    for step in range(1, me.plane):
        target = lax.rem(me.p + step, me.plane)
        pl.semaphore_signal(barrier, inc=1, device_id=me.at(me.z, target), device_id_type=MESH)
    for step in range(1, LINE):
        target = lax.rem(me.z + step, LINE)
        pl.semaphore_signal(barrier, inc=1, device_id=me.at(target, me.p), device_id_type=MESH)
    pl.semaphore_signal(barrier, inc=1, device_id=me.sibling(), device_id_type=MESH)
    pl.semaphore_wait(barrier, me.plane + LINE - 1)


def reach(me, way, k):
    return (me.z >= k, me.z - k) if way == 0 else (me.z + k < LINE, me.z + k)


class Chain:
    def __init__(self, me, first, held, send, recv, pieces=1):
        self.me, self.first, self.held, self.send, self.recv = me, first, held, send, recv
        self.pieces = pieces
        self.rows = first.shape[0] // pieces

    def piece(self, ref, i):
        return ref.at[pl.ds(i * self.rows, self.rows)]

    def copy(self, way, k, i):
        me = self.me
        _, origin = reach(me, way, k)
        target = me.z + 1 if way == 0 else me.z - 1
        src = self.first if k == 0 else self.held(origin)
        return remote(
            self.piece(src, i), self.piece(self.held(origin), i), self.send.at[way, k, i],
            self.recv.at[way, k + 1, i], me.at(target, me.p),
        )

    def goes(self, way, k):
        have, _ = reach(self.me, way, k)
        ahead, _ = reach(self.me, 1 - way, 1)
        return jnp.logical_and(have, ahead)

    def start(self, way, k, i=0):
        if k < LINE - 1:

            @pl.when(self.goes(way, k))
            def _():
                self.copy(way, k, i).start()

    def wait_block(self, way, k, i=0):
        _, origin = reach(self.me, way, k)
        arrival(self.piece(self.held(origin), i), self.recv.at[way, k, i])

    def finish(self):
        for way in range(2):
            for k in range(LINE - 1):

                @pl.when(self.goes(way, k))
                def _():
                    for i in range(self.pieces):
                        self.copy(way, k, i).wait_send()


class PlaneGather:
    def __init__(self, me, job, held, rows, send, recv):
        self.me, self.job, self.held, self.send, self.recv = me, job, held, send, recv
        self.half = rows // 2

    def piece(self, z, p, half):
        return self.held.at[z * self.me.plane + p, pl.ds(half * self.half, self.half)]

    def copy(self, z, kind, first=None):
        me = self.me
        if me.plane != 4:
            ref = first if first is not None else self.held.at[z * me.plane + me.p]
            target = lax.rem(me.p + kind + 1, me.plane)
            dst = self.held.at[z * me.plane + me.p]
        else:
            owner = (me.p, me.p, me.p, me.p, me.px, me.py)[kind]
            half = (0, 1, 1, 0, 0, 1)[kind]
            target = (me.px, me.px, me.py, me.py, me.py, me.px)[kind]
            dst = self.piece(z, owner, half)
            ref = dst if first is None else first.at[pl.ds(half * self.half, self.half)]
        return remote(
            ref, dst, self.send.at[self.job, z, kind], self.recv.at[self.job, z, kind], me.at(me.z, target)
        )

    def start(self, z, first=None):
        kinds = (0, 2, 1, 3) if self.me.plane == 4 else range(self.me.plane - 1)
        for kind in kinds:
            self.copy(z, kind, first).start()

    def forward(self, z):
        if self.me.plane == 4:
            self.copy(z, 0).wait_recv()
            self.copy(z, 4).start()
            self.copy(z, 2).wait_recv()
            self.copy(z, 5).start()

    def finish(self, zs=range(LINE)):
        kinds = 6 if self.me.plane == 4 else self.me.plane - 1
        for z in zs:
            for kind in range(kinds):
                copy = self.copy(z, kind)
                if self.me.plane != 4 or kind not in (0, 2):
                    copy.wait_recv()
                copy.wait_send()


class Quad:
    def __init__(self, me, blocks, send, recv):
        self.me, self.blocks, self.send, self.recv = me, blocks, send, recv

    def copy(self, i, first=None):
        me = self.me
        dst = self.blocks.at[me.h if i < 2 else 1 - me.h, me.t]
        device = me.mate() if i == 1 else me.sibling()
        return remote(dst if first is None else first, dst, self.send.at[i], self.recv.at[i], device)

    def start(self, first=None):
        for i in (1, 0):
            self.copy(i, first).start()

    def forward(self):
        arrival(self.blocks.at[1 - self.me.h, self.me.t], self.recv.at[1])
        self.copy(2).start()

    def finish(self):
        me = self.me
        arrival(self.blocks.at[me.h, 1 - me.t], self.recv.at[0])
        arrival(self.blocks.at[1 - me.h, 1 - me.t], self.recv.at[2])

    def finish_sends(self):
        for i in range(3):
            self.copy(i).wait_send()


class QuadSum:
    def __init__(self, me, part, from_pair, low, from_mate, send, recv):
        self.me, self.part, self.from_pair, self.low, self.from_mate = me, part, from_pair, low, from_mate
        self.send, self.recv = send, recv
        self.mate = remote(low, from_mate, send.at[2], recv.at[2], me.mate())

    def pair(self, h):
        me = self.me
        return remote(
            self.part.at[h, 1 - me.t], self.from_pair.at[h], self.send.at[h], self.recv.at[h], me.sibling()
        )

    def start(self, h):
        self.pair(h).start()

    def to_mate(self):
        me = self.me
        self.pair(1 - me.h).wait_recv()

        def act(at):
            total = self.part[1 - me.h, me.t, at, :] + self.from_pair[1 - me.h, at, :]
            self.low[at, :] = total.astype(BF16)

        row_loop(self.low.shape[0], 32, act)
        self.mate.start()

    def wait(self):
        self.pair(self.me.h).wait_recv()
        self.mate.wait_recv()

    def rows(self, at):
        me = self.me
        total = self.part[me.h, me.t, at, :] + self.from_pair[me.h, at, :]
        return total + self.from_mate[at, :].astype(F32)

    def finish_sends(self):
        for h in range(2):
            self.pair(h).wait_send()
        self.mate.wait_send()


def copy_in(src, dst, sem):
    return pltpu.make_async_copy(src, dst, sem)


def row_loop(rows, step, act):
    @pl.loop(0, rows // step)
    def _(i):
        act(pl.ds(pl.multiple_of(i * step, step), step))


def gather_kernel(
    count, len_ref, seq_ref, gain_ref, q_ref, k_ref, v_ref, o_ref, g_ref, u_ref, d_ref, tok_ref, cot_ref,
    a_all, gate_all, up_soon, up, down_t, gain_all, tok_all, dm_all, o_v, a_v, g_v, u_v, d_v, d_t, dm,
    gain_v, chain_send, chain_recv, part_send, part_recv, plane_send, plane_recv, gain_send, gain_recv,
    pair_send, pair_recv, tok_send, tok_recv, local_sem,
):
    plane = count // LINE
    me = Place(plane)
    rows = q_ref.shape[0]
    units = g_ref.shape[1] // LINE
    q_half, kv_half = q_ref.shape[1] // 2, k_ref.shape[1] // 2
    qkv_half = q_half + 2 * kv_half

    def columns(ref, z):
        return ref.at[:, pl.ds(pl.multiple_of(z * units, units), units)]

    local = [copy_in(o_ref, o_v, local_sem.at[0])]
    for h in range(2):
        start = 0
        for ref, width in ((q_ref, q_half), (k_ref, kv_half), (v_ref, kv_half)):
            src = ref.at[:, pl.ds(h * width, width)]
            local.append(copy_in(src, a_v.at[h, :, pl.ds(start, width)], local_sem.at[len(local)]))
            start += width
    early = len(local)
    for src, dst in (
        (d_ref, d_v), (cot_ref, dm), (columns(g_ref, me.z), g_v), (columns(u_ref, me.z), u_v),
        (tok_ref, tok_all.at[me.h, me.t]),
    ):
        local.append(copy_in(src, dst, local_sem.at[len(local)]))
    for copy in local[:early]:
        copy.start()
    keep_a = copy_in(a_v.at[me.h], a_all.at[me.d], local_sem.at[12])
    keep_down = copy_in(d_t, down_t, local_sem.at[13])
    keep_dm = copy_in(dm, dm_all.at[me.z, me.t], local_sem.at[14])
    keep_gate = copy_in(g_v, gate_all.at[me.d], local_sem.at[15])
    keep_up = copy_in(u_v, up.at[me.z], local_sem.at[16])
    keep_gain = copy_in(gain_v, gain_all.at[me.d], local_sem.at[17])

    dms = Chain(me, dm, lambda z: dm_all.at[z, me.t], chain_send, chain_recv)
    planes = (
        PlaneGather(me, 0, a_all, rows, plane_send, plane_recv),
        PlaneGather(me, 1, gate_all, rows, plane_send, plane_recv),
        PlaneGather(me, 2, up_soon, rows, plane_send, plane_recv),
    )

    def part(way, k, kind):
        _, target = reach(me, 1 - way, k)
        src = columns((g_ref, u_ref)[kind - 1], target) if kind else a_v.at[lax.rem(target, 2)]
        dst = (a_all.at[me.d], gate_all.at[me.d], up.at[me.z])[kind]
        return remote(
            src, dst, part_send.at[way, k, kind], part_recv.at[way, k, kind], me.at(target, me.p)
        )

    def pair(z, first=None):
        src = dm_all.at[z, me.t] if first is None else first
        return remote(src, dm_all.at[z, me.t], pair_send.at[z], pair_recv.at[z], me.sibling())

    def keep_soon(soon, src):
        return copy_in(src, up_soon.at[soon * plane + me.p], local_sem.at[18 + soon])

    def start_parts(k, kinds):
        for way in range(2):

            @pl.when(reach(me, 1 - way, k)[0])
            def _():
                for kind in kinds:
                    part(way, k, kind).start()

    def each(k, act):
        for way in range(2):
            have, z = reach(me, way, k)

            @pl.when(have)
            def _():
                act(way, k, z)

    def attn_step(way, k, z):
        arrival(a_all.at[z * plane + me.p], part_recv.at[way, k, 0])
        planes[0].start(z)

    def gate_step(way, k, z):
        arrival(gate_all.at[z * plane + me.p], part_recv.at[way, k, 1])
        planes[1].start(z)

    def up_step(way, k, z):
        arrival(up.at[z], part_recv.at[way, k, 2])

        @pl.when(z == me.z + 1 - 2 * me.h)
        def _():
            planes[2].start(1 - me.h, up.at[z])
            keep_soon(1 - me.h, up.at[z]).start()

    def dm_step(way, k, z):
        dms.wait_block(way, k)
        pair(z).start()

    def give_gain(step):
        target = lax.rem(me.d + step, count)
        return remote(
            gain_v, gain_all.at[me.d], gain_send.at[step], gain_recv.at[step], (target, me.t)
        )

    chosen = len_ref[seq_ref[0]]
    kind_of = lax.broadcasted_iota(jnp.int32, gain_ref.shape, 0)
    gain_v[...] = jnp.where(kind_of == 2, chosen.astype(F32), gain_ref[...].astype(F32)).astype(BF16)
    local[0].wait()
    for h in range(2):
        a_v[h, :, qkv_half:] = o_v[h * q_half : (h + 1) * q_half, :].T
    greet_all(me, count)
    for copy in local[1:early]:
        copy.wait()
    toks = Quad(me, tok_all, tok_send, tok_recv)
    levels = [(0, 1), (0, 2), (0, 3), (3, 1), (1, 1), (1, 2), (1, 3), (3, 2), (2, 1), (2, 2), (2, 3), (3, 3)]

    def start_level(kind, k):
        if kind < 3:
            start_parts(k, (kind,))
        elif k == 1:
            for way in range(2):
                dms.start(way, 0)
            pair(me.z, dm).start()
        else:
            each(k - 1, lambda way, k, z: dms.start(way, k))

    def finish_level(kind, k):
        each(k, (attn_step, gate_step, up_step, dm_step)[kind])

    def forward_level(kind, k):
        if kind < 2:
            each(k, lambda way, k, z: planes[kind].forward(z))

    for level in levels[:2]:
        start_level(*level)
    planes[0].start(me.z, a_v.at[me.h])
    toks.start(tok_ref)
    for step in range(1, count):
        give_gain(step).start()
    for copy in local[early:]:
        copy.start()
    keep_a.start()
    keep_gain.start()

    local[early].wait()
    for z in range(LINE):
        d_t[z] = d_v[z * units : (z + 1) * units, :].T
    keep_down.start()
    local[early + 1].wait()

    def mask(at):
        value = dm[at, :].astype(F32)
        row = lax.broadcasted_iota(jnp.int32, value.shape, 0) + (me.t * dm.shape[0] + at.start)
        dm[at, :] = jnp.where(row < chosen, value, 0.0).astype(BF16)

    row_loop(dm.shape[0], 32, mask)
    keep_dm.start()

    for i, level in enumerate(levels):
        if i == 0:
            for more in levels[2:AHEAD]:
                start_level(*more)
        finish_level(*level)
        if i + AHEAD < len(levels):
            start_level(*levels[i + AHEAD])
        if level == (0, 1):
            toks.forward()
            planes[0].forward(me.z)
            for copy in local[early + 2 : early + 4]:
                copy.wait()
            keep_gate.start()
            keep_up.start()
            planes[1].start(me.z, g_v)
        if level == (0, 3):
            planes[1].forward(me.z)
        if level == (1, 3):
            planes[2].start(me.h, u_v)
            keep_soon(me.h, u_v).start()
        if level == (3, 3):
            planes[2].forward(me.h)
        if i:
            forward_level(*levels[i - 1])
    planes[2].forward(1 - me.h)

    dms.finish()
    for k in range(1, LINE):
        for way in range(2):

            @pl.when(reach(me, 1 - way, k)[0])
            def _():
                for kind in range(3):
                    part(way, k, kind).wait_send()

    for step in range(1, count):
        give_gain(step).wait()
    toks.finish()
    toks.finish_sends()
    for z in range(LINE):
        pair(z).wait()
    for job, zs in zip(planes, (LINE, LINE, SOON)):
        job.finish(range(zs))
    for soon in range(SOON):
        keep_soon(soon, u_v).wait()
    for copy in local[early + 4 :] + [keep_a, keep_down, keep_dm, keep_gate, keep_up, keep_gain]:
        copy.wait()


ANY = pl.BlockSpec(memory_space=pl.ANY)
VMEM = pl.BlockSpec(memory_space=pltpu.VMEM)
SMEM = pl.BlockSpec(memory_space=pltpu.SMEM)
DMA = pltpu.SemaphoreType.DMA


def gather_all(count, lengths, seq, gains, weights, tokens, cotangent):
    w_query, key_weight, _, w_out, w_gate, _, w_down = weights
    rows, q_width = w_query.shape
    width = q_width + key_weight.shape[1]
    units = w_gate.shape[1] // LINE
    plane = count // LINE
    kinds = max(6, plane - 1)
    return pl.pallas_call(
        functools.partial(gather_kernel, count),
        name="gather_all",
        out_shape=(
            jax.ShapeDtypeStruct((count, rows, width), BF16),
            jax.ShapeDtypeStruct((count, rows, units), BF16),
            jax.ShapeDtypeStruct((plane * SOON, rows, units), BF16),
            jax.ShapeDtypeStruct((LINE, rows, units), BF16),
            jax.ShapeDtypeStruct((LINE, rows, units), BF16),
            jax.ShapeDtypeStruct((count,) + gains.shape, gains.dtype),
            jax.ShapeDtypeStruct((2, 2) + tokens.shape, BF16),
            jax.ShapeDtypeStruct((LINE, 2) + cotangent.shape, BF16),
        ),
        in_specs=[SMEM] * 2 + [VMEM] + [ANY] * 9,
        out_specs=(ANY,) * 8,
        scratch_shapes=[
            pltpu.VMEM(w_out.shape, BF16),
            pltpu.VMEM((2, rows, width), BF16),
            pltpu.VMEM((rows, units), BF16),
            pltpu.VMEM((rows, units), BF16),
            pltpu.VMEM(w_down.shape, BF16),
            pltpu.VMEM((LINE, rows, units), BF16),
            pltpu.VMEM(cotangent.shape, BF16),
            pltpu.VMEM(gains.shape, BF16),
            DMA((2, LINE, 1)), DMA((2, LINE, 1)), DMA((2, LINE, 3)), DMA((2, LINE, 3)),
            DMA((3, LINE, kinds)), DMA((3, LINE, kinds)), DMA((count,)), DMA((count,)),
            DMA((LINE,)), DMA((LINE,)), DMA((3,)), DMA((3,)), DMA((18 + SOON,)),
        ],
        compiler_params=pltpu.CompilerParams(
            collective_id=0, has_side_effects=True, vmem_limit_bytes=60 * MB
        ),
    )(lengths, seq, gains, *weights, tokens, cotangent)


RANKS = ((3, 2, 1, 0), (3, 0, 2, 1), (0, 3, 1, 2), (0, 1, 2, 3))
FAR_FIRST = [(way, k) for k in range(LINE - 1, 0, -1) for way in range(2)]


def ranked(me, rank):
    z = jnp.int32(RANKS[0][rank])
    for at in range(1, LINE):
        z = jnp.where(me.z == at, RANKS[at][rank], z)
    return z


def way_to(me, z):
    down = (z < me.z).astype(jnp.int32)
    return down, jnp.where(z < me.z, me.z - z, z - me.z)


def add_rows(target, terms, rows, start=0):
    step = 16

    @pl.loop(0, rows // step)
    def _(i):
        at = pl.ds(pl.multiple_of(start + i * step, step), step)
        total = terms[0][at].astype(F32)
        for term in terms[1:]:
            total += term[at].astype(F32)
        target[at] = total.astype(target.dtype)


def grad_rows(at, per, left_ref, right_ref, first, targets, there):
    tile = 512
    tokens = left_ref.shape[0]

    @pl.loop(0, per // tile)
    def _(n):
        left = left_ref[:, pl.ds(pl.multiple_of(at + n * tile, tile), tile)].T
        for job, ref, start in targets:
            block, units = ref.shape[1], right_ref.shape[1]
            rows = pl.ds(there + n * (tile // block), tile // block)
            for c in range(units // tile):
                grad = jnp.dot(
                    left, right_ref[pl.ds(first + job * tokens, tokens), c * tile : (c + 1) * tile],
                    preferred_element_type=F32,
                )
                ref[rows, :, start + c * tile : start + (c + 1) * tile] = grad.astype(BF16).reshape(
                    tile // block, block, tile
                )


class PlaneSum:
    def __init__(self, me, grad, own, other, first, second, sems, ranks=range(LINE)):
        self.me, self.grad, self.own, self.other, self.first, self.second = me, grad, own, other, first, second
        (
            self.first_send, self.first_recv, self.second_send, self.second_recv, self.load_sem, self.other_sem,
        ) = sems
        self.ranks = ranks
        self.rows = own.shape[1]
        half = self.rows // 2
        self.half = half
        self.halves = (pl.ds(0, half), pl.ds(half, half))
        self.square = me.plane == 4
        if self.square:
            self.near = (me.px, me.py)
            self.far = (me.py, me.px)

    def slot(self, rank):
        return rank - self.ranks[0]

    def block(self, rank, p):
        if callable(self.grad):
            return self.grad(rank, p)
        return self.grad.at[ranked(self.me, rank) * self.me.plane + p]

    def load(self, rank):
        s = self.slot(rank)
        return pltpu.make_async_copy(self.block(rank, self.me.p), self.own.at[s], self.load_sem.at[s])

    def load_other(self, rank, i):
        s = self.slot(rank)
        return pltpu.make_async_copy(
            self.block(rank, self.far[i]).at[self.halves[i]], self.other.at[s, self.halves[i]],
            self.other_sem.at[s, i],
        )

    def load_rank(self, rank):
        self.load(rank).start()
        if self.square:
            for i in range(2):
                self.load_other(rank, i).start()

    def load_all(self):
        for rank in self.ranks:
            self.load_rank(rank)

    def give(self, rank, i, which):
        me, s = self.me, self.slot(rank)
        if not self.square:
            target = lax.rem(me.p + which + 1, me.plane)
            return remote(
                self.block(rank, target), self.first.at[s, which], self.first_send.at[s, which],
                self.first_recv.at[s, which], me.at(me.z, target),
            )
        owner = (self.near[i], me.pd)[which]
        return remote(
            self.block(rank, owner).at[self.halves[i]], self.first.at[s, which, self.halves[i]],
            self.first_send.at[s, 2 * i + which], self.first_recv.at[s, 2 * i + which],
            me.at(me.z, self.near[i]),
        )

    def give_both(self, rank, i):
        s = self.slot(rank)
        return remote(
            self.other.at[s, self.halves[i]], self.second.at[s, self.halves[i]],
            self.second_send.at[s, i], self.second_recv.at[s, i], self.me.at(self.me.z, self.far[i]),
        )

    def gives(self, rank):
        if self.square:
            return [self.give(rank, i, which) for which in (1, 0) for i in range(2)]
        return [self.give(rank, 0, which) for which in range(self.me.plane - 1)]

    def begin(self, rank):
        for copy in self.gives(rank):
            copy.start()

    def middle(self, rank):
        if not self.square:
            return
        s = self.slot(rank)
        for i in range(2):
            arrival(self.first.at[s, 1, self.halves[i]], self.first_recv.at[s, 2 * i + 1])
            self.load_other(rank, i).wait()
            add_rows(
                self.other.at[s], (self.other.at[s], self.first.at[s, 1]), self.half, i * self.half
            )
            self.give_both(rank, i).start()

    def end(self, rank):
        s = self.slot(rank)
        self.load(rank).wait()
        if self.square:
            for i in range(2):
                arrival(self.first.at[s, 0, self.halves[i]], self.first_recv.at[s, 2 * i])
                arrival(self.second.at[s, self.halves[i]], self.second_recv.at[s, i])
            terms = (self.first.at[s, 0], self.second.at[s])
        else:
            for which in range(self.me.plane - 1):
                arrival(self.first.at[s, which], self.first_recv.at[s, which])
            terms = tuple(self.first.at[s, which] for which in range(self.me.plane - 1))
        add_rows(self.own.at[s], (self.own.at[s],) + terms, self.rows)

    def finish(self):
        for rank in self.ranks:
            for copy in self.gives(rank):
                copy.wait_send()
            if self.square:
                for i in range(2):
                    self.give_both(rank, i).wait_send()

    @staticmethod
    def scratch(count, rows, width, ranks=LINE):
        plane = count // LINE
        square = plane == 4
        slots = 2 if square else plane - 1
        small = (ranks, rows, width) if square else (1, 16, 128)
        return [
            pltpu.VMEM((ranks, rows, width), BF16),
            pltpu.VMEM(small, BF16),
            pltpu.VMEM((ranks, slots, rows, width), BF16),
            pltpu.VMEM(small, BF16),
        ], [
            DMA((ranks, max(4, slots))), DMA((ranks, max(4, slots))), DMA((ranks, 2)), DMA((ranks, 2)),
            DMA((ranks,)), DMA((ranks, 2)),
        ]


def dot_cols(left, right):
    return lax.dot_general(left, right, (((1,), (1,)), ((), ())), preferred_element_type=F32)


def feed_forward_kernel(
    plane, h_ref, dm_ref, gate_ref, up_soon, up_rest, down, total_ref, out_ref, grad_ref, sum_ref,
    h_out, inner_out, rows_in, weights, inner, down_grad, part,
    from_pair, from_line, own, other, first, second, first_send, first_recv, second_send, second_recv,
    own_sem, other_sem, chain_send, chain_recv, pass_send, pass_recv, pair_send, pair_recv,
    line_send, line_recv, plane_send, plane_recv, load_sem, dm_sem, grad_sem, out_sem, sum_sem,
):
    me = Place(plane)
    rows, model = h_ref.shape
    units = inner.shape[1]
    wide = 2 * rows
    tokens = LINE * wide
    block = down.shape[1]
    soon = up_soon.shape[0]
    tile = 512

    def slot(z, t):
        return rows_in.at[pl.ds(pl.multiple_of((z * 2 + t) * rows, rows), rows)]

    loads = [
        copy_in(gate_ref, weights.at[:, :, pl.ds(0, units)], load_sem.at[0]),
        copy_in(
            up_soon, weights.at[pl.ds((me.z - me.h) * plane, soon), :, pl.ds(units, units)], load_sem.at[2]
        ),
        copy_in(
            up_rest, weights.at[pl.ds((SOON - me.z + me.h) * plane, soon), :, pl.ds(units, units)],
            load_sem.at[3],
        ),
    ]
    own_down = [
        copy_in(
            down.at[z], weights.at[z * plane + me.p, :, pl.ds(2 * units, units)], load_sem.at[4 + z]
        )
        for z in range(LINE)
    ]
    for load in loads:
        load.start()
    load_dm = pltpu.make_async_copy(dm_ref, rows_in.at[pl.ds(tokens, tokens)], dm_sem)
    load_dm.start()
    keep = pltpu.make_async_copy(h_ref, slot(me.z, me.t), load_sem.at[1])
    keep.start()
    greet_near(me)
    gather = PlaneGather(
        me, 0, weights.at[:, :, pl.ds(2 * units, units)], block, plane_send, plane_recv
    )
    summed = PlaneSum(
        me, down_grad, own, other, first, second,
        (first_send, first_recv, second_send, second_recv, own_sem, other_sem),
    )
    chain = Chain(me, h_ref, lambda z: slot(z, me.t), chain_send, chain_recv, 2)

    def share(z, i, first=None):
        src = slot(z, me.t) if first is None else first
        return remote(
            chain.piece(src, i), chain.piece(slot(z, me.t), i), pass_send.at[z, i], pass_recv.at[z, i],
            me.sibling(),
        )

    for i in range(2):
        for way in range(2):
            chain.start(way, 0, i)
    for i in range(2):
        share(me.z, i, h_ref).start()
    for z in range(2):
        gather.start(z, down.at[z])
    for copy in own_down:
        copy.start()

    def w_rows(n, width, column):
        return weights[pl.ds(n * (width // block), width // block), :, pl.ds(column, units)].reshape(
            width, units
        )

    def pair_rows(z, job=0):
        return pl.ds(pl.multiple_of(job * tokens + z * wide, wide), wide)

    def columns(c, job):
        return weights[:, :, pl.ds(pl.multiple_of(job * units + c * tile, tile), tile)].reshape(model, tile)

    def project(z):
        @pl.loop(0, units // tile)
        def _(c):
            here = pl.ds(pl.multiple_of(c * tile, tile), tile)
            h = rows_in[pair_rows(z), :]
            gate = jnp.dot(h, columns(c, 0), preferred_element_type=F32)
            up = jnp.dot(h, columns(c, 1), preferred_element_type=F32)
            sigmoid = jax.nn.sigmoid(gate)
            silu = gate * sigmoid
            inner[pair_rows(z), here] = (silu * up).astype(BF16)
            inner[pair_rows(z, 1), here] = (up * sigmoid * (1.0 + gate * (1.0 - sigmoid))).astype(BF16)
            inner[pair_rows(z, 2), here] = silu.astype(BF16)

    def back(z):
        @pl.loop(0, units // tile)
        def _(c):
            here = pl.ds(pl.multiple_of(c * tile, tile), tile)
            grad_hidden = jnp.dot(rows_in[pair_rows(z, 1), :], columns(c, 2), preferred_element_type=F32)
            for job in range(1, 3):
                at = pair_rows(z, job)
                inner[at, here] = (grad_hidden * inner[at, here].astype(F32)).astype(BF16)

        @pl.loop(0, model // tile)
        def _(n):
            here = pl.ds(pl.multiple_of(n * tile, tile), tile)
            grad = dot_cols(inner[pair_rows(z, 1)], w_rows(n, tile, 0))
            grad += dot_cols(inner[pair_rows(z, 2)], w_rows(n, tile, units))
            part[0, z, :, :, here] = grad.astype(BF16).reshape(2, rows, tile)

        pair(z).start()

    def out(z):
        @pl.loop(0, model // tile)
        def _(n):
            here = pl.ds(pl.multiple_of(n * tile, tile), tile)
            value = dot_cols(inner[pair_rows(z), :], w_rows(n, tile, 2 * units))
            part[1, z, :, :, here] = value.astype(BF16).reshape(2, rows, tile)

        keep_out(z).start()

    def pair(z):
        return remote(
            part.at[0, z, 1 - me.t], from_pair.at[z], pair_send.at[z], pair_recv.at[z], me.sibling()
        )

    half = rows // 2
    halves = (pl.ds(0, half), pl.ds(half, half))

    def pass_on(way, k, i):
        _, target = reach(me, 1 - way, k)
        ahead = me.z + 1 if way == 0 else me.z - 1
        return remote(
            part.at[0, target, me.t, halves[i]], from_line.at[way, k - 1, halves[i]],
            line_send.at[way, k, i], line_recv.at[way, k - 1, i], me.at(ahead, me.p),
        )

    def line(way, k, behind):
        have, z = reach(me, 1 - way, k)
        before = me.z if way == 0 else LINE - 1 - me.z

        @pl.when(jnp.logical_and(have, before == behind))
        def _():
            pair(z).wait_recv()
            terms = (part.at[0, z, me.t], from_pair.at[z])
            if behind:
                terms += (from_line.at[way, k],)
            for i in range(2):
                if behind:
                    arrival(from_line.at[way, k, halves[i]], line_recv.at[way, k, i])
                add_rows(part.at[0, z, me.t], terms, half, i * half)
                pass_on(way, k, i).start()

    def total():
        pair(me.z).wait_recv()
        add_rows(total_ref, (part.at[0, me.z, me.t], from_pair.at[me.z]), rows)
        for way in range(2):

            @pl.when(reach(me, way, 1)[0])
            def _():
                for i in range(2):
                    arrival(from_line.at[way, 0, halves[i]], line_recv.at[way, 0, i])
                    add_rows(total_ref, (total_ref, from_line.at[way, 0]), half, i * half)

    per = plane * block

    def down_grads(rank):
        z = ranked(me, rank)
        grad_rows(
            z * per, per, rows_in.at[pl.ds(tokens, tokens)], inner, 0, [(0, down_grad, 0)], z * plane
        )
        summed.load_rank(rank)

    keeps = [
        copy_in(weights.at[pl.ds(0, plane), :, pl.ds(0, 2 * units)], grad_ref, grad_sem.at[0]),
        copy_in(rows_in.at[pl.ds(0, tokens)], h_out, grad_sem.at[1]),
        copy_in(inner.at[pl.ds(tokens, 2 * tokens)], inner_out, grad_sem.at[2]),
    ]

    def grads():
        targets = [(0, weights, 0), (1, weights, units)]
        z = ranked(me, 0)
        grad_rows(z * per, per, rows_in.at[pl.ds(0, tokens)], inner, tokens, targets, 0)

    def keep_sum(rank):
        return copy_in(own.at[rank], sum_ref.at[rank], sum_sem.at[rank])

    keep.wait()
    for load in loads:
        load.wait()
    for k in range(LINE):
        for way in range(2 if k else 1):
            have, z = reach(me, way, k)

            @pl.when(have)
            def _():
                for i in range(2):
                    if k:
                        chain.wait_block(way, k, i)
                        chain.start(way, k, i)
                        share(z, i).start()
                for i in range(2):
                    arrival(chain.piece(slot(z, 1 - me.t), i), pass_recv.at[z, i])
                project(z)

        gather.forward(k)
        if k + 2 < LINE:
            gather.start(k + 2, down.at[k + 2])
    def keep_out(z):
        return copy_in(part.at[1, z], out_ref.at[z], out_sem.at[z])

    load_dm.wait()
    keeps[1].start()
    down_grads(0)
    summed.begin(0)
    for copy in own_down:
        copy.wait()
    gather.finish()
    passing = {1: (1, 2), 2: (2, 1), 3: (1, 1)}
    for rank in range(LINE):
        if rank:
            down_grads(rank)
            if rank - 1 in passing:
                for way in range(2):
                    line(way, passing[rank - 1][1], passing[rank - 1][0])
            summed.middle(rank - 1)
            summed.begin(rank)
            if rank > 1:
                summed.end(rank - 2)
                keep_sum(rank - 2).start()
        back(ranked(me, rank))
        if rank < LINE - 1:
            out(ranked(me, rank))
            for way in range(2):
                line(way, LINE - 1 - rank, 0)
    for way in range(2):
        line(way, passing[LINE - 1][1], passing[LINE - 1][0])
    keeps[2].start()
    summed.middle(LINE - 1)
    summed.end(LINE - 2)
    keep_sum(LINE - 2).start()
    grads()
    keeps[0].start()
    out(ranked(me, LINE - 1))
    summed.end(LINE - 1)
    keep_sum(LINE - 1).start()
    total()
    summed.finish()
    chain.finish()
    for z in range(LINE):
        for i in range(2):
            share(z, i).wait_send()
        keep_out(z).wait()
        keep_sum(z).wait()
        pair(z).wait_send()
    for copy in keeps:
        copy.wait()
    for k in range(1, LINE):
        for way in range(2):

            @pl.when(reach(me, 1 - way, k)[0])
            def _():
                for i in range(2):
                    pass_on(way, k, i).wait_send()


def feed_forward(count, h, dm_all, gate_all, up_soon, up_rest, down):
    rows, model = h.shape
    _, block, units = down.shape
    kinds = max(6, count // LINE - 1)
    buffers, sems = PlaneSum.scratch(count, block, units)
    tokens = LINE * 2 * rows
    vmem = pl.BlockSpec(memory_space=pltpu.VMEM)
    return pl.pallas_call(
        functools.partial(feed_forward_kernel, count // LINE),
        name="feed_forward",
        out_shape=(
            jax.ShapeDtypeStruct((rows, model), F32),
            jax.ShapeDtypeStruct((LINE, 2, rows, model), BF16),
            jax.ShapeDtypeStruct((count // LINE, block, 2 * units), BF16),
            jax.ShapeDtypeStruct((LINE, block, units), BF16),
            jax.ShapeDtypeStruct((tokens, model), BF16),
            jax.ShapeDtypeStruct((2 * tokens, units), BF16),
        ),
        in_specs=[ANY] * 6,
        out_specs=(vmem,) + (ANY,) * 5,
        scratch_shapes=[
            pltpu.VMEM((2 * tokens, model), BF16),
            pltpu.VMEM((count, block, 3 * units), BF16),
            pltpu.VMEM((3 * tokens, units), BF16),
            pltpu.VMEM((count, block, units), BF16),
            pltpu.VMEM((2, LINE, 2, rows, model), BF16),
            pltpu.VMEM((LINE, rows, model), BF16),
            pltpu.VMEM((2, LINE - 1, rows, model), BF16),
            *buffers,
            *sems,
            DMA((2, LINE, 2)), DMA((2, LINE, 2)), DMA((LINE, 2)), DMA((LINE, 2)), DMA((LINE,)), DMA((LINE,)),
            DMA((2, LINE, 2)), DMA((2, LINE, 2)), DMA((1, LINE, kinds)), DMA((1, LINE, kinds)),
            DMA((4 + LINE,)), DMA, DMA((LINE,)), DMA((LINE,)), DMA((LINE,)),
        ],
        compiler_params=pltpu.CompilerParams(
            collective_id=1, has_side_effects=True, vmem_limit_bytes=60 * MB
        ),
    )(h, dm_all, gate_all, up_soon, up_rest, down)


def columns_of(weights, start, width):
    count, rows, _ = weights.shape
    return weights[:, :, pl.ds(start, width)].reshape(count * rows, width)


def rows_of(weights, n, height, start, width):
    _, rows, _ = weights.shape
    per = height // rows
    return weights[pl.ds(n * per, per), :, pl.ds(start, width)].reshape(height, width)


def attention_forward_kernel(
    plane, lens_ref, cos_ref, sin_ref, tok_in, a_ref, up, down_t, gain_ref, x1_out, h2_out, h1_out,
    qkv_out, probs_out, o_out, up_rest, down, weights, tok_ref, x1_ref, h2_ref, h1_ref, qkv_ref, probs_ref,
    o_ref, part, from_pair, low, from_mate, plane_send, plane_recv, part_send, part_recv, sum_send,
    sum_recv, load_sem, keep_sem,
):
    me = Place(plane)
    _, _, rows, model = tok_ref.shape
    wide = 2 * rows
    q_width = o_ref.shape[1]
    heads = q_width // HEAD_SIZE
    kv_width = (qkv_ref.shape[1] - q_width) // 2
    kv_heads = kv_width // HEAD_SIZE
    half = HEAD_SIZE // 2
    load_tok = copy_in(tok_in, tok_ref, load_sem.at[0])
    load_tok.start()
    load = copy_in(a_ref, weights, load_sem.at[1])
    load.start()
    far = SOON - (me.z - me.h)
    keep = [
        copy_in(up.at[far + z], up_rest.at[z * plane + me.p], load_sem.at[2 + z])
        for z in range(LINE - SOON)
    ]
    keep.append(copy_in(down_t.at[me.z], down.at[me.z], load_sem.at[2 + LINE]))
    for copy in keep:
        copy.start()
    outs = [
        copy_in(src, dst, keep_sem.at[i])
        for i, (src, dst) in enumerate(
            (
                (h1_ref, h1_out), (qkv_ref, qkv_out), (probs_ref, probs_out), (o_ref, o_out),
                (x1_ref, x1_out), (h2_ref, h2_out),
            )
        )
    ]
    greet_near(me)
    gather = PlaneGather(me, 0, up_rest, up.shape[1], plane_send, plane_recv)
    for z in range(LINE - SOON):
        gather.start(z, up.at[far + z])

    def give_down(way, k):
        _, target = reach(me, 1 - way, k)
        return remote(
            down_t.at[target], down.at[me.z], part_send.at[way, k], part_recv.at[way, k],
            me.at(target, me.p),
        )

    for k in range(1, LINE):
        for way in range(2):

            @pl.when(reach(me, 1 - way, k)[0])
            def _():
                give_down(way, k).start()

    span = model // (plane * LINE)
    for d in range(plane * LINE):
        gain_ref[:, d * span : (d + 1) * span] = lens_ref[d].astype(F32)[0:2, :span]
    load_tok.wait()

    for n in range(4):

        def norm(at, n=n):
            x = tok_ref[n // 2, n % 2, at, :].astype(F32)
            factor = lax.rsqrt(jnp.mean(x * x, -1, keepdims=True) + EPS)
            h1_ref[pl.ds(n * rows + at.start, at.size), :] = (x * factor * gain_ref[0:1, :]).astype(BF16)

        row_loop(rows, 32, norm)
    outs[0].start()
    load.wait()

    def project(i):
        start = pl.multiple_of(i * HEAD_SIZE, HEAD_SIZE)
        return start, jnp.dot(
            h1_ref[...], columns_of(weights, start, HEAD_SIZE), preferred_element_type=F32
        )

    @pl.loop(0, heads + kv_heads)
    def _(i):
        start, values = project(i)
        cos, sin = cos_ref[...], sin_ref[...]
        for n in range(2):
            at = slice(n * wide, (n + 1) * wide)
            first, second = values[at, :half], values[at, half:]
            qkv_ref[at, pl.ds(start, half)] = (first * cos - second * sin).astype(BF16)
            qkv_ref[at, pl.ds(start + half, half)] = (second * cos + first * sin).astype(BF16)

    @pl.loop(heads + kv_heads, heads + 2 * kv_heads)
    def _(i):
        start, values = project(i)
        qkv_ref[:, pl.ds(start, HEAD_SIZE)] = values.astype(BF16)

    outs[1].start()
    gather.forward(0)
    row = lax.broadcasted_iota(jnp.int32, (wide, wide), 0)
    key = lax.broadcasted_iota(jnp.int32, (wide, wide), 1)
    tile = 512
    total = QuadSum(me, part, from_pair, low, from_mate, sum_send, sum_recv)

    def attend(n):
        length = lens_ref[me.d + (n - me.h) * plane].astype(F32)[2:3, 0:1]
        allowed = jnp.logical_and(key <= row, key.astype(F32) < length)
        at = pl.ds(pl.multiple_of(n * wide, wide), wide)
        for i in range(heads):
            m = i * kv_heads // heads
            q = qkv_ref[at, i * HEAD_SIZE : (i + 1) * HEAD_SIZE]
            k = qkv_ref[at, q_width + m * HEAD_SIZE : q_width + (m + 1) * HEAD_SIZE]
            v_start = q_width + kv_width + m * HEAD_SIZE
            v = qkv_ref[at, v_start : v_start + HEAD_SIZE]
            scores = dot_cols(q, k) * HEAD_SIZE ** (-0.5)
            scores = jnp.where(allowed, scores, -1e30)
            grown = jnp.exp(scores - jnp.max(scores, -1, keepdims=True))
            probs = grown / jnp.sum(grown, -1, keepdims=True)
            probs_ref[n * heads + i] = probs
            o_ref[at, i * HEAD_SIZE : (i + 1) * HEAD_SIZE] = jnp.dot(
                probs.astype(BF16), v, preferred_element_type=F32
            ).astype(BF16)

        @pl.loop(0, model // tile)
        def _(c):
            here = pl.ds(pl.multiple_of(c * tile, tile), tile)
            value = dot_cols(o_ref[at, :], rows_of(weights, c, tile, q_width + 2 * kv_width, q_width))
            part[n, :, :, here] = value.reshape(2, rows, tile)

        total.start(n)

    attend(1 - me.h)
    total.to_mate()
    attend(me.h)
    outs[2].start()
    outs[3].start()
    for z in range(1, LINE - SOON):
        gather.forward(z)
    total.wait()

    def add(at):
        x1 = tok_ref[me.h, me.t, at, :].astype(F32) + total.rows(at)
        x1_ref[at, :] = x1
        factor = lax.rsqrt(jnp.mean(x1 * x1, -1, keepdims=True) + EPS)
        h2_ref[at, :] = (x1 * factor * gain_ref[1:2, :]).astype(BF16)

    row_loop(rows, 32, add)
    outs[4].start()
    outs[5].start()
    total.finish_sends()
    gather.finish(range(LINE - SOON))
    for k in range(1, LINE):
        for way in range(2):

            @pl.when(reach(me, 1 - way, k)[0])
            def _():
                give_down(way, k).wait_send()

            @pl.when(reach(me, way, k)[0])
            def _():
                arrival(down.at[me.z], part_recv.at[way, k])

    for copy in keep + outs:
        copy.wait()


def attention_forward(count, q_width, kv_width, lens, cos, sin, tokens_all, attn_all, up, down_t):
    _, _, rows, model = tokens_all.shape
    wide = 2 * rows
    plane = count // LINE
    kinds = max(6, plane - 1)
    outs = (
        jax.ShapeDtypeStruct((rows, model), F32),
        jax.ShapeDtypeStruct((rows, model), BF16),
        jax.ShapeDtypeStruct((2 * wide, model), BF16),
        jax.ShapeDtypeStruct((2 * wide, q_width + 2 * kv_width), BF16),
        jax.ShapeDtypeStruct((2 * q_width // HEAD_SIZE, wide, wide), F32),
        jax.ShapeDtypeStruct((2 * wide, q_width), BF16),
    )
    return pl.pallas_call(
        functools.partial(attention_forward_kernel, plane),
        name="attention_forward",
        out_shape=(jax.ShapeDtypeStruct((2, model), F32),)
        + outs
        + (
            jax.ShapeDtypeStruct((count - SOON * plane,) + up.shape[1:], BF16),
            jax.ShapeDtypeStruct(down_t.shape, BF16),
        ),
        in_specs=[VMEM] * 3 + [ANY] * 4,
        out_specs=(VMEM,) + (ANY,) * 8,
        scratch_shapes=[
            pltpu.VMEM(attn_all.shape, BF16),
            pltpu.VMEM(tokens_all.shape, BF16),
            *[pltpu.VMEM(out.shape, out.dtype) for out in outs],
            pltpu.VMEM((2, 2, rows, model), F32),
            pltpu.VMEM((2, rows, model), F32),
            pltpu.VMEM((rows, model), BF16),
            pltpu.VMEM((rows, model), BF16),
            DMA((1, LINE, kinds)), DMA((1, LINE, kinds)), DMA((2, LINE)), DMA((2, LINE)), DMA((3,)),
            DMA((3,)), DMA((3 + LINE,)), DMA((6,)),
        ],
        compiler_params=pltpu.CompilerParams(
            collective_id=2, has_side_effects=True, vmem_limit_bytes=60 * MB
        ),
    )(lens, cos, sin, tokens_all, attn_all, up, down_t)


def attention_backward_kernel(
    plane, gain_ref, cos_ref, sin_ref, total_in, x1_in, dm_in, tok_in, h1_in, qkv_in, probs_in, o_in,
    a_ref, gw_ref, sum_ref, h_in, inner_in, ga_ref, w_out, grad_tokens, gain_blocks, gain_parts, weights, own, other, first, second,
    total_ref, x1_ref, dm_ref, tok_ref, h1_ref, qkv_ref, probs_ref, o_ref, rows_in, inner, gw, dx, da, do,
    dqkv, dh1, from_pair, low, from_mate, first_send, first_recv, second_send, second_recv, load_sem,
    other_sem, part_send, part_recv, da_send, da_recv, sum_send, sum_recv, a_sem, keep_sem, grad_sem, in_sem,
):
    me = Place(plane)
    rows, model = tok_ref.shape
    block = weights.shape[1]
    q_width = o_ref.shape[1]
    heads = q_width // HEAD_SIZE
    seq = 2 * rows
    qkv_width = qkv_ref.shape[1]
    kv_width = (qkv_width - q_width) // 2
    kv_heads = kv_width // HEAD_SIZE
    half = HEAD_SIZE // 2
    scale = HEAD_SIZE ** (-0.5)
    summed = PlaneSum(
        me, lambda rank, p: gw.at[(rank - 1) * plane + p] if rank else gw_ref.at[p],
        own, other, first, second,
        (first_send, first_recv, second_send, second_recv, load_sem, other_sem),
    )
    ins = [
        copy_in(src, dst, in_sem.at[i])
        for i, (src, dst) in enumerate(
            (
                (total_in, total_ref), (x1_in, x1_ref), (dm_in.at[me.z, me.t], dm_ref),
                (tok_in.at[me.h, me.t], tok_ref),
                (h1_in, h1_ref), (qkv_in, qkv_ref), (probs_in, probs_ref), (o_in, o_ref),
                (h_in, rows_in), (inner_in, inner),
            )
        )
    ]
    for copy in ins[:3] + ins[8:]:
        copy.start()
    load = pltpu.make_async_copy(a_ref, weights, a_sem)
    load.start()
    for copy in ins[3:8]:
        copy.start()
    summed.load_rank(0)
    greet_near(me)

    wide = own.shape[2]
    spans = (pl.ds(0, wide), pl.ds(wide, sum_ref.shape[2]))

    def part(rank, kind):
        target = ranked(me, rank)
        way, k = way_to(me, target)
        return remote(
            (own, sum_ref)[kind].at[rank], w_out.at[me.z, :, spans[kind]], part_send.at[way, k, kind],
            part_recv.at[way, k, kind], me.at(target, me.p),
        )

    keeps = [
        copy_in((own, sum_ref)[kind].at[LINE - 1], w_out.at[me.z, :, spans[kind]], keep_sem.at[kind])
        for kind in range(2)
    ]
    das = Quad(me, da, da_send, da_recv)
    dh1_sum = QuadSum(me, dh1, from_pair, low, from_mate, sum_send, sum_recv)

    def mid_norm():
        gain_parts[...] = jnp.zeros_like(gain_parts)

        def act(at):
            x, up = x1_ref[at, :], total_ref[at, :]
            factor = lax.rsqrt(jnp.mean(x * x, -1, keepdims=True) + EPS)
            scaled = up * gain_ref[1:2, :]
            grad = dm_ref[at, :].astype(F32) + (
                factor * scaled - x * factor**3 * jnp.mean(scaled * x, -1, keepdims=True)
            )
            dx[at, :] = grad
            da[me.h, me.t, at, :] = grad.astype(BF16)
            gain_parts[1:2, :] += jnp.sum(up * x * factor, 0, keepdims=True)

        row_loop(rows, 32, act)
        das.start()

    def grad_o():
        load.wait()
        das.finish()

        @pl.loop(0, q_width // HEAD_SIZE)
        def _(c):
            here = pl.multiple_of(c * HEAD_SIZE, HEAD_SIZE)
            value = jnp.dot(
                da[...].reshape(2 * seq, model),
                columns_of(weights, qkv_width + here, HEAD_SIZE),
                preferred_element_type=F32,
            )
            do[:, pl.ds(here, HEAD_SIZE)] = value.astype(BF16)

    def rotate(values, rows_at, start):
        first, second = values[:, :half], values[:, half:]
        cos, sin = cos_ref[...], sin_ref[...]
        dqkv[rows_at, start : start + half] = (first * cos + second * sin).astype(BF16)
        dqkv[rows_at, start + half : start + 2 * half] = (second * cos - first * sin).astype(BF16)

    def grad_heads(n):
        group = heads // kv_heads
        here = slice(n * seq, (n + 1) * seq)
        for m in range(kv_heads):
            at_k = q_width + m * HEAD_SIZE
            at_v = at_k + kv_width
            k = qkv_ref[here, at_k : at_k + HEAD_SIZE]
            v = qkv_ref[here, at_v : at_v + HEAD_SIZE]
            grad_k = grad_v = None
            for i in range(m * group, (m + 1) * group):
                at = slice(i * HEAD_SIZE, (i + 1) * HEAD_SIZE)
                probs = probs_ref[n * heads + i]
                grad_probs = dot_cols(do[here, at], v)
                grad_scores = probs * (
                    grad_probs - jnp.sum(probs * grad_probs, -1, keepdims=True)
                )
                low_scores = grad_scores.astype(BF16)
                rotate(
                    jnp.dot(low_scores, k, preferred_element_type=F32) * scale, here, i * HEAD_SIZE
                )
                more_k = dot_tn(low_scores, qkv_ref[here, at])
                more_v = dot_tn(probs.astype(BF16), do[here, at])
                grad_k = more_k if grad_k is None else grad_k + more_k
                grad_v = more_v if grad_v is None else grad_v + more_v
            rotate(grad_k * scale, here, at_k)
            dqkv[here, at_v : at_v + HEAD_SIZE] = grad_v.astype(BF16)

    tile = 512

    def grad_h1():
        @pl.loop(0, model // tile)
        def _(n):
            here = pl.ds(pl.multiple_of(n * tile, tile), tile)
            value = dot_cols(dqkv[...], rows_of(weights, n, tile, 0, qkv_width))
            dh1[:, :, :, here] = value.reshape(2, 2, rows, tile)

        for h in range(2):
            dh1_sum.start(h)

    def keep_grads(n):
        per = tile // block
        return pltpu.make_async_copy(
            weights.at[pl.ds(n * per, per)], ga_ref.at[pl.ds(n * per, per)], grad_sem.at[n]
        )

    def grads():
        @pl.loop(0, model // tile)
        def _(n):
            here = pl.ds(pl.multiple_of(n * tile, tile), tile)
            there = pl.ds(n * (tile // block), tile // block)
            left = h1_ref[:, here].T
            for c in range(qkv_width // tile):
                at = slice(c * tile, (c + 1) * tile)
                value = jnp.dot(left, dqkv[:, at], preferred_element_type=F32)
                weights[there, :, at] = value.astype(BF16).reshape(tile // block, block, tile)
            left = da[:, :, :, here].reshape(2 * seq, tile).T
            for c in range(q_width // tile):
                at = slice(c * tile, (c + 1) * tile)
                value = jnp.dot(left, o_ref[:, at], preferred_element_type=F32)
                at = slice(qkv_width + c * tile, qkv_width + (c + 1) * tile)
                weights[there, :, at] = value.astype(BF16).reshape(tile // block, block, tile)

        for n in range(model // tile):
            keep_grads(n).start()

    def in_norm():
        dh1_sum.wait()

        def act(at):
            x = tok_ref[at, :].astype(F32)
            up = dh1_sum.rows(at)
            factor = lax.rsqrt(jnp.mean(x * x, -1, keepdims=True) + EPS)
            scaled = up * gain_ref[0:1, :]
            grad_tokens[at, :] = dx[at, :] + (
                factor * scaled - x * factor**3 * jnp.mean(scaled * x, -1, keepdims=True)
            )
            gain_parts[0:1, :] += jnp.sum(up * x * factor, 0, keepdims=True)

        row_loop(rows, 32, act)

    summed.begin(0)
    for rank in range(LINE - 1):
        part(rank, 1).start()
    keeps[1].start()
    def mlp_grads(rank):
        per = plane * block
        targets = [(0, gw, 0), (1, gw, inner.shape[1])]
        z = ranked(me, rank)
        grad_rows(z * per, per, rows_in, inner, 0, targets, (rank - 1) * plane)
        summed.load_rank(rank)

    for copy in ins[:3]:
        copy.wait()
    mid_norm()
    for copy in ins[8:]:
        copy.wait()
    mlp_grads(1)
    summed.middle(0)
    summed.begin(1)
    mlp_grads(2)
    das.forward()
    for copy in ins[3:8]:
        copy.wait()
    summed.end(0)
    part(0, 0).start()
    grad_o()
    summed.middle(1)
    summed.begin(2)
    grad_heads(0)
    grad_heads(1)
    mlp_grads(3)
    summed.end(1)
    part(1, 0).start()
    grad_h1()
    summed.middle(2)
    summed.begin(3)
    dh1_sum.to_mate()
    grads()
    summed.end(2)
    part(2, 0).start()
    summed.middle(3)
    in_norm()
    summed.end(3)

    span = model // gain_blocks.shape[0]
    gain_blocks[...] = jnp.zeros_like(gain_blocks)
    for d in range(gain_blocks.shape[0]):
        gain_blocks[d, 0:2, :span] = gain_parts[:, d * span : (d + 1) * span]
    keeps[0].start()
    for kind in range(2):
        for rank in range(LINE - 1):
            part(rank, kind).wait_send()
        for way, k in FAR_FIRST:

            @pl.when(reach(me, way, k)[0])
            def _():
                arrival(w_out.at[me.z, :, spans[kind]], part_recv.at[way, k, kind])

    summed.finish()
    das.finish_sends()
    dh1_sum.finish_sends()
    for n in range(model // tile):
        keep_grads(n).wait()
    for copy in keeps:
        copy.wait()


def attention_backward(
    count, gains, cos, sin, total, x1, dm_all, tokens_all, h1, qkv, probs, o, attn_all, grad_mlp, first_sum, rows_in,
    inner,
):
    _, _, rows, model = tokens_all.shape
    _, block, _ = attn_all.shape
    buffers, sems = PlaneSum.scratch(count, block, grad_mlp.shape[2])
    return pl.pallas_call(
        functools.partial(attention_backward_kernel, count // LINE),
        name="attention_backward",
        out_shape=(
            jax.ShapeDtypeStruct(attn_all.shape, BF16),
            jax.ShapeDtypeStruct((LINE, block, grad_mlp.shape[2] + first_sum.shape[2]), BF16),
            jax.ShapeDtypeStruct((rows, model), F32),
            jax.ShapeDtypeStruct((count, 8, max(128, model // count)), F32),
        ),
        in_specs=[VMEM] * 3 + [ANY] * 13,
        out_specs=(ANY, ANY, VMEM, VMEM),
        scratch_shapes=[
            pltpu.VMEM((2, model), F32),
            pltpu.VMEM(attn_all.shape, BF16),
            *buffers,
            *[
                pltpu.VMEM(ref.shape, ref.dtype)
                for ref in (total, x1, dm_all[0, 0], dm_all[0, 0], h1, qkv, probs, o, rows_in, inner)
            ],
            pltpu.VMEM(((LINE - 1) * grad_mlp.shape[0],) + grad_mlp.shape[1:], BF16),
            pltpu.VMEM((rows, model), F32),
            pltpu.VMEM((2, 2, rows, model), BF16),
            pltpu.VMEM(o.shape, BF16),
            pltpu.VMEM(qkv.shape, BF16),
            pltpu.VMEM((2, 2, rows, model), F32),
            pltpu.VMEM((2, rows, model), F32),
            pltpu.VMEM((rows, model), BF16),
            pltpu.VMEM((rows, model), BF16),
            *sems,
            DMA((2, LINE, 2)), DMA((2, LINE, 2)), DMA((3,)), DMA((3,)), DMA((3,)), DMA((3,)), DMA, DMA((2,)),
            DMA((model // 512,)), DMA((10,)),
        ],
        compiler_params=pltpu.CompilerParams(
            collective_id=3, has_side_effects=True, vmem_limit_bytes=60 * MB
        ),
    )(gains, cos, sin, total, x1, dm_all, tokens_all, h1, qkv, probs, o, attn_all, grad_mlp, first_sum, rows_in, inner)


def grad_sum_kernel(
    count, gain_ref, x1_in, ga_ref, out_ref, a_out, output, gain_out, own, other, first, second, x1_ref,
    landed, out_own, out_pair, out_line, gain_in, gain_pair, first_send, first_recv, second_send, second_recv,
    load_sem, other_sem, part_send, part_recv, out_send, out_recv, load_out_sem, pair_send, pair_recv, gain_send, gain_recv,
):
    plane = count // LINE
    me = Place(plane)
    rows = a_out.shape[1]
    summed = PlaneSum(
        me, ga_ref, own, other, first, second,
        (first_send, first_recv, second_send, second_recv, load_sem, other_sem),
    )

    class Line:
        def __init__(self, held, landing, send, recv):
            self.held, self.landing, self.send, self.recv = held, landing, send, recv

        def pass_on(self, rank):
            way, k = way_to(me, ranked(me, rank))
            ahead = jnp.where(way == 0, me.z + 1, me.z - 1)
            return remote(
                self.held(rank), self.landing.at[way, k - 1], self.send.at[way, k],
                self.recv.at[way, k - 1], me.at(ahead, me.p),
            )

        def step(self, rank):
            way, k = way_to(me, ranked(me, rank))
            before = jnp.where(way == 0, me.z, LINE - 1 - me.z)
            held = self.held(rank)

            @pl.when(before > 0)
            def _():
                arrival(self.landing.at[way, k], self.recv.at[way, k])
                add_rows(held, (held, self.landing.at[way, k]), held.shape[0])

            self.pass_on(rank).start()

        def total(self, act):
            for way in range(2):

                @pl.when(reach(me, way, 1)[0])
                def _():
                    arrival(self.landing.at[way, 0], self.recv.at[way, 0])
                    act(self.landing.at[way, 0])

        def finish(self):
            for rank in range(LINE - 1):
                self.pass_on(rank).wait_send()

    def part(rank):
        target = ranked(me, rank)
        way, k = way_to(me, target)
        return remote(
            own.at[rank], landed.at[me.z], part_send.at[way, k], part_recv.at[way, k],
            me.at(target, me.p),
        )

    outs = Line(lambda rank: out_own.at[ranked(me, rank)], out_line, out_send, out_recv)
    summed.load_all()
    load_out = copy_in(out_ref.at[:, me.t], out_own, load_out_sem.at[0])
    load_out.start()
    load_x1 = copy_in(x1_in, x1_ref, load_out_sem.at[1])
    load_x1.start()
    greet_all(me, count)

    def give_gain(step):
        target = lax.rem(me.d + step, count)
        return remote(
            gain_ref.at[target], gain_in.at[step], gain_send.at[step], gain_recv.at[step], (target, me.t)
        )

    summed.begin(0)
    for step in range(1, count):
        give_gain(step).start()
    pairs = [
        remote(
            out_ref.at[ranked(me, rank), 1 - me.t], out_pair.at[ranked(me, rank)], pair_send.at[rank],
            pair_recv.at[rank], me.sibling(),
        )
        for rank in range(LINE)
    ]
    for copy in pairs:
        copy.start()
    load_out.wait()
    def out_step(rank):
        z = ranked(me, rank)
        pairs[rank].wait_recv()
        add_rows(out_own.at[z], (out_own.at[z], out_pair.at[z]), out_own.shape[1])
        if rank < LINE - 1:

            @pl.when(jnp.logical_or(me.z == 0, me.z == LINE - 1))
            def _():
                outs.step(rank)

    out_step(0)
    at_end = jnp.logical_or(me.z == 0, me.z == LINE - 1)

    def out_start(at):
        x1_ref[at, :] = x1_ref[at, :] + out_own[me.z, at, :].astype(F32)

    def add_out(landed):
        def act(at):
            x1_ref[at, :] = x1_ref[at, :] + landed[at, :].astype(F32)

        row_loop(output.shape[0], 16, act)

    def out_end(at):
        output[at, :] = x1_ref[at, :].astype(BF16)

    for rank in range(LINE):
        summed.middle(rank)
        if rank + 1 < LINE:
            summed.begin(rank + 1)
            out_step(rank + 1)
        else:
            load_x1.wait()
            total = gain_ref[me.d]
            for step in range(1, count):
                give_gain(step).wait()
                total += gain_in[step]
            gain_pair[0] = total
            swap = remote(
                gain_pair.at[0], gain_pair.at[1], gain_send.at[0], gain_recv.at[0], me.sibling()
            )
            swap.start()
            swap.wait()
            gain_out[...] = gain_pair[0] + gain_pair[1]
        summed.end(rank)
        if rank < LINE - 1:
            part(rank).start()
        for late in {0: (0,), 1: (2, 1)}.get(rank, ()):
            @pl.when(jnp.logical_not(at_end))
            def _():
                outs.step(late)


    row_loop(output.shape[0], 16, out_start)
    outs.total(add_out)
    row_loop(output.shape[0], 16, out_end)
    keep = copy_in(own.at[LINE - 1], landed.at[me.z], load_out_sem.at[2])
    keep.start()
    for way, k in FAR_FIRST:
        have, z = reach(me, way, k)

        @pl.when(have)
        def _():
            arrival(landed.at[z], part_recv.at[way, k])

    keep.wait()
    for h in range(2):
        add_rows(a_out.at[h], tuple(landed.at[z] for z in range(h, LINE, 2)), rows)
    for rank in range(LINE - 1):
        part(rank).wait_send()
    for copy in pairs:
        copy.wait_send()
    outs.finish()
    summed.finish()


def grad_sum(count, x1, ga, out_parts, gains):
    _, block, width = ga.shape
    _, _, rows, model = out_parts.shape
    buffers, sems = PlaneSum.scratch(count, block, width)
    return pl.pallas_call(
        functools.partial(grad_sum_kernel, count),
        name="grad_sum",
        out_shape=(
            jax.ShapeDtypeStruct((2, block, width), F32),
            jax.ShapeDtypeStruct((rows, model), BF16),
            jax.ShapeDtypeStruct(gains.shape[1:], F32),
        ),
        in_specs=[VMEM] + [ANY] * 3,
        out_specs=(VMEM,) * 3,
        scratch_shapes=[
            *buffers,
            pltpu.VMEM((rows, model), F32),
            pltpu.VMEM((LINE, block, width), BF16),
            pltpu.VMEM((LINE, rows, model), BF16),
            pltpu.VMEM((LINE, rows, model), BF16),
            pltpu.VMEM((2, LINE - 1, rows, model), BF16),
            pltpu.VMEM(gains.shape, F32),
            pltpu.VMEM((2,) + gains.shape[1:], F32),
            *sems,
            DMA((2, LINE)), DMA((2, LINE)), DMA((2, LINE)), DMA((2, LINE)), DMA((3,)), DMA((LINE,)),
            DMA((LINE,)), DMA((count,)), DMA((count,)),
        ],
        compiler_params=pltpu.CompilerParams(
            collective_id=4, has_side_effects=True, vmem_limit_bytes=60 * MB
        ),
    )(gains, x1, ga, out_parts)


def layouts_kernel(
    gain_ref, a_ref, mlp_ref, output_ref, tokens_ref, gain_attn, gain_mlp, q_out, k_out, v_out, o_out, gate_out, up_out, down_out,
    output_out, tokens_out, a_v, mlp_v, output_v, tokens_v, q_v, k_v, v_v, o_v, gate_v, up_v, down_v,
    in_sem, out_sem,
):
    ins = [
        copy_in(src, dst, in_sem.at[i])
        for i, (src, dst) in enumerate(
            ((mlp_ref, mlp_v), (a_ref, a_v), (tokens_ref, tokens_v), (output_ref, output_v))
        )
    ]
    for copy in ins:
        copy.start()
    sent = []

    def give(src, dst):
        sent.append(copy_in(src, dst, out_sem.at[len(sent)]))
        sent[-1].start()

    span = gain_attn.shape[1]
    gain_attn[...] = gain_ref[0:1, :span]
    gain_mlp[...] = gain_ref[1:2, :span]
    units = mlp_v.shape[2] // 3
    ins[0].wait()
    for z in range(LINE):
        here = pl.ds(z * units, units)
        gate_v[:, here] = mlp_v[z, :, :units].astype(F32)
        give(gate_v.at[:, here], gate_out.at[:, here])
        up_v[:, here] = mlp_v[z, :, units : 2 * units].astype(F32)
        give(up_v.at[:, here], up_out.at[:, here])
        down_v[here, :] = mlp_v[z, :, 2 * units :].astype(F32).T
        give(down_v.at[here], down_out.at[here])
    for copy in ins[1:]:
        copy.wait()
    give(tokens_v, tokens_out)
    give(output_v, output_out)
    start = 0
    for src, dst in ((q_v, q_out), (k_v, k_out), (v_v, v_out)):
        half = src.shape[1] // 2
        for h in range(2):
            src[:, h * half : (h + 1) * half] = a_v[h, :, start : start + half]
        start += half
        give(src, dst)
    half = o_v.shape[0] // 2
    for h in range(2):
        o_v[h * half : (h + 1) * half, :] = a_v[h, :, start:].T
    give(o_v, o_out)
    for copy in sent:
        copy.wait()


def layouts(q_width, kv_width, gain_sum, a, mlp, output, grad_tokens):
    block = a.shape[1]
    hidden = LINE * (mlp.shape[2] // 3)
    outs = (
        jax.ShapeDtypeStruct((block, q_width), F32),
        jax.ShapeDtypeStruct((block, kv_width), F32),
        jax.ShapeDtypeStruct((block, kv_width), F32),
        jax.ShapeDtypeStruct((q_width, block), F32),
        jax.ShapeDtypeStruct((block, hidden), F32),
        jax.ShapeDtypeStruct((block, hidden), F32),
        jax.ShapeDtypeStruct((hidden, block), F32),
    )
    ins = (a, mlp, output, grad_tokens)
    return pl.pallas_call(
        layouts_kernel,
        name="layouts",
        out_shape=(jax.ShapeDtypeStruct((1, block), F32),) * 2
        + outs
        + tuple(jax.ShapeDtypeStruct(ref.shape, ref.dtype) for ref in ins[2:]),
        in_specs=[VMEM] + [ANY] * 4,
        out_specs=(VMEM,) * 2 + (ANY,) * 9,
        scratch_shapes=[
            *[pltpu.VMEM(ref.shape, ref.dtype) for ref in ins + outs],
            DMA((4,)), DMA((3 * LINE + 6,)),
        ],
        compiler_params=pltpu.CompilerParams(vmem_limit_bytes=60 * MB),
    )(gain_sum, *ins)


def shards(
    tokens, w_query, key_weight, value_weight, w_out, gain_attn, w_gate, w_up, w_down, gain_mlp,
    cotangent, lengths, seq_of_group,
):
    count = lax.axis_size("dp")
    rows, q_width = w_query.shape
    kv_width = key_weight.shape[1]
    model = rows * count
    cos, sin = rope_tables(tokens.shape[0] * lax.axis_size("tensor"), HEAD_SIZE)
    lanes = -rows % 128
    gains = jnp.pad(jnp.stack([gain_attn, gain_mlp]), ((0, 14), (0, lanes)))
    attn_all, gate_all, up_soon, up, down_t, gains_all, tokens_all, dm_all = gather_all(
        count, lengths, seq_of_group, gains,
        (w_query, key_weight, value_weight, w_out, w_gate, w_up, w_down), tokens, cotangent,
    )
    gains_full, x1, h2, h1, qkv, probs, attended, up_rest, down = attention_forward(
        count, q_width // 2, kv_width // 2, gains_all, cos, sin, tokens_all, attn_all, up, down_t
    )
    grad_h2, out_parts, grad_mlp_w, down_sum, rows_in, inner = feed_forward(
        count, h2, dm_all.reshape(-1, model), gate_all, up_soon, up_rest, down
    )
    grad_attn_w, mlp_sum, grad_tokens, gain_parts = attention_backward(
        count, gains_full, cos, sin, grad_h2, x1, dm_all, tokens_all, h1, qkv, probs, attended, attn_all,
        grad_mlp_w, down_sum, rows_in, inner,
    )
    attn_sum, output, gain_sum = grad_sum(count, x1, grad_attn_w, out_parts, gain_parts)
    (
        grad_gain_attn, grad_gain_mlp, grad_query, grad_key, grad_value, grad_out, grad_gate, grad_up,
        grad_down, output, grad_tokens,
    ) = layouts(q_width, kv_width, gain_sum, attn_sum, mlp_sum, output, grad_tokens)
    return (
        output, grad_tokens, grad_query, grad_key, grad_value, grad_out, grad_gain_attn.reshape(rows),
        grad_gate, grad_up, grad_down, grad_gain_mlp.reshape(rows),
    )


def solution(mesh):
    both = P(("dp", "tensor"), None)
    row = P("dp", "tensor")
    column = P("tensor", "dp")
    in_specs = (
        both, row, row, row, column, P("dp"), row, row, column, P("dp"), both, P(), P("dp"),
    )
    out_specs = (both, both, row, row, row, column, P("dp"), row, row, column, P("dp"))
    return jax.shard_map(shards, mesh=mesh, in_specs=in_specs, out_specs=out_specs, check_vma=False)
```
